32 devices in a mesh: scan: 4 (over y, x), blk: 8 (over z, core).
Axes of the slice: x: 2, y: 2, z: 4, core: 2. Of those that a mesh axis runs over, the one named last changes fastest.
Arguments:
- ref_feats: bfloat16 [4, 4096, 256], P('scan', 'blk'), may hold values from -120 to 120
- src_feats: bfloat16 [4, 1024, 256], P('scan', 'blk'), may hold values from -120 to 120
- grad_out: bfloat16 [4, 4096, 256], P('scan', 'blk'), may hold values from -6 to 6
- w_query: bfloat16 [256, 256], replicated, may hold values from -1 to 1
- w_key: bfloat16 [256, 256], replicated, may hold values from -1 to 1
- w_value: bfloat16 [256, 256], replicated, may hold values from -0.375 to 0.375
- w_out: bfloat16 [256, 256], replicated, may hold values from -0.375 to 0.375
- intersection: int32 [4, 32, 8], P('scan', 'blk'), may hold values from 0 to 1, as said below
Outputs:
- matched: bfloat16 [4, 4096, 256], P('scan', 'blk')
- grad_ref: bfloat16 [4, 4096, 256], P('scan', 'blk')
- grad_src: bfloat16 [4, 1024, 256], P('scan', 'blk')
- grad_w_query: float32 [256, 256], replicated
- grad_w_key: float32 [256, 256], replicated
- grad_w_value: float32 [256, 256], replicated
- grad_w_out: float32 [256, 256], replicated
The draws below stay inside these ranges and needn't reach their ends.
Inputs may be any that keep to these rules, and one draw needn't show every extreme that they name: intersection[p, b, c] is 1 for c = b * 8 // 32, so every reference block and every source block of a pair has a listed partner.
All inputs are finite; a program needn't handle non-finite values.
Results may differ from the reference program's by a relative error of at most 0.035.
Values may be sent and summed in bfloat16 or wider, within the bound.
No kernel may reach another device: no remote copies, remote signals or barrier semaphores. Data moves between devices by JAX's collectives and lax.ppermute only.
A program may use at most 64 MiB of HBM per device.

```python
import math
import jax
import jax.numpy as jnp
from jax import lax

D = 256
HEADS = 4
HEAD_DIM = 64
BLOCK = 128
PAIRS = 4
NQ = 4096
NK = 1024
NQB = 32
NKB = 8


def spread_scales(key, shape):
    return jnp.exp(jax.random.uniform(key, shape, jnp.float32, math.log(0.3), math.log(3.0)))


def base_values(key, shape):
    return jax.random.normal(key, shape, jnp.float32)


def source_values(key):
    values_out = base_values(jax.random.fold_in(key, 601), (PAIRS, NK, D))
    values_out = values_out * spread_scales(jax.random.fold_in(key, 602), (PAIRS, NK))[:, :, None]
    return jnp.clip(values_out, -120.0, 120.0)


def draw_src_feats(key, part):
    return source_values(key).astype(jnp.bfloat16)


def draw_ref_feats(key, part):
    position = 0.6 + 1.2 * jnp.arange(NQ, dtype=jnp.float32) / NQ
    row_scale = spread_scales(jax.random.fold_in(key, 702), (PAIRS, NQ)) * position[None, :]
    values_out = base_values(jax.random.fold_in(key, 701), (PAIRS, NQ, D)) * row_scale[:, :, None]
    return jnp.clip(values_out, -120.0, 120.0).astype(jnp.bfloat16)


def draw_w_query(key, part):
    return (jax.random.normal(jax.random.fold_in(key, 801), (D, D), jnp.float32) / math.sqrt(D)).astype(jnp.bfloat16)


def draw_w_key(key, part):
    return (jax.random.normal(jax.random.fold_in(key, 803), (D, D), jnp.float32) / math.sqrt(D)).astype(jnp.bfloat16)


def draw_intersection(key, part):
    query_block = jnp.arange(NQB)
    key_block = jnp.arange(NKB)
    band_block = query_block * NKB // NQB
    run_start = jax.random.randint(jax.random.fold_in(key, 901), (PAIRS, NQB), 0, NKB)
    run_length = jax.random.randint(jax.random.fold_in(key, 902), (PAIRS, NQB), 0, NKB // 2 + 1)
    offset = (key_block[None, None, :] - run_start[:, :, None]) % NKB
    listed = (offset < run_length[:, :, None]) | (key_block[None, None, :] == band_block[None, :, None])
    return listed.astype(jnp.int32)


def with_spikes(values, own_key, source, target, parts, factor):
    def block_of(axis_at):
        return (jnp.arange(values.shape[axis_at]) // (values.shape[axis_at] // parts)).reshape((-1,) + (1,) * (values.ndim - 1 - axis_at))

    near = jax.random.permutation(own_key, parts)[block_of(target)]
    other_side = (block_of(target) + parts // 2) % parts
    return jnp.where((block_of(source) == near) | (block_of(source) == other_side), factor * values, values)


def levels(key, extent, split, low, high):
    def one(dim, shards_of):
        heights = jax.random.uniform(jax.random.fold_in(jax.random.fold_in(key, 6), dim), (shards_of,), jnp.float32, low / len(split), high / len(split))
        return jnp.repeat(jnp.exp(heights), extent[dim] // shards_of).reshape((-1,) + (1,) * (len(extent) - dim - 1))

    gain = one(*split[0])
    for cut in split[1:]:
        gain = gain * one(*cut)
    return gain


def bell_draw(own_key, shape, spread, limit, shards=(), kind=jnp.bfloat16):
    loudness = levels(own_key, shape, shards, -0.22, 0.18) if shards else 1.0
    entries = jax.random.normal(own_key, shape, jnp.float32) * spread * loudness
    return jnp.minimum(jnp.maximum(entries, -limit), limit).astype(kind)


def noise_with(key, dims, width, bound, cuts, heavy, kind=jnp.bfloat16):
    values = width * jax.random.normal(key, dims, jnp.float32)
    if cuts:
        values = values * levels(key, dims, cuts, -0.22, 0.18)
    return jnp.clip(with_spikes(values, jax.random.fold_in(key, 3), *heavy), -bound, bound).astype(kind)


def setup_inputs(seed: int = 0) -> dict:
    key_list = jax.random.split(jax.random.key(seed), 9)
    ref_feats = draw_ref_feats(jax.random.fold_in(key_list[8], 71), 0)
    src_feats = draw_src_feats(jax.random.fold_in(key_list[8], 71), 0)
    grad_out = noise_with(key_list[2], (PAIRS, NQ, D), 1.0, 6.0, ((0, 4), (1, 8)), (1, 2, 8, 2.0))
    w_query = draw_w_query(jax.random.fold_in(key_list[8], 71), 0)
    w_key = draw_w_key(jax.random.fold_in(key_list[8], 71), 0)
    w_value = bell_draw(key_list[5], (D, D), D ** -0.5, 0.375)
    w_out = bell_draw(key_list[6], (D, D), D ** -0.5, 0.375)
    intersection = draw_intersection(jax.random.fold_in(key_list[8], 71), 0)
    return {"ref_feats": ref_feats, "src_feats": src_feats, "grad_out": grad_out, "w_query": w_query, "w_key": w_key, "w_value": w_value, "w_out": w_out, "intersection": intersection}


NEG = -1.0e30


def allowed_mask(block_rows):
    return jnp.repeat(jnp.repeat(block_rows == 1, BLOCK, axis=0), BLOCK, axis=1)


def exact_dot(left, right):
    return jnp.dot(left, right, precision=lax.Precision.HIGHEST)


def head_pass(allowed, query_head, key_head, value_head, grad_head):
    score_scale = HEAD_DIM ** -0.5
    scores = exact_dot(query_head, key_head.T) * score_scale
    masked = jnp.where(allowed, scores, NEG)
    row_peak = masked.max(axis=1, keepdims=True)
    row_exp = jnp.where(allowed, jnp.exp(scores - row_peak), 0.0)
    row_prob = row_exp / row_exp.sum(axis=1, keepdims=True)
    col_peak = masked.max(axis=0, keepdims=True)
    col_exp = jnp.where(allowed, jnp.exp(scores - col_peak), 0.0)
    col_prob = col_exp / col_exp.sum(axis=0, keepdims=True)
    match_prob = lax.optimization_barrier((row_prob * col_prob).astype(jnp.bfloat16)).astype(jnp.float32)
    attended = exact_dot(match_prob, value_head)
    grad_prob = exact_dot(grad_head, value_head.T)
    product = match_prob * grad_prob
    row_dot = product.sum(axis=1, keepdims=True)
    col_dot = product.sum(axis=0, keepdims=True)
    grad_score = score_scale * (2.0 * product - row_prob * row_dot - col_prob * col_dot)
    grad_score = lax.optimization_barrier(grad_score.astype(jnp.bfloat16)).astype(jnp.float32)
    grad_query = exact_dot(grad_score, key_head)
    grad_key = exact_dot(grad_score.T, query_head)
    grad_value = exact_dot(match_prob.T, grad_head)
    return attended, grad_query, grad_key, grad_value


def reference(ref_feats, src_feats, grad_out, w_query, w_key, w_value, w_out, intersection):
    def split_heads(matrix):
        return matrix.astype(jnp.float32).reshape(matrix.shape[0], HEADS, HEAD_DIM).transpose(1, 0, 2)

    def join_heads(stack):
        return stack.transpose(1, 0, 2).reshape(stack.shape[1], D)

    def one_pair(pair_inputs):
        ref_rows, src_rows, out_grad, block_rows = pair_inputs
        allowed = allowed_mask(block_rows)
        queries = jnp.dot(ref_rows, w_query, preferred_element_type=jnp.float32).astype(jnp.bfloat16)
        key_rows = jnp.dot(src_rows, w_key, preferred_element_type=jnp.float32).astype(jnp.bfloat16)
        values = jnp.dot(src_rows, w_value, preferred_element_type=jnp.float32).astype(jnp.bfloat16)
        grad_att = jnp.dot(out_grad, w_out.T, preferred_element_type=jnp.float32).astype(jnp.bfloat16)

        def one_head(head_inputs):
            return head_pass(allowed, head_inputs[0], head_inputs[1], head_inputs[2], head_inputs[3])

        attended, grad_query, grad_keys, grad_values = lax.map(
            one_head, (split_heads(queries), split_heads(key_rows), split_heads(values), split_heads(grad_att)))
        attended = join_heads(attended).astype(jnp.bfloat16)
        matched = (ref_rows.astype(jnp.float32) + jnp.dot(attended, w_out, preferred_element_type=jnp.float32)).astype(jnp.bfloat16)
        grad_query = join_heads(grad_query).astype(jnp.bfloat16)
        grad_keys = join_heads(grad_keys)
        grad_values = join_heads(grad_values)
        grad_ref = (out_grad.astype(jnp.float32) + jnp.dot(grad_query, w_query.T, preferred_element_type=jnp.float32)).astype(jnp.bfloat16)
        grad_src = (exact_dot(grad_keys, w_key.T.astype(jnp.float32)) + exact_dot(grad_values, w_value.T.astype(jnp.float32))).astype(jnp.bfloat16)
        source_wide = src_rows.astype(jnp.float32)
        weight_query = jnp.dot(ref_rows.T, grad_query, preferred_element_type=jnp.float32)
        weight_key = exact_dot(source_wide.T, grad_keys)
        weight_value = exact_dot(source_wide.T, grad_values)
        weight_out = jnp.dot(attended.T, out_grad, preferred_element_type=jnp.float32)
        return matched, grad_ref, grad_src, weight_query, weight_key, weight_value, weight_out

    results = lax.map(one_pair, (ref_feats, src_feats, grad_out, intersection))
    return (results[0], results[1], results[2], results[3].sum(axis=0), results[4].sum(axis=0),
            results[5].sum(axis=0), results[6].sum(axis=0))
```

```python
import functools

import jax
import jax.numpy as jnp
from jax import lax
from jax.experimental import pallas as pl
from jax.experimental.pallas import tpu as pltpu
from jax.sharding import PartitionSpec as P

HEADS = 4
BLOCK = 128
NEG = -1e30
FLOOR = -1e29
VMEM_LIMIT = 56 * 1024 * 1024

NT = (((1,), (1,)), ((), ()))
TN = (((0,), (0,)), ((), ()))
TT = (((0,), (1,)), ((), ()))


def mm(left, right):
    return jnp.dot(left, right, preferred_element_type=jnp.float32)


def mm_general(left, right, dims):
    return lax.dot_general(left, right, dims, preferred_element_type=jnp.float32)


def bf(x):
    return x.astype(jnp.bfloat16)


def lane_head(shape, head_dim):
    return lax.broadcasted_iota(jnp.int32, shape, 1) // head_dim


def fill_bias(inter_ref, bias_ref, head_dim):
    query_blocks, key_blocks = inter_ref.shape
    width = bias_ref.shape[1]
    lane = lax.broadcasted_iota(jnp.int32, (1, width), 1) % head_dim
    for key_block in range(key_blocks):
        row = jnp.zeros((1, width), jnp.float32)
        for query_block in range(query_blocks):
            listed = inter_ref[query_block, key_block] == 1
            row = jnp.where(lane == query_block, jnp.where(listed, 0.0, NEG), row)
        bias_ref[pl.ds(key_block * BLOCK, BLOCK), :] = bf(
            jnp.broadcast_to(row, (BLOCK, width))
        )


def masked_query(head, queries, head_dim):
    rows, width = queries.shape
    heads = width // head_dim
    lanes = lane_head((rows, width), head_dim)
    lane = lax.broadcasted_iota(jnp.int32, (rows, width), 1)
    block = lax.broadcasted_iota(jnp.int32, (rows, width), 0) // BLOCK
    other = (head + 1) % heads
    hot = jnp.where((lanes == other) & (lane - other * head_dim == block), 1.0, 0.0)
    return bf(jnp.where(lanes == head, queries.astype(jnp.float32), hot))


def masked_key(head, keys, bias, head_dim):
    heads = keys.shape[1] // head_dim
    lanes = lane_head(keys.shape, head_dim)
    other = jnp.where(lanes == (head + 1) % heads, bias.astype(jnp.float32), 0.0)
    return bf(jnp.where(lanes == head, keys.astype(jnp.float32), other))


def only_head(head, values, head_dim):
    lanes = lane_head(values.shape, head_dim)
    return bf(jnp.where(lanes == head, values.astype(jnp.float32), 0.0))


def fill_scores(head, query_ref, key_ref, bias_ref, grad_ref, value_ref, score_ref, prob_ref, head_dim):
    left = masked_query(head, query_ref[...], head_dim)
    left_grad = only_head(head, grad_ref[...], head_dim)
    key_total = key_ref.shape[0]
    step = min(256, key_total)
    for first in range(0, key_total, step):
        span = pl.ds(first, step)
        right = masked_key(head, key_ref[span, :], bias_ref[span, :], head_dim)
        score_ref[:, span] = mm_general(left, right, NT)
        prob_ref[:, span] = mm_general(left_grad, value_ref[span, :], NT)


def stats_kernel(
    head_count, inter_ref, ref_ref, gout_ref, src_ref, wq_ref, wk_ref, wv_ref, wo_ref,
    row_ref, col_ref, query_ref, grad_ref, key_ref, value_ref, bias_ref, score_ref, prob_ref,
):
    rows, width = ref_ref.shape
    key_total = src_ref.shape[0]
    head_dim = width // head_count
    scale = head_dim ** -0.5
    query_ref[...] = bf(bf(mm(ref_ref[...], wq_ref[...])).astype(jnp.float32) * scale)
    grad_ref[...] = bf(mm_general(gout_ref[...], wo_ref[...], NT))
    key_ref[...] = bf(mm(src_ref[...], wk_ref[...]))
    value_ref[...] = bf(mm(src_ref[...], wv_ref[...]))
    fill_bias(inter_ref, bias_ref, head_dim)
    for head in range(head_count):
        fill_scores(
            head, query_ref, key_ref, bias_ref, grad_ref, value_ref, score_ref, prob_ref, head_dim
        )

        def peaks(step, col_peak):
            span = pl.ds(step * 8, 8)
            scores = score_ref[span, :]
            row_ref[span, head : head + 1] = scores.max(axis=1, keepdims=True)
            return jnp.maximum(col_peak, scores)

        col_peak = lax.fori_loop(
            0, rows // 8, peaks, jnp.full((8, key_total), FLOOR, jnp.float32), unroll=4
        )
        col_peak = jnp.broadcast_to(col_peak.max(axis=0, keepdims=True), (8, key_total))
        col_ref[head : head + 1, :] = col_peak[:1]

        def totals(step, col_total):
            span = pl.ds(step * 8, 8)
            scores = score_ref[span, :]
            row_exp = jnp.exp(scores - row_ref[span, head : head + 1])
            row_total = row_exp.sum(axis=1, keepdims=True)
            at = head_count + head
            row_ref[span, at : at + 1] = 1.0 / row_total
            col_exp = jnp.exp(scores - col_peak)
            prob_ref[span, :] = row_exp * col_exp * prob_ref[span, :]
            return col_total + col_exp

        zero = jnp.zeros((8, key_total), jnp.float32)
        col_total = lax.fori_loop(0, rows // 8, totals, zero, unroll=2)
        at = head_count + head
        col_ref[at : at + 1, :] = col_total.sum(axis=0, keepdims=True)

        def dots(step, col_dot):
            span = pl.ds(step * 8, 8)
            at = head_count + head
            return col_dot + prob_ref[span, :] * row_ref[span, at : at + 1]

        col_dot = lax.fori_loop(0, rows // 8, dots, zero, unroll=4)
        at = 2 * head_count + head
        col_ref[at : at + 1, :] = col_dot.sum(axis=0, keepdims=True)


def grads_kernel(
    head_count, inter_ref, ref_ref, gout_ref, src_ref, wq_ref, wk_ref, wv_ref, wo_ref, row_ref, all_ref,
    matched_ref, gref_ref, gsrc_ref, weight_ref,
    query_ref, grad_ref, key_ref, value_ref, bias_ref, score_ref, prob_ref,
    match_ref, gscore_ref, query_t_ref, grad_t_ref, gkey_ref, gvalue_ref, att_ref, gquery_ref, col_ref,
):
    rows, width = ref_ref.shape
    key_total = src_ref.shape[0]
    head_dim = width // head_count
    scale = head_dim ** -0.5
    queries = bf(mm(ref_ref[...], wq_ref[...])).astype(jnp.float32)
    query_ref[...] = bf(queries * scale)
    grad_ref[...] = bf(mm_general(gout_ref[...], wo_ref[...], NT))
    queries_t = bf(mm_general(wq_ref[...], ref_ref[...], TT)).astype(jnp.float32)
    query_t_ref[...] = bf(queries_t * (2.0 * scale))
    grad_t_ref[...] = bf(mm_general(wo_ref[...], gout_ref[...], NT))
    key_ref[...] = bf(mm(src_ref[...], wk_ref[...]))
    value_ref[...] = bf(mm(src_ref[...], wv_ref[...]))
    fill_bias(inter_ref, bias_ref, head_dim)

    devices = all_ref.shape[0]
    peak = all_ref[0, :head_count, :]
    for device in range(1, devices):
        peak = jnp.maximum(peak, all_ref[device, :head_count, :])
    total = jnp.zeros_like(peak)
    dots = jnp.zeros_like(peak)
    for device in range(devices):
        factor = jnp.exp(all_ref[device, :head_count, :] - peak)
        total = total + factor * all_ref[device, head_count : 2 * head_count, :]
        dots = dots + factor * all_ref[device, 2 * head_count : 3 * head_count, :]
    inverse = 1.0 / total
    col_ref[:head_count, :] = peak
    col_ref[head_count : 2 * head_count, :] = inverse
    col_ref[2 * head_count : 3 * head_count, :] = dots * inverse * 0.5

    for head in range(head_count):
        fill_scores(
            head, query_ref, key_ref, bias_ref, grad_ref, value_ref, score_ref, prob_ref, head_dim
        )
        strip = 16

        def col_row(kind):
            at = kind * head_count + head
            return jnp.broadcast_to(col_ref[at : at + 1, :], (8, key_total))

        col_peak, col_inverse, col_half = col_row(0), col_row(1), col_row(2)

        def tile(step, carry):
            matches, grads = [], []
            for part in range(strip // 8):
                span = pl.ds(step * strip + part * 8, 8)
                scores = score_ref[span, :]
                row_inverse = row_ref[span, head_count + head : head_count + head + 1]
                row_prob = jnp.exp(scores - row_ref[span, head : head + 1]) * row_inverse
                col_prob = jnp.exp(scores - col_peak) * col_inverse
                match = row_prob * col_prob
                product = match * prob_ref[span, :]
                row_half = product.sum(axis=1, keepdims=True) * 0.5
                grads.append(product - row_prob * row_half - col_prob * col_half)
                matches.append(match)
            span = pl.ds(step * strip, strip)
            match_ref[span, :] = bf(jnp.concatenate(matches, axis=0))
            gscore_ref[span, :] = bf(jnp.concatenate(grads, axis=0))
            return carry

        lax.fori_loop(0, rows // strip, tile, 0)

        values = only_head(head, value_ref[...], head_dim)
        keys = only_head(head, key_ref[...].astype(jnp.float32) * (2.0 * scale), head_dim)
        attended = mm(match_ref[...], values)
        gquery = mm(gscore_ref[...], keys)
        if head == 0:
            att_ref[...] = attended
            gquery_ref[...] = gquery
        else:
            att_ref[...] += attended
            gquery_ref[...] += gquery
        span = pl.ds(head * head_dim, head_dim)
        gkey_ref[span, :] = bf(mm(query_t_ref[span, :], gscore_ref[...]))
        gvalue_ref[span, :] = bf(mm(grad_t_ref[span, :], match_ref[...]))

    attended = bf(att_ref[...])
    gquery = bf(gquery_ref[...])
    matched_ref[...] = bf(ref_ref[...].astype(jnp.float32) + mm(attended, wo_ref[...]))
    gref_ref[...] = bf(
        gout_ref[...].astype(jnp.float32) + mm_general(gquery, wq_ref[...], NT)
    )
    gsrc_t = mm(wk_ref[...], gkey_ref[...]) + mm(wv_ref[...], gvalue_ref[...])
    gsrc_ref[...] = bf(gsrc_t.T)
    weight_ref[0] = bf(mm_general(ref_ref[...], gquery, TN))
    weight_ref[1] = bf(mm(gkey_ref[...], src_ref[...]).T)
    weight_ref[2] = bf(mm(gvalue_ref[...], src_ref[...]).T)
    weight_ref[3] = bf(mm_general(attended, gout_ref[...], TN))


def vmem_call(kernel, name, out_shape, scratch, flops, moved, args):
    specs = [pl.BlockSpec(memory_space=pltpu.SMEM)]
    specs += [pl.BlockSpec(memory_space=pltpu.VMEM)] * (len(args) - 1)
    return pl.pallas_call(
        kernel,
        name=name,
        out_shape=out_shape,
        in_specs=specs,
        out_specs=[pl.BlockSpec(memory_space=pltpu.VMEM)] * len(out_shape),
        scratch_shapes=scratch,
        compiler_params=pltpu.CompilerParams(vmem_limit_bytes=VMEM_LIMIT),
        cost_estimate=pl.CostEstimate(flops=flops, bytes_accessed=moved, transcendentals=0),
    )(*args)


def on_device(ref_feats, src_feats, grad_out, w_query, w_key, w_value, w_out, intersection):
    ref_rows = ref_feats[0]
    src_rows = src_feats[0]
    out_grad = grad_out[0]
    listed = intersection[0]
    rows, width = ref_rows.shape
    blk = lax.axis_size("blk")
    everyone = lax.axis_size("scan") * blk
    key_rows = src_rows.shape[0]
    key_total = key_rows * blk
    source_all = lax.all_gather(src_rows, "blk", axis=0, tiled=True)

    f32, b16 = jnp.float32, jnp.bfloat16
    shape = jax.ShapeDtypeStruct
    common = [
        pltpu.VMEM((rows, width), b16),
        pltpu.VMEM((rows, width), b16),
        pltpu.VMEM((key_total, width), b16),
        pltpu.VMEM((key_total, width), b16),
        pltpu.VMEM((key_total, width), b16),
        pltpu.VMEM((rows, key_total), f32),
        pltpu.VMEM((rows, key_total), f32),
    ]
    base = (listed, ref_rows, out_grad, source_all, w_query, w_key, w_value, w_out)
    tile_flops = 2 * rows * key_total * width
    row_stats, col_stats = vmem_call(
        functools.partial(stats_kernel, HEADS),
        "match_stats",
        [shape((rows, 2 * HEADS), f32), shape((3 * HEADS, key_total), f32)],
        common,
        2 * tile_flops,
        2 << 20,
        base,
    )
    all_stats = lax.all_gather(col_stats, "blk", axis=0)
    matched, grad_ref, source_part, weight_part = vmem_call(
        functools.partial(grads_kernel, HEADS),
        "match_grads",
        [
            shape((rows, width), b16),
            shape((rows, width), b16),
            shape((key_total, width), b16),
            shape((4, width, width), b16),
        ],
        common
        + [
            pltpu.VMEM((rows, key_total), b16),
            pltpu.VMEM((rows, key_total), b16),
            pltpu.VMEM((width, rows), b16),
            pltpu.VMEM((width, rows), b16),
            pltpu.VMEM((width, key_total), b16),
            pltpu.VMEM((width, key_total), b16),
            pltpu.VMEM((rows, width), f32),
            pltpu.VMEM((rows, width), f32),
            pltpu.VMEM((3 * HEADS, key_total), f32),
        ],
        6 * tile_flops,
        4 << 20,
        base + (row_stats, all_stats),
    )

    source_parts = lax.all_to_all(
        source_part.reshape(blk, key_rows, width), "blk", split_axis=0, concat_axis=0
    )
    grad_src = source_parts.astype(f32).sum(axis=0).astype(b16)

    weight_rows = 4 * width // everyone
    weight_parts = lax.all_to_all(
        weight_part.reshape(everyone, weight_rows, width), ("scan", "blk"), split_axis=0, concat_axis=0
    )
    weight_sum = weight_parts.astype(f32).sum(axis=0).astype(b16)
    weights = lax.all_gather(weight_sum, ("scan", "blk"), axis=0, tiled=True)
    weights = weights.astype(f32).reshape(4, width, width)
    return (
        matched[None],
        grad_ref[None],
        grad_src[None],
        weights[0],
        weights[1],
        weights[2],
        weights[3],
    )


def solution(mesh):
    split = P("scan", "blk", None)
    whole = P()
    return jax.shard_map(
        on_device,
        mesh=mesh,
        in_specs=(split, split, split, whole, whole, whole, whole, split),
        out_specs=(split, split, split, whole, whole, whole, whole),
        check_vma=False,
    )
```

```python
import functools

import jax
import jax.numpy as jnp
from jax import lax
from jax.experimental import pallas as pl
from jax.experimental.pallas import tpu as pltpu
from jax.sharding import PartitionSpec as P

HEADS = 4
BLOCK = 128
NEG = -1e30
FLOOR = -1e29
VMEM_LIMIT = 56 * 1024 * 1024

NT = (((1,), (1,)), ((), ()))
TN = (((0,), (0,)), ((), ()))
TT = (((0,), (1,)), ((), ()))


def mm(left, right):
    return jnp.dot(left, right, preferred_element_type=jnp.float32)


def mm_general(left, right, dims):
    return lax.dot_general(left, right, dims, preferred_element_type=jnp.float32)


def bf(x):
    return x.astype(jnp.bfloat16)


def lane_row(width, head, head_dim):
    lanes = lax.broadcasted_iota(jnp.int32, (1, width), 1) // head_dim
    return bf(jnp.where(lanes == head, 1.0, 0.0))


def fill_bias(inter_ref, bias_ref, head_dim):
    query_blocks, key_blocks = inter_ref.shape
    width = bias_ref.shape[1]
    lane = lax.broadcasted_iota(jnp.int32, (1, width), 1) % head_dim
    for key_block in range(key_blocks):
        row = jnp.zeros((1, width), jnp.float32)
        for query_block in range(query_blocks):
            listed = inter_ref[query_block, key_block] == 1
            row = jnp.where(lane == query_block, jnp.where(listed, 0.0, NEG), row)
        bias_ref[pl.ds(key_block * BLOCK, BLOCK), :] = bf(
            jnp.broadcast_to(row, (BLOCK, width))
        )


def fill_hot(hot_ref, head_dim):
    rows, width = hot_ref.shape
    lane = lax.broadcasted_iota(jnp.int32, (1, width), 1) % head_dim
    for block in range(rows // BLOCK):
        row = bf(jnp.where(lane == block, 1.0, 0.0))
        hot_ref[pl.ds(block * BLOCK, BLOCK), :] = jnp.broadcast_to(row, (BLOCK, width))


def fill_scores(
    head, heads, query_ref, hot_ref, key_ref, bias_ref, grad_ref, value_ref, score_ref, prob_ref,
    peak_ref=None,
):
    rows, width = query_ref.shape
    own = lane_row(width, head, width // heads)
    other = lane_row(width, (head + 1) % heads, width // heads)
    left = query_ref[...] * own + hot_ref[...] * other
    left_grad = grad_ref[...] * own
    key_total = key_ref.shape[0]
    step = min(256, key_total)
    row_peak = None
    col_peaks = []
    for first in range(0, key_total, step):
        span = pl.ds(first, step)
        right = key_ref[span, :] * own + bias_ref[span, :] * other
        scores = mm_general(left, right, NT)
        score_ref[:, span] = scores
        if peak_ref is not None:
            for at in range(0, step, 128):
                piece = scores[:, at : at + 128]
                row_peak = piece if row_peak is None else jnp.maximum(row_peak, piece)
            col_peaks.append(scores.max(axis=0, keepdims=True))
        prob_ref[:, span] = mm_general(left_grad, value_ref[span, :], NT)
    if peak_ref is not None:
        peak_ref[...] = row_peak
        return jnp.concatenate(col_peaks, axis=1)


def spread(reduced, like):
    return jnp.broadcast_to(reduced, like.shape)


def fold8(x):
    return x.reshape(x.shape[0] // 8, 8, x.shape[1]).sum(axis=0)


STRIP = 32


def stats_kernel(
    head_count, inter_ref, ref_ref, gout_ref, src_ref, wq_ref, wk_ref, wv_ref, wo_ref,
    row_ref, col_ref, query_ref, grad_ref, key_ref, value_ref, bias_ref, hot_ref, score_ref, prob_ref,
    part_ref,
):
    rows, width = ref_ref.shape
    key_total = src_ref.shape[0]
    tiles = key_total // 128
    head_dim = width // head_count
    scale = head_dim ** -0.5
    query_ref[...] = bf(bf(mm(ref_ref[...], wq_ref[...])).astype(jnp.float32) * scale)
    grad_ref[...] = bf(mm_general(gout_ref[...], wo_ref[...], NT))
    key_ref[...] = bf(mm(src_ref[...], wk_ref[...]))
    value_ref[...] = bf(mm(src_ref[...], wv_ref[...]))
    fill_bias(inter_ref, bias_ref, head_dim)
    fill_hot(hot_ref, head_dim)
    for head in range(head_count):
        peak_at, total_at, dot_at = head, head_count + head, 2 * head_count + head
        col_peak = fill_scores(
            head, head_count, query_ref, hot_ref, key_ref, bias_ref, grad_ref, value_ref,
            score_ref, prob_ref, part_ref,
        )
        col_ref[peak_at : peak_at + 1, :] = jnp.maximum(col_peak, FLOOR)
        row_ref[head] = spread(part_ref[...].max(axis=1, keepdims=True), part_ref)

        def totals(step, col_totals):
            span = pl.ds(step * STRIP, STRIP)
            row_peak = row_ref[head, span, :]
            row_total = jnp.zeros((STRIP, 128), jnp.float32)
            out = []
            for tile in range(tiles):
                lanes = slice(tile * 128, tile * 128 + 128)
                scores = score_ref[span, lanes]
                row_exp = jnp.exp(scores - row_peak)
                col_exp = jnp.exp(scores - col_ref[peak_at : peak_at + 1, lanes])
                row_total = row_total + row_exp
                prob_ref[span, lanes] = row_exp * col_exp * prob_ref[span, lanes]
                out.append(col_totals[tile] + fold8(col_exp))
            part_ref[span, :] = row_total
            return tuple(out)

        zeros = tuple(jnp.zeros((8, 128), jnp.float32) for _ in range(tiles))
        col_totals = lax.fori_loop(0, rows // STRIP, totals, zeros)
        row_total = part_ref[...].sum(axis=1, keepdims=True)
        row_ref[head_count + head] = spread(1.0 / row_total, part_ref)

        def dots(step, col_dots):
            span = pl.ds(step * STRIP, STRIP)
            row_inverse = row_ref[head_count + head, span, :]
            return tuple(
                col_dots[tile]
                + fold8(prob_ref[span, tile * 128 : tile * 128 + 128] * row_inverse)
                for tile in range(tiles)
            )

        col_dots = lax.fori_loop(0, rows // STRIP, dots, zeros)
        for tile in range(tiles):
            lanes = slice(tile * 128, tile * 128 + 128)
            col_ref[total_at : total_at + 1, lanes] = col_totals[tile].sum(axis=0, keepdims=True)
            col_ref[dot_at : dot_at + 1, lanes] = col_dots[tile].sum(axis=0, keepdims=True)


def grads_kernel(
    head_count, inter_ref, ref_ref, gout_ref, src_ref, wq_ref, wk_ref, wv_ref, wo_ref, row_ref, all_ref,
    matched_ref, gref_ref, gsrc_ref, weight_ref,
    query_ref, grad_ref, key_ref, value_ref, bias_ref, hot_ref, score_ref, prob_ref, part_ref,
    match_ref, gscore_ref, query_t_ref, grad_t_ref, gkey_ref, gvalue_ref, att_ref, gquery_ref,
    col_ref,
):
    rows, width = ref_ref.shape
    key_total = src_ref.shape[0]
    tiles = key_total // 128
    head_dim = width // head_count
    scale = head_dim ** -0.5
    queries = bf(mm(ref_ref[...], wq_ref[...])).astype(jnp.float32)
    query_ref[...] = bf(queries * scale)
    grad_ref[...] = bf(mm_general(gout_ref[...], wo_ref[...], NT))
    queries_t = bf(mm_general(wq_ref[...], ref_ref[...], TT)).astype(jnp.float32)
    query_t_ref[...] = bf(queries_t * (2.0 * scale))
    grad_t_ref[...] = bf(mm_general(wo_ref[...], gout_ref[...], NT))
    key_ref[...] = bf(mm(src_ref[...], wk_ref[...]))
    value_ref[...] = bf(mm(src_ref[...], wv_ref[...]))
    fill_bias(inter_ref, bias_ref, head_dim)
    fill_hot(hot_ref, head_dim)

    devices = all_ref.shape[0]
    peak = all_ref[0, :head_count, :]
    for device in range(1, devices):
        peak = jnp.maximum(peak, all_ref[device, :head_count, :])
    total = jnp.zeros_like(peak)
    dots = jnp.zeros_like(peak)
    for device in range(devices):
        factor = jnp.exp(all_ref[device, :head_count, :] - peak)
        total = total + factor * all_ref[device, head_count : 2 * head_count, :]
        dots = dots + factor * all_ref[device, 2 * head_count : 3 * head_count, :]
    inverse = 1.0 / total
    col_ref[:head_count, :] = peak
    col_ref[head_count : 2 * head_count, :] = inverse
    col_ref[2 * head_count : 3 * head_count, :] = dots * inverse * 0.5

    for head in range(head_count):
        peak_at, inverse_at, half_at = head, head_count + head, 2 * head_count + head
        fill_scores(
            head, head_count, query_ref, hot_ref, key_ref, bias_ref, grad_ref, value_ref,
            score_ref, prob_ref,
        )

        def products(step, carry):
            span = pl.ds(step * STRIP, STRIP)
            row_peak = row_ref[head, span, :]
            row_inverse = row_ref[head_count + head, span, :]
            row_dot = jnp.zeros((STRIP, 128), jnp.float32)
            for tile in range(tiles):
                lanes = slice(tile * 128, tile * 128 + 128)
                scores = score_ref[span, lanes]
                row_prob = jnp.exp(scores - row_peak) * row_inverse
                col_prob = (
                    jnp.exp(scores - col_ref[peak_at : peak_at + 1, lanes])
                    * col_ref[inverse_at : inverse_at + 1, lanes]
                )
                match = row_prob * col_prob
                product = match * prob_ref[span, lanes]
                row_dot = row_dot + product
                match_ref[span, lanes] = bf(match)
                score_ref[span, lanes] = row_prob
                prob_ref[span, lanes] = product - col_prob * col_ref[half_at : half_at + 1, lanes]
            part_ref[span, :] = row_dot
            return carry

        lax.fori_loop(0, rows // STRIP, products, 0)
        part_ref[...] = spread(part_ref[...].sum(axis=1, keepdims=True) * 0.5, part_ref)

        def score_grads(step, carry):
            span = pl.ds(step * STRIP, STRIP)
            row_half = part_ref[span, :]
            for tile in range(tiles):
                lanes = slice(tile * 128, tile * 128 + 128)
                gscore_ref[span, lanes] = bf(
                    prob_ref[span, lanes] - score_ref[span, lanes] * row_half
                )
            return carry

        lax.fori_loop(0, rows // STRIP, score_grads, 0)

        own = lane_row(width, head, head_dim)
        attended = mm(match_ref[...], value_ref[...] * own)
        gquery = mm(gscore_ref[...], key_ref[...] * bf(own.astype(jnp.float32) * (2.0 * scale)))
        if head == 0:
            att_ref[...] = attended
            gquery_ref[...] = gquery
        else:
            att_ref[...] += attended
            gquery_ref[...] += gquery
        span = pl.ds(head * head_dim, head_dim)
        gkey_ref[span, :] = bf(mm(query_t_ref[span, :], gscore_ref[...]))
        gvalue_ref[span, :] = bf(mm(grad_t_ref[span, :], match_ref[...]))

    attended = bf(att_ref[...])
    gquery = bf(gquery_ref[...])
    matched_ref[...] = bf(ref_ref[...].astype(jnp.float32) + mm(attended, wo_ref[...]))
    gref_ref[...] = bf(
        gout_ref[...].astype(jnp.float32) + mm_general(gquery, wq_ref[...], NT)
    )
    gsrc_t = mm(wk_ref[...], gkey_ref[...]) + mm(wv_ref[...], gvalue_ref[...])
    gsrc_ref[...] = bf(gsrc_t.T)
    weight_ref[0] = bf(mm_general(ref_ref[...], gquery, TN))
    weight_ref[1] = bf(mm(gkey_ref[...], src_ref[...]).T)
    weight_ref[2] = bf(mm(gvalue_ref[...], src_ref[...]).T)
    weight_ref[3] = bf(mm_general(attended, gout_ref[...], TN))


def unshuffle_kernel(bits, me_ref, piece_ref, *out_refs):
    pieces, piece_rows, _ = piece_ref.shape
    per_out = pieces // len(out_refs)
    for chunk in range(pieces):
        apart = me_ref[0] ^ chunk
        place = 0
        for at, bit in enumerate(bits):
            place = place + ((apart // bit) % 2) * (1 << at)
        rows = pl.ds((chunk % per_out) * piece_rows, piece_rows)
        out_refs[chunk // per_out][rows, :] = piece_ref[place].astype(jnp.float32)


def gather_by_doubling(chunk, steps):
    held = chunk[None]
    for axis, bit in steps:
        pairs = [(i, i ^ bit) for i in range(lax.axis_size(axis))]
        held = jnp.concatenate([held, lax.ppermute(held, axis, pairs)], axis=0)
    return held


def axis_bits(axis):
    return [1 << at for at in range(lax.axis_size(axis).bit_length() - 1)]


def vmem_call(kernel, name, out_shape, scratch, flops, moved, args):
    specs = [pl.BlockSpec(memory_space=pltpu.SMEM)]
    specs += [pl.BlockSpec(memory_space=pltpu.VMEM)] * (len(args) - 1)
    return pl.pallas_call(
        kernel,
        name=name,
        out_shape=out_shape,
        in_specs=specs,
        out_specs=[pl.BlockSpec(memory_space=pltpu.VMEM)] * len(out_shape),
        scratch_shapes=scratch,
        compiler_params=pltpu.CompilerParams(vmem_limit_bytes=VMEM_LIMIT),
        cost_estimate=pl.CostEstimate(flops=flops, bytes_accessed=moved, transcendentals=0),
    )(*args)


def on_device(ref_feats, src_feats, grad_out, w_query, w_key, w_value, w_out, intersection):
    ref_rows = ref_feats[0]
    src_rows = src_feats[0]
    out_grad = grad_out[0]
    listed = intersection[0]
    rows, width = ref_rows.shape
    blk = lax.axis_size("blk")
    everyone = lax.axis_size("scan") * blk
    key_rows = src_rows.shape[0]
    key_total = key_rows * blk
    source_all = lax.all_gather(src_rows, "blk", axis=0, tiled=True)

    f32, b16 = jnp.float32, jnp.bfloat16
    shape = jax.ShapeDtypeStruct
    common = [
        pltpu.VMEM((rows, width), b16),
        pltpu.VMEM((rows, width), b16),
        pltpu.VMEM((key_total, width), b16),
        pltpu.VMEM((key_total, width), b16),
        pltpu.VMEM((key_total, width), b16),
        pltpu.VMEM((rows, width), b16),
        pltpu.VMEM((rows, key_total), f32),
        pltpu.VMEM((rows, key_total), f32),
        pltpu.VMEM((rows, 128), f32),
    ]
    base = (listed, ref_rows, out_grad, source_all, w_query, w_key, w_value, w_out)
    tile_flops = 2 * rows * key_total * width
    row_stats, col_stats = vmem_call(
        functools.partial(stats_kernel, HEADS),
        "match_stats",
        [shape((2 * HEADS, rows, 128), f32), shape((3 * HEADS, key_total), f32)],
        common,
        2 * tile_flops,
        2 << 20,
        base,
    )
    all_stats = lax.all_gather(col_stats, "blk", axis=0)
    matched, grad_ref, source_part, weight_part = vmem_call(
        functools.partial(grads_kernel, HEADS),
        "match_grads",
        [
            shape((rows, width), b16),
            shape((rows, width), b16),
            shape((key_total, width), b16),
            shape((4, width, width), b16),
        ],
        common
        + [
            pltpu.VMEM((rows, key_total), b16),
            pltpu.VMEM((rows, key_total), b16),
            pltpu.VMEM((width, rows), b16),
            pltpu.VMEM((width, rows), b16),
            pltpu.VMEM((width, key_total), b16),
            pltpu.VMEM((width, key_total), b16),
            pltpu.VMEM((rows, width), f32),
            pltpu.VMEM((rows, width), f32),
            pltpu.VMEM((3 * HEADS, key_total), f32),
        ],
        6 * tile_flops,
        4 << 20,
        base + (row_stats, all_stats),
    )

    weight_rows = 4 * width // everyone
    weight_parts = lax.all_to_all(
        weight_part.reshape(everyone, weight_rows, width), ("scan", "blk"), split_axis=0, concat_axis=0
    )
    weight_sum = weight_parts.astype(f32).sum(axis=0).astype(b16)
    blk_bits, scan_bits = axis_bits("blk"), axis_bits("scan")
    steps = [("blk", bit) for bit in blk_bits[1:]]
    steps += [("scan", bit) for bit in reversed(scan_bits)]
    steps += [("blk", bit) for bit in blk_bits[:1]]
    pieces = gather_by_doubling(weight_sum, steps)
    me = lax.axis_index("scan") * blk + lax.axis_index("blk")
    weights = vmem_call(
        functools.partial(
            unshuffle_kernel, [bit * (blk if axis == "scan" else 1) for axis, bit in steps]
        ),
        "unshuffle_weights",
        [shape((width, width), f32)] * 4,
        [],
        0,
        3 << 20,
        (me.astype(jnp.int32)[None], pieces),
    )

    source_part, weight_parts = lax.optimization_barrier((source_part, weight_parts))
    source_parts = lax.all_to_all(
        source_part.reshape(blk, key_rows, width), "blk", split_axis=0, concat_axis=0
    )
    grad_src = source_parts.astype(f32).sum(axis=0).astype(b16)
    return (matched[None], grad_ref[None], grad_src[None], *weights)


def solution(mesh):
    split = P("scan", "blk", None)
    whole = P()
    return jax.shard_map(
        on_device,
        mesh=mesh,
        in_specs=(split, split, split, whole, whole, whole, whole, split),
        out_specs=(split, split, split, whole, whole, whole, whole),
        check_vma=False,
    )
```

```python
import functools

import jax
import jax.numpy as jnp
from jax import lax
from jax.experimental import pallas as pl
from jax.experimental.pallas import tpu as pltpu
from jax.sharding import PartitionSpec as P

HEADS = 4
BLOCK = 128
NEG = -1e30
FLOOR = -1e29
VMEM_LIMIT = 56 * 1024 * 1024

NT = (((1,), (1,)), ((), ()))
TN = (((0,), (0,)), ((), ()))
TT = (((0,), (1,)), ((), ()))


def mm(left, right):
    return jnp.dot(left, right, preferred_element_type=jnp.float32)


def mm_general(left, right, dims):
    return lax.dot_general(left, right, dims, preferred_element_type=jnp.float32)


def bf(x):
    return x.astype(jnp.bfloat16)


def lane_row(width, head, head_dim):
    lanes = lax.broadcasted_iota(jnp.int32, (1, width), 1) // head_dim
    return bf(jnp.where(lanes == head, 1.0, 0.0))


def fill_bias(inter_ref, bias_ref, head_dim):
    query_blocks, key_blocks = inter_ref.shape
    width = bias_ref.shape[1]
    lane = lax.broadcasted_iota(jnp.int32, (1, width), 1) % head_dim
    for key_block in range(key_blocks):
        row = jnp.zeros((1, width), jnp.float32)
        for query_block in range(query_blocks):
            listed = inter_ref[query_block, key_block] == 1
            row = jnp.where(lane == query_block, jnp.where(listed, 0.0, NEG), row)
        bias_ref[pl.ds(key_block * BLOCK, BLOCK), :] = bf(
            jnp.broadcast_to(row, (BLOCK, width))
        )


def fill_hot(hot_ref, head_dim):
    rows, width = hot_ref.shape
    lane = lax.broadcasted_iota(jnp.int32, (1, width), 1) % head_dim
    for block in range(rows // BLOCK):
        row = bf(jnp.where(lane == block, 1.0, 0.0))
        hot_ref[pl.ds(block * BLOCK, BLOCK), :] = jnp.broadcast_to(row, (BLOCK, width))


def fill_scores(
    head, heads, query_ref, hot_ref, key_ref, bias_ref, grad_ref, value_ref, score_ref, prob_ref,
    peak_ref=None,
):
    rows, width = query_ref.shape
    own = lane_row(width, head, width // heads)
    other = lane_row(width, (head + 1) % heads, width // heads)
    left = query_ref[...] * own + hot_ref[...] * other
    left_grad = grad_ref[...] * own
    key_total = key_ref.shape[0]
    step = min(256, key_total)
    row_peak = None
    col_peaks = []
    for first in range(0, key_total, step):
        span = pl.ds(first, step)
        right = key_ref[span, :] * own + bias_ref[span, :] * other
        scores = mm_general(left, right, NT)
        score_ref[:, span] = scores
        if peak_ref is not None:
            for at in range(0, step, 128):
                piece = scores[:, at : at + 128]
                row_peak = piece if row_peak is None else jnp.maximum(row_peak, piece)
            col_peaks.append(scores.max(axis=0, keepdims=True))
        prob_ref[:, span] = mm_general(left_grad, value_ref[span, :], NT)
    if peak_ref is not None:
        peak_ref[...] = row_peak
        return jnp.concatenate(col_peaks, axis=1)


def spread(reduced, like):
    return jnp.broadcast_to(reduced, like.shape)


def fold8(x):
    return x.reshape(x.shape[0] // 8, 8, x.shape[1]).sum(axis=0)


STRIP = 32


def stats_kernel(
    head_count, inter_ref, ref_ref, gout_ref, src_ref, wq_ref, wk_ref, wv_ref, wo_ref,
    row_ref, col_ref, query_ref, grad_ref, key_ref, value_ref, bias_ref, hot_ref, score_ref, prob_ref,
    part_ref,
):
    rows, width = ref_ref.shape
    key_total = src_ref.shape[0]
    tiles = key_total // 128
    head_dim = width // head_count
    scale = head_dim ** -0.5
    query_ref[...] = bf(bf(mm(ref_ref[...], wq_ref[...])).astype(jnp.float32) * scale)
    grad_ref[...] = bf(mm_general(gout_ref[...], wo_ref[...], NT))
    key_ref[...] = bf(mm(src_ref[...], wk_ref[...]))
    value_ref[...] = bf(mm(src_ref[...], wv_ref[...]))
    fill_bias(inter_ref, bias_ref, head_dim)
    fill_hot(hot_ref, head_dim)
    for head in range(head_count):
        mine = slice(head, head + 1)
        col_peak = fill_scores(
            head, head_count, query_ref, hot_ref, key_ref, bias_ref, grad_ref, value_ref,
            score_ref, prob_ref, part_ref,
        )
        col_ref[0, mine, :] = jnp.maximum(col_peak, FLOOR)
        row_ref[head] = spread(part_ref[...].max(axis=1, keepdims=True), part_ref)

        def totals(step, col_totals):
            span = pl.ds(step * STRIP, STRIP)
            row_peak = row_ref[head, span, :]
            row_total = jnp.zeros((STRIP, 128), jnp.float32)
            out = []
            for tile in range(tiles):
                lanes = slice(tile * 128, tile * 128 + 128)
                scores = score_ref[span, lanes]
                row_exp = jnp.exp(scores - row_peak)
                col_exp = jnp.exp(scores - col_ref[0, mine, lanes])
                row_total = row_total + row_exp
                prob_ref[span, lanes] = row_exp * col_exp * prob_ref[span, lanes]
                out.append(col_totals[tile] + fold8(col_exp))
            part_ref[span, :] = row_total
            return tuple(out)

        zeros = tuple(jnp.zeros((8, 128), jnp.float32) for _ in range(tiles))
        col_totals = lax.fori_loop(0, rows // STRIP, totals, zeros)
        row_total = part_ref[...].sum(axis=1, keepdims=True)
        row_ref[head_count + head] = spread(1.0 / row_total, part_ref)

        def dots(step, col_dots):
            span = pl.ds(step * STRIP, STRIP)
            row_inverse = row_ref[head_count + head, span, :]
            return tuple(
                col_dots[tile]
                + fold8(prob_ref[span, tile * 128 : tile * 128 + 128] * row_inverse)
                for tile in range(tiles)
            )

        col_dots = lax.fori_loop(0, rows // STRIP, dots, zeros)
        for tile in range(tiles):
            lanes = slice(tile * 128, tile * 128 + 128)
            col_ref[1, mine, lanes] = col_totals[tile].sum(axis=0, keepdims=True)
            col_ref[2, mine, lanes] = col_dots[tile].sum(axis=0, keepdims=True)


def grads_kernel(
    head_count, inter_ref, ref_ref, gout_ref, src_ref, wq_ref, wk_ref, wv_ref, wo_ref, row_ref, near_ref,
    far_ref, matched_ref, gref_ref, gsrc_ref, weight_ref,
    query_ref, grad_ref, key_ref, value_ref, bias_ref, hot_ref, score_ref, prob_ref, part_ref,
    match_ref, gscore_ref, query_t_ref, grad_t_ref, gkey_ref, gvalue_ref, att_ref, gquery_ref,
    col_ref,
):
    rows, width = ref_ref.shape
    key_total = src_ref.shape[0]
    tiles = key_total // 128
    head_dim = width // head_count
    scale = head_dim ** -0.5
    queries = bf(mm(ref_ref[...], wq_ref[...])).astype(jnp.float32)
    query_ref[...] = bf(queries * scale)
    grad_ref[...] = bf(mm_general(gout_ref[...], wo_ref[...], NT))
    queries_t = bf(mm_general(wq_ref[...], ref_ref[...], TT)).astype(jnp.float32)
    query_t_ref[...] = bf(queries_t * (2.0 * scale))
    grad_t_ref[...] = bf(mm_general(wo_ref[...], gout_ref[...], NT))
    key_ref[...] = bf(mm(src_ref[...], wk_ref[...]))
    value_ref[...] = bf(mm(src_ref[...], wv_ref[...]))
    fill_bias(inter_ref, bias_ref, head_dim)
    fill_hot(hot_ref, head_dim)

    peak = jnp.maximum(near_ref[0], far_ref[0])
    near, far = jnp.exp(near_ref[0] - peak), jnp.exp(far_ref[0] - peak)
    inverse = 1.0 / (near * near_ref[1] + far * far_ref[1])
    col_ref[0] = peak
    col_ref[1] = inverse
    col_ref[2] = (near * near_ref[2] + far * far_ref[2]) * inverse * 0.5

    for head in range(head_count):
        mine = slice(head, head + 1)
        fill_scores(
            head, head_count, query_ref, hot_ref, key_ref, bias_ref, grad_ref, value_ref,
            score_ref, prob_ref,
        )

        def products(step, carry):
            span = pl.ds(step * STRIP, STRIP)
            row_peak = row_ref[head, span, :]
            row_inverse = row_ref[head_count + head, span, :]
            row_dot = jnp.zeros((STRIP, 128), jnp.float32)
            for tile in range(tiles):
                lanes = slice(tile * 128, tile * 128 + 128)
                scores = score_ref[span, lanes]
                row_prob = jnp.exp(scores - row_peak) * row_inverse
                col_prob = (
                    jnp.exp(scores - col_ref[0, mine, lanes])
                    * col_ref[1, mine, lanes]
                )
                match = row_prob * col_prob
                product = match * prob_ref[span, lanes]
                row_dot = row_dot + product
                match_ref[span, lanes] = bf(match)
                score_ref[span, lanes] = row_prob
                prob_ref[span, lanes] = product - col_prob * col_ref[2, mine, lanes]
            part_ref[span, :] = row_dot
            return carry

        lax.fori_loop(0, rows // STRIP, products, 0)
        part_ref[...] = spread(part_ref[...].sum(axis=1, keepdims=True) * 0.5, part_ref)

        def score_grads(step, carry):
            span = pl.ds(step * STRIP, STRIP)
            row_half = part_ref[span, :]
            for tile in range(tiles):
                lanes = slice(tile * 128, tile * 128 + 128)
                gscore_ref[span, lanes] = bf(
                    prob_ref[span, lanes] - score_ref[span, lanes] * row_half
                )
            return carry

        lax.fori_loop(0, rows // STRIP, score_grads, 0)

        own = lane_row(width, head, head_dim)
        attended = mm(match_ref[...], value_ref[...] * own)
        gquery = mm(gscore_ref[...], key_ref[...] * bf(own.astype(jnp.float32) * (2.0 * scale)))
        if head == 0:
            att_ref[...] = attended
            gquery_ref[...] = gquery
        else:
            att_ref[...] += attended
            gquery_ref[...] += gquery
        span = pl.ds(head * head_dim, head_dim)
        gkey_ref[span, :] = bf(mm(query_t_ref[span, :], gscore_ref[...]))
        gvalue_ref[span, :] = bf(mm(grad_t_ref[span, :], match_ref[...]))

    attended = bf(att_ref[...])
    gquery = bf(gquery_ref[...])
    matched_ref[...] = bf(ref_ref[...].astype(jnp.float32) + mm(attended, wo_ref[...]))
    gref_ref[...] = bf(
        gout_ref[...].astype(jnp.float32) + mm_general(gquery, wq_ref[...], NT)
    )
    gsrc_t = mm(wk_ref[...], gkey_ref[...]) + mm(wv_ref[...], gvalue_ref[...])
    gsrc_ref[...] = bf(gsrc_t.T)
    weight_ref[0] = bf(mm_general(ref_ref[...], gquery, TN))
    weight_ref[1] = bf(mm(gkey_ref[...], src_ref[...]).T)
    weight_ref[2] = bf(mm(gvalue_ref[...], src_ref[...]).T)
    weight_ref[3] = bf(mm_general(attended, gout_ref[...], TN))


def swap(x, axis, apart):
    pairs = [(i, i ^ apart) for i in range(lax.axis_size(axis))]
    return lax.ppermute(x, axis, pairs)


def at(x, index, axis=0):
    return lax.dynamic_index_in_dim(x, index, axis, False)


def laid(pieces, places, axis=0):
    out = jnp.zeros(pieces[0].shape[:axis] + (len(pieces),) + pieces[0].shape[axis:], pieces[0].dtype)
    for piece, place in zip(pieces, places):
        out = lax.dynamic_update_index_in_dim(out, piece, place, axis)
    return out


def gather_direct(x, axis, me, count, stride):
    pieces = [x] + [swap(x, axis, k * stride) for k in range(1, count)]
    return laid(pieces, [me ^ k for k in range(count)])


def scatter_direct(x, axis, me, count, stride):
    total = at(x, me).astype(jnp.float32)
    for piece in [swap(at(x, me ^ k), axis, k * stride) for k in range(1, count)]:
        total = total + piece.astype(jnp.float32)
    return total.astype(x.dtype)


def combine_stats(parts):
    peak = functools.reduce(jnp.maximum, [part[0] for part in parts])
    factors = [jnp.exp(part[0] - peak) for part in parts]
    total = sum(factor * part[1] for factor, part in zip(factors, parts))
    dots = sum(factor * part[2] for factor, part in zip(factors, parts))
    return jnp.stack([peak, total, dots])


def vmem_call(kernel, name, out_shape, scratch, flops, moved, args):
    specs = [pl.BlockSpec(memory_space=pltpu.SMEM)]
    specs += [pl.BlockSpec(memory_space=pltpu.VMEM)] * (len(args) - 1)
    return pl.pallas_call(
        kernel,
        name=name,
        out_shape=out_shape,
        in_specs=specs,
        out_specs=[pl.BlockSpec(memory_space=pltpu.VMEM)] * len(out_shape),
        scratch_shapes=scratch,
        compiler_params=pltpu.CompilerParams(vmem_limit_bytes=VMEM_LIMIT),
        cost_estimate=pl.CostEstimate(flops=flops, bytes_accessed=moved, transcendentals=0),
    )(*args)


def on_device(ref_feats, src_feats, grad_out, w_query, w_key, w_value, w_out, intersection):
    ref_rows = ref_feats[0]
    src_rows = src_feats[0]
    out_grad = grad_out[0]
    listed = intersection[0]
    rows, width = ref_rows.shape
    scans, chips = lax.axis_size("scan"), lax.axis_size("blk") // 2
    scan, core = lax.axis_index("scan"), lax.axis_index("blk") % 2
    chip = lax.axis_index("blk") // 2
    key_rows = src_rows.shape[0]
    key_total = key_rows * chips * 2

    same_core = gather_direct(src_rows, "blk", chip, chips, 2)
    source_all = laid([same_core, swap(same_core, "blk", 1)], [core, 1 - core], axis=1)
    source_all = source_all.reshape(key_total, width)

    f32, b16 = jnp.float32, jnp.bfloat16
    shape = jax.ShapeDtypeStruct
    common = [
        pltpu.VMEM((rows, width), b16),
        pltpu.VMEM((rows, width), b16),
        pltpu.VMEM((key_total, width), b16),
        pltpu.VMEM((key_total, width), b16),
        pltpu.VMEM((key_total, width), b16),
        pltpu.VMEM((rows, width), b16),
        pltpu.VMEM((rows, key_total), f32),
        pltpu.VMEM((rows, key_total), f32),
        pltpu.VMEM((rows, 128), f32),
    ]
    base = (listed, ref_rows, out_grad, source_all, w_query, w_key, w_value, w_out)
    tile_flops = 2 * rows * key_total * width
    row_stats, col_stats = vmem_call(
        functools.partial(stats_kernel, HEADS),
        "match_stats",
        [shape((2 * HEADS, rows, 128), f32), shape((3, HEADS, key_total), f32)],
        common,
        2 * tile_flops,
        2 << 20,
        base,
    )
    near_stats = combine_stats(
        [col_stats] + [swap(col_stats, "blk", 2 * k) for k in range(1, chips)]
    )
    far_stats = swap(near_stats, "blk", 1)
    matched, grad_ref, source_part, weight_part = vmem_call(
        functools.partial(grads_kernel, HEADS),
        "match_grads",
        [
            shape((rows, width), b16),
            shape((rows, width), b16),
            shape((key_total, width), b16),
            shape((4, width, width), b16),
        ],
        common
        + [
            pltpu.VMEM((rows, key_total), b16),
            pltpu.VMEM((rows, key_total), b16),
            pltpu.VMEM((width, rows), b16),
            pltpu.VMEM((width, rows), b16),
            pltpu.VMEM((width, key_total), b16),
            pltpu.VMEM((width, key_total), b16),
            pltpu.VMEM((rows, width), f32),
            pltpu.VMEM((rows, width), f32),
            pltpu.VMEM((3, HEADS, key_total), f32),
        ],
        6 * tile_flops,
        4 << 20,
        base + (row_stats, near_stats, far_stats),
    )

    weights = weight_part.reshape(2, scans, chips, -1, width)
    sources = source_part.reshape(chips, 2, key_rows, width)
    weights = scatter_direct(weights, "blk", core, 2, 1)
    near, far = at(sources, core, 1), at(sources, 1 - core, 1)
    sources = (near.astype(f32) + swap(far, "blk", 1).astype(f32)).astype(b16)
    weights = scatter_direct(weights, "scan", scan, scans, 1)
    grad_src = scatter_direct(sources, "blk", chip, chips, 2)
    weights = scatter_direct(weights, "blk", chip, chips, 2)
    weights = gather_direct(weights, "blk", chip, chips, 2)
    weights = gather_direct(weights, "scan", scan, scans, 1)
    weights = gather_direct(weights, "blk", core, 2, 1)
    weights = weights.reshape(4, width, width).astype(f32)
    return (
        matched[None],
        grad_ref[None],
        grad_src[None],
        weights[0],
        weights[1],
        weights[2],
        weights[3],
    )


def solution(mesh):
    split = P("scan", "blk", None)
    whole = P()
    return jax.shard_map(
        on_device,
        mesh=mesh,
        in_specs=(split, split, split, whole, whole, whole, whole, split),
        out_specs=(split, split, split, whole, whole, whole, whole),
        check_vma=False,
    )
```

```python
import functools

import jax
import jax.numpy as jnp
from jax import lax
from jax.experimental import pallas as pl
from jax.experimental.pallas import tpu as pltpu
from jax.sharding import PartitionSpec as P

HEADS = 4
BLOCK = 128
NEG = -1e30
FLOOR = -1e29
VMEM_LIMIT = 30 * 1024 * 1024

NT = (((1,), (1,)), ((), ()))
TN = (((0,), (0,)), ((), ()))
TT = (((0,), (1,)), ((), ()))


def mm(left, right):
    return jnp.dot(left, right, preferred_element_type=jnp.float32)


def mm_general(left, right, dims):
    return lax.dot_general(left, right, dims, preferred_element_type=jnp.float32)


def bf(x):
    return x.astype(jnp.bfloat16)


def lane_row(width, head, head_dim):
    lanes = lax.broadcasted_iota(jnp.int32, (1, width), 1) // head_dim
    return bf(jnp.where(lanes == head, 1.0, 0.0))


def fill_bias(inter_ref, bias_ref, head_dim):
    query_blocks, key_blocks = inter_ref.shape
    width = bias_ref.shape[1]
    lane = lax.broadcasted_iota(jnp.int32, (1, width), 1) % head_dim
    for key_block in range(key_blocks):
        row = jnp.zeros((1, width), jnp.float32)
        for query_block in range(query_blocks):
            listed = inter_ref[query_block, key_block] == 1
            row = jnp.where(lane == query_block, jnp.where(listed, 0.0, NEG), row)
        bias_ref[pl.ds(key_block * BLOCK, BLOCK), :] = bf(
            jnp.broadcast_to(row, (BLOCK, width))
        )


def fill_hot(hot_ref, head_dim):
    rows, width = hot_ref.shape
    lane = lax.broadcasted_iota(jnp.int32, (1, width), 1) % head_dim
    for block in range(rows // BLOCK):
        row = bf(jnp.where(lane == block, 1.0, 0.0))
        hot_ref[pl.ds(block * BLOCK, BLOCK), :] = jnp.broadcast_to(row, (BLOCK, width))


def fill_scores(
    head, heads, query_ref, hot_ref, key_ref, bias_ref, grad_ref, value_ref, score_ref, prob_ref,
    peak_ref=None,
):
    rows, width = query_ref.shape
    own = lane_row(width, head, width // heads)
    other = lane_row(width, (head + 1) % heads, width // heads)
    left = query_ref[...] * own + hot_ref[...] * other
    left_grad = grad_ref[...] * own
    key_total = key_ref.shape[0]
    step = min(256, key_total)
    row_peak = None
    col_peaks = []
    for first in range(0, key_total, step):
        span = pl.ds(first, step)
        right = key_ref[span, :] * own + bias_ref[span, :] * other
        scores = mm_general(left, right, NT)
        score_ref[:, span] = scores
        if peak_ref is not None:
            for at in range(0, step, 128):
                piece = scores[:, at : at + 128]
                row_peak = piece if row_peak is None else jnp.maximum(row_peak, piece)
            col_peaks.append(scores.max(axis=0, keepdims=True))
        prob_ref[:, span] = mm_general(left_grad, value_ref[span, :], NT)
    if peak_ref is not None:
        peak_ref[...] = row_peak
        return jnp.concatenate(col_peaks, axis=1)


def spread(reduced, like):
    return jnp.broadcast_to(reduced, like.shape)


def fold8(x):
    return x.reshape(x.shape[0] // 8, 8, x.shape[1]).sum(axis=0)


STRIP = 32


def stats_kernel(
    head_count, inter_ref, ref_ref, gout_ref, src_ref, wq_ref, wk_ref, wv_ref, wo_ref,
    row_ref, col_ref, query_ref, grad_ref, key_ref, value_ref, bias_ref, hot_ref, score_ref, prob_ref,
    part_ref,
):
    rows, width = ref_ref.shape
    key_total = src_ref.shape[0]
    tiles = key_total // 128
    head_dim = width // head_count
    scale = head_dim ** -0.5
    query_ref[...] = bf(bf(mm(ref_ref[...], wq_ref[...])).astype(jnp.float32) * scale)
    grad_ref[...] = bf(mm_general(gout_ref[...], wo_ref[...], NT))
    key_ref[...] = bf(mm(src_ref[...], wk_ref[...]))
    value_ref[...] = bf(mm(src_ref[...], wv_ref[...]))
    fill_bias(inter_ref, bias_ref, head_dim)
    fill_hot(hot_ref, head_dim)
    for head in range(head_count):
        mine = slice(head, head + 1)
        col_peak = fill_scores(
            head, head_count, query_ref, hot_ref, key_ref, bias_ref, grad_ref, value_ref,
            score_ref, prob_ref, part_ref,
        )
        col_ref[0, mine, :] = jnp.maximum(col_peak, FLOOR)
        row_ref[head] = spread(part_ref[...].max(axis=1, keepdims=True), part_ref)

        def totals(step, col_totals):
            span = pl.ds(step * STRIP, STRIP)
            row_peak = row_ref[head, span, :]
            row_total = jnp.zeros((STRIP, 128), jnp.float32)
            out = []
            for tile in range(tiles):
                lanes = slice(tile * 128, tile * 128 + 128)
                scores = score_ref[span, lanes]
                row_exp = jnp.exp(scores - row_peak)
                col_exp = jnp.exp(scores - col_ref[0, mine, lanes])
                row_total = row_total + row_exp
                prob_ref[span, lanes] = row_exp * col_exp * prob_ref[span, lanes]
                out.append(col_totals[tile] + fold8(col_exp))
            part_ref[span, :] = row_total
            return tuple(out)

        zeros = tuple(jnp.zeros((8, 128), jnp.float32) for _ in range(tiles))
        col_totals = lax.fori_loop(0, rows // STRIP, totals, zeros)
        row_total = part_ref[...].sum(axis=1, keepdims=True)
        row_ref[head_count + head] = spread(1.0 / row_total, part_ref)

        def dots(step, col_dots):
            span = pl.ds(step * STRIP, STRIP)
            row_inverse = row_ref[head_count + head, span, :]
            return tuple(
                col_dots[tile]
                + fold8(prob_ref[span, tile * 128 : tile * 128 + 128] * row_inverse)
                for tile in range(tiles)
            )

        col_dots = lax.fori_loop(0, rows // STRIP, dots, zeros)
        for tile in range(tiles):
            lanes = slice(tile * 128, tile * 128 + 128)
            col_ref[1, mine, lanes] = col_totals[tile].sum(axis=0, keepdims=True)
            col_ref[2, mine, lanes] = col_dots[tile].sum(axis=0, keepdims=True)


def grads_kernel(
    head_count, inter_ref, ref_ref, gout_ref, src_ref, wq_ref, wk_ref, wv_ref, wo_ref, row_ref, near_ref,
    far_ref, matched_ref, gref_ref, gsrc_ref, weight_ref,
    query_ref, grad_ref, key_ref, value_ref, bias_ref, hot_ref, score_ref, prob_ref, part_ref,
    match_ref, gscore_ref, query_t_ref, grad_t_ref, gkey_ref, gvalue_ref, att_ref, gquery_ref,
    col_ref,
):
    rows, width = ref_ref.shape
    key_total = src_ref.shape[0]
    tiles = key_total // 128
    head_dim = width // head_count
    scale = head_dim ** -0.5
    queries = bf(mm(ref_ref[...], wq_ref[...])).astype(jnp.float32)
    query_ref[...] = bf(queries * scale)
    grad_ref[...] = bf(mm_general(gout_ref[...], wo_ref[...], NT))
    queries_t = bf(mm_general(wq_ref[...], ref_ref[...], TT)).astype(jnp.float32)
    query_t_ref[...] = bf(queries_t * (2.0 * scale))
    grad_t_ref[...] = bf(mm_general(wo_ref[...], gout_ref[...], NT))
    key_ref[...] = bf(mm(src_ref[...], wk_ref[...]))
    value_ref[...] = bf(mm(src_ref[...], wv_ref[...]))
    fill_bias(inter_ref, bias_ref, head_dim)
    fill_hot(hot_ref, head_dim)

    peak = jnp.maximum(near_ref[0], far_ref[0])
    near, far = jnp.exp(near_ref[0] - peak), jnp.exp(far_ref[0] - peak)
    inverse = 1.0 / (near * near_ref[1] + far * far_ref[1])
    col_ref[0] = peak
    col_ref[1] = inverse
    col_ref[2] = (near * near_ref[2] + far * far_ref[2]) * inverse * 0.5

    for head in range(head_count):
        mine = slice(head, head + 1)
        fill_scores(
            head, head_count, query_ref, hot_ref, key_ref, bias_ref, grad_ref, value_ref,
            score_ref, prob_ref,
        )

        def products(step, carry):
            span = pl.ds(step * STRIP, STRIP)
            row_peak = row_ref[head, span, :]
            row_inverse = row_ref[head_count + head, span, :]
            row_dot = jnp.zeros((STRIP, 128), jnp.float32)
            for tile in range(tiles):
                lanes = slice(tile * 128, tile * 128 + 128)
                scores = score_ref[span, lanes]
                row_prob = jnp.exp(scores - row_peak) * row_inverse
                col_prob = (
                    jnp.exp(scores - col_ref[0, mine, lanes])
                    * col_ref[1, mine, lanes]
                )
                match = row_prob * col_prob
                product = match * prob_ref[span, lanes]
                row_dot = row_dot + product
                match_ref[span, lanes] = bf(match)
                score_ref[span, lanes] = row_prob
                prob_ref[span, lanes] = product - col_prob * col_ref[2, mine, lanes]
            part_ref[span, :] = row_dot
            return carry

        lax.fori_loop(0, rows // STRIP, products, 0)
        part_ref[...] = spread(part_ref[...].sum(axis=1, keepdims=True) * 0.5, part_ref)

        def score_grads(step, carry):
            span = pl.ds(step * STRIP, STRIP)
            row_half = part_ref[span, :]
            for tile in range(tiles):
                lanes = slice(tile * 128, tile * 128 + 128)
                gscore_ref[span, lanes] = bf(
                    prob_ref[span, lanes] - score_ref[span, lanes] * row_half
                )
            return carry

        lax.fori_loop(0, rows // STRIP, score_grads, 0)

        own = lane_row(width, head, head_dim)
        attended = mm(match_ref[...], value_ref[...] * own)
        gquery = mm(gscore_ref[...], key_ref[...] * bf(own.astype(jnp.float32) * (2.0 * scale)))
        if head == 0:
            att_ref[...] = attended
            gquery_ref[...] = gquery
        else:
            att_ref[...] += attended
            gquery_ref[...] += gquery
        span = pl.ds(head * head_dim, head_dim)
        gkey_ref[span, :] = bf(mm(query_t_ref[span, :], gscore_ref[...]))
        gvalue_ref[span, :] = bf(mm(grad_t_ref[span, :], match_ref[...]))

    attended = bf(att_ref[...])
    gquery = bf(gquery_ref[...])
    matched_ref[...] = bf(ref_ref[...].astype(jnp.float32) + mm(attended, wo_ref[...]))
    gref_ref[...] = bf(
        gout_ref[...].astype(jnp.float32) + mm_general(gquery, wq_ref[...], NT)
    )
    gsrc_t = mm(wk_ref[...], gkey_ref[...]) + mm(wv_ref[...], gvalue_ref[...])
    gsrc_ref[...] = bf(gsrc_t.T)
    weight_ref[0] = bf(mm_general(ref_ref[...], gquery, TN))
    weight_ref[1] = bf(mm(gkey_ref[...], src_ref[...]).T)
    weight_ref[2] = bf(mm(gvalue_ref[...], src_ref[...]).T)
    weight_ref[3] = bf(mm_general(attended, gout_ref[...], TN))


def swap(x, axis, apart):
    pairs = [(i, i ^ apart) for i in range(lax.axis_size(axis))]
    return lax.ppermute(x, axis, pairs)


def at(x, index, axis=0):
    return lax.dynamic_index_in_dim(x, index, axis, False)


def laid(near, far, side, axis=0):
    shape = near.shape[:axis] + (2,) + near.shape[axis:]
    out = lax.dynamic_update_index_in_dim(jnp.zeros(shape, near.dtype), near, side, axis)
    return lax.dynamic_update_index_in_dim(out, far, 1 - side, axis)


def add(near, far):
    return (near.astype(jnp.float32) + far.astype(jnp.float32)).astype(near.dtype)


def halve(x, step, axis=0):
    mesh_axis, bit, side = step
    return add(at(x, side, axis), swap(at(x, 1 - side, axis), mesh_axis, bit))


def double(x, step, axis=0):
    mesh_axis, bit, side = step
    return laid(x, swap(x, mesh_axis, bit), side, axis)


def bit_steps(mesh_axis, first=1):
    count, me = lax.axis_size(mesh_axis), lax.axis_index(mesh_axis)
    steps = []
    while first < count:
        steps.append((mesh_axis, first, (me // first) % 2))
        first *= 2
    return steps


def combine_stats(parts):
    peak = functools.reduce(jnp.maximum, [part[0] for part in parts])
    factors = [jnp.exp(part[0] - peak) for part in parts]
    total = sum(factor * part[1] for factor, part in zip(factors, parts))
    dots = sum(factor * part[2] for factor, part in zip(factors, parts))
    return jnp.stack([peak, total, dots])


def vmem_call(kernel, name, out_shape, scratch, flops, moved, args):
    specs = [pl.BlockSpec(memory_space=pltpu.SMEM)]
    specs += [pl.BlockSpec(memory_space=pltpu.VMEM)] * (len(args) - 1)
    return pl.pallas_call(
        kernel,
        name=name,
        out_shape=out_shape,
        in_specs=specs,
        out_specs=[pl.BlockSpec(memory_space=pltpu.VMEM)] * len(out_shape),
        scratch_shapes=scratch,
        compiler_params=pltpu.CompilerParams(vmem_limit_bytes=VMEM_LIMIT),
        cost_estimate=pl.CostEstimate(flops=flops, bytes_accessed=moved, transcendentals=0),
    )(*args)


def on_device(ref_feats, src_feats, grad_out, w_query, w_key, w_value, w_out, intersection):
    ref_rows = ref_feats[0]
    src_rows = src_feats[0]
    out_grad = grad_out[0]
    listed = intersection[0]
    rows, width = ref_rows.shape
    core_step = bit_steps("blk")[0]
    chip_steps = bit_steps("blk", 2)
    scan_steps = bit_steps("scan")
    key_rows = src_rows.shape[0]
    key_total = key_rows * lax.axis_size("blk")

    source_all = src_rows
    for count, step in enumerate(chip_steps[::-1]):
        source_all = double(source_all, step, count)
    source_all = double(source_all, core_step, len(chip_steps)).reshape(key_total, width)

    f32, b16 = jnp.float32, jnp.bfloat16
    shape = jax.ShapeDtypeStruct
    common = [
        pltpu.VMEM((rows, width), b16),
        pltpu.VMEM((rows, width), b16),
        pltpu.VMEM((key_total, width), b16),
        pltpu.VMEM((key_total, width), b16),
        pltpu.VMEM((key_total, width), b16),
        pltpu.VMEM((rows, width), b16),
        pltpu.VMEM((rows, key_total), f32),
        pltpu.VMEM((rows, key_total), f32),
        pltpu.VMEM((rows, 128), f32),
    ]
    base = (listed, ref_rows, out_grad, source_all, w_query, w_key, w_value, w_out)
    tile_flops = 2 * rows * key_total * width
    row_stats, col_stats = vmem_call(
        functools.partial(stats_kernel, HEADS),
        "match_stats",
        [shape((2 * HEADS, rows, 128), f32), shape((3, HEADS, key_total), f32)],
        common,
        2 * tile_flops,
        2 << 20,
        base,
    )
    near_stats = col_stats
    for mesh_axis, bit, _ in chip_steps:
        near_stats = combine_stats([near_stats, swap(near_stats, mesh_axis, bit)])
    far_stats = swap(near_stats, "blk", 1)
    matched, grad_ref, source_part, weight_part = vmem_call(
        functools.partial(grads_kernel, HEADS),
        "match_grads",
        [
            shape((rows, width), b16),
            shape((rows, width), b16),
            shape((key_total, width), b16),
            shape((4, width, width), b16),
        ],
        common
        + [
            pltpu.VMEM((rows, key_total), b16),
            pltpu.VMEM((rows, key_total), b16),
            pltpu.VMEM((width, rows), b16),
            pltpu.VMEM((width, rows), b16),
            pltpu.VMEM((width, key_total), b16),
            pltpu.VMEM((width, key_total), b16),
            pltpu.VMEM((rows, width), f32),
            pltpu.VMEM((rows, width), f32),
            pltpu.VMEM((3, HEADS, key_total), f32),
        ],
        6 * tile_flops,
        4 << 20,
        base + (row_stats, near_stats, far_stats),
    )

    halves = [core_step] + scan_steps
    weights = weight_part.reshape((2,) * len(halves) + (-1, width))
    sources = source_part.reshape((2,) * (len(chip_steps) + 1) + (key_rows, width))
    weights = halve(weights, halves[0])
    sources = halve(sources, core_step, len(chip_steps))
    for step in halves[1:]:
        weights = halve(weights, step)
    for count in range(len(chip_steps)):
        sources = halve(sources, chip_steps[count], len(chip_steps) - 1 - count)
    grad_src = sources
    for mesh_axis, bit, _ in chip_steps:
        weights = add(weights, swap(weights, mesh_axis, bit))
    for step in halves[::-1]:
        weights = double(weights, step)
    weights = weights.reshape(4, width, width).astype(f32)
    return (
        matched[None],
        grad_ref[None],
        grad_src[None],
        weights[0],
        weights[1],
        weights[2],
        weights[3],
    )


def solution(mesh):
    split = P("scan", "blk", None)
    whole = P()
    return jax.shard_map(
        on_device,
        mesh=mesh,
        in_specs=(split, split, split, whole, whole, whole, whole, split),
        out_specs=(split, split, split, whole, whole, whole, whole),
        check_vma=False,
    )
```

```python
import functools

import jax
import jax.numpy as jnp
from jax import lax
from jax.experimental import pallas as pl
from jax.experimental.pallas import tpu as pltpu
from jax.sharding import PartitionSpec as P

HEADS = 4
BLOCK = 128
NEG = -1e30
FLOOR = -1e29
VMEM_LIMIT = 30 * 1024 * 1024

NT = (((1,), (1,)), ((), ()))
TN = (((0,), (0,)), ((), ()))
TT = (((0,), (1,)), ((), ()))


def mm(left, right):
    return jnp.dot(left, right, preferred_element_type=jnp.float32)


def mm_general(left, right, dims):
    return lax.dot_general(left, right, dims, preferred_element_type=jnp.float32)


def bf(x):
    return x.astype(jnp.bfloat16)


def lane_row(width, head, head_dim):
    lanes = lax.broadcasted_iota(jnp.int32, (1, width), 1) // head_dim
    return bf(jnp.where(lanes == head, 1.0, 0.0))


def fill_bias(inter_ref, bias_ref, head_dim):
    query_blocks, key_blocks = inter_ref.shape
    width = bias_ref.shape[1]
    lane = lax.broadcasted_iota(jnp.int32, (1, width), 1) % head_dim
    for key_block in range(key_blocks):
        row = jnp.zeros((1, width), jnp.float32)
        for query_block in range(query_blocks):
            listed = inter_ref[query_block, key_block] == 1
            row = jnp.where(lane == query_block, jnp.where(listed, 0.0, NEG), row)
        bias_ref[pl.ds(key_block * BLOCK, BLOCK), :] = bf(
            jnp.broadcast_to(row, (BLOCK, width))
        )


def fill_hot(hot_ref, head_dim):
    rows, width = hot_ref.shape
    lane = lax.broadcasted_iota(jnp.int32, (1, width), 1) % head_dim
    for block in range(rows // BLOCK):
        row = bf(jnp.where(lane == block, 1.0, 0.0))
        hot_ref[pl.ds(block * BLOCK, BLOCK), :] = jnp.broadcast_to(row, (BLOCK, width))


def fill_scores(
    head, heads, query_ref, hot_ref, key_ref, bias_ref, grad_ref, value_ref, score_ref, prob_ref,
    peak_ref=None,
):
    rows, width = query_ref.shape
    own = lane_row(width, head, width // heads)
    other = lane_row(width, (head + 1) % heads, width // heads)
    left = query_ref[...] * own + hot_ref[...] * other
    left_grad = grad_ref[...] * own
    key_total = key_ref.shape[0]
    step = min(256, key_total)
    row_peak = None
    col_peaks = []
    for first in range(0, key_total, step):
        span = pl.ds(first, step)
        right = key_ref[span, :] * own + bias_ref[span, :] * other
        scores = mm_general(left, right, NT)
        score_ref[:, span] = scores
        if peak_ref is not None:
            for at in range(0, step, 128):
                piece = scores[:, at : at + 128]
                row_peak = piece if row_peak is None else jnp.maximum(row_peak, piece)
            col_peaks.append(scores.max(axis=0, keepdims=True))
        prob_ref[:, span] = mm_general(left_grad, value_ref[span, :], NT)
    if peak_ref is not None:
        peak_ref[...] = row_peak
        return jnp.concatenate(col_peaks, axis=1)


def spread(reduced, like):
    return jnp.broadcast_to(reduced, like.shape)


def fold8(x):
    return x.reshape(x.shape[0] // 8, 8, x.shape[1]).sum(axis=0)


STRIP = 32


def stats_kernel(
    head_count, inter_ref, ref_ref, gout_ref, src_ref, wq_ref, wk_ref, wv_ref, wo_ref,
    row_ref, col_ref, query_ref, grad_ref, key_ref, value_ref, bias_ref, hot_ref, score_ref, prob_ref,
    part_ref,
):
    rows, width = ref_ref.shape
    key_total = src_ref.shape[0]
    tiles = key_total // 128
    head_dim = width // head_count
    scale = head_dim ** -0.5
    query_ref[...] = bf(bf(mm(ref_ref[...], wq_ref[...])).astype(jnp.float32) * scale)
    grad_ref[...] = bf(mm_general(gout_ref[...], wo_ref[...], NT))
    key_ref[...] = bf(mm(src_ref[...], wk_ref[...]))
    value_ref[...] = bf(mm(src_ref[...], wv_ref[...]))
    fill_bias(inter_ref, bias_ref, head_dim)
    fill_hot(hot_ref, head_dim)
    for head in range(head_count):
        mine = slice(head, head + 1)
        col_peak = fill_scores(
            head, head_count, query_ref, hot_ref, key_ref, bias_ref, grad_ref, value_ref,
            score_ref, prob_ref, part_ref,
        )
        col_ref[0, mine, :] = jnp.maximum(col_peak, FLOOR)
        row_ref[head] = spread(part_ref[...].max(axis=1, keepdims=True), part_ref)

        def totals(step, col_totals):
            span = pl.ds(step * STRIP, STRIP)
            row_peak = row_ref[head, span, :]
            row_total = jnp.zeros((STRIP, 128), jnp.float32)
            out = []
            for tile in range(tiles):
                lanes = slice(tile * 128, tile * 128 + 128)
                scores = score_ref[span, lanes]
                row_exp = jnp.exp(scores - row_peak)
                col_exp = jnp.exp(scores - col_ref[0, mine, lanes])
                row_total = row_total + row_exp
                prob_ref[span, lanes] = row_exp * col_exp * prob_ref[span, lanes]
                out.append(col_totals[tile] + fold8(col_exp))
            part_ref[span, :] = row_total
            return tuple(out)

        zeros = tuple(jnp.zeros((8, 128), jnp.float32) for _ in range(tiles))
        col_totals = lax.fori_loop(0, rows // STRIP, totals, zeros)
        row_total = part_ref[...].sum(axis=1, keepdims=True)
        row_ref[head_count + head] = spread(1.0 / row_total, part_ref)

        def dots(step, col_dots):
            span = pl.ds(step * STRIP, STRIP)
            row_inverse = row_ref[head_count + head, span, :]
            return tuple(
                col_dots[tile]
                + fold8(prob_ref[span, tile * 128 : tile * 128 + 128] * row_inverse)
                for tile in range(tiles)
            )

        col_dots = lax.fori_loop(0, rows // STRIP, dots, zeros)
        for tile in range(tiles):
            lanes = slice(tile * 128, tile * 128 + 128)
            col_ref[1, mine, lanes] = col_totals[tile].sum(axis=0, keepdims=True)
            col_ref[2, mine, lanes] = col_dots[tile].sum(axis=0, keepdims=True)


def grads_kernel(
    head_count, inter_ref, ref_ref, gout_ref, src_ref, wq_ref, wk_ref, wv_ref, wo_ref, row_ref, near_ref,
    far_ref, matched_ref, gref_ref, gsrc_ref, weight_ref,
    query_ref, grad_ref, key_ref, value_ref, bias_ref, hot_ref, score_ref, prob_ref, part_ref,
    match_ref, gscore_ref, query_t_ref, grad_t_ref, gkey_ref, gvalue_ref, att_ref, gquery_ref,
    col_ref,
):
    rows, width = ref_ref.shape
    key_total = src_ref.shape[0]
    tiles = key_total // 128
    head_dim = width // head_count
    scale = head_dim ** -0.5
    queries = bf(mm(ref_ref[...], wq_ref[...])).astype(jnp.float32)
    query_ref[...] = bf(queries * scale)
    grad_ref[...] = bf(mm_general(gout_ref[...], wo_ref[...], NT))
    queries_t = bf(mm_general(wq_ref[...], ref_ref[...], TT)).astype(jnp.float32)
    query_t_ref[...] = bf(queries_t * (2.0 * scale))
    grad_t_ref[...] = bf(mm_general(wo_ref[...], gout_ref[...], NT))
    key_ref[...] = bf(mm(src_ref[...], wk_ref[...]))
    value_ref[...] = bf(mm(src_ref[...], wv_ref[...]))
    fill_bias(inter_ref, bias_ref, head_dim)
    fill_hot(hot_ref, head_dim)

    peak = jnp.maximum(near_ref[0], far_ref[0])
    near, far = jnp.exp(near_ref[0] - peak), jnp.exp(far_ref[0] - peak)
    inverse = 1.0 / (near * near_ref[1] + far * far_ref[1])
    col_ref[0] = peak
    col_ref[1] = inverse
    col_ref[2] = (near * near_ref[2] + far * far_ref[2]) * inverse * 0.5

    for head in range(head_count):
        mine = slice(head, head + 1)
        fill_scores(
            head, head_count, query_ref, hot_ref, key_ref, bias_ref, grad_ref, value_ref,
            score_ref, prob_ref,
        )

        def products(step, carry):
            span = pl.ds(step * STRIP, STRIP)
            row_peak = row_ref[head, span, :]
            row_inverse = row_ref[head_count + head, span, :]
            row_dot = jnp.zeros((STRIP, 128), jnp.float32)
            for tile in range(tiles):
                lanes = slice(tile * 128, tile * 128 + 128)
                scores = score_ref[span, lanes]
                row_prob = jnp.exp(scores - row_peak) * row_inverse
                col_prob = (
                    jnp.exp(scores - col_ref[0, mine, lanes])
                    * col_ref[1, mine, lanes]
                )
                match = row_prob * col_prob
                product = match * prob_ref[span, lanes]
                row_dot = row_dot + product
                match_ref[span, lanes] = bf(match)
                score_ref[span, lanes] = row_prob
                prob_ref[span, lanes] = product - col_prob * col_ref[2, mine, lanes]
            part_ref[span, :] = row_dot
            return carry

        lax.fori_loop(0, rows // STRIP, products, 0)
        part_ref[...] = spread(part_ref[...].sum(axis=1, keepdims=True) * 0.5, part_ref)

        def score_grads(step, carry):
            span = pl.ds(step * STRIP, STRIP)
            row_half = part_ref[span, :]
            for tile in range(tiles):
                lanes = slice(tile * 128, tile * 128 + 128)
                gscore_ref[span, lanes] = bf(
                    prob_ref[span, lanes] - score_ref[span, lanes] * row_half
                )
            return carry

        lax.fori_loop(0, rows // STRIP, score_grads, 0)

        own = lane_row(width, head, head_dim)
        attended = mm(match_ref[...], value_ref[...] * own)
        gquery = mm(gscore_ref[...], key_ref[...] * bf(own.astype(jnp.float32) * (2.0 * scale)))
        if head == 0:
            att_ref[...] = attended
            gquery_ref[...] = gquery
        else:
            att_ref[...] += attended
            gquery_ref[...] += gquery
        span = pl.ds(head * head_dim, head_dim)
        gkey_ref[span, :] = bf(mm(query_t_ref[span, :], gscore_ref[...]))
        gvalue_ref[span, :] = bf(mm(grad_t_ref[span, :], match_ref[...]))

    attended = bf(att_ref[...])
    gquery = bf(gquery_ref[...])
    matched_ref[...] = bf(ref_ref[...].astype(jnp.float32) + mm(attended, wo_ref[...]))
    gref_ref[...] = bf(
        gout_ref[...].astype(jnp.float32) + mm_general(gquery, wq_ref[...], NT)
    )
    gsrc_t = mm(wk_ref[...], gkey_ref[...]) + mm(wv_ref[...], gvalue_ref[...])
    gsrc_ref[...] = bf(gsrc_t.T)
    weight_ref[0] = bf(mm_general(ref_ref[...], gquery, TN))
    weight_ref[1] = bf(mm(gkey_ref[...], src_ref[...]).T)
    weight_ref[2] = bf(mm(gvalue_ref[...], src_ref[...]).T)
    weight_ref[3] = bf(mm_general(attended, gout_ref[...], TN))


def swap(x, axis, apart):
    pairs = [(i, i ^ apart) for i in range(lax.axis_size(axis))]
    return lax.ppermute(x, axis, pairs)


def at(x, index, axis=0):
    return lax.dynamic_index_in_dim(x, index, axis, False)


def laid(near, far, side, axis=0):
    shape = near.shape[:axis] + (2,) + near.shape[axis:]
    out = lax.dynamic_update_index_in_dim(jnp.zeros(shape, near.dtype), near, side, axis)
    return lax.dynamic_update_index_in_dim(out, far, 1 - side, axis)


def add(near, far):
    return (near.astype(jnp.float32) + far.astype(jnp.float32)).astype(near.dtype)


def halve(x, step, axis=0):
    mesh_axis, bit, side = step
    return add(at(x, side, axis), swap(at(x, 1 - side, axis), mesh_axis, bit))


def double(x, step, axis=0):
    mesh_axis, bit, side = step
    return laid(x, swap(x, mesh_axis, bit), side, axis)


def bit_steps(mesh_axis, first=1):
    count, me = lax.axis_size(mesh_axis), lax.axis_index(mesh_axis)
    steps = []
    while first < count:
        steps.append((mesh_axis, first, (me // first) % 2))
        first *= 2
    return steps


def combine_stats(parts):
    peak = functools.reduce(jnp.maximum, [part[0] for part in parts])
    factors = [jnp.exp(part[0] - peak) for part in parts]
    total = sum(factor * part[1] for factor, part in zip(factors, parts))
    dots = sum(factor * part[2] for factor, part in zip(factors, parts))
    return jnp.stack([peak, total, dots])


def vmem_call(kernel, name, out_shape, scratch, flops, moved, args):
    specs = [pl.BlockSpec(memory_space=pltpu.SMEM)]
    specs += [pl.BlockSpec(memory_space=pltpu.VMEM)] * (len(args) - 1)
    return pl.pallas_call(
        kernel,
        name=name,
        out_shape=out_shape,
        in_specs=specs,
        out_specs=[pl.BlockSpec(memory_space=pltpu.VMEM)] * len(out_shape),
        scratch_shapes=scratch,
        compiler_params=pltpu.CompilerParams(vmem_limit_bytes=VMEM_LIMIT),
        cost_estimate=pl.CostEstimate(flops=flops, bytes_accessed=moved, transcendentals=0),
    )(*args)


def on_device(ref_feats, src_feats, grad_out, w_query, w_key, w_value, w_out, intersection):
    ref_rows = ref_feats[0]
    src_rows = src_feats[0]
    out_grad = grad_out[0]
    listed = intersection[0]
    rows, width = ref_rows.shape
    core_step = bit_steps("blk")[0]
    chip_steps = bit_steps("blk", 2)
    key_rows = src_rows.shape[0]
    key_total = key_rows * lax.axis_size("blk")

    source_all = src_rows
    for count, step in enumerate(chip_steps[::-1]):
        source_all = double(source_all, step, count)
    source_all = double(source_all, core_step, len(chip_steps)).reshape(key_total, width)

    f32, b16 = jnp.float32, jnp.bfloat16
    shape = jax.ShapeDtypeStruct
    common = [
        pltpu.VMEM((rows, width), b16),
        pltpu.VMEM((rows, width), b16),
        pltpu.VMEM((key_total, width), b16),
        pltpu.VMEM((key_total, width), b16),
        pltpu.VMEM((key_total, width), b16),
        pltpu.VMEM((rows, width), b16),
        pltpu.VMEM((rows, key_total), f32),
        pltpu.VMEM((rows, key_total), f32),
        pltpu.VMEM((rows, 128), f32),
    ]
    base = (listed, ref_rows, out_grad, source_all, w_query, w_key, w_value, w_out)
    tile_flops = 2 * rows * key_total * width
    row_stats, col_stats = vmem_call(
        functools.partial(stats_kernel, HEADS),
        "match_stats",
        [shape((2 * HEADS, rows, 128), f32), shape((3, HEADS, key_total), f32)],
        common,
        2 * tile_flops,
        2 << 20,
        base,
    )
    near_stats = col_stats
    for mesh_axis, bit, _ in chip_steps:
        near_stats = combine_stats([near_stats, swap(near_stats, mesh_axis, bit)])
    far_stats = swap(near_stats, "blk", 1)
    matched, grad_ref, source_part, weight_part = vmem_call(
        functools.partial(grads_kernel, HEADS),
        "match_grads",
        [
            shape((rows, width), b16),
            shape((rows, width), b16),
            shape((key_total, width), b16),
            shape((4, width, width), b16),
        ],
        common
        + [
            pltpu.VMEM((rows, key_total), b16),
            pltpu.VMEM((rows, key_total), b16),
            pltpu.VMEM((width, rows), b16),
            pltpu.VMEM((width, rows), b16),
            pltpu.VMEM((width, key_total), b16),
            pltpu.VMEM((width, key_total), b16),
            pltpu.VMEM((rows, width), f32),
            pltpu.VMEM((rows, width), f32),
            pltpu.VMEM((3, HEADS, key_total), f32),
        ],
        6 * tile_flops,
        4 << 20,
        base + (row_stats, near_stats, far_stats),
    )

    scans = lax.axis_size("scan")
    weights = weight_part.reshape((2, scans, -1, width))
    sources = source_part.reshape((2,) * (len(chip_steps) + 1) + (key_rows, width))
    weights = halve(weights, core_step)
    sources = halve(sources, core_step, len(chip_steps))
    weights, sources = lax.optimization_barrier((weights, sources))
    weights = lax.all_to_all(weights, "scan", 0, 0).astype(f32).sum(axis=0).astype(b16)
    for count in range(len(chip_steps)):
        sources = halve(sources, chip_steps[count], len(chip_steps) - 1 - count)
    weights, grad_src = lax.optimization_barrier((weights, sources))
    for mesh_axis, bit, _ in chip_steps:
        weights = add(weights, swap(weights, mesh_axis, bit))
    weights = lax.all_to_all(jnp.broadcast_to(weights, (scans,) + weights.shape), "scan", 0, 0)
    weights = double(weights, core_step).reshape(4, width, width).astype(f32)
    return (
        matched[None],
        grad_ref[None],
        grad_src[None],
        weights[0],
        weights[1],
        weights[2],
        weights[3],
    )


def solution(mesh):
    split = P("scan", "blk", None)
    whole = P()
    return jax.shard_map(
        on_device,
        mesh=mesh,
        in_specs=(split, split, split, whole, whole, whole, whole, split),
        out_specs=(split, split, split, whole, whole, whole, whole),
        check_vma=False,
    )
```

```python
import functools

import jax
import jax.numpy as jnp
from jax import lax
from jax.experimental import pallas as pl
from jax.experimental.pallas import tpu as pltpu
from jax.sharding import PartitionSpec as P

HEADS = 4
BLOCK = 128
NEG = -1e30
FLOOR = -1e29

NT = (((1,), (1,)), ((), ()))
TN = (((0,), (0,)), ((), ()))
TT = (((0,), (1,)), ((), ()))


def mm(left, right):
    return jnp.dot(left, right, preferred_element_type=jnp.float32)


def mm_general(left, right, dims):
    return lax.dot_general(left, right, dims, preferred_element_type=jnp.float32)


def bf(x):
    return x.astype(jnp.bfloat16)


def lane_row(width, head, head_dim):
    lanes = lax.broadcasted_iota(jnp.int32, (1, width), 1) // head_dim
    return bf(jnp.where(lanes == head, 1.0, 0.0))


def fill_bias(inter_ref, bias_ref, head_dim):
    query_blocks, key_blocks = inter_ref.shape
    width = bias_ref.shape[1]
    lane = lax.broadcasted_iota(jnp.int32, (1, width), 1) % head_dim
    for key_block in range(key_blocks):
        row = jnp.zeros((1, width), jnp.float32)
        for query_block in range(query_blocks):
            listed = inter_ref[query_block, key_block] == 1
            row = jnp.where(lane == query_block, jnp.where(listed, 0.0, NEG), row)
        bias_ref[pl.ds(key_block * BLOCK, BLOCK), :] = bf(
            jnp.broadcast_to(row, (BLOCK, width))
        )


def fill_hot(hot_ref, head_dim):
    rows, width = hot_ref.shape
    lane = lax.broadcasted_iota(jnp.int32, (1, width), 1) % head_dim
    for block in range(rows // BLOCK):
        row = bf(jnp.where(lane == block, 1.0, 0.0))
        hot_ref[pl.ds(block * BLOCK, BLOCK), :] = jnp.broadcast_to(row, (BLOCK, width))


def spread(reduced, like):
    return jnp.broadcast_to(reduced, like.shape)


STRIP = 32
STEP = 256


def by_eight(x):
    return x.reshape(x.shape[0] // 8, 8, x.shape[1])


def project_kernel(
    head_count, inter_ref, ref_ref, gout_ref, wq_ref, wo_ref,
    left_ref, gleft_ref, query_t_ref, grad_t_ref, bias_ref, hot_ref,
):
    rows, width = ref_ref.shape
    head_dim = width // head_count
    scale = head_dim ** -0.5
    query = bf(bf(mm(ref_ref[...], wq_ref[...])).astype(jnp.float32) * scale)
    grad = bf(mm_general(gout_ref[...], wo_ref[...], NT))
    query_t = bf(mm_general(wq_ref[...], ref_ref[...], TT)).astype(jnp.float32)
    query_t_ref[...] = bf(query_t * (2.0 * scale))
    grad_t_ref[...] = bf(mm_general(wo_ref[...], gout_ref[...], NT))
    fill_bias(inter_ref, bias_ref, head_dim)
    fill_hot(hot_ref, head_dim)
    for head in range(head_count):
        own = lane_row(width, head, head_dim)
        other = lane_row(width, (head + 1) % head_count, head_dim)
        left_ref[head] = query * own + hot_ref[...] * other
        gleft_ref[head] = grad * own


def fill_step(head, step, left_ref, gleft_ref, right_ref, value_ref, score_ref, prob_ref):
    span = pl.ds(pl.multiple_of(step * STEP, STEP), STEP)
    scores = mm_general(left_ref[head], right_ref[head, span, :], NT)
    score_ref[step] = scores
    prob_ref[step] = mm_general(gleft_ref[head], value_ref[span, :], NT)
    return scores


def strips(step, steps, rows):
    chunk = rows // steps
    for first in range(0, chunk, STRIP):
        yield pl.ds(pl.multiple_of(step * chunk + first, STRIP), STRIP)


def lanes_of(tile):
    first = tile * 128 % STEP
    return tile * 128 // STEP, slice(first, first + 128)


def stats_kernel(
    head_count, left_ref, gleft_ref, bias_ref, src_ref, wk_ref, wv_ref,
    row_ref, col_ref, right_ref, key_ref, value_ref,
    score_a, score_b, prob_a, prob_b, prob_c, sum_ref, top_ref, peak_ref,
):
    rows, width = left_ref.shape[1:]
    key_total = src_ref.shape[0]
    tiles, steps = key_total // 128, key_total // STEP
    head_dim = width // head_count
    key_ref[...] = bf(mm(src_ref[...], wk_ref[...]))
    value_ref[...] = bf(mm(src_ref[...], wv_ref[...]))
    for head in range(head_count):
        own = lane_row(width, head, head_dim)
        other = lane_row(width, (head + 1) % head_count, head_dim)
        right_ref[head] = key_ref[...] * own + bias_ref[...] * other
    scores_of, probs_of = (score_a, score_b), (prob_a, prob_b, prob_c)
    zeros = tuple(jnp.zeros((8, 128), jnp.float32) for _ in range(tiles))

    def fill(head, step):
        scores = fill_step(
            head, step, left_ref, gleft_ref, right_ref, value_ref,
            scores_of[head % 2], probs_of[head % 3],
        )
        top = top_ref[...]
        for first in range(0, STEP, 128):
            top = jnp.maximum(top, scores[:, first : first + 128])
        top_ref[...] = top
        peak = jnp.maximum(scores.max(axis=0, keepdims=True), FLOOR)
        peak_ref[head, step] = jnp.broadcast_to(peak, (8, STEP))

    def close_peaks(head):
        row_ref[head] = spread(top_ref[...].max(axis=1, keepdims=True), top_ref)
        top_ref[...] = jnp.full(top_ref.shape, 2.0 * NEG, jnp.float32)

    def totals(head, span, col_totals):
        score_ref, prob_ref = scores_of[head % 2], probs_of[head % 3]
        row_peak = by_eight(row_ref[head, span, :])
        row_total = jnp.zeros_like(row_peak)
        out = []
        for tile in range(tiles):
            at_step, lanes = lanes_of(tile)
            scores = by_eight(score_ref[at_step, span, lanes])
            row_exp = jnp.exp(scores - row_peak)
            col_exp = jnp.exp(scores - peak_ref[head, at_step, :, lanes][None])
            row_total = row_total + row_exp
            product = row_exp * col_exp * by_eight(prob_ref[at_step, span, lanes])
            prob_ref[at_step, span, lanes] = product.reshape(STRIP, 128)
            out.append(col_totals[tile] + col_exp.sum(axis=0))
        sum_ref[span, :] = row_total.reshape(STRIP, 128)
        return tuple(out)

    def dots(head, span, col_dots):
        prob_ref = probs_of[head % 3]
        row_inverse = by_eight(row_ref[head_count + head, span, :])
        out = []
        for tile in range(tiles):
            at_step, lanes = lanes_of(tile)
            product = by_eight(prob_ref[at_step, span, lanes]) * row_inverse
            out.append(col_dots[tile] + product.sum(axis=0))
        return tuple(out)

    top_ref[...] = jnp.full(top_ref.shape, 2.0 * NEG, jnp.float32)
    lax.fori_loop(0, steps, lambda step, carry: (fill(0, step), carry)[1], 0)
    for head in range(head_count + 1):
        if head < head_count:
            close_peaks(head)

        def body(step, carry, head=head):
            col_totals, col_dots = carry
            for span in strips(step, steps, rows):
                if head < head_count:
                    col_totals = totals(head, span, col_totals)
                if head > 0:
                    col_dots = dots(head - 1, span, col_dots)
            if head + 1 < head_count:
                fill(head + 1, step)
            return col_totals, col_dots

        col_totals, col_dots = lax.fori_loop(0, steps, body, (zeros, zeros))
        for tile in range(tiles):
            lanes = slice(tile * 128, tile * 128 + 128)
            at_step, near = lanes_of(tile)
            if head < head_count:
                col_ref[0, head : head + 1, lanes] = peak_ref[head, at_step, 0:1, near]
                col_ref[1, head : head + 1, lanes] = col_totals[tile].sum(axis=0, keepdims=True)
            if head > 0:
                col_ref[2, head - 1 : head, lanes] = col_dots[tile].sum(axis=0, keepdims=True)
        if head < head_count:
            row_total = sum_ref[...].sum(axis=1, keepdims=True)
            row_ref[head_count + head] = spread(1.0 / row_total, sum_ref)


def grads_kernel(
    head_count, left_ref, gleft_ref, right_ref, key_ref, value_ref, query_t_ref, grad_t_ref, row_ref,
    near_ref, far_ref, ref_ref, gout_ref, src_ref,
    attended_ref, gquery_ref, gkey_ref, gvalue_ref, weight_ref,
    score_a, score_b, prob_a, prob_b, match_a, match_b, gscore_a, gscore_b, att_ref, gq_ref, col_ref,
):
    rows, width = ref_ref.shape
    key_total = src_ref.shape[0]
    tiles, steps = key_total // 128, key_total // STEP
    head_dim = width // head_count
    scale = head_dim ** -0.5
    chunk = rows // steps

    peak = jnp.maximum(near_ref[0], far_ref[0])
    near, far = jnp.exp(near_ref[0] - peak), jnp.exp(far_ref[0] - peak)
    inverse = 1.0 / (near * near_ref[1] + far * far_ref[1])
    half = (near * near_ref[2] + far * far_ref[2]) * inverse * 0.5
    for kind, values in enumerate((peak, inverse, half)):
        for head in range(head_count):
            for step in range(steps):
                piece = values[head : head + 1, step * STEP : (step + 1) * STEP]
                col_ref[kind, head, step] = jnp.broadcast_to(piece, (8, STEP))
    att_ref[...] = jnp.zeros(att_ref.shape, jnp.float32)
    gq_ref[...] = jnp.zeros(gq_ref.shape, jnp.float32)
    scores_of, probs_of = (score_a, score_b), (prob_a, prob_b)
    matches_of, gscores_of = (match_a, match_b), (gscore_a, gscore_b)

    def fill(head, step):
        fill_step(
            head, step, left_ref, gleft_ref, right_ref, value_ref,
            scores_of[head % 2], probs_of[head % 2],
        )

    def products(head, span):
        score_ref, prob_ref, match_ref = scores_of[head % 2], probs_of[head % 2], matches_of[head % 2]
        row_peak = by_eight(row_ref[head, span, :])
        row_inverse = by_eight(row_ref[head_count + head, span, :])
        row_dot = jnp.zeros_like(row_peak)
        for tile in range(tiles):
            at_step, lanes = lanes_of(tile)
            scores = by_eight(score_ref[at_step, span, lanes])
            row_prob = jnp.exp(scores - row_peak) * row_inverse
            col_prob = jnp.exp(scores - col_ref[0, head, at_step, :, lanes][None])
            col_prob = col_prob * col_ref[1, head, at_step, :, lanes][None]
            match = row_prob * col_prob
            product = match * by_eight(prob_ref[at_step, span, lanes])
            row_dot = row_dot + product
            rest = product - col_prob * col_ref[2, head, at_step, :, lanes][None]
            match_ref[span, tile * 128 : tile * 128 + 128] = bf(match.reshape(STRIP, 128))
            score_ref[at_step, span, lanes] = row_prob.reshape(STRIP, 128)
            prob_ref[at_step, span, lanes] = rest.reshape(STRIP, 128)
        return row_dot.reshape(STRIP, 128)

    def score_grads(head, span, row_half):
        score_ref, prob_ref, gscore_ref = scores_of[head % 2], probs_of[head % 2], gscores_of[head % 2]
        for tile in range(tiles):
            at_step, lanes = lanes_of(tile)
            grads = prob_ref[at_step, span, lanes] - score_ref[at_step, span, lanes] * row_half
            gscore_ref[span, tile * 128 : tile * 128 + 128] = bf(grads)

    def outputs(head, step):
        match_ref, gscore_ref = matches_of[head % 2], gscores_of[head % 2]
        own = lane_row(width, head, head_dim).astype(jnp.float32)
        span = pl.ds(pl.multiple_of(step * chunk, chunk), chunk)
        att_ref[span, :] += mm(match_ref[span, :], value_ref[...]) * own
        gq_ref[span, :] += mm(gscore_ref[span, :], key_ref[...]) * own
        lanes = pl.ds(pl.multiple_of(step * STEP, STEP), STEP)
        mine = slice(head * head_dim, (head + 1) * head_dim)
        gkey_ref[mine, lanes] = bf(mm(query_t_ref[mine, :], gscore_ref[:, lanes]))
        gvalue_ref[mine, lanes] = bf(mm(grad_t_ref[mine, :], match_ref[:, lanes]))

    lax.fori_loop(0, steps, lambda step, carry: (fill(0, step), carry)[1], 0)
    for head in range(head_count + 1):

        def body(step, carry, head=head):
            if head > 0:
                outputs(head - 1, step)
            if head + 1 < head_count:
                fill(head + 1, step)
            if head < head_count:
                spans = list(strips(step, steps, rows))
                row_dot = jnp.concatenate([products(head, span) for span in spans], axis=0)
                row_half = spread(row_dot.sum(axis=1, keepdims=True) * 0.5, row_dot)
                for at_strip, span in enumerate(spans):
                    first = at_strip * STRIP
                    score_grads(head, span, row_half[first : first + STRIP])
            return carry

        lax.fori_loop(0, steps, body, 0)

    attended = bf(att_ref[...])
    gquery = bf(gq_ref[...] * (2.0 * scale))
    attended_ref[...] = attended
    gquery_ref[...] = gquery
    weight_ref[0] = bf(mm_general(ref_ref[...], gquery, TN))
    weight_ref[1] = bf(mm(gkey_ref[...], src_ref[...]).T)
    weight_ref[2] = bf(mm(gvalue_ref[...], src_ref[...]).T)
    weight_ref[3] = bf(mm_general(attended, gout_ref[...], TN))


def finish_kernel(
    ref_ref, gout_ref, attended_ref, gquery_ref, gkey_ref, gvalue_ref, wq_ref, wk_ref, wv_ref, wo_ref,
    matched_ref, gref_ref, gsrc_ref,
):
    gsrc_t = mm(wk_ref[...], gkey_ref[...]) + mm(wv_ref[...], gvalue_ref[...])
    gsrc_ref[...] = bf(gsrc_t.T)
    matched = ref_ref[...].astype(jnp.float32) + mm(attended_ref[...], wo_ref[...])
    matched_ref[...] = bf(matched)
    gref = gout_ref[...].astype(jnp.float32) + mm_general(gquery_ref[...], wq_ref[...], NT)
    gref_ref[...] = bf(gref)


def swap(x, axis, apart):
    pairs = [(i, i ^ apart) for i in range(lax.axis_size(axis))]
    return lax.ppermute(x, axis, pairs)


def at(x, index, axis=0):
    return lax.dynamic_index_in_dim(x, index, axis, False)


def laid(near, far, side, axis=0):
    shape = near.shape[:axis] + (2,) + near.shape[axis:]
    out = lax.dynamic_update_index_in_dim(jnp.zeros(shape, near.dtype), near, side, axis)
    return lax.dynamic_update_index_in_dim(out, far, 1 - side, axis)


def add(near, far):
    return (near.astype(jnp.float32) + far.astype(jnp.float32)).astype(near.dtype)


def halve(x, step, axis=0):
    mesh_axis, bit, side = step
    return add(at(x, side, axis), swap(at(x, 1 - side, axis), mesh_axis, bit))


def double(x, step, axis=0):
    mesh_axis, bit, side = step
    return laid(x, swap(x, mesh_axis, bit), side, axis)


def bit_steps(mesh_axis, first=1):
    count, me = lax.axis_size(mesh_axis), lax.axis_index(mesh_axis)
    steps = []
    while first < count:
        steps.append((mesh_axis, first, (me // first) % 2))
        first *= 2
    return steps


def combine_stats(parts):
    peak = functools.reduce(jnp.maximum, [part[0] for part in parts])
    factors = [jnp.exp(part[0] - peak) for part in parts]
    total = sum(factor * part[1] for factor, part in zip(factors, parts))
    dots = sum(factor * part[2] for factor, part in zip(factors, parts))
    return jnp.stack([peak, total, dots])


def vmem_call(kernel, name, out_shape, scratch, limit, flops, moved, args, scalars=0):
    specs = [pl.BlockSpec(memory_space=pltpu.SMEM)] * scalars
    specs += [pl.BlockSpec(memory_space=pltpu.VMEM)] * (len(args) - scalars)
    return pl.pallas_call(
        kernel,
        name=name,
        out_shape=out_shape,
        in_specs=specs,
        out_specs=[pl.BlockSpec(memory_space=pltpu.VMEM)] * len(out_shape),
        scratch_shapes=scratch,
        compiler_params=pltpu.CompilerParams(vmem_limit_bytes=limit),
        cost_estimate=pl.CostEstimate(flops=flops, bytes_accessed=moved, transcendentals=0),
    )(*args)


def on_device(ref_feats, src_feats, grad_out, w_query, w_key, w_value, w_out, intersection):
    ref_rows = ref_feats[0]
    src_rows = src_feats[0]
    out_grad = grad_out[0]
    listed = intersection[0]
    rows, width = ref_rows.shape
    core_step = bit_steps("blk")[0]
    chip_steps = bit_steps("blk", 2)
    key_rows = src_rows.shape[0]
    key_total = key_rows * lax.axis_size("blk")

    source_all = src_rows
    for count, step in enumerate(chip_steps[::-1]):
        source_all = double(source_all, step, count)
    source_all = double(source_all, core_step, len(chip_steps)).reshape(key_total, width)

    f32, b16 = jnp.float32, jnp.bfloat16
    shape, vmem = jax.ShapeDtypeStruct, pltpu.VMEM
    unit = 2 * rows * width * width
    limit = (8 << 20) + rows * key_total * 44
    left, grad_left, query_t, grad_t, bias = vmem_call(
        functools.partial(project_kernel, HEADS),
        "project_reference",
        [
            shape((HEADS, rows, width), b16),
            shape((HEADS, rows, width), b16),
            shape((width, rows), b16),
            shape((width, rows), b16),
            shape((key_total, width), b16),
        ],
        [vmem((rows, width), b16)],
        16 << 20,
        16 * unit,
        4 << 20,
        (listed, ref_rows, out_grad, w_query, w_out),
        scalars=1,
    )
    steps = key_total // STEP
    tile = vmem((steps, rows, STEP), f32)
    row_stats, col_stats, right, keys, values = vmem_call(
        functools.partial(stats_kernel, HEADS),
        "match_stats",
        [
            shape((2 * HEADS, rows, 128), f32),
            shape((3, HEADS, key_total), f32),
            shape((HEADS, key_total, width), b16),
            shape((key_total, width), b16),
            shape((key_total, width), b16),
        ],
        [tile] * 5
        + [vmem((rows, 128), f32), vmem((rows, 128), f32), vmem((HEADS, steps, 8, STEP), f32)],
        limit,
        60 * unit,
        8 << 20,
        (left, grad_left, bias, source_all, w_key, w_value),
    )
    near_stats = col_stats
    for mesh_axis, bit, _ in chip_steps:
        near_stats = combine_stats([near_stats, swap(near_stats, mesh_axis, bit)])
    far_stats = swap(near_stats, "blk", 1)
    attended, grad_query, grad_key, grad_value, weight_part = vmem_call(
        functools.partial(grads_kernel, HEADS),
        "match_grads",
        [
            shape((rows, width), b16),
            shape((rows, width), b16),
            shape((width, key_total), b16),
            shape((width, key_total), b16),
            shape((4, width, width), b16),
        ],
        [tile] * 4
        + [vmem((rows, key_total), b16)] * 4
        + [vmem((rows, width), f32)] * 2
        + [vmem((3, HEADS, steps, 8, STEP), f32)],
        limit,
        100 * unit,
        8 << 20,
        (left, grad_left, right, keys, values, query_t, grad_t, row_stats, near_stats, far_stats,
         ref_rows, out_grad, source_all),
    )
    matched, grad_ref, source_part = vmem_call(
        finish_kernel,
        "finish_rows",
        [
            shape((rows, width), b16),
            shape((rows, width), b16),
            shape((key_total, width), b16),
        ],
        [],
        16 << 20,
        16 * unit,
        4 << 20,
        (ref_rows, out_grad, attended, grad_query, grad_key, grad_value,
         w_query, w_key, w_value, w_out),
    )

    scans = lax.axis_size("scan")
    weights = weight_part.reshape((2, scans, -1, width))
    sources = source_part.reshape((2,) * (len(chip_steps) + 1) + (key_rows, width))
    weights = halve(weights, core_step)
    sources = halve(sources, core_step, len(chip_steps))
    weights = lax.all_to_all(weights, "scan", 0, 0).astype(f32).sum(axis=0).astype(b16)
    for mesh_axis, bit, _ in chip_steps:
        weights = add(weights, swap(weights, mesh_axis, bit))
    sources = halve(sources, chip_steps[0], len(chip_steps) - 1)
    weights, sources = lax.optimization_barrier((weights, sources))
    weights = lax.all_to_all(jnp.broadcast_to(weights, (scans,) + weights.shape), "scan", 0, 0)
    for count in range(1, len(chip_steps)):
        sources = halve(sources, chip_steps[count], len(chip_steps) - 1 - count)
    grad_src = sources
    weights = double(weights, core_step).reshape(4, width, width).astype(f32)
    return (
        matched[None],
        grad_ref[None],
        grad_src[None],
        weights[0],
        weights[1],
        weights[2],
        weights[3],
    )


def solution(mesh):
    split = P("scan", "blk", None)
    whole = P()
    return jax.shard_map(
        on_device,
        mesh=mesh,
        in_specs=(split, split, split, whole, whole, whole, whole, split),
        out_specs=(split, split, split, whole, whole, whole, whole),
        check_vma=False,
    )
```

```python
import functools
import math

import jax
import jax.numpy as jnp
from jax import lax
from jax.experimental import pallas as pl
from jax.experimental.pallas import tpu as pltpu
from jax.sharding import PartitionSpec as P

HEADS = 4
BLOCK = 128
NEG = -1e30
FLOOR = -1e29
LOG2E = math.log2(math.e)

NT = (((1,), (1,)), ((), ()))
TN = (((0,), (0,)), ((), ()))
TT = (((0,), (1,)), ((), ()))


def mm(left, right):
    return jnp.dot(left, right, preferred_element_type=jnp.float32)


def mm_general(left, right, dims):
    return lax.dot_general(left, right, dims, preferred_element_type=jnp.float32)


def bf(x):
    return x.astype(jnp.bfloat16)


def lane_row(width, head, head_dim):
    lanes = lax.broadcasted_iota(jnp.int32, (1, width), 1) // head_dim
    return bf(jnp.where(lanes == head, 1.0, 0.0))


def fill_bias(inter_ref, bias_ref):
    query_blocks, key_blocks = inter_ref.shape
    block_of = lax.broadcasted_iota(jnp.int32, (bias_ref.shape[0], BLOCK), 0)
    for key_block in range(key_blocks):
        piece = jnp.zeros(block_of.shape, jnp.float32)
        for query_block in range(query_blocks):
            listed = inter_ref[query_block, key_block] == 1
            piece = jnp.where(block_of == query_block, jnp.where(listed, 0.0, NEG), piece)
        bias_ref[:, key_block * BLOCK : (key_block + 1) * BLOCK] = bf(piece)


def fill_hot(hot_ref, head_dim):
    rows, width = hot_ref.shape
    lane = lax.broadcasted_iota(jnp.int32, (1, width), 1) % head_dim
    for block in range(rows // BLOCK):
        row = bf(jnp.where(lane == block, 1.0, 0.0))
        hot_ref[pl.ds(block * BLOCK, BLOCK), :] = jnp.broadcast_to(row, (BLOCK, width))


def spread(reduced, like):
    return jnp.broadcast_to(reduced, like.shape)


STRIP = 32
STEP = 256


def by_eight(x):
    return x.reshape(x.shape[0] // 8, 8, x.shape[1])


def project_kernel(
    head_count, inter_ref, ref_ref, gout_ref, wq_ref, wo_ref, left_ref, gleft_ref, bias_ref, hot_ref
):
    rows, width = ref_ref.shape
    head_dim = width // head_count
    scale = head_dim ** -0.5
    query = bf(bf(mm(ref_ref[...], wq_ref[...])).astype(jnp.float32) * scale)
    grad = bf(mm_general(gout_ref[...], wo_ref[...], NT))
    fill_bias(inter_ref, bias_ref)
    fill_hot(hot_ref, head_dim)
    for head in range(head_count):
        own = lane_row(width, head, head_dim)
        other = lane_row(width, (head + 1) % head_count, head_dim)
        left_ref[head] = query * own + hot_ref[...] * other
        gleft_ref[head] = grad * own


def side_kernel(
    head_count, ref_ref, gout_ref, src_ref, wq_ref, wk_ref, wv_ref, wo_ref,
    key_ref, value_ref, query_t_ref, grad_t_ref,
):
    scale = (ref_ref.shape[1] // head_count) ** -0.5
    key_ref[...] = bf(mm(src_ref[...], wk_ref[...]))
    value_ref[...] = bf(mm(src_ref[...], wv_ref[...]))
    query_t = bf(mm_general(wq_ref[...], ref_ref[...], TT)).astype(jnp.float32)
    query_t_ref[...] = bf(query_t * (2.0 * scale))
    grad_t_ref[...] = bf(mm_general(wo_ref[...], gout_ref[...], NT))


def fill_step(head, step, left_ref, gleft_ref, right_ref, value_t_ref, score_ref, prob_ref):
    span = pl.ds(pl.multiple_of(step * STEP, STEP), STEP)
    score_ref[step] = mm(left_ref[head], right_ref[head, :, span]) * LOG2E
    prob_ref[step] = mm(gleft_ref[head], value_t_ref[:, span])


def strips(step, steps, rows):
    chunk = rows // steps
    for first in range(0, chunk, STRIP):
        yield pl.ds(pl.multiple_of(step * chunk + first, STRIP), STRIP)


def lanes_of(tile):
    first = tile * 128 % STEP
    return tile * 128 // STEP, slice(first, first + 128)


def stats_kernel(
    head_count, left_ref, gleft_ref, bias_ref, src_ref, wk_ref, wv_ref,
    row_ref, col_ref, right_ref, value_t_ref,
    score_a, score_b, prob_a, prob_b, prob_c, sum_ref, top_ref, peak_ref,
):
    rows, width = left_ref.shape[1:]
    key_total = src_ref.shape[0]
    tiles, steps = key_total // 128, key_total // STEP
    head_dim = width // head_count
    key_t = bf(mm_general(wk_ref[...], src_ref[...], TT))
    value_t_ref[...] = bf(mm_general(wv_ref[...], src_ref[...], TT))
    right_ref[...] = jnp.zeros(right_ref.shape, jnp.bfloat16)
    for head in range(head_count):
        own = slice(head * head_dim, (head + 1) * head_dim)
        other = (head + 1) % head_count * head_dim
        right_ref[head, own, :] = key_t[own]
        right_ref[head, other : other + head_dim, :] = bias_ref[...]
    scores_of, probs_of = (score_a, score_b), (prob_a, prob_b, prob_c)
    zeros = tuple(jnp.zeros((8, 128), jnp.float32) for _ in range(tiles))

    def fill(head, step):
        score_ref = scores_of[head % 2]
        fill_step(
            head, step, left_ref, gleft_ref, right_ref, value_t_ref, score_ref, probs_of[head % 3]
        )
        peaks = [jnp.full((8, 128), FLOOR, jnp.float32)] * (STEP // 128)
        for first in range(0, rows, 4 * STRIP):
            span = slice(first, first + 4 * STRIP)
            top = top_ref[span, :]
            for piece in range(STEP // 128):
                scores = score_ref[step, span, piece * 128 : piece * 128 + 128]
                top = jnp.maximum(top, scores)
                peaks[piece] = jnp.maximum(peaks[piece], by_eight(scores).max(axis=0))
            top_ref[span, :] = top
        for piece in range(STEP // 128):
            peak = jnp.broadcast_to(peaks[piece].max(axis=0, keepdims=True), (8, 128))
            peak_ref[head, step, :, piece * 128 : piece * 128 + 128] = peak

    def close_peaks(head):
        row_ref[head] = spread(top_ref[...].max(axis=1, keepdims=True), top_ref)
        top_ref[...] = jnp.full(top_ref.shape, 2.0 * NEG, jnp.float32)

    def totals(head, span, col_totals):
        score_ref, prob_ref = scores_of[head % 2], probs_of[head % 3]
        row_peak = by_eight(row_ref[head, span, :])
        row_total = jnp.zeros_like(row_peak)
        out = []
        for tile in range(tiles):
            at_step, lanes = lanes_of(tile)
            scores = by_eight(score_ref[at_step, span, lanes])
            row_exp = jnp.exp2(scores - row_peak)
            col_exp = jnp.exp2(scores - peak_ref[head, at_step, :, lanes][None])
            row_total = row_total + row_exp
            product = row_exp * col_exp * by_eight(prob_ref[at_step, span, lanes])
            prob_ref[at_step, span, lanes] = product.reshape(STRIP, 128)
            out.append(col_totals[tile] + col_exp.sum(axis=0))
        sum_ref[span, :] = row_total.reshape(STRIP, 128)
        return tuple(out)

    def dots(head, span, col_dots):
        prob_ref = probs_of[head % 3]
        row_inverse = by_eight(row_ref[head_count + head, span, :])
        out = []
        for tile in range(tiles):
            at_step, lanes = lanes_of(tile)
            product = by_eight(prob_ref[at_step, span, lanes]) * row_inverse
            out.append(col_dots[tile] + product.sum(axis=0))
        return tuple(out)

    top_ref[...] = jnp.full(top_ref.shape, 2.0 * NEG, jnp.float32)
    lax.fori_loop(0, steps, lambda step, carry: (fill(0, step), carry)[1], 0)
    for head in range(head_count + 1):
        if head < head_count:
            close_peaks(head)

        def body(step, carry, head=head):
            col_totals, col_dots = carry
            for span in strips(step, steps, rows):
                if head < head_count:
                    col_totals = totals(head, span, col_totals)
                if head > 0:
                    col_dots = dots(head - 1, span, col_dots)
            if head + 1 < head_count:
                fill(head + 1, step)
            return col_totals, col_dots

        col_totals, col_dots = lax.fori_loop(0, steps, body, (zeros, zeros))
        for tile in range(tiles):
            lanes = slice(tile * 128, tile * 128 + 128)
            at_step, near = lanes_of(tile)
            if head < head_count:
                col_ref[0, head : head + 1, lanes] = peak_ref[head, at_step, 0:1, near]
                col_ref[1, head : head + 1, lanes] = col_totals[tile].sum(axis=0, keepdims=True)
            if head > 0:
                col_ref[2, head - 1 : head, lanes] = col_dots[tile].sum(axis=0, keepdims=True)
        if head < head_count:
            row_total = sum_ref[...].sum(axis=1, keepdims=True)
            row_ref[head_count + head] = spread(1.0 / row_total, sum_ref)


def grads_kernel(
    head_count, left_ref, gleft_ref, right_ref, value_t_ref, key_ref, value_ref, query_t_ref, grad_t_ref,
    row_ref, near_ref, far_ref, ref_ref, gout_ref, src_ref,
    attended_ref, gquery_ref, gkey_ref, gvalue_ref, weight_ref,
    score_a, score_b, prob_a, prob_b, match_a, match_b, gscore_a, gscore_b, att_ref, gq_ref, col_ref,
):
    rows, width = ref_ref.shape
    key_total = src_ref.shape[0]
    tiles, steps = key_total // 128, key_total // STEP
    head_dim = width // head_count
    scale = head_dim ** -0.5
    chunk = rows // steps

    peak = jnp.maximum(near_ref[0], far_ref[0])
    near, far = jnp.exp2(near_ref[0] - peak), jnp.exp2(far_ref[0] - peak)
    inverse = 1.0 / (near * near_ref[1] + far * far_ref[1])
    half = (near * near_ref[2] + far * far_ref[2]) * inverse * 0.5
    for kind, values in enumerate((peak, inverse, half)):
        for head in range(head_count):
            for step in range(steps):
                piece = values[head : head + 1, step * STEP : (step + 1) * STEP]
                col_ref[kind, head, step] = jnp.broadcast_to(piece, (8, STEP))
    att_ref[...] = jnp.zeros(att_ref.shape, jnp.float32)
    gq_ref[...] = jnp.zeros(gq_ref.shape, jnp.float32)
    scores_of, probs_of = (score_a, score_b), (prob_a, prob_b)
    matches_of, gscores_of = (match_a, match_b), (gscore_a, gscore_b)

    def fill(head, step):
        fill_step(
            head, step, left_ref, gleft_ref, right_ref, value_t_ref,
            scores_of[head % 2], probs_of[head % 2],
        )

    def products(head, span):
        score_ref, prob_ref, match_ref = scores_of[head % 2], probs_of[head % 2], matches_of[head % 2]
        row_peak = by_eight(row_ref[head, span, :])
        row_inverse = by_eight(row_ref[head_count + head, span, :])
        row_dot = jnp.zeros_like(row_peak)
        for tile in range(tiles):
            at_step, lanes = lanes_of(tile)
            scores = by_eight(score_ref[at_step, span, lanes])
            row_prob = jnp.exp2(scores - row_peak) * row_inverse
            col_prob = jnp.exp2(scores - col_ref[0, head, at_step, :, lanes][None])
            col_prob = col_prob * col_ref[1, head, at_step, :, lanes][None]
            match = row_prob * col_prob
            product = match * by_eight(prob_ref[at_step, span, lanes])
            row_dot = row_dot + product
            rest = product - col_prob * col_ref[2, head, at_step, :, lanes][None]
            match_ref[span, tile * 128 : tile * 128 + 128] = bf(match.reshape(STRIP, 128))
            score_ref[at_step, span, lanes] = row_prob.reshape(STRIP, 128)
            prob_ref[at_step, span, lanes] = rest.reshape(STRIP, 128)
        return row_dot.reshape(STRIP, 128)

    def score_grads(head, span, row_half):
        score_ref, prob_ref, gscore_ref = scores_of[head % 2], probs_of[head % 2], gscores_of[head % 2]
        for tile in range(tiles):
            at_step, lanes = lanes_of(tile)
            grads = prob_ref[at_step, span, lanes] - score_ref[at_step, span, lanes] * row_half
            gscore_ref[span, tile * 128 : tile * 128 + 128] = bf(grads)

    def outputs(head, step):
        match_ref, gscore_ref = matches_of[head % 2], gscores_of[head % 2]
        own = lane_row(width, head, head_dim).astype(jnp.float32)
        span = pl.ds(pl.multiple_of(step * chunk, chunk), chunk)
        att_ref[span, :] += mm(match_ref[span, :], value_ref[...]) * own
        gq_ref[span, :] += mm(gscore_ref[span, :], key_ref[...]) * own
        lanes = pl.ds(pl.multiple_of(step * STEP, STEP), STEP)
        mine = slice(head * head_dim, (head + 1) * head_dim)
        gkey_ref[mine, lanes] = bf(mm(query_t_ref[mine, :], gscore_ref[:, lanes]))
        gvalue_ref[mine, lanes] = bf(mm(grad_t_ref[mine, :], match_ref[:, lanes]))

    lax.fori_loop(0, steps, lambda step, carry: (fill(0, step), carry)[1], 0)
    for head in range(head_count + 1):

        def body(step, carry, head=head):
            if head > 0:
                outputs(head - 1, step)
            if head + 1 < head_count:
                fill(head + 1, step)
            if head < head_count:
                spans = list(strips(step, steps, rows))
                row_dot = jnp.concatenate([products(head, span) for span in spans], axis=0)
                row_half = spread(row_dot.sum(axis=1, keepdims=True) * 0.5, row_dot)
                for at_strip, span in enumerate(spans):
                    first = at_strip * STRIP
                    score_grads(head, span, row_half[first : first + STRIP])
            return carry

        lax.fori_loop(0, steps, body, 0)

    attended = bf(att_ref[...])
    gquery = bf(gq_ref[...] * (2.0 * scale))
    attended_ref[...] = attended
    gquery_ref[...] = gquery
    weight_ref[0] = bf(mm_general(ref_ref[...], gquery, TN))
    weight_ref[1] = bf(mm(gkey_ref[...], src_ref[...]).T)
    weight_ref[2] = bf(mm(gvalue_ref[...], src_ref[...]).T)
    weight_ref[3] = bf(mm_general(attended, gout_ref[...], TN))


def finish_kernel(
    ref_ref, gout_ref, attended_ref, gquery_ref, gkey_ref, gvalue_ref, wq_ref, wk_ref, wv_ref, wo_ref,
    matched_ref, gref_ref, gsrc_ref,
):
    gsrc_t = mm(wk_ref[...], gkey_ref[...]) + mm(wv_ref[...], gvalue_ref[...])
    gsrc_ref[...] = bf(gsrc_t.T)
    matched = ref_ref[...].astype(jnp.float32) + mm(attended_ref[...], wo_ref[...])
    matched_ref[...] = bf(matched)
    gref = gout_ref[...].astype(jnp.float32) + mm_general(gquery_ref[...], wq_ref[...], NT)
    gref_ref[...] = bf(gref)


def swap(x, axis, apart):
    pairs = [(i, i ^ apart) for i in range(lax.axis_size(axis))]
    return lax.ppermute(x, axis, pairs)


def at(x, index, axis=0):
    return lax.dynamic_index_in_dim(x, index, axis, False)


def laid(near, far, side, axis=0):
    shape = near.shape[:axis] + (2,) + near.shape[axis:]
    out = lax.dynamic_update_index_in_dim(jnp.zeros(shape, near.dtype), near, side, axis)
    return lax.dynamic_update_index_in_dim(out, far, 1 - side, axis)


def add(near, far):
    return (near.astype(jnp.float32) + far.astype(jnp.float32)).astype(near.dtype)


def halve(x, step, axis=0):
    mesh_axis, bit, side = step
    return add(at(x, side, axis), swap(at(x, 1 - side, axis), mesh_axis, bit))


def double(x, step, axis=0):
    mesh_axis, bit, side = step
    return laid(x, swap(x, mesh_axis, bit), side, axis)


def bit_steps(mesh_axis, first=1):
    count, me = lax.axis_size(mesh_axis), lax.axis_index(mesh_axis)
    steps = []
    while first < count:
        steps.append((mesh_axis, first, (me // first) % 2))
        first *= 2
    return steps


def combine_stats(parts):
    peak = functools.reduce(jnp.maximum, [part[0] for part in parts])
    factors = [jnp.exp2(part[0] - peak) for part in parts]
    total = sum(factor * part[1] for factor, part in zip(factors, parts))
    dots = sum(factor * part[2] for factor, part in zip(factors, parts))
    return jnp.stack([peak, total, dots])


def vmem_call(kernel, name, out_shape, scratch, limit, flops, moved, args, scalars=0):
    specs = [pl.BlockSpec(memory_space=pltpu.SMEM)] * scalars
    specs += [pl.BlockSpec(memory_space=pltpu.VMEM)] * (len(args) - scalars)
    return pl.pallas_call(
        kernel,
        name=name,
        out_shape=out_shape,
        in_specs=specs,
        out_specs=[pl.BlockSpec(memory_space=pltpu.VMEM)] * len(out_shape),
        scratch_shapes=scratch,
        compiler_params=pltpu.CompilerParams(vmem_limit_bytes=limit),
        cost_estimate=pl.CostEstimate(flops=flops, bytes_accessed=moved, transcendentals=0),
    )(*args)


def on_device(ref_feats, src_feats, grad_out, w_query, w_key, w_value, w_out, intersection):
    ref_rows = ref_feats[0]
    src_rows = src_feats[0]
    out_grad = grad_out[0]
    listed = intersection[0]
    rows, width = ref_rows.shape
    core_step = bit_steps("blk")[0]
    chip_steps = bit_steps("blk", 2)
    key_rows = src_rows.shape[0]
    key_total = key_rows * lax.axis_size("blk")

    source_all = src_rows
    for count, step in enumerate(chip_steps[::-1]):
        source_all = double(source_all, step, count)
    ref_near, grad_near, source_all = lax.optimization_barrier((ref_rows, out_grad, source_all))
    source_all = double(source_all, core_step, len(chip_steps)).reshape(key_total, width)

    f32, b16 = jnp.float32, jnp.bfloat16
    shape, vmem = jax.ShapeDtypeStruct, pltpu.VMEM
    unit = 2 * rows * width * width
    left, grad_left, bias = vmem_call(
        functools.partial(project_kernel, HEADS),
        "project_reference",
        [
            shape((HEADS, rows, width), b16),
            shape((HEADS, rows, width), b16),
            shape((width // HEADS, key_total), b16),
        ],
        [vmem((rows, width), b16)],
        8 << 20,
        8 * unit,
        2 << 20,
        (listed, ref_near, grad_near, w_query, w_out),
        scalars=1,
    )
    steps = key_total // STEP
    tile = vmem((steps, rows, STEP), f32)
    row_stats, col_stats, right, value_t = vmem_call(
        functools.partial(stats_kernel, HEADS),
        "match_stats",
        [
            shape((2 * HEADS, rows, 128), f32),
            shape((3, HEADS, key_total), f32),
            shape((HEADS, width, key_total), b16),
            shape((width, key_total), b16),
        ],
        [tile] * 5
        + [vmem((rows, 128), f32), vmem((rows, 128), f32), vmem((HEADS, steps, 8, STEP), f32)],
        (6 << 20) + rows * key_total * 24,
        60 * unit,
        8 << 20,
        (left, grad_left, bias, source_all, w_key, w_value),
    )
    ref_near, grad_near, source_near, near_stats = lax.optimization_barrier(
        (ref_rows, out_grad, source_all, col_stats)
    )
    keys, values, query_t, grad_t = vmem_call(
        functools.partial(side_kernel, HEADS),
        "project_for_grads",
        [
            shape((key_total, width), b16),
            shape((key_total, width), b16),
            shape((width, rows), b16),
            shape((width, rows), b16),
        ],
        [],
        8 << 20,
        8 * unit,
        2 << 20,
        (ref_near, grad_near, source_near, w_query, w_key, w_value, w_out),
    )
    for mesh_axis, bit, _ in chip_steps:
        near_stats = combine_stats([near_stats, swap(near_stats, mesh_axis, bit)])
    far_stats = swap(near_stats, "blk", 1)
    attended, grad_query, grad_key, grad_value, weight_part = vmem_call(
        functools.partial(grads_kernel, HEADS),
        "match_grads",
        [
            shape((rows, width), b16),
            shape((rows, width), b16),
            shape((width, key_total), b16),
            shape((width, key_total), b16),
            shape((4, width, width), b16),
        ],
        [tile] * 4
        + [vmem((rows, key_total), b16)] * 4
        + [vmem((rows, width), f32)] * 2
        + [vmem((3, HEADS, steps, 8, STEP), f32)],
        (6 << 20) + rows * key_total * 32,
        100 * unit,
        8 << 20,
        (left, grad_left, right, value_t, keys, values, query_t, grad_t, row_stats, near_stats, far_stats,
         ref_rows, out_grad, source_all),
    )
    matched, grad_ref, source_part = vmem_call(
        finish_kernel,
        "finish_rows",
        [
            shape((rows, width), b16),
            shape((rows, width), b16),
            shape((key_total, width), b16),
        ],
        [],
        8 << 20,
        8 * unit,
        2 << 20,
        (ref_rows, out_grad, attended, grad_query, grad_key, grad_value,
         w_query, w_key, w_value, w_out),
    )

    scan_steps = bit_steps("scan")
    weights = weight_part.reshape((2,) * (1 + len(scan_steps)) + (-1, width))
    sources = source_part.reshape((2,) * (len(chip_steps) + 1) + (key_rows, width))
    weights = halve(weights, core_step)
    sources = halve(sources, core_step, len(chip_steps))
    for count in range(max(len(scan_steps), len(chip_steps))):
        weights, sources = lax.optimization_barrier((weights, sources))
        if count < len(scan_steps):
            weights = halve(weights, scan_steps[count])
        if count < len(chip_steps):
            sources = halve(sources, chip_steps[count], len(chip_steps) - 1 - count)
    weights, grad_src = lax.optimization_barrier((weights, sources))
    for mesh_axis, bit, _ in chip_steps:
        weights = add(weights, swap(weights, mesh_axis, bit))
    for step in scan_steps[::-1] + [core_step]:
        weights = double(weights, step)
    weights = weights.reshape(4, width, width).astype(f32)
    return (
        matched[None],
        grad_ref[None],
        grad_src[None],
        weights[0],
        weights[1],
        weights[2],
        weights[3],
    )


def solution(mesh):
    split = P("scan", "blk", None)
    whole = P()
    return jax.shard_map(
        on_device,
        mesh=mesh,
        in_specs=(split, split, split, whole, whole, whole, whole, split),
        out_specs=(split, split, split, whole, whole, whole, whole),
        check_vma=False,
    )
```

```python
import functools
import math

import jax
import jax.numpy as jnp
from jax import lax
from jax.experimental import pallas as pl
from jax.experimental.pallas import tpu as pltpu
from jax.sharding import PartitionSpec as P

HEADS = 4
BLOCK = 128
NEG = -1e30
FLOOR = -1e29
LOG2E = math.log2(math.e)

NT = (((1,), (1,)), ((), ()))
TN = (((0,), (0,)), ((), ()))
TT = (((0,), (1,)), ((), ()))


def mm(left, right):
    return jnp.dot(left, right, preferred_element_type=jnp.float32)


def mm_general(left, right, dims):
    return lax.dot_general(left, right, dims, preferred_element_type=jnp.float32)


def bf(x):
    return x.astype(jnp.bfloat16)


def lane_row(width, head, head_dim):
    lanes = lax.broadcasted_iota(jnp.int32, (1, width), 1) // head_dim
    return bf(jnp.where(lanes == head, 1.0, 0.0))


def spread(reduced, like):
    return jnp.broadcast_to(reduced, like.shape)


STRIP = 32
STEP = 256


def by_eight(x):
    return x.reshape(x.shape[0] // 8, 8, x.shape[1])


def listed_steps(inter_ref, query_block, work):
    per_step = STEP // BLOCK

    def visit(step, carry):
        listed = [inter_ref[query_block, step * per_step + k] == 1 for k in range(per_step)]

        @pl.when(functools.reduce(jnp.logical_or, listed))
        def _():
            work(query_block, step, listed)

        return carry

    lax.fori_loop(0, inter_ref.shape[1] // per_step, visit, 0)


def each_listed(inter_ref, work):
    def visit(query_block, carry):
        listed_steps(inter_ref, query_block, work)
        return carry

    lax.fori_loop(0, inter_ref.shape[0], visit, 0)


def head_strips(heads):
    for head in range(heads):
        spans = [slice(first, first + STRIP) for first in range(0, BLOCK, STRIP)]
        yield head, [slice(head * BLOCK + a.start, head * BLOCK + a.stop) for a in spans]


def score_block(query_block, step, listed, left_ref, key_t_ref, score_ref):
    span = pl.ds(pl.multiple_of(step * STEP, STEP), STEP)
    bias = jnp.concatenate(
        [jnp.full((1, BLOCK), jnp.where(flag, 0.0, NEG), jnp.float32) for flag in listed], axis=1
    )
    score_ref[...] = mm(left_ref[query_block], key_t_ref[:, span]) * LOG2E + bias


def stats_kernel(
    heads, inter_ref, ref_ref, gout_ref, src_ref, wq_ref, wk_ref, wv_ref, wo_ref,
    peak_ref, inverse_ref, col_ref, left_ref, gleft_ref, key_t_ref, value_t_ref,
    score_ref, prob_ref, total_ref, col_peak_ref, col_total_ref, col_dot_ref,
):
    rows, width = ref_ref.shape
    key_total = src_ref.shape[0]
    head_dim = width // heads
    query = bf(bf(mm(ref_ref[...], wq_ref[...])).astype(jnp.float32) * head_dim ** -0.5)
    grad = bf(mm_general(gout_ref[...], wo_ref[...], NT))
    for query_block in range(rows // BLOCK):
        span = slice(query_block * BLOCK, (query_block + 1) * BLOCK)
        for head in range(heads):
            own = lane_row(width, head, head_dim)
            left_ref[query_block, head * BLOCK : (head + 1) * BLOCK, :] = query[span] * own
            gleft_ref[query_block, head * BLOCK : (head + 1) * BLOCK, :] = grad[span] * own
    key_t_ref[...] = bf(mm_general(wk_ref[...], src_ref[...], TT))
    value_t_ref[...] = bf(mm_general(wv_ref[...], src_ref[...], TT))
    steps = key_total // STEP
    peak_ref[...] = jnp.full(peak_ref.shape, 2.0 * NEG, jnp.float32)
    total_ref[...] = jnp.zeros(total_ref.shape, jnp.float32)
    col_peak_ref[...] = jnp.full(col_peak_ref.shape, FLOOR, jnp.float32)
    col_total_ref[...] = jnp.zeros(col_total_ref.shape, jnp.float32)
    col_dot_ref[...] = jnp.zeros(col_dot_ref.shape, jnp.float32)
    tiles = [slice(first, first + 128) for first in range(0, STEP, 128)]

    def peaks(query_block, step, listed):
        block_ref = score_ref.at[query_block * steps + step]
        score_block(query_block, step, listed, left_ref, key_t_ref, block_ref)
        for head, spans in head_strips(heads):
            col_peaks = [col_peak_ref[step, head, :, lanes] for lanes in tiles]
            for span in spans:
                row_peak = peak_ref[query_block, span, :]
                for at, lanes in enumerate(tiles):
                    scores = block_ref[span, lanes]
                    row_peak = jnp.maximum(row_peak, scores)
                    col_peaks[at] = jnp.maximum(col_peaks[at], by_eight(scores).max(axis=0))
                peak_ref[query_block, span, :] = row_peak
            for at, lanes in enumerate(tiles):
                col_peak_ref[step, head, :, lanes] = col_peaks[at]

    each_listed(inter_ref, peaks)
    for query_block in range(rows // BLOCK):
        peak = peak_ref[query_block]
        peak_ref[query_block] = spread(peak.max(axis=1, keepdims=True), peak)
    for step in range(steps):
        for head in range(heads):
            peak = col_peak_ref[step, head]
            col_peak_ref[step, head] = spread(peak.max(axis=0, keepdims=True), peak)

    def totals(query_block, step, listed):
        score_now, prob_now = [ref.at[query_block * steps + step] for ref in (score_ref, prob_ref)]
        span = pl.ds(pl.multiple_of(step * STEP, STEP), STEP)
        prob_now[...] = mm(gleft_ref[query_block], value_t_ref[:, span])
        for head, spans in head_strips(heads):
            col_totals = [col_total_ref[step, head, :, lanes] for lanes in tiles]
            for span in spans:
                row_peak = by_eight(peak_ref[query_block, span, :])
                row_total = by_eight(total_ref[query_block, span, :])
                for at, lanes in enumerate(tiles):
                    scores = by_eight(score_now[span, lanes])
                    row_exp = jnp.exp2(scores - row_peak)
                    col_exp = jnp.exp2(scores - col_peak_ref[step, head, :, lanes][None])
                    row_total = row_total + row_exp
                    product = row_exp * col_exp * by_eight(prob_now[span, lanes])
                    prob_now[span, lanes] = product.reshape(STRIP, 128)
                    col_totals[at] = col_totals[at] + col_exp.sum(axis=0)
                total_ref[query_block, span, :] = row_total.reshape(STRIP, 128)
            for at, lanes in enumerate(tiles):
                col_total_ref[step, head, :, lanes] = col_totals[at]

    each_listed(inter_ref, totals)
    for query_block in range(rows // BLOCK):
        total = total_ref[query_block]
        inverse_ref[query_block] = spread(1.0 / total.sum(axis=1, keepdims=True), total)

    def dots(query_block, step, listed):
        prob_now = prob_ref.at[query_block * steps + step]
        for head, spans in head_strips(heads):
            col_dots = [col_dot_ref[step, head, :, lanes] for lanes in tiles]
            for span in spans:
                inverse = inverse_ref[query_block, span, :]
                for at, lanes in enumerate(tiles):
                    product = by_eight(prob_now[span, lanes] * inverse)
                    col_dots[at] = col_dots[at] + product.sum(axis=0)
            for at, lanes in enumerate(tiles):
                col_dot_ref[step, head, :, lanes] = col_dots[at]

    each_listed(inter_ref, dots)
    for step in range(steps):
        lanes = slice(step * STEP, (step + 1) * STEP)
        for head in range(heads):
            mine = slice(head, head + 1)
            col_ref[0, mine, lanes] = col_peak_ref[step, head, 0:1, :]
            col_ref[1, mine, lanes] = col_total_ref[step, head].sum(axis=0, keepdims=True)
            col_ref[2, mine, lanes] = col_dot_ref[step, head].sum(axis=0, keepdims=True)


def side_kernel(
    heads, ref_ref, gout_ref, src_ref, wq_ref, wk_ref, wv_ref, wo_ref,
    key_ref, value_ref, query_t_ref, grad_t_ref,
):
    rows, width = ref_ref.shape
    scale = (width // heads) ** -0.5
    key_ref[...] = bf(mm(src_ref[...], wk_ref[...]))
    value_ref[...] = bf(mm(src_ref[...], wv_ref[...]))
    query_t = bf(mm_general(wq_ref[...], ref_ref[...], TT)).astype(jnp.float32) * (2.0 * scale)
    grad_t = mm_general(wo_ref[...], gout_ref[...], NT)
    for query_block in range(rows // BLOCK):
        span = slice(query_block * BLOCK, (query_block + 1) * BLOCK)
        query_t_ref[query_block] = bf(query_t[:, span])
        grad_t_ref[query_block] = bf(grad_t[:, span])


def grads_kernel(
    heads, inter_ref, left_ref, gleft_ref, key_t_ref, value_t_ref, key_ref, value_ref,
    query_t_ref, grad_t_ref, peak_ref, inverse_ref, near_ref, far_ref, ref_ref, gout_ref, src_ref,
    attended_ref, gquery_ref, gkey_ref, gvalue_ref, weight_ref,
    row_prob_ref, rest_ref, match_ref, gscore_ref, score_ref, prob_ref, dot_ref, col_ref,
    att_ref, gq_ref, gk_ref, gv_ref,
):
    rows, width = ref_ref.shape
    key_total = src_ref.shape[0]
    steps = key_total // STEP
    head_dim = width // heads
    tiles = [slice(first, first + 128) for first in range(0, STEP, 128)]

    peak = jnp.maximum(near_ref[0], far_ref[0])
    near, far = jnp.exp2(near_ref[0] - peak), jnp.exp2(far_ref[0] - peak)
    inverse = 1.0 / (near * near_ref[1] + far * far_ref[1])
    half = (near * near_ref[2] + far * far_ref[2]) * inverse * 0.5
    for kind, values in enumerate((peak, inverse, half)):
        for head in range(heads):
            for step in range(steps):
                piece = values[head : head + 1, step * STEP : (step + 1) * STEP]
                col_ref[kind, step, head] = jnp.broadcast_to(piece, (8, STEP))
    for ref in (att_ref, gq_ref, gk_ref, gv_ref):
        ref[...] = jnp.zeros(ref.shape, jnp.float32)

    def products(query_block, step, listed):
        row_prob_now, rest_now, match_now = [
            ref.at[step] for ref in (row_prob_ref, rest_ref, match_ref)
        ]
        score_block(query_block, step, listed, left_ref, key_t_ref, score_ref)
        span = pl.ds(pl.multiple_of(step * STEP, STEP), STEP)
        prob_ref[...] = mm(gleft_ref[query_block], value_t_ref[:, span])
        for head, spans in head_strips(heads):
            for span in spans:
                row_peak = by_eight(peak_ref[query_block, span, :])
                row_inverse = by_eight(inverse_ref[query_block, span, :])
                row_dot = by_eight(dot_ref[span, :])
                for lanes in tiles:
                    scores = by_eight(score_ref[span, lanes])
                    row_prob = jnp.exp2(scores - row_peak) * row_inverse
                    col_prob = jnp.exp2(scores - col_ref[0, step, head, :, lanes][None])
                    col_prob = col_prob * col_ref[1, step, head, :, lanes][None]
                    match = row_prob * col_prob
                    product = match * by_eight(prob_ref[span, lanes])
                    row_dot = row_dot + product
                    rest = product - col_prob * col_ref[2, step, head, :, lanes][None]
                    match_now[span, lanes] = bf(match.reshape(STRIP, 128))
                    row_prob_now[span, lanes] = row_prob.reshape(STRIP, 128)
                    rest_now[span, lanes] = rest.reshape(STRIP, 128)
                dot_ref[span, :] = row_dot.reshape(STRIP, 128)

    def own_lanes(stacked):
        total = None
        for head in range(heads):
            own = lane_row(width, head, head_dim).astype(jnp.float32)
            piece = stacked[head * BLOCK : (head + 1) * BLOCK] * own
            total = piece if total is None else total + piece
        return total

    def outputs(query_block, step, listed):
        row_prob_now, rest_now, match_now = [
            ref.at[step] for ref in (row_prob_ref, rest_ref, match_ref)
        ]
        for _, spans in head_strips(heads):
            for span in spans:
                row_half = dot_ref[span, :]
                for lanes in tiles:
                    grads = rest_now[span, lanes] - row_prob_now[span, lanes] * row_half
                    gscore_ref[span, lanes] = bf(grads)
        span = pl.ds(pl.multiple_of(step * STEP, STEP), STEP)
        att_ref[query_block] += own_lanes(mm(match_now[...], value_ref[span, :]))
        gq_ref[query_block] += own_lanes(mm(gscore_ref[...], key_ref[span, :]))
        for head in range(heads):
            mine = slice(head * head_dim, (head + 1) * head_dim)
            stacked = slice(head * BLOCK, (head + 1) * BLOCK)
            gk_ref[step, mine, :] += mm(query_t_ref[query_block, mine, :], gscore_ref[stacked, :])
            gv_ref[step, mine, :] += mm(grad_t_ref[query_block, mine, :], match_now[stacked, :])

    def query_rows(query_block, carry):
        dot_ref[...] = jnp.zeros(dot_ref.shape, jnp.float32)
        listed_steps(inter_ref, query_block, products)
        dot = dot_ref[...]
        dot_ref[...] = spread(dot.sum(axis=1, keepdims=True) * 0.5, dot)
        listed_steps(inter_ref, query_block, outputs)
        return carry

    lax.fori_loop(0, rows // BLOCK, query_rows, 0)
    attended = bf(att_ref[...]).reshape(rows, width)
    gquery = bf(gq_ref[...] * (2.0 * head_dim ** -0.5)).reshape(rows, width)
    attended_ref[...] = attended
    gquery_ref[...] = gquery
    for step in range(steps):
        gkey_ref[:, step * STEP : (step + 1) * STEP] = bf(gk_ref[step])
        gvalue_ref[:, step * STEP : (step + 1) * STEP] = bf(gv_ref[step])
    weight_ref[0] = bf(mm_general(ref_ref[...], gquery, TN))
    weight_ref[1] = bf(mm(gkey_ref[...], src_ref[...]).T)
    weight_ref[2] = bf(mm(gvalue_ref[...], src_ref[...]).T)
    weight_ref[3] = bf(mm_general(attended, gout_ref[...], TN))


def finish_kernel(
    ref_ref, gout_ref, attended_ref, gquery_ref, gkey_ref, gvalue_ref, wq_ref, wk_ref, wv_ref, wo_ref,
    matched_ref, gref_ref, gsrc_ref,
):
    gsrc_t = mm(wk_ref[...], gkey_ref[...]) + mm(wv_ref[...], gvalue_ref[...])
    gsrc_ref[...] = bf(gsrc_t.T)
    matched = ref_ref[...].astype(jnp.float32) + mm(attended_ref[...], wo_ref[...])
    matched_ref[...] = bf(matched)
    gref = gout_ref[...].astype(jnp.float32) + mm_general(gquery_ref[...], wq_ref[...], NT)
    gref_ref[...] = bf(gref)


def swap(x, axis, apart):
    pairs = [(i, i ^ apart) for i in range(lax.axis_size(axis))]
    return lax.ppermute(x, axis, pairs)


def at(x, index, axis=0):
    return lax.dynamic_index_in_dim(x, index, axis, False)


def laid(near, far, side, axis=0):
    shape = near.shape[:axis] + (2,) + near.shape[axis:]
    out = lax.dynamic_update_index_in_dim(jnp.zeros(shape, near.dtype), near, side, axis)
    return lax.dynamic_update_index_in_dim(out, far, 1 - side, axis)


def add(near, far):
    return (near.astype(jnp.float32) + far.astype(jnp.float32)).astype(near.dtype)


def halve(x, step, axis=0):
    mesh_axis, bit, side = step
    return add(at(x, side, axis), swap(at(x, 1 - side, axis), mesh_axis, bit))


def double(x, step, axis=0):
    mesh_axis, bit, side = step
    return laid(x, swap(x, mesh_axis, bit), side, axis)


def bit_steps(mesh_axis, first=1):
    count, me = lax.axis_size(mesh_axis), lax.axis_index(mesh_axis)
    steps = []
    while first < count:
        steps.append((mesh_axis, first, (me // first) % 2))
        first *= 2
    return steps


def combine_stats(parts):
    peak = functools.reduce(jnp.maximum, [part[0] for part in parts])
    factors = [jnp.exp2(part[0] - peak) for part in parts]
    total = sum(factor * part[1] for factor, part in zip(factors, parts))
    dots = sum(factor * part[2] for factor, part in zip(factors, parts))
    return jnp.stack([peak, total, dots])


def vmem_call(kernel, name, out_shape, scratch, limit, flops, moved, args, scalars=0):
    specs = [pl.BlockSpec(memory_space=pltpu.SMEM)] * scalars
    specs += [pl.BlockSpec(memory_space=pltpu.VMEM)] * (len(args) - scalars)
    return pl.pallas_call(
        kernel,
        name=name,
        out_shape=out_shape,
        in_specs=specs,
        out_specs=[pl.BlockSpec(memory_space=pltpu.VMEM)] * len(out_shape),
        scratch_shapes=scratch,
        compiler_params=pltpu.CompilerParams(vmem_limit_bytes=limit),
        cost_estimate=pl.CostEstimate(flops=flops, bytes_accessed=moved, transcendentals=0),
    )(*args)


def on_device(ref_feats, src_feats, grad_out, w_query, w_key, w_value, w_out, intersection):
    ref_rows = ref_feats[0]
    src_rows = src_feats[0]
    out_grad = grad_out[0]
    listed = intersection[0]
    rows, width = ref_rows.shape
    core_step = bit_steps("blk")[0]
    chip_steps = bit_steps("blk", 2)
    key_rows = src_rows.shape[0]
    key_total = key_rows * lax.axis_size("blk")

    source_all = src_rows
    for count, step in enumerate(chip_steps[::-1]):
        source_all = double(source_all, step, count)
    source_all = double(source_all, core_step, len(chip_steps)).reshape(key_total, width)

    f32, b16 = jnp.float32, jnp.bfloat16
    shape, vmem = jax.ShapeDtypeStruct, pltpu.VMEM
    unit = 2 * rows * width * width
    query_blocks, steps = rows // BLOCK, key_total // STEP
    stacked = HEADS * BLOCK
    blocks = vmem((query_blocks * steps, stacked, STEP), f32)
    row_like = shape((query_blocks, stacked, 128), f32)
    col_like = vmem((steps, HEADS, 8, STEP), f32)
    row_peak, row_inverse, col_stats, left, grad_left, key_t, value_t = vmem_call(
        functools.partial(stats_kernel, HEADS),
        "match_stats",
        [
            row_like,
            row_like,
            shape((3, HEADS, key_total), f32),
            shape((query_blocks, stacked, width), b16),
            shape((query_blocks, stacked, width), b16),
            shape((width, key_total), b16),
            shape((width, key_total), b16),
        ],
        [blocks, blocks, vmem(row_like.shape, f32), col_like, col_like, col_like],
        (6 << 20) + rows * key_total * HEADS * 9,
        60 * unit,
        8 << 20,
        (listed, ref_rows, out_grad, source_all, w_query, w_key, w_value, w_out),
        scalars=1,
    )
    ref_near, grad_near, source_near, near_stats = lax.optimization_barrier(
        (ref_rows, out_grad, source_all, col_stats)
    )
    keys, values, query_t, grad_t = vmem_call(
        functools.partial(side_kernel, HEADS),
        "project_for_grads",
        [
            shape((key_total, width), b16),
            shape((key_total, width), b16),
            shape((query_blocks, width, BLOCK), b16),
            shape((query_blocks, width, BLOCK), b16),
        ],
        [],
        8 << 20,
        8 * unit,
        2 << 20,
        (ref_near, grad_near, source_near, w_query, w_key, w_value, w_out),
    )
    for mesh_axis, bit, _ in chip_steps:
        near_stats = combine_stats([near_stats, swap(near_stats, mesh_axis, bit)])
    far_stats = swap(near_stats, "blk", 1)
    attended, grad_query, grad_key, grad_value, weight_part = vmem_call(
        functools.partial(grads_kernel, HEADS),
        "match_grads",
        [
            shape((rows, width), b16),
            shape((rows, width), b16),
            shape((width, key_total), b16),
            shape((width, key_total), b16),
            shape((4, width, width), b16),
        ],
        [
            vmem((steps, stacked, STEP), f32),
            vmem((steps, stacked, STEP), f32),
            vmem((steps, stacked, STEP), b16),
            vmem((stacked, STEP), b16),
            vmem((stacked, STEP), f32),
            vmem((stacked, STEP), f32),
            vmem((stacked, 128), f32),
            vmem((3, steps, HEADS, 8, STEP), f32),
            vmem((query_blocks, BLOCK, width), f32),
            vmem((query_blocks, BLOCK, width), f32),
            vmem((steps, width, STEP), f32),
            vmem((steps, width, STEP), f32),
        ],
        (10 << 20) + BLOCK * key_total * HEADS * 20,
        100 * unit,
        8 << 20,
        (listed, left, grad_left, key_t, value_t, keys, values, query_t, grad_t, row_peak, row_inverse,
         near_stats, far_stats, ref_rows, out_grad, source_all),
        scalars=1,
    )
    matched, grad_ref, source_part = vmem_call(
        finish_kernel,
        "finish_rows",
        [
            shape((rows, width), b16),
            shape((rows, width), b16),
            shape((key_total, width), b16),
        ],
        [],
        8 << 20,
        8 * unit,
        2 << 20,
        (ref_rows, out_grad, attended, grad_query, grad_key, grad_value,
         w_query, w_key, w_value, w_out),
    )

    scan_steps = bit_steps("scan")
    weights = weight_part.reshape((2,) * (1 + len(scan_steps)) + (-1, width))
    sources = source_part.reshape((2,) * (len(chip_steps) + 1) + (key_rows, width))
    source_steps = list(zip(chip_steps, range(len(chip_steps) - 1, -1, -1)))
    weights = halve(weights, core_step)
    sources = halve(sources, core_step, len(chip_steps))
    for count, step in enumerate(scan_steps):
        weights, sources = lax.optimization_barrier((weights, sources))
        weights = halve(weights, step)
        if count == 0:
            sources = halve(sources, *source_steps.pop(0))
    for mesh_axis, bit, _ in chip_steps:
        weights = add(weights, swap(weights, mesh_axis, bit))
    for count, step in enumerate(scan_steps[::-1]):
        weights, sources = lax.optimization_barrier((weights, sources))
        weights = double(weights, step)
        if source_steps and count >= len(scan_steps) - len(source_steps):
            sources = halve(sources, *source_steps.pop(0))
    for step in source_steps:
        sources = halve(sources, *step)
    grad_src = sources
    weights = double(weights, core_step)
    weights = weights.reshape(4, width, width).astype(f32)
    return (
        matched[None],
        grad_ref[None],
        grad_src[None],
        weights[0],
        weights[1],
        weights[2],
        weights[3],
    )


def solution(mesh):
    split = P("scan", "blk", None)
    whole = P()
    return jax.shard_map(
        on_device,
        mesh=mesh,
        in_specs=(split, split, split, whole, whole, whole, whole, split),
        out_specs=(split, split, split, whole, whole, whole, whole),
        check_vma=False,
    )
```

```python
import functools
import math

import jax
import jax.numpy as jnp
from jax import lax
from jax.experimental import pallas as pl
from jax.experimental.pallas import tpu as pltpu
from jax.sharding import PartitionSpec as P

HEADS = 4
BLOCK = 128
NEG = -1e30
FLOOR = -1e29
LOG2E = math.log2(math.e)

NT = (((1,), (1,)), ((), ()))
TN = (((0,), (0,)), ((), ()))
TT = (((0,), (1,)), ((), ()))


def mm(left, right):
    return jnp.dot(left, right, preferred_element_type=jnp.float32)


def mm_general(left, right, dims):
    return lax.dot_general(left, right, dims, preferred_element_type=jnp.float32)


def bf(x):
    return x.astype(jnp.bfloat16)


def lane_row(width, head, head_dim):
    lanes = lax.broadcasted_iota(jnp.int32, (1, width), 1) // head_dim
    return bf(jnp.where(lanes == head, 1.0, 0.0))


def spread(reduced, like):
    return jnp.broadcast_to(reduced, like.shape)


STRIP = 32
STEP = 256


def by_eight(x):
    return x.reshape(x.shape[0] // 8, 8, x.shape[1])


def listed_steps(inter_ref, query_block, work):
    per_step = STEP // BLOCK

    def visit(step, carry):
        listed = [inter_ref[query_block, step * per_step + k] == 1 for k in range(per_step)]

        @pl.when(functools.reduce(jnp.logical_or, listed))
        def _():
            work(query_block, step, listed)

        return carry

    lax.fori_loop(0, inter_ref.shape[1] // per_step, visit, 0)


def each_listed(inter_ref, work):
    def visit(query_block, carry):
        listed_steps(inter_ref, query_block, work)
        return carry

    lax.fori_loop(0, inter_ref.shape[0], visit, 0)


def head_strips(heads):
    for head in range(heads):
        spans = [slice(first, first + STRIP) for first in range(0, BLOCK, STRIP)]
        yield head, [slice(head * BLOCK + a.start, head * BLOCK + a.stop) for a in spans]


def score_block(query_block, step, listed, left_ref, key_t_ref, score_ref):
    span = pl.ds(pl.multiple_of(step * STEP, STEP), STEP)
    bias = jnp.concatenate(
        [jnp.full((1, BLOCK), jnp.where(flag, 0.0, NEG), jnp.float32) for flag in listed], axis=1
    )
    score_ref[...] = mm(left_ref[query_block], key_t_ref[:, span]) * LOG2E + bias


def stats_kernel(
    heads, inter_ref, ref_ref, gout_ref, src_ref, wq_ref, wk_ref, wv_ref, wo_ref,
    peak_ref, inverse_ref, col_ref, left_ref, gleft_ref, key_t_ref, value_t_ref,
    score_ref, prob_ref, total_ref, col_peak_ref, col_total_ref, col_dot_ref,
):
    rows, width = ref_ref.shape
    key_total = src_ref.shape[0]
    head_dim = width // heads
    query = bf(bf(mm(ref_ref[...], wq_ref[...])).astype(jnp.float32) * head_dim ** -0.5)
    grad = bf(mm_general(gout_ref[...], wo_ref[...], NT))
    for query_block in range(rows // BLOCK):
        span = slice(query_block * BLOCK, (query_block + 1) * BLOCK)
        for head in range(heads):
            own = lane_row(width, head, head_dim)
            left_ref[query_block, head * BLOCK : (head + 1) * BLOCK, :] = query[span] * own
            gleft_ref[query_block, head * BLOCK : (head + 1) * BLOCK, :] = grad[span] * own
    key_t_ref[...] = bf(mm_general(wk_ref[...], src_ref[...], TT))
    value_t_ref[...] = bf(mm_general(wv_ref[...], src_ref[...], TT))
    steps = key_total // STEP
    peak_ref[...] = jnp.full(peak_ref.shape, 2.0 * NEG, jnp.float32)
    total_ref[...] = jnp.zeros(total_ref.shape, jnp.float32)
    col_peak_ref[...] = jnp.full(col_peak_ref.shape, FLOOR, jnp.float32)
    col_total_ref[...] = jnp.zeros(col_total_ref.shape, jnp.float32)
    col_dot_ref[...] = jnp.zeros(col_dot_ref.shape, jnp.float32)
    tiles = [slice(first, first + 128) for first in range(0, STEP, 128)]

    def peaks(query_block, step, listed):
        block_ref = score_ref.at[query_block * steps + step]
        score_block(query_block, step, listed, left_ref, key_t_ref, block_ref)
        for head, spans in head_strips(heads):
            col_peaks = [col_peak_ref[step, head, :, lanes] for lanes in tiles]
            for span in spans:
                row_peak = peak_ref[query_block, span, :]
                for at, lanes in enumerate(tiles):
                    scores = block_ref[span, lanes]
                    row_peak = jnp.maximum(row_peak, scores)
                    col_peaks[at] = jnp.maximum(col_peaks[at], by_eight(scores).max(axis=0))
                peak_ref[query_block, span, :] = row_peak
            for at, lanes in enumerate(tiles):
                col_peak_ref[step, head, :, lanes] = col_peaks[at]

    each_listed(inter_ref, peaks)
    for query_block in range(rows // BLOCK):
        peak = peak_ref[query_block]
        peak_ref[query_block] = spread(peak.max(axis=1, keepdims=True), peak)
    for step in range(steps):
        for head in range(heads):
            peak = col_peak_ref[step, head]
            col_peak_ref[step, head] = spread(peak.max(axis=0, keepdims=True), peak)

    def totals(query_block, step, listed):
        score_now, prob_now = [ref.at[query_block * steps + step] for ref in (score_ref, prob_ref)]
        span = pl.ds(pl.multiple_of(step * STEP, STEP), STEP)
        prob_now[...] = mm(gleft_ref[query_block], value_t_ref[:, span])
        for head, spans in head_strips(heads):
            col_totals = [col_total_ref[step, head, :, lanes] for lanes in tiles]
            for span in spans:
                row_peak = by_eight(peak_ref[query_block, span, :])
                row_total = by_eight(total_ref[query_block, span, :])
                for at, lanes in enumerate(tiles):
                    scores = by_eight(score_now[span, lanes])
                    row_exp = jnp.exp2(scores - row_peak)
                    col_exp = jnp.exp2(scores - col_peak_ref[step, head, :, lanes][None])
                    row_total = row_total + row_exp
                    product = row_exp * col_exp * by_eight(prob_now[span, lanes])
                    prob_now[span, lanes] = product.reshape(STRIP, 128)
                    col_totals[at] = col_totals[at] + col_exp.sum(axis=0)
                total_ref[query_block, span, :] = row_total.reshape(STRIP, 128)
            for at, lanes in enumerate(tiles):
                col_total_ref[step, head, :, lanes] = col_totals[at]

    each_listed(inter_ref, totals)
    for query_block in range(rows // BLOCK):
        total = total_ref[query_block]
        inverse_ref[query_block] = spread(1.0 / total.sum(axis=1, keepdims=True), total)

    def dots(query_block, step, listed):
        prob_now = prob_ref.at[query_block * steps + step]
        for head, spans in head_strips(heads):
            col_dots = [col_dot_ref[step, head, :, lanes] for lanes in tiles]
            for span in spans:
                inverse = inverse_ref[query_block, span, :]
                for at, lanes in enumerate(tiles):
                    product = by_eight(prob_now[span, lanes] * inverse)
                    col_dots[at] = col_dots[at] + product.sum(axis=0)
            for at, lanes in enumerate(tiles):
                col_dot_ref[step, head, :, lanes] = col_dots[at]

    each_listed(inter_ref, dots)
    for step in range(steps):
        lanes = slice(step * STEP, (step + 1) * STEP)
        for head in range(heads):
            mine = slice(head, head + 1)
            col_ref[0, mine, lanes] = col_peak_ref[step, head, 0:1, :]
            col_ref[1, mine, lanes] = col_total_ref[step, head].sum(axis=0, keepdims=True)
            col_ref[2, mine, lanes] = col_dot_ref[step, head].sum(axis=0, keepdims=True)


def side_kernel(
    heads, ref_ref, gout_ref, src_ref, wq_ref, wk_ref, wv_ref, wo_ref,
    key_ref, value_ref, query_t_ref, grad_t_ref,
):
    rows, width = ref_ref.shape
    scale = (width // heads) ** -0.5
    key_ref[...] = bf(mm(src_ref[...], wk_ref[...]))
    value_ref[...] = bf(mm(src_ref[...], wv_ref[...]))
    query_t = bf(mm_general(wq_ref[...], ref_ref[...], TT)).astype(jnp.float32) * (2.0 * scale)
    grad_t = mm_general(wo_ref[...], gout_ref[...], NT)
    for query_block in range(rows // BLOCK):
        span = slice(query_block * BLOCK, (query_block + 1) * BLOCK)
        query_t_ref[query_block] = bf(query_t[:, span])
        grad_t_ref[query_block] = bf(grad_t[:, span])


def grads_kernel(
    heads, inter_ref, left_ref, gleft_ref, key_t_ref, value_t_ref, key_ref, value_ref,
    query_t_ref, grad_t_ref, peak_ref, inverse_ref, near_ref, far_ref, ref_ref, gout_ref, src_ref,
    attended_ref, gquery_ref, gkey_ref, gvalue_ref, weight_ref,
    row_prob_ref, rest_ref, match_ref, gscore_ref, score_ref, prob_ref, dot_ref, col_ref,
    att_ref, gq_ref, gk_ref, gv_ref,
):
    rows, width = ref_ref.shape
    key_total = src_ref.shape[0]
    steps = key_total // STEP
    head_dim = width // heads
    tiles = [slice(first, first + 128) for first in range(0, STEP, 128)]

    peak = jnp.maximum(near_ref[0], far_ref[0])
    near, far = jnp.exp2(near_ref[0] - peak), jnp.exp2(far_ref[0] - peak)
    inverse = 1.0 / (near * near_ref[1] + far * far_ref[1])
    half = (near * near_ref[2] + far * far_ref[2]) * inverse * 0.5
    for kind, values in enumerate((peak, inverse, half)):
        for head in range(heads):
            for step in range(steps):
                piece = values[head : head + 1, step * STEP : (step + 1) * STEP]
                col_ref[kind, step, head] = jnp.broadcast_to(piece, (8, STEP))
    for ref in (att_ref, gq_ref, gk_ref, gv_ref):
        ref[...] = jnp.zeros(ref.shape, jnp.float32)

    def products(query_block, step, listed):
        row_prob_now, rest_now, match_now = [
            ref.at[step] for ref in (row_prob_ref, rest_ref, match_ref)
        ]
        score_block(query_block, step, listed, left_ref, key_t_ref, score_ref)
        span = pl.ds(pl.multiple_of(step * STEP, STEP), STEP)
        prob_ref[...] = mm(gleft_ref[query_block], value_t_ref[:, span])
        for head, spans in head_strips(heads):
            for span in spans:
                row_peak = by_eight(peak_ref[query_block, span, :])
                row_inverse = by_eight(inverse_ref[query_block, span, :])
                row_dot = by_eight(dot_ref[span, :])
                for lanes in tiles:
                    scores = by_eight(score_ref[span, lanes])
                    row_prob = jnp.exp2(scores - row_peak) * row_inverse
                    col_prob = jnp.exp2(scores - col_ref[0, step, head, :, lanes][None])
                    col_prob = col_prob * col_ref[1, step, head, :, lanes][None]
                    match = row_prob * col_prob
                    product = match * by_eight(prob_ref[span, lanes])
                    row_dot = row_dot + product
                    rest = product - col_prob * col_ref[2, step, head, :, lanes][None]
                    match_now[span, lanes] = bf(match.reshape(STRIP, 128))
                    row_prob_now[span, lanes] = row_prob.reshape(STRIP, 128)
                    rest_now[span, lanes] = rest.reshape(STRIP, 128)
                dot_ref[span, :] = row_dot.reshape(STRIP, 128)

    def own_lanes(stacked):
        total = None
        for head in range(heads):
            own = lane_row(width, head, head_dim).astype(jnp.float32)
            piece = stacked[head * BLOCK : (head + 1) * BLOCK] * own
            total = piece if total is None else total + piece
        return total

    def outputs(query_block, step, listed):
        row_prob_now, rest_now, match_now = [
            ref.at[step] for ref in (row_prob_ref, rest_ref, match_ref)
        ]
        for _, spans in head_strips(heads):
            for span in spans:
                row_half = dot_ref[span, :]
                for lanes in tiles:
                    grads = rest_now[span, lanes] - row_prob_now[span, lanes] * row_half
                    gscore_ref[span, lanes] = bf(grads)
        span = pl.ds(pl.multiple_of(step * STEP, STEP), STEP)
        att_ref[query_block] += own_lanes(mm(match_now[...], value_ref[span, :]))
        gq_ref[query_block] += own_lanes(mm(gscore_ref[...], key_ref[span, :]))
        for head in range(heads):
            mine = slice(head * head_dim, (head + 1) * head_dim)
            stacked = slice(head * BLOCK, (head + 1) * BLOCK)
            gk_ref[step, mine, :] += mm(query_t_ref[query_block, mine, :], gscore_ref[stacked, :])
            gv_ref[step, mine, :] += mm(grad_t_ref[query_block, mine, :], match_now[stacked, :])

    def query_rows(query_block, carry):
        dot_ref[...] = jnp.zeros(dot_ref.shape, jnp.float32)
        listed_steps(inter_ref, query_block, products)
        dot = dot_ref[...]
        dot_ref[...] = spread(dot.sum(axis=1, keepdims=True) * 0.5, dot)
        listed_steps(inter_ref, query_block, outputs)
        return carry

    lax.fori_loop(0, rows // BLOCK, query_rows, 0)
    attended = bf(att_ref[...]).reshape(rows, width)
    gquery = bf(gq_ref[...] * (2.0 * head_dim ** -0.5)).reshape(rows, width)
    attended_ref[...] = attended
    gquery_ref[...] = gquery
    for step in range(steps):
        gkey_ref[:, step * STEP : (step + 1) * STEP] = bf(gk_ref[step])
        gvalue_ref[:, step * STEP : (step + 1) * STEP] = bf(gv_ref[step])
    weight_ref[0] = bf(mm_general(ref_ref[...], gquery, TN))
    weight_ref[1] = bf(mm(gkey_ref[...], src_ref[...]).T)
    weight_ref[2] = bf(mm(gvalue_ref[...], src_ref[...]).T)
    weight_ref[3] = bf(mm_general(attended, gout_ref[...], TN))


def finish_kernel(
    ref_ref, gout_ref, attended_ref, gquery_ref, gkey_ref, gvalue_ref, wq_ref, wk_ref, wv_ref, wo_ref,
    matched_ref, gref_ref, gsrc_ref,
):
    gsrc_t = mm(wk_ref[...], gkey_ref[...]) + mm(wv_ref[...], gvalue_ref[...])
    gsrc_ref[...] = bf(gsrc_t.T)
    matched = ref_ref[...].astype(jnp.float32) + mm(attended_ref[...], wo_ref[...])
    matched_ref[...] = bf(matched)
    gref = gout_ref[...].astype(jnp.float32) + mm_general(gquery_ref[...], wq_ref[...], NT)
    gref_ref[...] = bf(gref)


def swap(x, axis, apart):
    pairs = [(i, i ^ apart) for i in range(lax.axis_size(axis))]
    return lax.ppermute(x, axis, pairs)


def at(x, index, axis=0):
    return lax.dynamic_index_in_dim(x, index, axis, False)


def laid(near, far, side, axis=0):
    shape = near.shape[:axis] + (2,) + near.shape[axis:]
    out = lax.dynamic_update_index_in_dim(jnp.zeros(shape, near.dtype), near, side, axis)
    return lax.dynamic_update_index_in_dim(out, far, 1 - side, axis)


def add(near, far):
    return (near.astype(jnp.float32) + far.astype(jnp.float32)).astype(near.dtype)


def halve(x, step, axis=0):
    mesh_axis, bit, side = step
    return add(at(x, side, axis), swap(at(x, 1 - side, axis), mesh_axis, bit))


def double(x, step, axis=0):
    mesh_axis, bit, side = step
    return laid(x, swap(x, mesh_axis, bit), side, axis)


def bit_steps(mesh_axis):
    me = lax.axis_index(mesh_axis)
    bits = range(lax.axis_size(mesh_axis).bit_length() - 1)
    return [(mesh_axis, 1 << bit, (me >> bit) % 2) for bit in bits]


def combine_stats(parts):
    peak = functools.reduce(jnp.maximum, [part[0] for part in parts])
    factors = [jnp.exp2(part[0] - peak) for part in parts]
    total = sum(factor * part[1] for factor, part in zip(factors, parts))
    dots = sum(factor * part[2] for factor, part in zip(factors, parts))
    return jnp.stack([peak, total, dots])


def vmem_call(kernel, name, out_shape, scratch, limit, flops, moved, args, scalars=0):
    specs = [pl.BlockSpec(memory_space=pltpu.SMEM)] * scalars
    specs += [pl.BlockSpec(memory_space=pltpu.VMEM)] * (len(args) - scalars)
    return pl.pallas_call(
        kernel,
        name=name,
        out_shape=out_shape,
        in_specs=specs,
        out_specs=[pl.BlockSpec(memory_space=pltpu.VMEM)] * len(out_shape),
        scratch_shapes=scratch,
        compiler_params=pltpu.CompilerParams(vmem_limit_bytes=limit),
        cost_estimate=pl.CostEstimate(flops=flops, bytes_accessed=moved, transcendentals=0),
    )(*args)


def on_device(ref_feats, src_feats, grad_out, w_query, w_key, w_value, w_out, intersection):
    ref_rows = ref_feats[0]
    src_rows = src_feats[0]
    out_grad = grad_out[0]
    listed = intersection[0]
    rows, width = ref_rows.shape
    core_step = bit_steps("core")[0]
    chip_steps = bit_steps("chip")
    key_rows = src_rows.shape[0]
    key_total = key_rows * lax.axis_size("chip") * lax.axis_size("core")

    source_all = src_rows
    for count, step in enumerate(chip_steps[::-1]):
        source_all = double(source_all, step, count)
    source_all = double(source_all, core_step, len(chip_steps)).reshape(key_total, width)

    f32, b16 = jnp.float32, jnp.bfloat16
    shape, vmem = jax.ShapeDtypeStruct, pltpu.VMEM
    unit = 2 * rows * width * width
    query_blocks, steps = rows // BLOCK, key_total // STEP
    stacked = HEADS * BLOCK
    blocks = vmem((query_blocks * steps, stacked, STEP), f32)
    row_like = shape((query_blocks, stacked, 128), f32)
    col_like = vmem((steps, HEADS, 8, STEP), f32)
    row_peak, row_inverse, col_stats, left, grad_left, key_t, value_t = vmem_call(
        functools.partial(stats_kernel, HEADS),
        "match_stats",
        [
            row_like,
            row_like,
            shape((3, HEADS, key_total), f32),
            shape((query_blocks, stacked, width), b16),
            shape((query_blocks, stacked, width), b16),
            shape((width, key_total), b16),
            shape((width, key_total), b16),
        ],
        [blocks, blocks, vmem(row_like.shape, f32), col_like, col_like, col_like],
        (6 << 20) + rows * key_total * HEADS * 9,
        60 * unit,
        8 << 20,
        (listed, ref_rows, out_grad, source_all, w_query, w_key, w_value, w_out),
        scalars=1,
    )
    ref_near, grad_near, source_near, near_stats = lax.optimization_barrier(
        (ref_rows, out_grad, source_all, col_stats)
    )
    keys, values, query_t, grad_t = vmem_call(
        functools.partial(side_kernel, HEADS),
        "project_for_grads",
        [
            shape((key_total, width), b16),
            shape((key_total, width), b16),
            shape((query_blocks, width, BLOCK), b16),
            shape((query_blocks, width, BLOCK), b16),
        ],
        [],
        8 << 20,
        8 * unit,
        2 << 20,
        (ref_near, grad_near, source_near, w_query, w_key, w_value, w_out),
    )
    for mesh_axis, bit, _ in chip_steps:
        near_stats = combine_stats([near_stats, swap(near_stats, mesh_axis, bit)])
    far_stats = swap(near_stats, "core", 1)
    attended, grad_query, grad_key, grad_value, weight_part = vmem_call(
        functools.partial(grads_kernel, HEADS),
        "match_grads",
        [
            shape((rows, width), b16),
            shape((rows, width), b16),
            shape((width, key_total), b16),
            shape((width, key_total), b16),
            shape((4, width, width), b16),
        ],
        [
            vmem((steps, stacked, STEP), f32),
            vmem((steps, stacked, STEP), f32),
            vmem((steps, stacked, STEP), b16),
            vmem((stacked, STEP), b16),
            vmem((stacked, STEP), f32),
            vmem((stacked, STEP), f32),
            vmem((stacked, 128), f32),
            vmem((3, steps, HEADS, 8, STEP), f32),
            vmem((query_blocks, BLOCK, width), f32),
            vmem((query_blocks, BLOCK, width), f32),
            vmem((steps, width, STEP), f32),
            vmem((steps, width, STEP), f32),
        ],
        (10 << 20) + BLOCK * key_total * HEADS * 20,
        100 * unit,
        8 << 20,
        (listed, left, grad_left, key_t, value_t, keys, values, query_t, grad_t, row_peak, row_inverse,
         near_stats, far_stats, ref_rows, out_grad, source_all),
        scalars=1,
    )
    matched, grad_ref, source_part = vmem_call(
        finish_kernel,
        "finish_rows",
        [
            shape((rows, width), b16),
            shape((rows, width), b16),
            shape((key_total, width), b16),
        ],
        [],
        8 << 20,
        8 * unit,
        2 << 20,
        (ref_rows, out_grad, attended, grad_query, grad_key, grad_value,
         w_query, w_key, w_value, w_out),
    )

    peers = ("scan", "chip")
    count = lax.axis_size("scan") * lax.axis_size("chip")
    weights = weight_part.reshape((2, count, -1, width))
    sources = source_part.reshape((2,) * (len(chip_steps) + 1) + (key_rows, width))
    source_steps = list(zip(chip_steps, range(len(chip_steps) - 1, -1, -1)))
    weights = halve(weights, core_step)
    sources = halve(sources, core_step, len(chip_steps))
    weights, sources = lax.optimization_barrier((weights, sources))
    weights = lax.all_to_all(weights, peers, 0, 0).astype(f32).sum(axis=0).astype(b16)
    sources = halve(sources, *source_steps[0])
    weights, sources = lax.optimization_barrier((weights, sources))
    weights = lax.all_to_all(jnp.broadcast_to(weights, (count,) + weights.shape), peers, 0, 0)
    for step in source_steps[1:]:
        sources = halve(sources, *step)
    grad_src = sources
    weights = double(weights, core_step)
    weights = weights.reshape(4, width, width).astype(f32)
    return (
        matched[None],
        grad_ref[None],
        grad_src[None],
        weights[0],
        weights[1],
        weights[2],
        weights[3],
    )


def solution(mesh):
    scans, blks = mesh.shape["scan"], mesh.shape["blk"]
    mesh = jax.sharding.Mesh(
        mesh.devices.reshape(scans, blks // 2, 2), ("scan", "chip", "core")
    )
    split = P("scan", ("chip", "core"), None)
    whole = P()
    return jax.shard_map(
        on_device,
        mesh=mesh,
        in_specs=(split, split, split, whole, whole, whole, whole, split),
        out_specs=(split, split, split, whole, whole, whole, whole),
        check_vma=False,
    )
```

```python
import functools
import math

import jax
import jax.numpy as jnp
from jax import lax
from jax.experimental import pallas as pl
from jax.experimental.pallas import tpu as pltpu
from jax.sharding import PartitionSpec as P

HEADS = 4
BLOCK = 128
NEG = -1e30
FLOOR = -1e29
LOG2E = math.log2(math.e)

NT = (((1,), (1,)), ((), ()))
TN = (((0,), (0,)), ((), ()))
TT = (((0,), (1,)), ((), ()))


def mm(left, right):
    return jnp.dot(left, right, preferred_element_type=jnp.float32)


def mm_general(left, right, dims):
    return lax.dot_general(left, right, dims, preferred_element_type=jnp.float32)


def bf(x):
    return x.astype(jnp.bfloat16)


def lane_row(width, head, head_dim):
    lanes = lax.broadcasted_iota(jnp.int32, (1, width), 1) // head_dim
    return bf(jnp.where(lanes == head, 1.0, 0.0))


def spread(reduced, like):
    return jnp.broadcast_to(reduced, like.shape)


STRIP = 32
STEP = 256


def by_eight(x):
    return x.reshape(x.shape[0] // 8, 8, x.shape[1])


def listed_steps(inter_ref, query_block, work):
    per_step = STEP // BLOCK

    def visit(step, carry):
        listed = [inter_ref[query_block, step * per_step + k] == 1 for k in range(per_step)]

        @pl.when(functools.reduce(jnp.logical_or, listed))
        def _():
            work(query_block, step, listed)

        return carry

    lax.fori_loop(0, inter_ref.shape[1] // per_step, visit, 0)


def each_listed(inter_ref, work):
    def visit(query_block, carry):
        listed_steps(inter_ref, query_block, work)
        return carry

    lax.fori_loop(0, inter_ref.shape[0], visit, 0)


def head_strips(heads):
    for head in range(heads):
        spans = [slice(first, first + STRIP) for first in range(0, BLOCK, STRIP)]
        yield head, [slice(head * BLOCK + a.start, head * BLOCK + a.stop) for a in spans]


def score_block(query_block, step, listed, left_ref, key_t_ref, score_ref):
    span = pl.ds(pl.multiple_of(step * STEP, STEP), STEP)
    bias = jnp.concatenate(
        [jnp.full((1, BLOCK), jnp.where(flag, 0.0, NEG), jnp.float32) for flag in listed], axis=1
    )
    score_ref[...] = mm(left_ref[query_block], key_t_ref[:, span]) * LOG2E + bias


def unpack(packed_ref):
    total, width = packed_ref.shape
    rows = (total - 4 * width) // 2
    sizes = [rows, rows, width, width, width, width]
    return [packed_ref.at[pl.ds(sum(sizes[:k]), sizes[k])] for k in range(len(sizes))]


def stats_kernel(
    heads, inter_ref, packed_ref, src_ref, peak_ref, inverse_ref, col_ref, score_ref, product_ref,
    left_ref, gleft_ref, key_t_ref, value_t_ref, prob_ref, total_ref,
    col_peak_ref, col_total_ref, col_dot_ref,
):
    ref_ref, gout_ref, wq_ref, wk_ref, wv_ref, wo_ref = unpack(packed_ref)
    rows, width = ref_ref.shape
    key_total = src_ref.shape[0]
    head_dim = width // heads
    key_t_ref[...] = bf(mm_general(wk_ref[...], src_ref[...], TT))
    value_t_ref[...] = bf(mm_general(wv_ref[...], src_ref[...], TT))
    query = bf(bf(mm(ref_ref[...], wq_ref[...])).astype(jnp.float32) * head_dim ** -0.5)
    grad = bf(mm_general(gout_ref[...], wo_ref[...], NT))
    for query_block in range(rows // BLOCK):
        span = slice(query_block * BLOCK, (query_block + 1) * BLOCK)
        for head in range(heads):
            own = lane_row(width, head, head_dim)
            left_ref[query_block, head * BLOCK : (head + 1) * BLOCK, :] = query[span] * own
            gleft_ref[query_block, head * BLOCK : (head + 1) * BLOCK, :] = grad[span] * own
    steps = key_total // STEP
    peak_ref[...] = jnp.full(peak_ref.shape, 2.0 * NEG, jnp.float32)
    total_ref[...] = jnp.zeros(total_ref.shape, jnp.float32)
    col_peak_ref[...] = jnp.full(col_peak_ref.shape, FLOOR, jnp.float32)
    col_total_ref[...] = jnp.zeros(col_total_ref.shape, jnp.float32)
    col_dot_ref[...] = jnp.zeros(col_dot_ref.shape, jnp.float32)
    tiles = [slice(first, first + 128) for first in range(0, STEP, 128)]

    def peaks(query_block, step, listed):
        block_ref = score_ref.at[query_block * steps + step]
        score_block(query_block, step, listed, left_ref, key_t_ref, block_ref)
        for head, spans in head_strips(heads):
            col_peaks = [col_peak_ref[step, head, :, lanes] for lanes in tiles]
            for span in spans:
                row_peak = peak_ref[query_block, span, :]
                for at, lanes in enumerate(tiles):
                    scores = block_ref[span, lanes]
                    row_peak = jnp.maximum(row_peak, scores)
                    col_peaks[at] = jnp.maximum(col_peaks[at], by_eight(scores).max(axis=0))
                peak_ref[query_block, span, :] = row_peak
            for at, lanes in enumerate(tiles):
                col_peak_ref[step, head, :, lanes] = col_peaks[at]

    each_listed(inter_ref, peaks)
    for query_block in range(rows // BLOCK):
        peak = peak_ref[query_block]
        peak_ref[query_block] = spread(peak.max(axis=1, keepdims=True), peak)
    for step in range(steps):
        for head in range(heads):
            peak = col_peak_ref[step, head]
            col_peak_ref[step, head] = spread(peak.max(axis=0, keepdims=True), peak)

    def totals(query_block, step, listed):
        score_now, product_now = [
            ref.at[query_block * steps + step] for ref in (score_ref, product_ref)
        ]
        span = pl.ds(pl.multiple_of(step * STEP, STEP), STEP)
        prob_ref[...] = mm(gleft_ref[query_block], value_t_ref[:, span])
        for head, spans in head_strips(heads):
            col_totals = [col_total_ref[step, head, :, lanes] for lanes in tiles]
            for span in spans:
                row_peak = by_eight(peak_ref[query_block, span, :])
                row_total = by_eight(total_ref[query_block, span, :])
                for at, lanes in enumerate(tiles):
                    scores = by_eight(score_now[span, lanes])
                    row_exp = jnp.exp2(scores - row_peak)
                    col_exp = jnp.exp2(scores - col_peak_ref[step, head, :, lanes][None])
                    row_total = row_total + row_exp
                    product = row_exp * col_exp * by_eight(prob_ref[span, lanes])
                    product_now[span, lanes] = bf(product.reshape(STRIP, 128))
                    col_totals[at] = col_totals[at] + col_exp.sum(axis=0)
                total_ref[query_block, span, :] = row_total.reshape(STRIP, 128)
            for at, lanes in enumerate(tiles):
                col_total_ref[step, head, :, lanes] = col_totals[at]

    each_listed(inter_ref, totals)
    for query_block in range(rows // BLOCK):
        total = total_ref[query_block]
        inverse_ref[query_block] = spread(1.0 / total.sum(axis=1, keepdims=True), total)

    def dots(query_block, step, listed):
        product_now = product_ref.at[query_block * steps + step]
        for head, spans in head_strips(heads):
            col_dots = [col_dot_ref[step, head, :, lanes] for lanes in tiles]
            for span in spans:
                inverse = inverse_ref[query_block, span, :]
                for at, lanes in enumerate(tiles):
                    product = by_eight(product_now[span, lanes].astype(jnp.float32) * inverse)
                    col_dots[at] = col_dots[at] + product.sum(axis=0)
            for at, lanes in enumerate(tiles):
                col_dot_ref[step, head, :, lanes] = col_dots[at]

    each_listed(inter_ref, dots)
    for step in range(steps):
        lanes = slice(step * STEP, (step + 1) * STEP)
        for head in range(heads):
            mine = slice(head, head + 1)
            col_ref[0, mine, lanes] = col_peak_ref[step, head, 0:1, :]
            col_ref[1, mine, lanes] = col_total_ref[step, head].sum(axis=0, keepdims=True)
            col_ref[2, mine, lanes] = col_dot_ref[step, head].sum(axis=0, keepdims=True)


def side_kernel(
    heads, packed_ref, src_ref, key_ref, value_ref, query_t_ref, grad_t_ref
):
    ref_ref, gout_ref, wq_ref, wk_ref, wv_ref, wo_ref = unpack(packed_ref)
    rows, width = ref_ref.shape
    scale = (width // heads) ** -0.5
    key_ref[...] = bf(mm(src_ref[...], wk_ref[...]))
    value_ref[...] = bf(mm(src_ref[...], wv_ref[...]))
    query_t = bf(mm_general(wq_ref[...], ref_ref[...], TT)).astype(jnp.float32) * (2.0 * scale)
    grad_t = mm_general(wo_ref[...], gout_ref[...], NT)
    for query_block in range(rows // BLOCK):
        span = slice(query_block * BLOCK, (query_block + 1) * BLOCK)
        query_t_ref[query_block] = bf(query_t[:, span])
        grad_t_ref[query_block] = bf(grad_t[:, span])


def grads_kernel(
    heads, inter_ref, score_ref, product_ref, key_ref, value_ref,
    query_t_ref, grad_t_ref, peak_ref, inverse_ref, own_ref, near_ref, far_ref, packed_ref, src_ref,
    attended_ref, gquery_ref, gkey_ref, gvalue_ref, weight_ref,
    rest_ref, match_ref, gscore_ref, dot_ref, col_ref,
    att_ref, gq_ref, gk_ref, gv_ref,
):
    ref_ref, gout_ref = unpack(packed_ref)[:2]
    rows, width = ref_ref.shape
    key_total = src_ref.shape[0]
    steps = key_total // STEP
    head_dim = width // heads
    tiles = [slice(first, first + 128) for first in range(0, STEP, 128)]

    peak = jnp.maximum(near_ref[0], far_ref[0])
    near, far = jnp.exp2(near_ref[0] - peak), jnp.exp2(far_ref[0] - peak)
    inverse = 1.0 / (near * near_ref[1] + far * far_ref[1])
    half = (near * near_ref[2] + far * far_ref[2]) * inverse * 0.5
    factor = jnp.exp2(own_ref[0] - peak) * inverse
    for kind, values in enumerate((peak, inverse, factor, half)):
        for head in range(heads):
            for step in range(steps):
                piece = values[head : head + 1, step * STEP : (step + 1) * STEP]
                col_ref[kind, step, head] = jnp.broadcast_to(piece, (8, STEP))
    for ref in (att_ref, gq_ref, gk_ref, gv_ref):
        ref[...] = jnp.zeros(ref.shape, jnp.float32)

    def products(query_block, step, listed):
        score_now, product_now = [
            ref.at[query_block * steps + step] for ref in (score_ref, product_ref)
        ]
        rest_now, match_now = rest_ref.at[step], match_ref.at[step]
        for head, spans in head_strips(heads):
            for span in spans:
                row_peak = by_eight(peak_ref[query_block, span, :])
                row_inverse = by_eight(inverse_ref[query_block, span, :])
                row_dot = by_eight(dot_ref[span, :])
                for lanes in tiles:
                    col_peak, col_inverse, col_factor, col_half = [
                        col_ref[kind, step, head, :, lanes][None] for kind in range(4)
                    ]
                    scores = by_eight(score_now[span, lanes])
                    row_prob = jnp.exp2(scores - row_peak) * row_inverse
                    col_prob = jnp.exp2(scores - col_peak) * col_inverse
                    product = by_eight(product_now[span, lanes].astype(jnp.float32))
                    product = product * row_inverse * col_factor
                    row_dot = row_dot + product
                    match_now[span, lanes] = bf((row_prob * col_prob).reshape(STRIP, 128))
                    rest_now[span, lanes] = (product - col_prob * col_half).reshape(STRIP, 128)
                dot_ref[span, :] = row_dot.reshape(STRIP, 128)

    def own_lanes(stacked):
        total = None
        for head in range(heads):
            own = lane_row(width, head, head_dim).astype(jnp.float32)
            piece = stacked[head * BLOCK : (head + 1) * BLOCK] * own
            total = piece if total is None else total + piece
        return total

    def outputs(query_block, step, listed):
        score_now, rest_now, match_now = [
            score_ref.at[query_block * steps + step], rest_ref.at[step], match_ref.at[step]
        ]
        for _, spans in head_strips(heads):
            for span in spans:
                row_peak = peak_ref[query_block, span, :]
                row_half = dot_ref[span, :] * inverse_ref[query_block, span, :]
                for lanes in tiles:
                    row_part = jnp.exp2(score_now[span, lanes] - row_peak) * row_half
                    gscore_ref[span, lanes] = bf(rest_now[span, lanes] - row_part)
        span = pl.ds(pl.multiple_of(step * STEP, STEP), STEP)
        att_ref[query_block] += own_lanes(mm(match_now[...], value_ref[span, :]))
        gq_ref[query_block] += own_lanes(mm(gscore_ref[...], key_ref[span, :]))
        for head in range(heads):
            mine = slice(head * head_dim, (head + 1) * head_dim)
            stacked = slice(head * BLOCK, (head + 1) * BLOCK)
            gk_ref[step, mine, :] += mm(query_t_ref[query_block, mine, :], gscore_ref[stacked, :])
            gv_ref[step, mine, :] += mm(grad_t_ref[query_block, mine, :], match_now[stacked, :])

    def query_rows(query_block, carry):
        dot_ref[...] = jnp.zeros(dot_ref.shape, jnp.float32)
        listed_steps(inter_ref, query_block, products)
        dot = dot_ref[...]
        dot_ref[...] = spread(dot.sum(axis=1, keepdims=True) * 0.5, dot)
        listed_steps(inter_ref, query_block, outputs)
        return carry

    lax.fori_loop(0, rows // BLOCK, query_rows, 0)
    attended = bf(att_ref[...]).reshape(rows, width)
    gquery = bf(gq_ref[...] * (2.0 * head_dim ** -0.5)).reshape(rows, width)
    attended_ref[...] = attended
    gquery_ref[...] = gquery
    for step in range(steps):
        gkey_ref[:, step * STEP : (step + 1) * STEP] = bf(gk_ref[step])
        gvalue_ref[:, step * STEP : (step + 1) * STEP] = bf(gv_ref[step])
    weight_ref[0] = bf(mm_general(ref_ref[...], gquery, TN))
    weight_ref[1] = bf(mm(gkey_ref[...], src_ref[...]).T)
    weight_ref[2] = bf(mm(gvalue_ref[...], src_ref[...]).T)
    weight_ref[3] = bf(mm_general(attended, gout_ref[...], TN))


def finish_kernel(
    packed_ref, attended_ref, gquery_ref, gkey_ref, gvalue_ref, matched_ref, gref_ref, gsrc_ref
):
    ref_ref, gout_ref, wq_ref, wk_ref, wv_ref, wo_ref = unpack(packed_ref)
    gsrc_t = mm(wk_ref[...], gkey_ref[...]) + mm(wv_ref[...], gvalue_ref[...])
    gsrc_ref[...] = bf(gsrc_t.T)
    matched = ref_ref[...].astype(jnp.float32) + mm(attended_ref[...], wo_ref[...])
    matched_ref[...] = bf(matched)
    gref = gout_ref[...].astype(jnp.float32) + mm_general(gquery_ref[...], wq_ref[...], NT)
    gref_ref[...] = bf(gref)


def swap(x, axis, apart):
    pairs = [(i, i ^ apart) for i in range(lax.axis_size(axis))]
    return lax.ppermute(x, axis, pairs)


def at(x, index, axis=0):
    return lax.dynamic_index_in_dim(x, index, axis, False)


def laid(near, far, side, axis=0):
    shape = near.shape[:axis] + (2,) + near.shape[axis:]
    out = lax.dynamic_update_index_in_dim(jnp.zeros(shape, near.dtype), near, side, axis)
    return lax.dynamic_update_index_in_dim(out, far, 1 - side, axis)


def add(near, far):
    return (near.astype(jnp.float32) + far.astype(jnp.float32)).astype(near.dtype)


def halve(x, step, axis=0):
    mesh_axis, bit, side = step
    return add(at(x, side, axis), swap(at(x, 1 - side, axis), mesh_axis, bit))


def double(x, step, axis=0):
    mesh_axis, bit, side = step
    return laid(x, swap(x, mesh_axis, bit), side, axis)


def bit_steps(mesh_axis):
    me = lax.axis_index(mesh_axis)
    bits = range(lax.axis_size(mesh_axis).bit_length() - 1)
    return [(mesh_axis, 1 << bit, (me >> bit) % 2) for bit in bits]


def scatter_direct(x, mesh_axis):
    me, count = lax.axis_index(mesh_axis), lax.axis_size(mesh_axis)
    total = at(x, me).astype(jnp.float32)
    for piece in [swap(at(x, me ^ apart), mesh_axis, apart) for apart in range(1, count)]:
        total = total + piece.astype(jnp.float32)
    return total.astype(x.dtype)


def gather_direct(x, mesh_axis):
    me, count = lax.axis_index(mesh_axis), lax.axis_size(mesh_axis)
    pieces = [x] + [swap(x, mesh_axis, apart) for apart in range(1, count)]
    out = jnp.zeros((count,) + x.shape, x.dtype)
    for apart, piece in enumerate(pieces):
        out = lax.dynamic_update_index_in_dim(out, piece, me ^ apart, 0)
    return out


def combine_stats(parts):
    peak = functools.reduce(jnp.maximum, [part[0] for part in parts])
    factors = [jnp.exp2(part[0] - peak) for part in parts]
    total = sum(factor * part[1] for factor, part in zip(factors, parts))
    dots = sum(factor * part[2] for factor, part in zip(factors, parts))
    return jnp.stack([peak, total, dots])


def vmem_call(kernel, name, out_shape, scratch, limit, flops, moved, args, scalars=0):
    specs = [pl.BlockSpec(memory_space=pltpu.SMEM)] * scalars
    specs += [pl.BlockSpec(memory_space=pltpu.VMEM)] * (len(args) - scalars)
    return pl.pallas_call(
        kernel,
        name=name,
        out_shape=out_shape,
        in_specs=specs,
        out_specs=[pl.BlockSpec(memory_space=pltpu.VMEM)] * len(out_shape),
        scratch_shapes=scratch,
        compiler_params=pltpu.CompilerParams(vmem_limit_bytes=limit),
        cost_estimate=pl.CostEstimate(flops=flops, bytes_accessed=moved, transcendentals=0),
    )(*args)


def on_device(ref_feats, src_feats, grad_out, w_query, w_key, w_value, w_out, intersection):
    ref_rows = ref_feats[0]
    src_rows = src_feats[0]
    out_grad = grad_out[0]
    listed = intersection[0]
    rows, width = ref_rows.shape
    core_step = bit_steps("core")[0]
    chip_steps = bit_steps("chip")
    key_rows = src_rows.shape[0]
    key_total = key_rows * lax.axis_size("chip") * lax.axis_size("core")

    packed = jnp.concatenate([ref_rows, out_grad, w_query, w_key, w_value, w_out], axis=0)
    source_all = src_rows
    for count, step in enumerate(chip_steps[::-1]):
        source_all = double(source_all, step, count)
    source_all = double(source_all, core_step, len(chip_steps)).reshape(key_total, width)

    f32, b16 = jnp.float32, jnp.bfloat16
    shape, vmem = jax.ShapeDtypeStruct, pltpu.VMEM
    unit = 2 * rows * width * width
    query_blocks, steps = rows // BLOCK, key_total // STEP
    stacked = HEADS * BLOCK
    blocks = (query_blocks * steps, stacked, STEP)
    row_like = (query_blocks, stacked, 128)
    col_like = vmem((steps, HEADS, 8, STEP), f32)
    room = (16 << 20) + max(0, rows * key_total * HEADS * 10 - (20 << 20))
    row_peak, row_inverse, col_stats, scores, product = vmem_call(
        functools.partial(stats_kernel, HEADS),
        "match_stats",
        [
            shape(row_like, f32),
            shape(row_like, f32),
            shape((3, HEADS, key_total), f32),
            shape(blocks, f32),
            shape(blocks, b16),
        ],
        [
            vmem((query_blocks, stacked, width), b16),
            vmem((query_blocks, stacked, width), b16),
            vmem((width, key_total), b16),
            vmem((width, key_total), b16),
            vmem((stacked, STEP), f32),
            vmem(row_like, f32),
            col_like,
            col_like,
            col_like,
        ],
        room,
        60 * unit,
        8 << 20,
        (listed, packed, source_all),
        scalars=1,
    )
    near_stats = col_stats
    keys, values, query_t, grad_t = vmem_call(
        functools.partial(side_kernel, HEADS),
        "project_for_grads",
        [
            shape((key_total, width), b16),
            shape((key_total, width), b16),
            shape((query_blocks, width, BLOCK), b16),
            shape((query_blocks, width, BLOCK), b16),
        ],
        [],
        8 << 20,
        8 * unit,
        2 << 20,
        (packed, source_all),
    )
    for mesh_axis, bit, _ in chip_steps:
        near_stats = combine_stats([near_stats, swap(near_stats, mesh_axis, bit)])
    far_stats = swap(near_stats, "core", 1)
    attended, grad_query, grad_key, grad_value, weight_part = vmem_call(
        functools.partial(grads_kernel, HEADS),
        "match_grads",
        [
            shape((rows, width), b16),
            shape((rows, width), b16),
            shape((width, key_total), b16),
            shape((width, key_total), b16),
            shape((4, width, width), b16),
        ],
        [
            vmem((steps, stacked, STEP), f32),
            vmem((steps, stacked, STEP), b16),
            vmem((stacked, STEP), b16),
            vmem((stacked, 128), f32),
            vmem((4, steps, HEADS, 8, STEP), f32),
            vmem((query_blocks, BLOCK, width), f32),
            vmem((query_blocks, BLOCK, width), f32),
            vmem((steps, width, STEP), f32),
            vmem((steps, width, STEP), f32),
        ],
        room,
        100 * unit,
        8 << 20,
        (listed, scores, product, keys, values, query_t, grad_t, row_peak, row_inverse, col_stats,
         near_stats, far_stats, packed, source_all),
        scalars=1,
    )
    matched, grad_ref, source_part = vmem_call(
        finish_kernel,
        "finish_rows",
        [
            shape((rows, width), b16),
            shape((rows, width), b16),
            shape((key_total, width), b16),
        ],
        [],
        8 << 20,
        8 * unit,
        2 << 20,
        (packed, attended, grad_query, grad_key, grad_value),
    )

    weights = weight_part.reshape((2, lax.axis_size("scan"), -1, width))
    sources = source_part.reshape((2,) * (len(chip_steps) + 1) + (key_rows, width))
    source_steps = list(zip(chip_steps, range(len(chip_steps) - 1, -1, -1)))
    weights = halve(weights, core_step)
    sources = halve(sources, core_step, len(chip_steps))
    weights = scatter_direct(weights, "scan")
    sources = halve(sources, *source_steps[0])
    weights, sources = lax.optimization_barrier((weights, sources))
    for mesh_axis, bit, _ in chip_steps:
        weights = add(weights, swap(weights, mesh_axis, bit))
    weights, sources = lax.optimization_barrier((weights, sources))
    weights = gather_direct(weights, "scan")
    for step in source_steps[1:]:
        sources = halve(sources, *step)
    grad_src = sources
    weights = double(weights, core_step)
    weights = weights.reshape(4, width, width).astype(f32)
    return (
        matched[None],
        grad_ref[None],
        grad_src[None],
        weights[0],
        weights[1],
        weights[2],
        weights[3],
    )


def solution(mesh):
    scans, blks = mesh.shape["scan"], mesh.shape["blk"]
    mesh = jax.sharding.Mesh(
        mesh.devices.reshape(scans, blks // 2, 2), ("scan", "chip", "core")
    )
    split = P("scan", ("chip", "core"), None)
    whole = P()
    return jax.shard_map(
        on_device,
        mesh=mesh,
        in_specs=(split, split, split, whole, whole, whole, whole, split),
        out_specs=(split, split, split, whole, whole, whole, whole),
        check_vma=False,
    )
```

```python
import functools
import math

import jax
import jax.numpy as jnp
from jax import lax
from jax.experimental import pallas as pl
from jax.experimental.pallas import tpu as pltpu
from jax.sharding import PartitionSpec as P

HEADS = 4
BLOCK = 128
NEG = -1e30
FLOOR = -1e29
LOG2E = math.log2(math.e)

NT = (((1,), (1,)), ((), ()))
TN = (((0,), (0,)), ((), ()))
TT = (((0,), (1,)), ((), ()))


def mm(left, right):
    return jnp.dot(left, right, preferred_element_type=jnp.float32)


def mm_general(left, right, dims):
    return lax.dot_general(left, right, dims, preferred_element_type=jnp.float32)


def bf(x):
    return x.astype(jnp.bfloat16)


def lane_row(width, head, head_dim):
    lanes = lax.broadcasted_iota(jnp.int32, (1, width), 1) // head_dim
    return bf(jnp.where(lanes == head, 1.0, 0.0))


def spread(reduced, like):
    return jnp.broadcast_to(reduced, like.shape)


STRIP = 32
STEP = 256


def by_eight(x):
    return x.reshape(x.shape[0] // 8, 8, x.shape[1])


def listed_steps(inter_ref, query_block, work):
    per_step = STEP // BLOCK

    def visit(step, carry):
        listed = [inter_ref[query_block, step * per_step + k] == 1 for k in range(per_step)]

        @pl.when(functools.reduce(jnp.logical_or, listed))
        def _():
            work(query_block, step, listed)

        return carry

    lax.fori_loop(0, inter_ref.shape[1] // per_step, visit, 0)


def each_listed(inter_ref, work):
    def visit(query_block, carry):
        listed_steps(inter_ref, query_block, work)
        return carry

    lax.fori_loop(0, inter_ref.shape[0], visit, 0)


def head_strips(heads):
    for head in range(heads):
        spans = [slice(first, first + STRIP) for first in range(0, BLOCK, STRIP)]
        yield head, [slice(head * BLOCK + a.start, head * BLOCK + a.stop) for a in spans]


def score_block(query_block, step, listed, left_ref, key_t_ref, score_ref):
    span = pl.ds(pl.multiple_of(step * STEP, STEP), STEP)
    bias = jnp.concatenate(
        [jnp.full((1, BLOCK), jnp.where(flag, 0.0, NEG), jnp.float32) for flag in listed], axis=1
    )
    score_ref[...] = mm(left_ref[query_block], key_t_ref[:, span]) * LOG2E + bias


def unpack(packed_ref):
    total, width = packed_ref.shape
    rows = (total - 4 * width) // 2
    sizes = [rows, rows, width, width, width, width]
    return [packed_ref.at[pl.ds(sum(sizes[:k]), sizes[k])] for k in range(len(sizes))]


def stats_kernel(
    heads, inter_ref, packed_ref, src_ref, peak_ref, inverse_ref, col_ref, score_ref, product_ref,
    left_ref, gleft_ref, key_t_ref, value_t_ref, prob_ref, total_ref,
    col_peak_ref, col_total_ref, col_dot_ref,
):
    ref_ref, gout_ref, wq_ref, wk_ref, wv_ref, wo_ref = unpack(packed_ref)
    rows, width = ref_ref.shape
    key_total = src_ref.shape[0]
    head_dim = width // heads
    key_t_ref[...] = bf(mm_general(wk_ref[...], src_ref[...], TT))
    value_t_ref[...] = bf(mm_general(wv_ref[...], src_ref[...], TT))
    query = bf(bf(mm(ref_ref[...], wq_ref[...])).astype(jnp.float32) * head_dim ** -0.5)
    grad = bf(mm_general(gout_ref[...], wo_ref[...], NT))
    for query_block in range(rows // BLOCK):
        span = slice(query_block * BLOCK, (query_block + 1) * BLOCK)
        for head in range(heads):
            own = lane_row(width, head, head_dim)
            left_ref[query_block, head * BLOCK : (head + 1) * BLOCK, :] = query[span] * own
            gleft_ref[query_block, head * BLOCK : (head + 1) * BLOCK, :] = grad[span] * own
    steps = key_total // STEP
    peak_ref[...] = jnp.full(peak_ref.shape, 2.0 * NEG, jnp.float32)
    total_ref[...] = jnp.zeros(total_ref.shape, jnp.float32)
    col_peak_ref[...] = jnp.full(col_peak_ref.shape, FLOOR, jnp.float32)
    col_total_ref[...] = jnp.zeros(col_total_ref.shape, jnp.float32)
    col_dot_ref[...] = jnp.zeros(col_dot_ref.shape, jnp.float32)
    tiles = [slice(first, first + 128) for first in range(0, STEP, 128)]

    def peaks(query_block, step, listed):
        block_ref = score_ref.at[query_block * steps + step]
        score_block(query_block, step, listed, left_ref, key_t_ref, block_ref)
        for head, spans in head_strips(heads):
            col_peaks = [col_peak_ref[step, head, :, lanes] for lanes in tiles]
            for span in spans:
                row_peak = peak_ref[query_block, span, :]
                for at, lanes in enumerate(tiles):
                    scores = block_ref[span, lanes]
                    row_peak = jnp.maximum(row_peak, scores)
                    col_peaks[at] = jnp.maximum(col_peaks[at], by_eight(scores).max(axis=0))
                peak_ref[query_block, span, :] = row_peak
            for at, lanes in enumerate(tiles):
                col_peak_ref[step, head, :, lanes] = col_peaks[at]

    each_listed(inter_ref, peaks)
    for query_block in range(rows // BLOCK):
        peak = peak_ref[query_block]
        peak_ref[query_block] = spread(peak.max(axis=1, keepdims=True), peak)
    for step in range(steps):
        for head in range(heads):
            peak = col_peak_ref[step, head]
            col_peak_ref[step, head] = spread(peak.max(axis=0, keepdims=True), peak)

    def totals(query_block, step, listed):
        score_now, product_now = [
            ref.at[query_block * steps + step] for ref in (score_ref, product_ref)
        ]
        span = pl.ds(pl.multiple_of(step * STEP, STEP), STEP)
        prob_ref[...] = mm(gleft_ref[query_block], value_t_ref[:, span])
        for head, spans in head_strips(heads):
            col_totals = [col_total_ref[step, head, :, lanes] for lanes in tiles]
            for span in spans:
                row_peak = by_eight(peak_ref[query_block, span, :])
                row_total = by_eight(total_ref[query_block, span, :])
                for at, lanes in enumerate(tiles):
                    scores = by_eight(score_now[span, lanes])
                    row_exp = jnp.exp2(scores - row_peak)
                    col_exp = jnp.exp2(scores - col_peak_ref[step, head, :, lanes][None])
                    row_total = row_total + row_exp
                    product = row_exp * col_exp * by_eight(prob_ref[span, lanes])
                    product_now[span, lanes] = bf(product.reshape(STRIP, 128))
                    col_totals[at] = col_totals[at] + col_exp.sum(axis=0)
                total_ref[query_block, span, :] = row_total.reshape(STRIP, 128)
            for at, lanes in enumerate(tiles):
                col_total_ref[step, head, :, lanes] = col_totals[at]

    each_listed(inter_ref, totals)
    for query_block in range(rows // BLOCK):
        total = total_ref[query_block]
        inverse_ref[query_block] = spread(1.0 / total.sum(axis=1, keepdims=True), total)

    def dots(query_block, step, listed):
        product_now = product_ref.at[query_block * steps + step]
        for head, spans in head_strips(heads):
            col_dots = [col_dot_ref[step, head, :, lanes] for lanes in tiles]
            for span in spans:
                inverse = inverse_ref[query_block, span, :]
                for at, lanes in enumerate(tiles):
                    product = by_eight(product_now[span, lanes].astype(jnp.float32) * inverse)
                    col_dots[at] = col_dots[at] + product.sum(axis=0)
            for at, lanes in enumerate(tiles):
                col_dot_ref[step, head, :, lanes] = col_dots[at]

    each_listed(inter_ref, dots)
    for step in range(steps):
        lanes = slice(step * STEP, (step + 1) * STEP)
        for head in range(heads):
            mine = slice(head, head + 1)
            col_ref[0, mine, lanes] = col_peak_ref[step, head, 0:1, :]
            col_ref[1, mine, lanes] = col_total_ref[step, head].sum(axis=0, keepdims=True)
            col_ref[2, mine, lanes] = col_dot_ref[step, head].sum(axis=0, keepdims=True)


def side_kernel(
    heads, packed_ref, src_ref, key_ref, value_ref, query_t_ref, grad_t_ref
):
    ref_ref, gout_ref, wq_ref, wk_ref, wv_ref, wo_ref = unpack(packed_ref)
    rows, width = ref_ref.shape
    scale = (width // heads) ** -0.5
    key_ref[...] = bf(mm(src_ref[...], wk_ref[...]))
    value_ref[...] = bf(mm(src_ref[...], wv_ref[...]))
    query_t = bf(mm_general(wq_ref[...], ref_ref[...], TT)).astype(jnp.float32) * (2.0 * scale)
    grad_t = mm_general(wo_ref[...], gout_ref[...], NT)
    for query_block in range(rows // BLOCK):
        span = slice(query_block * BLOCK, (query_block + 1) * BLOCK)
        query_t_ref[query_block] = bf(query_t[:, span])
        grad_t_ref[query_block] = bf(grad_t[:, span])


def grads_kernel(
    heads, inter_ref, score_ref, product_ref, key_ref, value_ref,
    query_t_ref, grad_t_ref, peak_ref, inverse_ref, own_ref, near_ref, far_ref, packed_ref, src_ref,
    attended_ref, gquery_ref, gkey_ref, gvalue_ref, weight_ref,
    rest_ref, match_ref, gscore_ref, dot_ref, col_ref,
    att_ref, gq_ref, gk_ref, gv_ref,
):
    ref_ref, gout_ref = unpack(packed_ref)[:2]
    rows, width = ref_ref.shape
    key_total = src_ref.shape[0]
    steps = key_total // STEP
    head_dim = width // heads
    tiles = [slice(first, first + 128) for first in range(0, STEP, 128)]

    peak = jnp.maximum(near_ref[0], far_ref[0])
    near, far = jnp.exp2(near_ref[0] - peak), jnp.exp2(far_ref[0] - peak)
    inverse = 1.0 / (near * near_ref[1] + far * far_ref[1])
    half = (near * near_ref[2] + far * far_ref[2]) * inverse * 0.5
    factor = jnp.exp2(own_ref[0] - peak) * inverse
    for kind, values in enumerate((peak, inverse, factor, half)):
        for head in range(heads):
            for step in range(steps):
                piece = values[head : head + 1, step * STEP : (step + 1) * STEP]
                col_ref[kind, step, head] = jnp.broadcast_to(piece, (8, STEP))
    for ref in (att_ref, gq_ref, gk_ref, gv_ref):
        ref[...] = jnp.zeros(ref.shape, jnp.float32)

    def products(query_block, step, listed):
        score_now, product_now = [
            ref.at[query_block * steps + step] for ref in (score_ref, product_ref)
        ]
        rest_now, match_now = rest_ref.at[step], match_ref.at[step]
        for head, spans in head_strips(heads):
            for span in spans:
                row_peak = by_eight(peak_ref[query_block, span, :])
                row_inverse = by_eight(inverse_ref[query_block, span, :])
                row_dot = by_eight(dot_ref[span, :])
                for lanes in tiles:
                    col_peak, col_inverse, col_factor, col_half = [
                        col_ref[kind, step, head, :, lanes][None] for kind in range(4)
                    ]
                    scores = by_eight(score_now[span, lanes])
                    row_prob = jnp.exp2(scores - row_peak) * row_inverse
                    col_prob = jnp.exp2(scores - col_peak) * col_inverse
                    product = by_eight(product_now[span, lanes].astype(jnp.float32))
                    product = product * row_inverse * col_factor
                    row_dot = row_dot + product
                    match_now[span, lanes] = bf((row_prob * col_prob).reshape(STRIP, 128))
                    rest_now[span, lanes] = (product - col_prob * col_half).reshape(STRIP, 128)
                dot_ref[span, :] = row_dot.reshape(STRIP, 128)

    def own_lanes(stacked):
        total = None
        for head in range(heads):
            own = lane_row(width, head, head_dim).astype(jnp.float32)
            piece = stacked[head * BLOCK : (head + 1) * BLOCK] * own
            total = piece if total is None else total + piece
        return total

    def outputs(query_block, step, listed):
        score_now, rest_now, match_now = [
            score_ref.at[query_block * steps + step], rest_ref.at[step], match_ref.at[step]
        ]
        for _, spans in head_strips(heads):
            for span in spans:
                row_peak = peak_ref[query_block, span, :]
                row_half = dot_ref[span, :] * inverse_ref[query_block, span, :]
                for lanes in tiles:
                    row_part = jnp.exp2(score_now[span, lanes] - row_peak) * row_half
                    gscore_ref[span, lanes] = bf(rest_now[span, lanes] - row_part)
        span = pl.ds(pl.multiple_of(step * STEP, STEP), STEP)
        att_ref[query_block] += own_lanes(mm(match_now[...], value_ref[span, :]))
        gq_ref[query_block] += own_lanes(mm(gscore_ref[...], key_ref[span, :]))
        for head in range(heads):
            mine = slice(head * head_dim, (head + 1) * head_dim)
            stacked = slice(head * BLOCK, (head + 1) * BLOCK)
            gk_ref[step, mine, :] += mm(query_t_ref[query_block, mine, :], gscore_ref[stacked, :])
            gv_ref[step, mine, :] += mm(grad_t_ref[query_block, mine, :], match_now[stacked, :])

    def query_rows(query_block, carry):
        dot_ref[...] = jnp.zeros(dot_ref.shape, jnp.float32)
        listed_steps(inter_ref, query_block, products)
        dot = dot_ref[...]
        dot_ref[...] = spread(dot.sum(axis=1, keepdims=True) * 0.5, dot)
        listed_steps(inter_ref, query_block, outputs)
        return carry

    lax.fori_loop(0, rows // BLOCK, query_rows, 0)
    attended = bf(att_ref[...]).reshape(rows, width)
    gquery = bf(gq_ref[...] * (2.0 * head_dim ** -0.5)).reshape(rows, width)
    attended_ref[...] = attended
    gquery_ref[...] = gquery
    for step in range(steps):
        gkey_ref[:, step * STEP : (step + 1) * STEP] = bf(gk_ref[step])
        gvalue_ref[:, step * STEP : (step + 1) * STEP] = bf(gv_ref[step])
    weight_ref[0] = bf(mm_general(ref_ref[...], gquery, TN))
    weight_ref[1] = bf(mm(gkey_ref[...], src_ref[...]).T)
    weight_ref[2] = bf(mm(gvalue_ref[...], src_ref[...]).T)
    weight_ref[3] = bf(mm_general(attended, gout_ref[...], TN))


def finish_kernel(
    packed_ref, attended_ref, gquery_ref, gkey_ref, gvalue_ref, matched_ref, gref_ref, gsrc_ref
):
    ref_ref, gout_ref, wq_ref, wk_ref, wv_ref, wo_ref = unpack(packed_ref)
    gsrc_t = mm(wk_ref[...], gkey_ref[...]) + mm(wv_ref[...], gvalue_ref[...])
    gsrc_ref[...] = bf(gsrc_t.T)
    matched = ref_ref[...].astype(jnp.float32) + mm(attended_ref[...], wo_ref[...])
    matched_ref[...] = bf(matched)
    gref = gout_ref[...].astype(jnp.float32) + mm_general(gquery_ref[...], wq_ref[...], NT)
    gref_ref[...] = bf(gref)


def swap(x, axis, apart):
    pairs = [(i, i ^ apart) for i in range(lax.axis_size(axis))]
    return lax.ppermute(x, axis, pairs)


def at(x, index, axis=0):
    return lax.dynamic_index_in_dim(x, index, axis, False)


def laid(near, far, side, axis=0):
    shape = near.shape[:axis] + (2,) + near.shape[axis:]
    out = lax.dynamic_update_index_in_dim(jnp.zeros(shape, near.dtype), near, side, axis)
    return lax.dynamic_update_index_in_dim(out, far, 1 - side, axis)


def add(near, far):
    return (near.astype(jnp.float32) + far.astype(jnp.float32)).astype(near.dtype)


def halve(x, step, axis=0):
    mesh_axis, bit, side = step
    return add(at(x, side, axis), swap(at(x, 1 - side, axis), mesh_axis, bit))


def double(x, step, axis=0):
    mesh_axis, bit, side = step
    return laid(x, swap(x, mesh_axis, bit), side, axis)


def bit_steps(mesh_axis):
    me = lax.axis_index(mesh_axis)
    bits = range(lax.axis_size(mesh_axis).bit_length() - 1)
    return [(mesh_axis, 1 << bit, (me >> bit) % 2) for bit in bits]


def scatter_direct(x, mesh_axis):
    me, count = lax.axis_index(mesh_axis), lax.axis_size(mesh_axis)
    total = at(x, me).astype(jnp.float32)
    for piece in [swap(at(x, me ^ apart), mesh_axis, apart) for apart in range(1, count)]:
        total = total + piece.astype(jnp.float32)
    return total.astype(x.dtype)


def gather_direct(x, mesh_axis):
    me, count = lax.axis_index(mesh_axis), lax.axis_size(mesh_axis)
    pieces = [x] + [swap(x, mesh_axis, apart) for apart in range(1, count)]
    out = jnp.zeros((count,) + x.shape, x.dtype)
    for apart, piece in enumerate(pieces):
        out = lax.dynamic_update_index_in_dim(out, piece, me ^ apart, 0)
    return out


def combine_stats(parts):
    peak = functools.reduce(jnp.maximum, [part[0] for part in parts])
    factors = [jnp.exp2(part[0] - peak) for part in parts]
    total = sum(factor * part[1] for factor, part in zip(factors, parts))
    dots = sum(factor * part[2] for factor, part in zip(factors, parts))
    return jnp.stack([peak, total, dots])


def vmem_call(kernel, name, out_shape, scratch, limit, flops, moved, args, scalars=0):
    specs = [pl.BlockSpec(memory_space=pltpu.SMEM)] * scalars
    specs += [pl.BlockSpec(memory_space=pltpu.VMEM)] * (len(args) - scalars)
    return pl.pallas_call(
        kernel,
        name=name,
        out_shape=out_shape,
        in_specs=specs,
        out_specs=[pl.BlockSpec(memory_space=pltpu.VMEM)] * len(out_shape),
        scratch_shapes=scratch,
        compiler_params=pltpu.CompilerParams(vmem_limit_bytes=limit),
        cost_estimate=pl.CostEstimate(flops=flops, bytes_accessed=moved, transcendentals=0),
    )(*args)


def on_device(ref_feats, src_feats, grad_out, w_query, w_key, w_value, w_out, intersection):
    ref_rows = ref_feats[0]
    src_rows = src_feats[0]
    out_grad = grad_out[0]
    listed = intersection[0]
    rows, width = ref_rows.shape
    core_step = bit_steps("core")[0]
    chip_steps = bit_steps("chip")
    key_rows = src_rows.shape[0]
    key_total = key_rows * lax.axis_size("chip") * lax.axis_size("core")

    source_all = src_rows
    projections = (w_query, w_key, w_value, w_out)
    for count, step in enumerate(chip_steps[::-1]):
        source_all = double(source_all, step, count)
        if count == 0:
            source_all, projections = lax.optimization_barrier((source_all, projections))
    packed = jnp.concatenate([ref_rows, out_grad, *projections], axis=0)
    source_all = double(source_all, core_step, len(chip_steps)).reshape(key_total, width)

    f32, b16 = jnp.float32, jnp.bfloat16
    shape, vmem = jax.ShapeDtypeStruct, pltpu.VMEM
    unit = 2 * rows * width * width
    query_blocks, steps = rows // BLOCK, key_total // STEP
    stacked = HEADS * BLOCK
    blocks = (query_blocks * steps, stacked, STEP)
    row_like = (query_blocks, stacked, 128)
    col_like = vmem((steps, HEADS, 8, STEP), f32)
    room = (16 << 20) + max(0, rows * key_total * HEADS * 10 - (20 << 20))
    row_peak, row_inverse, col_stats, scores, product = vmem_call(
        functools.partial(stats_kernel, HEADS),
        "match_stats",
        [
            shape(row_like, f32),
            shape(row_like, f32),
            shape((3, HEADS, key_total), f32),
            shape(blocks, f32),
            shape(blocks, b16),
        ],
        [
            vmem((query_blocks, stacked, width), b16),
            vmem((query_blocks, stacked, width), b16),
            vmem((width, key_total), b16),
            vmem((width, key_total), b16),
            vmem((stacked, STEP), f32),
            vmem(row_like, f32),
            col_like,
            col_like,
            col_like,
        ],
        room,
        60 * unit,
        8 << 20,
        (listed, packed, source_all),
        scalars=1,
    )
    near_stats = col_stats
    keys, values, query_t, grad_t = vmem_call(
        functools.partial(side_kernel, HEADS),
        "project_for_grads",
        [
            shape((key_total, width), b16),
            shape((key_total, width), b16),
            shape((query_blocks, width, BLOCK), b16),
            shape((query_blocks, width, BLOCK), b16),
        ],
        [],
        8 << 20,
        8 * unit,
        2 << 20,
        (packed, source_all),
    )
    for mesh_axis, bit, _ in chip_steps:
        near_stats = combine_stats([near_stats, swap(near_stats, mesh_axis, bit)])
    far_stats = swap(near_stats, "core", 1)
    attended, grad_query, grad_key, grad_value, weight_part = vmem_call(
        functools.partial(grads_kernel, HEADS),
        "match_grads",
        [
            shape((rows, width), b16),
            shape((rows, width), b16),
            shape((width, key_total), b16),
            shape((width, key_total), b16),
            shape((4, width, width), b16),
        ],
        [
            vmem((steps, stacked, STEP), f32),
            vmem((steps, stacked, STEP), b16),
            vmem((stacked, STEP), b16),
            vmem((stacked, 128), f32),
            vmem((4, steps, HEADS, 8, STEP), f32),
            vmem((query_blocks, BLOCK, width), f32),
            vmem((query_blocks, BLOCK, width), f32),
            vmem((steps, width, STEP), f32),
            vmem((steps, width, STEP), f32),
        ],
        room,
        100 * unit,
        8 << 20,
        (listed, scores, product, keys, values, query_t, grad_t, row_peak, row_inverse, col_stats,
         near_stats, far_stats, packed, source_all),
        scalars=1,
    )
    matched, grad_ref, source_part = vmem_call(
        finish_kernel,
        "finish_rows",
        [
            shape((rows, width), b16),
            shape((rows, width), b16),
            shape((key_total, width), b16),
        ],
        [],
        8 << 20,
        8 * unit,
        2 << 20,
        (packed, attended, grad_query, grad_key, grad_value),
    )

    scans = lax.axis_size("scan")
    weights = weight_part.reshape((2, scans // 2, 2, -1, width))
    sources = source_part.reshape((2,) * (len(chip_steps) + 1) + (key_rows, width))
    source_steps = list(zip(chip_steps, range(len(chip_steps) - 1, -1, -1)))
    weights = halve(weights, core_step)
    sources = halve(sources, core_step, len(chip_steps))
    weights, sources = lax.optimization_barrier((weights, sources))
    weights = scatter_direct(weights.reshape((scans,) + weights.shape[2:]), "scan")
    sources = halve(sources, *source_steps[0])
    weights, sources = lax.optimization_barrier((weights, sources))
    for step in source_steps[1:]:
        sources = halve(sources, *step)
    for mesh_axis, bit, _ in chip_steps:
        weights = add(weights, swap(weights, mesh_axis, bit))
    weights, grad_src = lax.optimization_barrier((weights, sources))
    weights = gather_direct(weights, "scan")
    weights = double(weights, core_step)
    weights = weights.reshape(4, width, width).astype(f32)
    return (
        matched[None],
        grad_ref[None],
        grad_src[None],
        weights[0],
        weights[1],
        weights[2],
        weights[3],
    )


def solution(mesh):
    scans, blks = mesh.shape["scan"], mesh.shape["blk"]
    mesh = jax.sharding.Mesh(
        mesh.devices.reshape(scans, blks // 2, 2), ("scan", "chip", "core")
    )
    split = P("scan", ("chip", "core"), None)
    whole = P()
    return jax.shard_map(
        on_device,
        mesh=mesh,
        in_specs=(split, split, split, whole, whole, whole, whole, split),
        out_specs=(split, split, split, whole, whole, whole, whole),
        check_vma=False,
    )
```

```python
import functools
import math

import jax
import jax.numpy as jnp
from jax import lax
from jax.experimental import pallas as pl
from jax.experimental.pallas import tpu as pltpu
from jax.sharding import PartitionSpec as P

HEADS = 4
BLOCK = 128
NEG = -1e30
FLOOR = -1e29
LOG2E = math.log2(math.e)

NT = (((1,), (1,)), ((), ()))
TN = (((0,), (0,)), ((), ()))
TT = (((0,), (1,)), ((), ()))


def mm(left, right):
    return jnp.dot(left, right, preferred_element_type=jnp.float32)


def mm_general(left, right, dims):
    return lax.dot_general(left, right, dims, preferred_element_type=jnp.float32)


def bf(x):
    return x.astype(jnp.bfloat16)


def lane_row(width, head, head_dim):
    lanes = lax.broadcasted_iota(jnp.int32, (1, width), 1) // head_dim
    return bf(jnp.where(lanes == head, 1.0, 0.0))


def spread(reduced, like):
    return jnp.broadcast_to(reduced, like.shape)


STRIP = 32
STEP = 256


def by_eight(x):
    return x.reshape(x.shape[0] // 8, 8, x.shape[1])


def listed_steps(inter_ref, query_block, work):
    per_step = STEP // BLOCK

    def visit(step, carry):
        listed = [inter_ref[query_block, step * per_step + k] == 1 for k in range(per_step)]

        @pl.when(functools.reduce(jnp.logical_or, listed))
        def _():
            work(query_block, step, listed)

        return carry

    lax.fori_loop(0, inter_ref.shape[1] // per_step, visit, 0)


def each_listed(inter_ref, work):
    def visit(query_block, carry):
        listed_steps(inter_ref, query_block, work)
        return carry

    lax.fori_loop(0, inter_ref.shape[0], visit, 0)


def head_strips(heads):
    for head in range(heads):
        spans = [slice(first, first + STRIP) for first in range(0, BLOCK, STRIP)]
        yield head, [slice(head * BLOCK + a.start, head * BLOCK + a.stop) for a in spans]


def side_by_side(head, lanes):
    return slice(head * STEP + lanes.start, head * STEP + lanes.stop)


def score_block(query_block, step, listed, left_ref, key_t_ref, score_ref):
    span = pl.ds(pl.multiple_of(step * STEP, STEP), STEP)
    bias = jnp.concatenate(
        [jnp.full((1, BLOCK), jnp.where(flag, 0.0, NEG), jnp.float32) for flag in listed], axis=1
    )
    score_ref[...] = mm(left_ref[query_block], key_t_ref[:, span]) * LOG2E + bias


def unpack(packed_ref, count):
    total, width = packed_ref.shape
    rows = (total - 2 * width) // 2
    sizes = [rows] * (count - 2) + [width, width]
    return [packed_ref.at[pl.ds(sum(sizes[:k]), sizes[k])] for k in range(count)]


def project_kernel(heads, near_ref, left_ref, gleft_ref):
    ref_ref, gout_ref, wq_ref, wo_ref = unpack(near_ref, 4)
    rows, width = ref_ref.shape
    head_dim = width // heads
    query = bf(bf(mm(ref_ref[...], wq_ref[...])).astype(jnp.float32) * head_dim ** -0.5)
    grad = bf(mm_general(gout_ref[...], wo_ref[...], NT))
    for query_block in range(rows // BLOCK):
        span = slice(query_block * BLOCK, (query_block + 1) * BLOCK)
        for head in range(heads):
            own = lane_row(width, head, head_dim)
            left_ref[query_block, head * BLOCK : (head + 1) * BLOCK, :] = query[span] * own
            gleft_ref[query_block, head * BLOCK : (head + 1) * BLOCK, :] = grad[span] * own


def stats_kernel(
    heads, inter_ref, left_ref, gleft_ref, far_ref, src_ref,
    peak_ref, inverse_ref, col_ref, score_ref, product_ref,
    key_t_ref, value_t_ref, prob_ref, total_ref, col_peak_ref, col_total_ref, col_dot_ref,
):
    wk_ref, wv_ref = unpack(far_ref, 2)
    rows, key_total = left_ref.shape[0] * BLOCK, src_ref.shape[0]
    key_t_ref[...] = bf(mm_general(wk_ref[...], src_ref[...], TT))
    value_t_ref[...] = bf(mm_general(wv_ref[...], src_ref[...], TT))
    steps = key_total // STEP
    peak_ref[...] = jnp.full(peak_ref.shape, 2.0 * NEG, jnp.float32)
    total_ref[...] = jnp.zeros(total_ref.shape, jnp.float32)
    col_peak_ref[...] = jnp.full(col_peak_ref.shape, FLOOR, jnp.float32)
    col_total_ref[...] = jnp.zeros(col_total_ref.shape, jnp.float32)
    col_dot_ref[...] = jnp.zeros(col_dot_ref.shape, jnp.float32)
    tiles = [slice(first, first + 128) for first in range(0, STEP, 128)]

    def peaks(query_block, step, listed):
        block_ref = score_ref.at[query_block * steps + step]
        score_block(query_block, step, listed, left_ref, key_t_ref, block_ref)
        for head, spans in head_strips(heads):
            col_peaks = [col_peak_ref[step, head, :, lanes] for lanes in tiles]
            for span in spans:
                row_peak = peak_ref[query_block, span, :]
                for at, lanes in enumerate(tiles):
                    scores = block_ref[span, lanes]
                    row_peak = jnp.maximum(row_peak, scores)
                    col_peaks[at] = jnp.maximum(col_peaks[at], by_eight(scores).max(axis=0))
                peak_ref[query_block, span, :] = row_peak
            for at, lanes in enumerate(tiles):
                col_peak_ref[step, head, :, lanes] = col_peaks[at]

    each_listed(inter_ref, peaks)
    for query_block in range(rows // BLOCK):
        peak = peak_ref[query_block]
        peak_ref[query_block] = spread(peak.max(axis=1, keepdims=True), peak)
    for step in range(steps):
        for head in range(heads):
            peak = col_peak_ref[step, head]
            col_peak_ref[step, head] = spread(peak.max(axis=0, keepdims=True), peak)

    def totals(query_block, step, listed):
        score_now, product_now = [
            ref.at[query_block * steps + step] for ref in (score_ref, product_ref)
        ]
        span = pl.ds(pl.multiple_of(step * STEP, STEP), STEP)
        prob_ref[...] = mm(gleft_ref[query_block], value_t_ref[:, span])
        for head, spans in head_strips(heads):
            col_totals = [col_total_ref[step, head, :, lanes] for lanes in tiles]
            for span in spans:
                row_peak = by_eight(peak_ref[query_block, span, :])
                row_total = by_eight(total_ref[query_block, span, :])
                for at, lanes in enumerate(tiles):
                    scores = by_eight(score_now[span, lanes])
                    row_exp = jnp.exp2(scores - row_peak)
                    col_exp = jnp.exp2(scores - col_peak_ref[step, head, :, lanes][None])
                    row_total = row_total + row_exp
                    product = row_exp * col_exp * by_eight(prob_ref[span, lanes])
                    product_now[span, lanes] = bf(product.reshape(STRIP, 128))
                    col_totals[at] = col_totals[at] + col_exp.sum(axis=0)
                total_ref[query_block, span, :] = row_total.reshape(STRIP, 128)
            for at, lanes in enumerate(tiles):
                col_total_ref[step, head, :, lanes] = col_totals[at]

    each_listed(inter_ref, totals)
    for query_block in range(rows // BLOCK):
        total = total_ref[query_block]
        inverse_ref[query_block] = spread(1.0 / total.sum(axis=1, keepdims=True), total)

    def dots(query_block, step, listed):
        product_now = product_ref.at[query_block * steps + step]
        for head, spans in head_strips(heads):
            col_dots = [col_dot_ref[step, head, :, lanes] for lanes in tiles]
            for span in spans:
                inverse = inverse_ref[query_block, span, :]
                for at, lanes in enumerate(tiles):
                    product = by_eight(product_now[span, lanes].astype(jnp.float32) * inverse)
                    col_dots[at] = col_dots[at] + product.sum(axis=0)
            for at, lanes in enumerate(tiles):
                col_dot_ref[step, head, :, lanes] = col_dots[at]

    each_listed(inter_ref, dots)
    for step in range(steps):
        lanes = slice(step * STEP, (step + 1) * STEP)
        for head in range(heads):
            mine = slice(head, head + 1)
            col_ref[0, mine, lanes] = col_peak_ref[step, head, 0:1, :]
            col_ref[1, mine, lanes] = col_total_ref[step, head].sum(axis=0, keepdims=True)
            col_ref[2, mine, lanes] = col_dot_ref[step, head].sum(axis=0, keepdims=True)


def side_kernel(
    heads, near_ref, far_ref, src_ref, key_ref, value_ref, query_t_ref, grad_t_ref
):
    ref_ref, gout_ref, wq_ref, wo_ref = unpack(near_ref, 4)
    wk_ref, wv_ref = unpack(far_ref, 2)
    rows, width = ref_ref.shape
    head_dim = width // heads
    for w_ref, out_ref in ((wk_ref, key_ref), (wv_ref, value_ref)):
        for step in range(src_ref.shape[0] // STEP):
            piece = bf(mm(src_ref[step * STEP : (step + 1) * STEP, :], w_ref[...]))
            for head in range(heads):
                own = lane_row(width, head, head_dim)
                out_ref[step, head * STEP : (head + 1) * STEP, :] = piece * own
    query_t = bf(mm_general(wq_ref[...], ref_ref[...], TT)).astype(jnp.float32)
    query_t = query_t * (2.0 * head_dim ** -0.5)
    grad_t = mm_general(wo_ref[...], gout_ref[...], NT)
    for query_block in range(rows // BLOCK):
        span = slice(query_block * BLOCK, (query_block + 1) * BLOCK)
        query_t_ref[query_block] = bf(query_t[:, span])
        grad_t_ref[query_block] = bf(grad_t[:, span])


def grads_kernel(
    heads, inter_ref, score_ref, product_ref, key_ref, value_ref,
    query_t_ref, grad_t_ref, peak_ref, inverse_ref, own_ref, near_ref, far_ref, packed_ref, src_ref,
    attended_ref, gquery_ref, gkey_ref, gvalue_ref, weight_ref,
    rest_ref, match_ref, gscore_ref, dot_ref, col_ref,
    att_ref, gq_ref, gk_ref, gv_ref,
):
    ref_ref, gout_ref = unpack(packed_ref, 4)[:2]
    rows, width = ref_ref.shape
    key_total = src_ref.shape[0]
    steps = key_total // STEP
    head_dim = width // heads
    tiles = [slice(first, first + 128) for first in range(0, STEP, 128)]

    peak = jnp.maximum(near_ref[0], far_ref[0])
    near, far = jnp.exp2(near_ref[0] - peak), jnp.exp2(far_ref[0] - peak)
    inverse = 1.0 / (near * near_ref[1] + far * far_ref[1])
    half = (near * near_ref[2] + far * far_ref[2]) * inverse * 0.5
    factor = jnp.exp2(own_ref[0] - peak) * inverse
    for kind, values in enumerate((peak, inverse, factor, half)):
        for head in range(heads):
            for step in range(steps):
                piece = values[head : head + 1, step * STEP : (step + 1) * STEP]
                col_ref[kind, step, head] = jnp.broadcast_to(piece, (8, STEP))
    for ref in (att_ref, gq_ref, gk_ref, gv_ref):
        ref[...] = jnp.zeros(ref.shape, jnp.float32)

    def products(query_block, step, listed):
        score_now, product_now = [
            ref.at[query_block * steps + step] for ref in (score_ref, product_ref)
        ]
        rest_now, match_now = rest_ref.at[step], match_ref.at[step]
        for head, spans in head_strips(heads):
            for span in spans:
                near_rows = slice(span.start - head * BLOCK, span.stop - head * BLOCK)
                row_peak = by_eight(peak_ref[query_block, span, :])
                row_inverse = by_eight(inverse_ref[query_block, span, :])
                row_dot = by_eight(dot_ref[span, :])
                for lanes in tiles:
                    col_peak, col_inverse, col_factor, col_half = [
                        col_ref[kind, step, head, :, lanes][None] for kind in range(4)
                    ]
                    scores = by_eight(score_now[span, lanes])
                    row_prob = jnp.exp2(scores - row_peak) * row_inverse
                    col_prob = jnp.exp2(scores - col_peak) * col_inverse
                    product = by_eight(product_now[span, lanes].astype(jnp.float32))
                    product = product * row_inverse * col_factor
                    row_dot = row_dot + product
                    match = bf((row_prob * col_prob).reshape(STRIP, 128))
                    match_now[near_rows, side_by_side(head, lanes)] = match
                    rest_now[span, lanes] = (product - col_prob * col_half).reshape(STRIP, 128)
                dot_ref[span, :] = row_dot.reshape(STRIP, 128)

    def outputs(query_block, step, listed):
        score_now, rest_now, match_now = [
            score_ref.at[query_block * steps + step], rest_ref.at[step], match_ref.at[step]
        ]
        for head, spans in head_strips(heads):
            for span in spans:
                near_rows = slice(span.start - head * BLOCK, span.stop - head * BLOCK)
                row_peak = peak_ref[query_block, span, :]
                row_half = dot_ref[span, :] * inverse_ref[query_block, span, :]
                for lanes in tiles:
                    row_part = jnp.exp2(score_now[span, lanes] - row_peak) * row_half
                    grads = bf(rest_now[span, lanes] - row_part)
                    gscore_ref[near_rows, side_by_side(head, lanes)] = grads
        att_ref[query_block] += mm(match_now[...], value_ref[step])
        gq_ref[query_block] += mm(gscore_ref[...], key_ref[step])
        for head in range(heads):
            mine = slice(head * head_dim, (head + 1) * head_dim)
            lanes = slice(head * STEP, (head + 1) * STEP)
            gk_ref[step, mine, :] += mm(query_t_ref[query_block, mine, :], gscore_ref[:, lanes])
            gv_ref[step, mine, :] += mm(grad_t_ref[query_block, mine, :], match_now[:, lanes])

    def query_rows(query_block, carry):
        dot_ref[...] = jnp.zeros(dot_ref.shape, jnp.float32)
        listed_steps(inter_ref, query_block, products)
        dot = dot_ref[...]
        dot_ref[...] = spread(dot.sum(axis=1, keepdims=True) * 0.5, dot)
        listed_steps(inter_ref, query_block, outputs)
        return carry

    lax.fori_loop(0, rows // BLOCK, query_rows, 0)
    attended = bf(att_ref[...]).reshape(rows, width)
    gquery = bf(gq_ref[...] * (2.0 * head_dim ** -0.5)).reshape(rows, width)
    attended_ref[...] = attended
    gquery_ref[...] = gquery
    for step in range(steps):
        gkey_ref[:, step * STEP : (step + 1) * STEP] = bf(gk_ref[step])
        gvalue_ref[:, step * STEP : (step + 1) * STEP] = bf(gv_ref[step])
    weight_ref[0] = bf(mm_general(ref_ref[...], gquery, TN))
    weight_ref[1] = bf(mm(gkey_ref[...], src_ref[...]).T)
    weight_ref[2] = bf(mm(gvalue_ref[...], src_ref[...]).T)
    weight_ref[3] = bf(mm_general(attended, gout_ref[...], TN))


def source_kernel(far_ref, gkey_ref, gvalue_ref, gsrc_ref):
    wk_ref, wv_ref = unpack(far_ref, 2)
    gsrc_t = mm(wk_ref[...], gkey_ref[...]) + mm(wv_ref[...], gvalue_ref[...])
    gsrc_ref[...] = bf(gsrc_t.T)


def rows_kernel(near_ref, attended_ref, gquery_ref, matched_ref, gref_ref):
    ref_ref, gout_ref, wq_ref, wo_ref = unpack(near_ref, 4)
    matched = ref_ref[...].astype(jnp.float32) + mm(attended_ref[...], wo_ref[...])
    matched_ref[...] = bf(matched)
    gref = gout_ref[...].astype(jnp.float32) + mm_general(gquery_ref[...], wq_ref[...], NT)
    gref_ref[...] = bf(gref)


def swap(x, axis, apart):
    pairs = [(i, i ^ apart) for i in range(lax.axis_size(axis))]
    return lax.ppermute(x, axis, pairs)


def at(x, index, axis=0):
    return lax.dynamic_index_in_dim(x, index, axis, False)


def laid(near, far, side, axis=0):
    shape = near.shape[:axis] + (2,) + near.shape[axis:]
    out = lax.dynamic_update_index_in_dim(jnp.zeros(shape, near.dtype), near, side, axis)
    return lax.dynamic_update_index_in_dim(out, far, 1 - side, axis)


def add(near, far):
    return (near.astype(jnp.float32) + far.astype(jnp.float32)).astype(near.dtype)


def halve(x, step, axis=0):
    mesh_axis, bit, side = step
    return add(at(x, side, axis), swap(at(x, 1 - side, axis), mesh_axis, bit))


def double(x, step, axis=0):
    mesh_axis, bit, side = step
    return laid(x, swap(x, mesh_axis, bit), side, axis)


def bit_steps(mesh_axis):
    me = lax.axis_index(mesh_axis)
    bits = range(lax.axis_size(mesh_axis).bit_length() - 1)
    return [(mesh_axis, 1 << bit, (me >> bit) % 2) for bit in bits]


def scatter_direct(x, mesh_axis):
    me, count = lax.axis_index(mesh_axis), lax.axis_size(mesh_axis)
    total = at(x, me).astype(jnp.float32)
    for piece in [swap(at(x, me ^ apart), mesh_axis, apart) for apart in range(1, count)]:
        total = total + piece.astype(jnp.float32)
    return total.astype(x.dtype)


def gather_direct(x, mesh_axis):
    me, count = lax.axis_index(mesh_axis), lax.axis_size(mesh_axis)
    pieces = [x] + [swap(x, mesh_axis, apart) for apart in range(1, count)]
    out = jnp.zeros((count,) + x.shape, x.dtype)
    for apart, piece in enumerate(pieces):
        out = lax.dynamic_update_index_in_dim(out, piece, me ^ apart, 0)
    return out


def combine_stats(parts):
    peak = functools.reduce(jnp.maximum, [part[0] for part in parts])
    factors = [jnp.exp2(part[0] - peak) for part in parts]
    total = sum(factor * part[1] for factor, part in zip(factors, parts))
    dots = sum(factor * part[2] for factor, part in zip(factors, parts))
    return jnp.stack([peak, total, dots])


def vmem_call(kernel, name, out_shape, scratch, limit, flops, moved, args, scalars=0):
    specs = [pl.BlockSpec(memory_space=pltpu.SMEM)] * scalars
    specs += [pl.BlockSpec(memory_space=pltpu.VMEM)] * (len(args) - scalars)
    return pl.pallas_call(
        kernel,
        name=name,
        out_shape=out_shape,
        in_specs=specs,
        out_specs=[pl.BlockSpec(memory_space=pltpu.VMEM)] * len(out_shape),
        scratch_shapes=scratch,
        compiler_params=pltpu.CompilerParams(vmem_limit_bytes=limit),
        cost_estimate=pl.CostEstimate(flops=flops, bytes_accessed=moved, transcendentals=0),
    )(*args)


def on_device(ref_feats, src_feats, grad_out, w_query, w_key, w_value, w_out, intersection):
    ref_rows = ref_feats[0]
    src_rows = src_feats[0]
    out_grad = grad_out[0]
    listed = jnp.where(intersection[0] == 1, 1, 0)
    rows, width = ref_rows.shape
    core_step = bit_steps("core")[0]
    chip_steps = bit_steps("chip")
    key_rows = src_rows.shape[0]
    key_total = key_rows * lax.axis_size("chip") * lax.axis_size("core")

    source_all = src_rows
    projections = (w_query, w_out, w_key, w_value)
    for count, step in enumerate(chip_steps[::-1]):
        source_all = double(source_all, step, count)
        if count == 0:
            source_all, projections = lax.optimization_barrier((source_all, projections))
    near_pack = jnp.concatenate([ref_rows, out_grad, *projections[:2]], axis=0)
    far_pack = jnp.concatenate(projections[2:], axis=0)
    source_all = double(source_all, core_step, len(chip_steps)).reshape(key_total, width)

    f32, b16 = jnp.float32, jnp.bfloat16
    shape, vmem = jax.ShapeDtypeStruct, pltpu.VMEM
    unit = 2 * rows * width * width
    query_blocks, steps = rows // BLOCK, key_total // STEP
    stacked = HEADS * BLOCK
    blocks = (query_blocks * steps, stacked, STEP)
    row_like = (query_blocks, stacked, 128)
    col_like = vmem((steps, HEADS, 8, STEP), f32)
    room = (16 << 20) + max(0, rows * key_total * HEADS * 18 - (36 << 20))
    left, grad_left = vmem_call(
        functools.partial(project_kernel, HEADS),
        "project_reference",
        [
            shape((query_blocks, stacked, width), b16),
            shape((query_blocks, stacked, width), b16),
        ],
        [],
        8 << 20,
        4 * unit,
        1 << 20,
        (near_pack,),
    )
    row_peak, row_inverse, col_stats, scores, product = vmem_call(
        functools.partial(stats_kernel, HEADS),
        "match_stats",
        [
            shape(row_like, f32),
            shape(row_like, f32),
            shape((3, HEADS, key_total), f32),
            shape(blocks, f32),
            shape(blocks, b16),
        ],
        [
            vmem((width, key_total), b16),
            vmem((width, key_total), b16),
            vmem((stacked, STEP), f32),
            vmem(row_like, f32),
            col_like,
            col_like,
            col_like,
        ],
        room,
        60 * unit,
        8 << 20,
        (listed, left, grad_left, far_pack, source_all),
        scalars=1,
    )
    near_stats = col_stats
    keys, values, query_t, grad_t = vmem_call(
        functools.partial(side_kernel, HEADS),
        "project_for_grads",
        [
            shape((steps, HEADS * STEP, width), b16),
            shape((steps, HEADS * STEP, width), b16),
            shape((query_blocks, width, BLOCK), b16),
            shape((query_blocks, width, BLOCK), b16),
        ],
        [],
        8 << 20,
        8 * unit,
        2 << 20,
        (near_pack, far_pack, source_all),
    )
    for mesh_axis, bit, _ in chip_steps:
        near_stats = combine_stats([near_stats, swap(near_stats, mesh_axis, bit)])
    far_stats = swap(near_stats, "core", 1)
    attended, grad_query, grad_key, grad_value, weight_part = vmem_call(
        functools.partial(grads_kernel, HEADS),
        "match_grads",
        [
            shape((rows, width), b16),
            shape((rows, width), b16),
            shape((width, key_total), b16),
            shape((width, key_total), b16),
            shape((4, width, width), b16),
        ],
        [
            vmem((steps, stacked, STEP), f32),
            vmem((steps, BLOCK, HEADS * STEP), b16),
            vmem((BLOCK, HEADS * STEP), b16),
            vmem((stacked, 128), f32),
            vmem((4, steps, HEADS, 8, STEP), f32),
            vmem((query_blocks, BLOCK, width), f32),
            vmem((query_blocks, BLOCK, width), f32),
            vmem((steps, width, STEP), f32),
            vmem((steps, width, STEP), f32),
        ],
        room,
        100 * unit,
        8 << 20,
        (listed, scores, product, keys, values, query_t, grad_t, row_peak, row_inverse, col_stats,
         near_stats, far_stats, near_pack, source_all),
        scalars=1,
    )
    (source_part,) = vmem_call(
        source_kernel,
        "source_grads",
        [shape((key_total, width), b16)],
        [],
        8 << 20,
        8 * unit,
        2 << 20,
        (far_pack, grad_key, grad_value),
    )

    scans = lax.axis_size("scan")
    weights = weight_part.reshape((2, scans // 2, 2, -1, width))
    sources = source_part.reshape((2,) * (len(chip_steps) + 1) + (key_rows, width))
    source_steps = list(zip(chip_steps, range(len(chip_steps) - 1, -1, -1)))
    weights = halve(weights, core_step)
    sources = halve(sources, core_step, len(chip_steps))
    weights, sources = lax.optimization_barrier((weights, sources))
    weights = scatter_direct(weights.reshape((scans,) + weights.shape[2:]), "scan")
    sources = halve(sources, *source_steps[0])
    weights, sources, attended, grad_query = lax.optimization_barrier(
        (weights, sources, attended, grad_query)
    )
    matched, grad_ref = vmem_call(
        rows_kernel,
        "row_outputs",
        [shape((rows, width), b16), shape((rows, width), b16)],
        [],
        8 << 20,
        4 * unit,
        2 << 20,
        (near_pack, attended, grad_query),
    )
    for step in source_steps[1:]:
        sources = halve(sources, *step)
    for mesh_axis, bit, _ in chip_steps:
        weights = add(weights, swap(weights, mesh_axis, bit))
    weights, grad_src = lax.optimization_barrier((weights, sources))
    weights = gather_direct(weights, "scan")
    weights = double(weights, core_step)
    weights = weights.reshape(4, width, width).astype(f32)
    return (
        matched[None],
        grad_ref[None],
        grad_src[None],
        weights[0],
        weights[1],
        weights[2],
        weights[3],
    )


def solution(mesh):
    scans, blks = mesh.shape["scan"], mesh.shape["blk"]
    mesh = jax.sharding.Mesh(
        mesh.devices.reshape(scans, blks // 2, 2), ("scan", "chip", "core")
    )
    split = P("scan", ("chip", "core"), None)
    whole = P()
    return jax.shard_map(
        on_device,
        mesh=mesh,
        in_specs=(split, split, split, whole, whole, whole, whole, split),
        out_specs=(split, split, split, whole, whole, whole, whole),
        check_vma=False,
    )
```

```python
import functools
import math

import jax
import jax.numpy as jnp
from jax import lax
from jax.experimental import pallas as pl
from jax.experimental.pallas import tpu as pltpu
from jax.sharding import PartitionSpec as P

HEADS = 4
BLOCK = 128
NEG = -1e30
FLOOR = -1e29
LOG2E = math.log2(math.e)

NT = (((1,), (1,)), ((), ()))
TN = (((0,), (0,)), ((), ()))
TT = (((0,), (1,)), ((), ()))


def mm(left, right):
    return jnp.dot(left, right, preferred_element_type=jnp.float32)


def mm_general(left, right, dims):
    return lax.dot_general(left, right, dims, preferred_element_type=jnp.float32)


def bf(x):
    return x.astype(jnp.bfloat16)


def lane_row(width, head, head_dim):
    lanes = lax.broadcasted_iota(jnp.int32, (1, width), 1) // head_dim
    return bf(jnp.where(lanes == head, 1.0, 0.0))


def spread(reduced, like):
    return jnp.broadcast_to(reduced, like.shape)


STRIP = 32
STEP = 256


def by_eight(x):
    return x.reshape(x.shape[0] // 8, 8, x.shape[1])


def listed_steps(inter_ref, query_block, work):
    per_step = STEP // BLOCK

    def visit(step, carry):
        listed = [inter_ref[query_block, step * per_step + k] == 1 for k in range(per_step)]

        @pl.when(functools.reduce(jnp.logical_or, listed))
        def _():
            work(query_block, step, listed)

        return carry

    lax.fori_loop(0, inter_ref.shape[1] // per_step, visit, 0)


def each_listed(inter_ref, work):
    def visit(query_block, carry):
        listed_steps(inter_ref, query_block, work)
        return carry

    lax.fori_loop(0, inter_ref.shape[0], visit, 0)


def head_strips(heads):
    for head in range(heads):
        spans = [slice(first, first + STRIP) for first in range(0, BLOCK, STRIP)]
        yield head, [slice(head * BLOCK + a.start, head * BLOCK + a.stop) for a in spans]


def step_columns(step):
    return pl.ds(pl.multiple_of(step * STEP, STEP), STEP)


def each_tile(listed, work, otherwise=None):
    for tile, flag in enumerate(listed):
        lanes = slice(tile * BLOCK, (tile + 1) * BLOCK)
        pl.when(flag)(functools.partial(work, lanes))
        if otherwise is not None:
            pl.when(jnp.logical_not(flag))(functools.partial(otherwise, lanes))


def unpack(packed_ref, count):
    total, width = packed_ref.shape
    rows = (total - 2 * width) // 2
    sizes = [rows] * (count - 2) + [width, width]
    return [packed_ref.at[pl.ds(sum(sizes[:k]), sizes[k])] for k in range(count)]


def project_kernel(heads, near_ref, left_ref, gleft_ref):
    ref_ref, gout_ref, wq_ref, wo_ref = unpack(near_ref, 4)
    rows, width = ref_ref.shape
    head_dim = width // heads
    query = bf(bf(mm(ref_ref[...], wq_ref[...])).astype(jnp.float32) * head_dim ** -0.5)
    grad = bf(mm_general(gout_ref[...], wo_ref[...], NT))
    for query_block in range(rows // BLOCK):
        span = slice(query_block * BLOCK, (query_block + 1) * BLOCK)
        for head in range(heads):
            own = lane_row(width, head, head_dim)
            left_ref[query_block, head * BLOCK : (head + 1) * BLOCK, :] = query[span] * own
            gleft_ref[query_block, head * BLOCK : (head + 1) * BLOCK, :] = grad[span] * own


def stats_kernel(
    heads, inter_ref, left_ref, gleft_ref, far_ref, src_ref,
    peak_ref, inverse_ref, col_ref, score_ref, product_ref,
    key_t_ref, value_t_ref, prob_ref, total_ref, col_peak_ref, col_total_ref, col_dot_ref,
):
    wk_ref, wv_ref = unpack(far_ref, 2)
    rows, key_total = left_ref.shape[0] * BLOCK, src_ref.shape[0]
    key_t_ref[...] = bf(mm_general(wk_ref[...], src_ref[...], TT))
    value_t_ref[...] = bf(mm_general(wv_ref[...], src_ref[...], TT))
    steps = key_total // STEP
    peak_ref[...] = jnp.full(peak_ref.shape, 2.0 * NEG, jnp.float32)
    total_ref[...] = jnp.zeros(total_ref.shape, jnp.float32)
    col_peak_ref[...] = jnp.full(col_peak_ref.shape, FLOOR, jnp.float32)
    col_total_ref[...] = jnp.zeros(col_total_ref.shape, jnp.float32)
    col_dot_ref[...] = jnp.zeros(col_dot_ref.shape, jnp.float32)

    def peaks(query_block, step, listed):
        score_now = score_ref.at[query_block * steps + step]
        score_now[...] = mm(left_ref[query_block], key_t_ref[:, step_columns(step)]) * LOG2E

        def tile(lanes):
            for head, spans in head_strips(heads):
                col_peak = col_peak_ref[step, head, :, lanes]
                for span in spans:
                    scores = score_now[span, lanes]
                    row_peak = peak_ref[query_block, span, :]
                    peak_ref[query_block, span, :] = jnp.maximum(row_peak, scores)
                    col_peak = jnp.maximum(col_peak, by_eight(scores).max(axis=0))
                col_peak_ref[step, head, :, lanes] = col_peak

        each_tile(listed, tile)

    each_listed(inter_ref, peaks)
    for query_block in range(rows // BLOCK):
        peak = peak_ref[query_block]
        peak_ref[query_block] = spread(peak.max(axis=1, keepdims=True), peak)
    for step in range(steps):
        for head in range(heads):
            peak = col_peak_ref[step, head]
            col_peak_ref[step, head] = spread(peak.max(axis=0, keepdims=True), peak)

    def totals(query_block, step, listed):
        score_now, product_now = [
            ref.at[query_block * steps + step] for ref in (score_ref, product_ref)
        ]
        prob_ref[...] = mm(gleft_ref[query_block], value_t_ref[:, step_columns(step)])

        def tile(lanes):
            for head, spans in head_strips(heads):
                col_peak = col_peak_ref[step, head, :, lanes][None]
                col_total = col_total_ref[step, head, :, lanes]
                for span in spans:
                    scores = by_eight(score_now[span, lanes])
                    row_exp = jnp.exp2(scores - by_eight(peak_ref[query_block, span, :]))
                    col_exp = jnp.exp2(scores - col_peak)
                    total_ref[query_block, span, :] += row_exp.reshape(STRIP, 128)
                    product = row_exp * col_exp * by_eight(prob_ref[span, lanes])
                    product_now[span, lanes] = bf(product.reshape(STRIP, 128))
                    col_total = col_total + col_exp.sum(axis=0)
                col_total_ref[step, head, :, lanes] = col_total

        each_tile(listed, tile)

    each_listed(inter_ref, totals)
    for query_block in range(rows // BLOCK):
        total = total_ref[query_block]
        inverse_ref[query_block] = spread(1.0 / total.sum(axis=1, keepdims=True), total)

    def dots(query_block, step, listed):
        product_now = product_ref.at[query_block * steps + step]

        def tile(lanes):
            for head, spans in head_strips(heads):
                col_dot = col_dot_ref[step, head, :, lanes]
                for span in spans:
                    product = product_now[span, lanes].astype(jnp.float32)
                    product = by_eight(product * inverse_ref[query_block, span, :])
                    col_dot = col_dot + product.sum(axis=0)
                col_dot_ref[step, head, :, lanes] = col_dot

        each_tile(listed, tile)

    each_listed(inter_ref, dots)
    for step in range(steps):
        lanes = slice(step * STEP, (step + 1) * STEP)
        for head in range(heads):
            mine = slice(head, head + 1)
            col_ref[0, mine, lanes] = col_peak_ref[step, head, 0:1, :]
            col_ref[1, mine, lanes] = col_total_ref[step, head].sum(axis=0, keepdims=True)
            col_ref[2, mine, lanes] = col_dot_ref[step, head].sum(axis=0, keepdims=True)


def side_kernel(
    heads, near_ref, far_ref, src_ref, key_ref, value_ref, query_t_ref, grad_t_ref
):
    ref_ref, gout_ref, wq_ref, wo_ref = unpack(near_ref, 4)
    wk_ref, wv_ref = unpack(far_ref, 2)
    rows, width = ref_ref.shape
    head_dim = width // heads
    key_ref[...] = bf(mm(src_ref[...], wk_ref[...]))
    value_ref[...] = bf(mm(src_ref[...], wv_ref[...]))
    query_t = bf(mm_general(wq_ref[...], ref_ref[...], TT)).astype(jnp.float32)
    query_t = bf(query_t * (2.0 * head_dim ** -0.5))
    grad_t = bf(mm_general(wo_ref[...], gout_ref[...], NT))
    for values, out_ref in ((query_t, query_t_ref), (grad_t, grad_t_ref)):
        out_ref[...] = jnp.zeros(out_ref.shape, jnp.bfloat16)
        for query_block in range(rows // BLOCK):
            span = slice(query_block * BLOCK, (query_block + 1) * BLOCK)
            for head in range(heads):
                mine = slice(head * head_dim, (head + 1) * head_dim)
                lanes = slice(head * BLOCK, (head + 1) * BLOCK)
                out_ref[query_block, mine, lanes] = values[mine, span]


def grads_kernel(
    heads, inter_ref, score_ref, product_ref, key_ref, value_ref,
    query_t_ref, grad_t_ref, peak_ref, inverse_ref, own_ref, near_ref, far_ref, packed_ref, src_ref,
    attended_ref, gquery_ref, gkey_ref, gvalue_ref, weight_ref,
    rest_ref, match_ref, gscore_ref, dot_ref, col_ref,
    att_ref, gq_ref, gk_ref, gv_ref,
):
    ref_ref, gout_ref = unpack(packed_ref, 4)[:2]
    rows, width = ref_ref.shape
    key_total = src_ref.shape[0]
    steps = key_total // STEP
    head_dim = width // heads

    peak = jnp.maximum(near_ref[0], far_ref[0])
    near, far = jnp.exp2(near_ref[0] - peak), jnp.exp2(far_ref[0] - peak)
    inverse = 1.0 / (near * near_ref[1] + far * far_ref[1])
    half = (near * near_ref[2] + far * far_ref[2]) * inverse * 0.5
    factor = jnp.exp2(own_ref[0] - peak) * inverse
    for kind, values in enumerate((peak, inverse, factor, half)):
        for head in range(heads):
            for step in range(steps):
                piece = values[head : head + 1, step * STEP : (step + 1) * STEP]
                col_ref[kind, step, head] = jnp.broadcast_to(piece, (8, STEP))
    for ref in (att_ref, gq_ref, gk_ref, gv_ref):
        ref[...] = jnp.zeros(ref.shape, jnp.float32)

    def products(query_block, step, listed):
        score_now, product_now = [
            ref.at[query_block * steps + step] for ref in (score_ref, product_ref)
        ]
        rest_now, match_now = rest_ref.at[step], match_ref.at[step]

        def tile(lanes):
            for head, spans in head_strips(heads):
                col_peak, col_inverse, col_factor, col_half = [
                    col_ref[kind, step, head, :, lanes][None] for kind in range(4)
                ]
                for span in spans:
                    row_inverse = by_eight(inverse_ref[query_block, span, :])
                    scores = by_eight(score_now[span, lanes])
                    row_prob = jnp.exp2(scores - by_eight(peak_ref[query_block, span, :]))
                    col_prob = jnp.exp2(scores - col_peak) * col_inverse
                    product = by_eight(product_now[span, lanes].astype(jnp.float32))
                    product = product * row_inverse * col_factor
                    dot_ref[span, :] += product.reshape(STRIP, 128)
                    match = row_prob * row_inverse * col_prob
                    match_now[span, lanes] = bf(match.reshape(STRIP, 128))
                    rest_now[span, lanes] = (product - col_prob * col_half).reshape(STRIP, 128)

        def empty(lanes):
            match_now[:, lanes] = jnp.zeros((heads * BLOCK, BLOCK), jnp.bfloat16)

        each_tile(listed, tile, empty)

    def own_lanes(stacked):
        total = None
        for head in range(heads):
            own = lane_row(width, head, head_dim).astype(jnp.float32)
            piece = stacked[head * BLOCK : (head + 1) * BLOCK] * own
            total = piece if total is None else total + piece
        return total

    def outputs(query_block, step, listed):
        score_now, rest_now, match_now = [
            score_ref.at[query_block * steps + step], rest_ref.at[step], match_ref.at[step]
        ]

        def tile(lanes):
            for _, spans in head_strips(heads):
                for span in spans:
                    row_half = dot_ref[span, :] * inverse_ref[query_block, span, :]
                    row_exp = jnp.exp2(score_now[span, lanes] - peak_ref[query_block, span, :])
                    gscore_ref[span, lanes] = bf(rest_now[span, lanes] - row_exp * row_half)

        def empty(lanes):
            gscore_ref[:, lanes] = jnp.zeros((heads * BLOCK, BLOCK), jnp.bfloat16)

        each_tile(listed, tile, empty)
        span = step_columns(step)
        att_ref[query_block] += own_lanes(mm(match_now[...], value_ref[span, :]))
        gq_ref[query_block] += own_lanes(mm(gscore_ref[...], key_ref[span, :]))
        gk_ref[step] += mm(query_t_ref[query_block], gscore_ref[...])
        gv_ref[step] += mm(grad_t_ref[query_block], match_now[...])

    def query_rows(query_block, carry):
        dot_ref[...] = jnp.zeros(dot_ref.shape, jnp.float32)
        listed_steps(inter_ref, query_block, products)
        dot = dot_ref[...]
        dot_ref[...] = spread(dot.sum(axis=1, keepdims=True) * 0.5, dot)
        listed_steps(inter_ref, query_block, outputs)
        return carry

    lax.fori_loop(0, rows // BLOCK, query_rows, 0)
    attended = bf(att_ref[...]).reshape(rows, width)
    gquery = bf(gq_ref[...] * (2.0 * head_dim ** -0.5)).reshape(rows, width)
    attended_ref[...] = attended
    gquery_ref[...] = gquery
    for step in range(steps):
        gkey_ref[:, step * STEP : (step + 1) * STEP] = bf(gk_ref[step])
        gvalue_ref[:, step * STEP : (step + 1) * STEP] = bf(gv_ref[step])
    weight_ref[0] = bf(mm_general(ref_ref[...], gquery, TN))
    weight_ref[1] = bf(mm(gkey_ref[...], src_ref[...]).T)
    weight_ref[2] = bf(mm(gvalue_ref[...], src_ref[...]).T)
    weight_ref[3] = bf(mm_general(attended, gout_ref[...], TN))


def source_kernel(far_ref, gkey_ref, gvalue_ref, gsrc_ref):
    wk_ref, wv_ref = unpack(far_ref, 2)
    gsrc_t = mm(wk_ref[...], gkey_ref[...]) + mm(wv_ref[...], gvalue_ref[...])
    gsrc_ref[...] = bf(gsrc_t.T)


def rows_kernel(near_ref, attended_ref, gquery_ref, matched_ref, gref_ref):
    ref_ref, gout_ref, wq_ref, wo_ref = unpack(near_ref, 4)
    matched = ref_ref[...].astype(jnp.float32) + mm(attended_ref[...], wo_ref[...])
    matched_ref[...] = bf(matched)
    gref = gout_ref[...].astype(jnp.float32) + mm_general(gquery_ref[...], wq_ref[...], NT)
    gref_ref[...] = bf(gref)


def swap(x, axis, apart):
    pairs = [(i, i ^ apart) for i in range(lax.axis_size(axis))]
    return lax.ppermute(x, axis, pairs)


def at(x, index, axis=0):
    return lax.dynamic_index_in_dim(x, index, axis, False)


def laid(near, far, side, axis=0):
    shape = near.shape[:axis] + (2,) + near.shape[axis:]
    out = lax.dynamic_update_index_in_dim(jnp.zeros(shape, near.dtype), near, side, axis)
    return lax.dynamic_update_index_in_dim(out, far, 1 - side, axis)


def add(near, far):
    return (near.astype(jnp.float32) + far.astype(jnp.float32)).astype(near.dtype)


def halve(x, step, axis=0):
    mesh_axis, bit, side = step
    return add(at(x, side, axis), swap(at(x, 1 - side, axis), mesh_axis, bit))


def double(x, step, axis=0):
    mesh_axis, bit, side = step
    return laid(x, swap(x, mesh_axis, bit), side, axis)


def bit_steps(mesh_axis):
    me = lax.axis_index(mesh_axis)
    bits = range(lax.axis_size(mesh_axis).bit_length() - 1)
    return [(mesh_axis, 1 << bit, (me >> bit) % 2) for bit in bits]


def scatter_direct(x, mesh_axis):
    me, count = lax.axis_index(mesh_axis), lax.axis_size(mesh_axis)
    total = at(x, me).astype(jnp.float32)
    for piece in [swap(at(x, me ^ apart), mesh_axis, apart) for apart in range(1, count)]:
        total = total + piece.astype(jnp.float32)
    return total.astype(x.dtype)


def gather_direct(x, mesh_axis):
    me, count = lax.axis_index(mesh_axis), lax.axis_size(mesh_axis)
    pieces = [x] + [swap(x, mesh_axis, apart) for apart in range(1, count)]
    out = jnp.zeros((count,) + x.shape, x.dtype)
    for apart, piece in enumerate(pieces):
        out = lax.dynamic_update_index_in_dim(out, piece, me ^ apart, 0)
    return out


def combine_stats(parts):
    peak = functools.reduce(jnp.maximum, [part[0] for part in parts])
    factors = [jnp.exp2(part[0] - peak) for part in parts]
    total = sum(factor * part[1] for factor, part in zip(factors, parts))
    dots = sum(factor * part[2] for factor, part in zip(factors, parts))
    return jnp.stack([peak, total, dots])


def vmem_call(kernel, name, out_shape, scratch, limit, flops, moved, args, scalars=0):
    specs = [pl.BlockSpec(memory_space=pltpu.SMEM)] * scalars
    specs += [pl.BlockSpec(memory_space=pltpu.VMEM)] * (len(args) - scalars)
    return pl.pallas_call(
        kernel,
        name=name,
        out_shape=out_shape,
        in_specs=specs,
        out_specs=[pl.BlockSpec(memory_space=pltpu.VMEM)] * len(out_shape),
        scratch_shapes=scratch,
        compiler_params=pltpu.CompilerParams(vmem_limit_bytes=limit),
        cost_estimate=pl.CostEstimate(flops=flops, bytes_accessed=moved, transcendentals=0),
    )(*args)


def on_device(ref_feats, src_feats, grad_out, w_query, w_key, w_value, w_out, intersection):
    ref_rows = ref_feats[0]
    src_rows = src_feats[0]
    out_grad = grad_out[0]
    listed = jnp.where(intersection[0] == 1, 1, 0)
    rows, width = ref_rows.shape
    core_step = bit_steps("core")[0]
    chip_steps = bit_steps("chip")
    key_rows = src_rows.shape[0]
    key_total = key_rows * lax.axis_size("chip") * lax.axis_size("core")

    source_all = src_rows
    projections = (w_query, w_out, w_key, w_value)
    for count, step in enumerate(chip_steps[::-1]):
        source_all = double(source_all, step, count)
        if count == 0:
            source_all, projections = lax.optimization_barrier((source_all, projections))
    near_pack = jnp.concatenate([ref_rows, out_grad, *projections[:2]], axis=0)
    far_pack = jnp.concatenate(projections[2:], axis=0)
    source_all = double(source_all, core_step, len(chip_steps)).reshape(key_total, width)

    f32, b16 = jnp.float32, jnp.bfloat16
    shape, vmem = jax.ShapeDtypeStruct, pltpu.VMEM
    unit = 2 * rows * width * width
    query_blocks, steps = rows // BLOCK, key_total // STEP
    stacked = HEADS * BLOCK
    blocks = (query_blocks * steps, stacked, STEP)
    row_like = (query_blocks, stacked, 128)
    col_like = vmem((steps, HEADS, 8, STEP), f32)
    room = (16 << 20) + max(0, rows * key_total * HEADS * 18 - (36 << 20))
    left, grad_left = vmem_call(
        functools.partial(project_kernel, HEADS),
        "project_reference",
        [
            shape((query_blocks, stacked, width), b16),
            shape((query_blocks, stacked, width), b16),
        ],
        [],
        8 << 20,
        4 * unit,
        1 << 20,
        (near_pack,),
    )
    row_peak, row_inverse, col_stats, scores, product = vmem_call(
        functools.partial(stats_kernel, HEADS),
        "match_stats",
        [
            shape(row_like, f32),
            shape(row_like, f32),
            shape((3, HEADS, key_total), f32),
            shape(blocks, f32),
            shape(blocks, b16),
        ],
        [
            vmem((width, key_total), b16),
            vmem((width, key_total), b16),
            vmem((stacked, STEP), f32),
            vmem(row_like, f32),
            col_like,
            col_like,
            col_like,
        ],
        room,
        60 * unit,
        8 << 20,
        (listed, left, grad_left, far_pack, source_all),
        scalars=1,
    )
    near_stats = col_stats
    keys, values, query_t, grad_t = vmem_call(
        functools.partial(side_kernel, HEADS),
        "project_for_grads",
        [
            shape((key_total, width), b16),
            shape((key_total, width), b16),
            shape((query_blocks, width, stacked), b16),
            shape((query_blocks, width, stacked), b16),
        ],
        [],
        8 << 20,
        8 * unit,
        2 << 20,
        (near_pack, far_pack, source_all),
    )
    for mesh_axis, bit, _ in chip_steps:
        near_stats = combine_stats([near_stats, swap(near_stats, mesh_axis, bit)])
    far_stats = swap(near_stats, "core", 1)
    attended, grad_query, grad_key, grad_value, weight_part = vmem_call(
        functools.partial(grads_kernel, HEADS),
        "match_grads",
        [
            shape((rows, width), b16),
            shape((rows, width), b16),
            shape((width, key_total), b16),
            shape((width, key_total), b16),
            shape((4, width, width), b16),
        ],
        [
            vmem((steps, stacked, STEP), f32),
            vmem((steps, stacked, STEP), b16),
            vmem((stacked, STEP), b16),
            vmem((stacked, 128), f32),
            vmem((4, steps, HEADS, 8, STEP), f32),
            vmem((query_blocks, BLOCK, width), f32),
            vmem((query_blocks, BLOCK, width), f32),
            vmem((steps, width, STEP), f32),
            vmem((steps, width, STEP), f32),
        ],
        room,
        100 * unit,
        8 << 20,
        (listed, scores, product, keys, values, query_t, grad_t, row_peak, row_inverse, col_stats,
         near_stats, far_stats, near_pack, source_all),
        scalars=1,
    )
    (source_part,) = vmem_call(
        source_kernel,
        "source_grads",
        [shape((key_total, width), b16)],
        [],
        8 << 20,
        8 * unit,
        2 << 20,
        (far_pack, grad_key, grad_value),
    )

    scans = lax.axis_size("scan")
    weights = weight_part.reshape((2, scans // 2, 2, -1, width))
    sources = source_part.reshape((2,) * (len(chip_steps) + 1) + (key_rows, width))
    source_steps = list(zip(chip_steps, range(len(chip_steps) - 1, -1, -1)))
    weights = halve(weights, core_step)
    sources = halve(sources, core_step, len(chip_steps))
    weights, sources = lax.optimization_barrier((weights, sources))
    weights = scatter_direct(weights.reshape((scans,) + weights.shape[2:]), "scan")
    sources = halve(sources, *source_steps[0])
    weights, sources, attended, grad_query = lax.optimization_barrier(
        (weights, sources, attended, grad_query)
    )
    matched, grad_ref = vmem_call(
        rows_kernel,
        "row_outputs",
        [shape((rows, width), b16), shape((rows, width), b16)],
        [],
        8 << 20,
        4 * unit,
        2 << 20,
        (near_pack, attended, grad_query),
    )
    for step in source_steps[1:]:
        sources = halve(sources, *step)
    for mesh_axis, bit, _ in chip_steps:
        weights = add(weights, swap(weights, mesh_axis, bit))
    weights, grad_src = lax.optimization_barrier((weights, sources))
    weights = gather_direct(weights, "scan")
    weights = double(weights, core_step)
    weights = weights.reshape(4, width, width).astype(f32)
    return (
        matched[None],
        grad_ref[None],
        grad_src[None],
        weights[0],
        weights[1],
        weights[2],
        weights[3],
    )


def solution(mesh):
    scans, blks = mesh.shape["scan"], mesh.shape["blk"]
    mesh = jax.sharding.Mesh(
        mesh.devices.reshape(scans, blks // 2, 2), ("scan", "chip", "core")
    )
    split = P("scan", ("chip", "core"), None)
    whole = P()
    return jax.shard_map(
        on_device,
        mesh=mesh,
        in_specs=(split, split, split, whole, whole, whole, whole, split),
        out_specs=(split, split, split, whole, whole, whole, whole),
        check_vma=False,
    )
```

```python
import functools
import math

import jax
import jax.numpy as jnp
from jax import lax
from jax.experimental import pallas as pl
from jax.experimental.pallas import tpu as pltpu
from jax.sharding import PartitionSpec as P

HEADS = 4
BLOCK = 128
NEG = -1e30
FLOOR = -1e29
LOG2E = math.log2(math.e)

NT = (((1,), (1,)), ((), ()))
TN = (((0,), (0,)), ((), ()))
TT = (((0,), (1,)), ((), ()))


def mm(left, right):
    return jnp.dot(left, right, preferred_element_type=jnp.float32)


def mm_general(left, right, dims):
    return lax.dot_general(left, right, dims, preferred_element_type=jnp.float32)


def bf(x):
    return x.astype(jnp.bfloat16)


def lane_row(width, head, head_dim):
    lanes = lax.broadcasted_iota(jnp.int32, (1, width), 1) // head_dim
    return bf(jnp.where(lanes == head, 1.0, 0.0))


def spread(reduced, like):
    return jnp.broadcast_to(reduced, like.shape)


STRIP = 32
STEP = 256


def by_eight(x):
    return x.reshape(x.shape[0] // 8, 8, x.shape[1])


def listed_steps(inter_ref, query_block, work):
    per_step = STEP // BLOCK

    def visit(step, carry):
        listed = [inter_ref[query_block, step * per_step + k] == 1 for k in range(per_step)]

        @pl.when(functools.reduce(jnp.logical_or, listed))
        def _():
            work(query_block, step, listed)

        return carry

    lax.fori_loop(0, inter_ref.shape[1] // per_step, visit, 0)


def each_listed(inter_ref, work):
    def visit(query_block, carry):
        listed_steps(inter_ref, query_block, work)
        return carry

    lax.fori_loop(0, inter_ref.shape[0], visit, 0)


def head_strips(heads):
    for head in range(heads):
        spans = [slice(first, first + STRIP) for first in range(0, BLOCK, STRIP)]
        yield head, [slice(head * BLOCK + a.start, head * BLOCK + a.stop) for a in spans]


def score_block(query_block, step, listed, left_ref, key_t_ref, score_ref):
    span = pl.ds(pl.multiple_of(step * STEP, STEP), STEP)
    bias = jnp.concatenate(
        [jnp.full((1, BLOCK), jnp.where(flag, 0.0, NEG), jnp.float32) for flag in listed], axis=1
    )
    score_ref[...] = mm(left_ref[query_block], key_t_ref[:, span]) * LOG2E + bias


def unpack(packed_ref, count):
    total, width = packed_ref.shape
    rows = (total - 2 * width) // 2
    sizes = [rows] * (count - 2) + [width, width]
    return [packed_ref.at[pl.ds(sum(sizes[:k]), sizes[k])] for k in range(count)]


def project_kernel(heads, near_ref, left_ref, gleft_ref):
    ref_ref, gout_ref, wq_ref, wo_ref = unpack(near_ref, 4)
    rows, width = ref_ref.shape
    head_dim = width // heads
    query = bf(bf(mm(ref_ref[...], wq_ref[...])).astype(jnp.float32) * head_dim ** -0.5)
    grad = bf(mm_general(gout_ref[...], wo_ref[...], NT))
    for query_block in range(rows // BLOCK):
        span = slice(query_block * BLOCK, (query_block + 1) * BLOCK)
        for head in range(heads):
            own = lane_row(width, head, head_dim)
            left_ref[query_block, head * BLOCK : (head + 1) * BLOCK, :] = query[span] * own
            gleft_ref[query_block, head * BLOCK : (head + 1) * BLOCK, :] = grad[span] * own


def stats_kernel(
    heads, inter_ref, left_ref, gleft_ref, far_ref, src_ref,
    peak_ref, inverse_ref, col_ref, score_ref, product_ref,
    key_t_ref, value_t_ref, prob_ref, total_ref, col_peak_ref, col_total_ref, col_dot_ref,
):
    wk_ref, wv_ref = unpack(far_ref, 2)
    rows, key_total = left_ref.shape[0] * BLOCK, src_ref.shape[0]
    key_t_ref[...] = bf(mm_general(wk_ref[...], src_ref[...], TT))
    value_t_ref[...] = bf(mm_general(wv_ref[...], src_ref[...], TT))
    steps = key_total // STEP
    peak_ref[...] = jnp.full(peak_ref.shape, 2.0 * NEG, jnp.float32)
    total_ref[...] = jnp.zeros(total_ref.shape, jnp.float32)
    col_peak_ref[...] = jnp.full(col_peak_ref.shape, FLOOR, jnp.float32)
    col_total_ref[...] = jnp.zeros(col_total_ref.shape, jnp.float32)
    col_dot_ref[...] = jnp.zeros(col_dot_ref.shape, jnp.float32)
    tiles = [slice(first, first + 128) for first in range(0, STEP, 128)]

    def peaks(query_block, step, listed):
        block_ref = score_ref.at[query_block * steps + step]
        score_block(query_block, step, listed, left_ref, key_t_ref, block_ref)
        for head, spans in head_strips(heads):
            col_peaks = [col_peak_ref[step, head, :, lanes] for lanes in tiles]
            for span in spans:
                row_peak = peak_ref[query_block, span, :]
                for at, lanes in enumerate(tiles):
                    scores = block_ref[span, lanes]
                    row_peak = jnp.maximum(row_peak, scores)
                    col_peaks[at] = jnp.maximum(col_peaks[at], by_eight(scores).max(axis=0))
                peak_ref[query_block, span, :] = row_peak
            for at, lanes in enumerate(tiles):
                col_peak_ref[step, head, :, lanes] = col_peaks[at]

    each_listed(inter_ref, peaks)
    for query_block in range(rows // BLOCK):
        peak = peak_ref[query_block]
        peak_ref[query_block] = spread(peak.max(axis=1, keepdims=True), peak)
    for step in range(steps):
        for head in range(heads):
            peak = col_peak_ref[step, head]
            col_peak_ref[step, head] = spread(peak.max(axis=0, keepdims=True), peak)

    def totals(query_block, step, listed):
        score_now, product_now = [
            ref.at[query_block * steps + step] for ref in (score_ref, product_ref)
        ]
        span = pl.ds(pl.multiple_of(step * STEP, STEP), STEP)
        prob_ref[...] = mm(gleft_ref[query_block], value_t_ref[:, span])
        for head, spans in head_strips(heads):
            col_totals = [col_total_ref[step, head, :, lanes] for lanes in tiles]
            for span in spans:
                row_peak = by_eight(peak_ref[query_block, span, :])
                row_total = by_eight(total_ref[query_block, span, :])
                for at, lanes in enumerate(tiles):
                    scores = by_eight(score_now[span, lanes])
                    row_exp = jnp.exp2(scores - row_peak)
                    col_exp = jnp.exp2(scores - col_peak_ref[step, head, :, lanes][None])
                    row_total = row_total + row_exp
                    product = row_exp * col_exp * by_eight(prob_ref[span, lanes])
                    product_now[span, lanes] = bf(product.reshape(STRIP, 128))
                    col_totals[at] = col_totals[at] + col_exp.sum(axis=0)
                total_ref[query_block, span, :] = row_total.reshape(STRIP, 128)
            for at, lanes in enumerate(tiles):
                col_total_ref[step, head, :, lanes] = col_totals[at]

    each_listed(inter_ref, totals)
    for query_block in range(rows // BLOCK):
        total = total_ref[query_block]
        inverse_ref[query_block] = spread(1.0 / total.sum(axis=1, keepdims=True), total)

    def dots(query_block, step, listed):
        product_now = product_ref.at[query_block * steps + step]
        for head, spans in head_strips(heads):
            col_dots = [col_dot_ref[step, head, :, lanes] for lanes in tiles]
            for span in spans:
                inverse = inverse_ref[query_block, span, :]
                for at, lanes in enumerate(tiles):
                    product = by_eight(product_now[span, lanes].astype(jnp.float32) * inverse)
                    col_dots[at] = col_dots[at] + product.sum(axis=0)
            for at, lanes in enumerate(tiles):
                col_dot_ref[step, head, :, lanes] = col_dots[at]

    each_listed(inter_ref, dots)
    for step in range(steps):
        lanes = slice(step * STEP, (step + 1) * STEP)
        for head in range(heads):
            mine = slice(head, head + 1)
            col_ref[0, mine, lanes] = col_peak_ref[step, head, 0:1, :]
            col_ref[1, mine, lanes] = col_total_ref[step, head].sum(axis=0, keepdims=True)
            col_ref[2, mine, lanes] = col_dot_ref[step, head].sum(axis=0, keepdims=True)


def side_kernel(
    heads, near_ref, far_ref, src_ref, key_ref, value_ref, query_t_ref, grad_t_ref
):
    ref_ref, gout_ref, wq_ref, wo_ref = unpack(near_ref, 4)
    wk_ref, wv_ref = unpack(far_ref, 2)
    rows, width = ref_ref.shape
    head_dim = width // heads
    key_ref[...] = bf(mm(src_ref[...], wk_ref[...]))
    value_ref[...] = bf(mm(src_ref[...], wv_ref[...]))
    query_t = bf(mm_general(wq_ref[...], ref_ref[...], TT)).astype(jnp.float32)
    query_t = bf(query_t * (2.0 * head_dim ** -0.5))
    grad_t = bf(mm_general(wo_ref[...], gout_ref[...], NT))
    for values, out_ref in ((query_t, query_t_ref), (grad_t, grad_t_ref)):
        out_ref[...] = jnp.zeros(out_ref.shape, jnp.bfloat16)
        for query_block in range(rows // BLOCK):
            span = slice(query_block * BLOCK, (query_block + 1) * BLOCK)
            for head in range(heads):
                mine = slice(head * head_dim, (head + 1) * head_dim)
                lanes = slice(head * BLOCK, (head + 1) * BLOCK)
                out_ref[query_block, mine, lanes] = values[mine, span]


def grads_kernel(
    heads, inter_ref, score_ref, product_ref, key_ref, value_ref,
    query_t_ref, grad_t_ref, peak_ref, inverse_ref, own_ref, near_ref, far_ref, packed_ref, src_ref,
    attended_ref, gquery_ref, gkey_ref, gvalue_ref, weight_ref,
    rest_ref, match_ref, gscore_ref, dot_ref, col_ref,
    att_ref, gq_ref, gk_ref, gv_ref,
):
    ref_ref, gout_ref = unpack(packed_ref, 4)[:2]
    rows, width = ref_ref.shape
    key_total = src_ref.shape[0]
    steps = key_total // STEP
    head_dim = width // heads
    tiles = [slice(first, first + 128) for first in range(0, STEP, 128)]

    peak = jnp.maximum(near_ref[0], far_ref[0])
    near, far = jnp.exp2(near_ref[0] - peak), jnp.exp2(far_ref[0] - peak)
    inverse = 1.0 / (near * near_ref[1] + far * far_ref[1])
    half = (near * near_ref[2] + far * far_ref[2]) * inverse * 0.5
    factor = jnp.exp2(own_ref[0] - peak) * inverse
    for kind, values in enumerate((peak, inverse, factor, half)):
        for head in range(heads):
            for step in range(steps):
                piece = values[head : head + 1, step * STEP : (step + 1) * STEP]
                col_ref[kind, step, head] = jnp.broadcast_to(piece, (8, STEP))
    for ref in (att_ref, gq_ref, gk_ref, gv_ref):
        ref[...] = jnp.zeros(ref.shape, jnp.float32)

    def products(query_block, step, listed):
        score_now, product_now = [
            ref.at[query_block * steps + step] for ref in (score_ref, product_ref)
        ]
        rest_now, match_now = rest_ref.at[step], match_ref.at[step]
        for head, spans in head_strips(heads):
            for span in spans:
                row_peak = by_eight(peak_ref[query_block, span, :])
                row_inverse = by_eight(inverse_ref[query_block, span, :])
                row_dot = by_eight(dot_ref[span, :])
                for lanes in tiles:
                    col_peak, col_inverse, col_factor, col_half = [
                        col_ref[kind, step, head, :, lanes][None] for kind in range(4)
                    ]
                    scores = by_eight(score_now[span, lanes])
                    row_prob = jnp.exp2(scores - row_peak) * row_inverse
                    col_prob = jnp.exp2(scores - col_peak) * col_inverse
                    product = by_eight(product_now[span, lanes].astype(jnp.float32))
                    product = product * row_inverse * col_factor
                    row_dot = row_dot + product
                    match_now[span, lanes] = bf((row_prob * col_prob).reshape(STRIP, 128))
                    rest_now[span, lanes] = (product - col_prob * col_half).reshape(STRIP, 128)
                dot_ref[span, :] = row_dot.reshape(STRIP, 128)

    def own_lanes(stacked):
        total = None
        for head in range(heads):
            own = lane_row(width, head, head_dim).astype(jnp.float32)
            piece = stacked[head * BLOCK : (head + 1) * BLOCK] * own
            total = piece if total is None else total + piece
        return total

    def outputs(query_block, step, listed):
        score_now, rest_now, match_now = [
            score_ref.at[query_block * steps + step], rest_ref.at[step], match_ref.at[step]
        ]
        for _, spans in head_strips(heads):
            for span in spans:
                row_peak = peak_ref[query_block, span, :]
                row_half = dot_ref[span, :] * inverse_ref[query_block, span, :]
                for lanes in tiles:
                    row_part = jnp.exp2(score_now[span, lanes] - row_peak) * row_half
                    gscore_ref[span, lanes] = bf(rest_now[span, lanes] - row_part)
        span = pl.ds(pl.multiple_of(step * STEP, STEP), STEP)
        att_ref[query_block] += own_lanes(mm(match_now[...], value_ref[span, :]))
        gq_ref[query_block] += own_lanes(mm(gscore_ref[...], key_ref[span, :]))
        gk_ref[step] += mm(query_t_ref[query_block], gscore_ref[...])
        gv_ref[step] += mm(grad_t_ref[query_block], match_now[...])

    def query_rows(query_block, carry):
        dot_ref[...] = jnp.zeros(dot_ref.shape, jnp.float32)
        listed_steps(inter_ref, query_block, products)
        dot = dot_ref[...]
        dot_ref[...] = spread(dot.sum(axis=1, keepdims=True) * 0.5, dot)
        listed_steps(inter_ref, query_block, outputs)
        return carry

    lax.fori_loop(0, rows // BLOCK, query_rows, 0)
    attended = bf(att_ref[...]).reshape(rows, width)
    gquery = bf(gq_ref[...] * (2.0 * head_dim ** -0.5)).reshape(rows, width)
    attended_ref[...] = attended
    gquery_ref[...] = gquery
    for step in range(steps):
        gkey_ref[:, step * STEP : (step + 1) * STEP] = bf(gk_ref[step])
        gvalue_ref[:, step * STEP : (step + 1) * STEP] = bf(gv_ref[step])
    weight_ref[0] = bf(mm_general(ref_ref[...], gquery, TN))
    weight_ref[1] = bf(mm(gkey_ref[...], src_ref[...]).T)
    weight_ref[2] = bf(mm(gvalue_ref[...], src_ref[...]).T)
    weight_ref[3] = bf(mm_general(attended, gout_ref[...], TN))


def source_kernel(far_ref, gkey_ref, gvalue_ref, gsrc_ref):
    wk_ref, wv_ref = unpack(far_ref, 2)
    gsrc_t = mm(wk_ref[...], gkey_ref[...]) + mm(wv_ref[...], gvalue_ref[...])
    gsrc_ref[...] = bf(gsrc_t.T)


def rows_kernel(near_ref, attended_ref, gquery_ref, matched_ref, gref_ref):
    ref_ref, gout_ref, wq_ref, wo_ref = unpack(near_ref, 4)
    matched = ref_ref[...].astype(jnp.float32) + mm(attended_ref[...], wo_ref[...])
    matched_ref[...] = bf(matched)
    gref = gout_ref[...].astype(jnp.float32) + mm_general(gquery_ref[...], wq_ref[...], NT)
    gref_ref[...] = bf(gref)


def swap(x, axis, apart):
    pairs = [(i, i ^ apart) for i in range(lax.axis_size(axis))]
    return lax.ppermute(x, axis, pairs)


def at(x, index, axis=0):
    return lax.dynamic_index_in_dim(x, index, axis, False)


def laid(near, far, side, axis=0):
    shape = near.shape[:axis] + (2,) + near.shape[axis:]
    out = lax.dynamic_update_index_in_dim(jnp.zeros(shape, near.dtype), near, side, axis)
    return lax.dynamic_update_index_in_dim(out, far, 1 - side, axis)


def add(near, far):
    return (near.astype(jnp.float32) + far.astype(jnp.float32)).astype(near.dtype)


def halve(x, step, axis=0):
    mesh_axis, bit, side = step
    return add(at(x, side, axis), swap(at(x, 1 - side, axis), mesh_axis, bit))


def double(x, step, axis=0):
    mesh_axis, bit, side = step
    return laid(x, swap(x, mesh_axis, bit), side, axis)


def bit_steps(mesh_axis):
    me = lax.axis_index(mesh_axis)
    bits = range(lax.axis_size(mesh_axis).bit_length() - 1)
    return [(mesh_axis, 1 << bit, (me >> bit) % 2) for bit in bits]


def scatter_direct(x, mesh_axis):
    me, count = lax.axis_index(mesh_axis), lax.axis_size(mesh_axis)
    total = at(x, me).astype(jnp.float32)
    for piece in [swap(at(x, me ^ apart), mesh_axis, apart) for apart in range(1, count)]:
        total = total + piece.astype(jnp.float32)
    return total.astype(x.dtype)


def gather_direct(x, mesh_axis):
    me, count = lax.axis_index(mesh_axis), lax.axis_size(mesh_axis)
    pieces = [x] + [swap(x, mesh_axis, apart) for apart in range(1, count)]
    out = jnp.zeros((count,) + x.shape, x.dtype)
    for apart, piece in enumerate(pieces):
        out = lax.dynamic_update_index_in_dim(out, piece, me ^ apart, 0)
    return out


def combine_stats(parts):
    peak = functools.reduce(jnp.maximum, [part[0] for part in parts])
    factors = [jnp.exp2(part[0] - peak) for part in parts]
    total = sum(factor * part[1] for factor, part in zip(factors, parts))
    dots = sum(factor * part[2] for factor, part in zip(factors, parts))
    return jnp.stack([peak, total, dots])


def vmem_call(kernel, name, out_shape, scratch, limit, flops, moved, args, scalars=0):
    specs = [pl.BlockSpec(memory_space=pltpu.SMEM)] * scalars
    specs += [pl.BlockSpec(memory_space=pltpu.VMEM)] * (len(args) - scalars)
    return pl.pallas_call(
        kernel,
        name=name,
        out_shape=out_shape,
        in_specs=specs,
        out_specs=[pl.BlockSpec(memory_space=pltpu.VMEM)] * len(out_shape),
        scratch_shapes=scratch,
        compiler_params=pltpu.CompilerParams(vmem_limit_bytes=limit),
        cost_estimate=pl.CostEstimate(flops=flops, bytes_accessed=moved, transcendentals=0),
    )(*args)


def on_device(ref_feats, src_feats, grad_out, w_query, w_key, w_value, w_out, intersection):
    ref_rows = ref_feats[0]
    src_rows = src_feats[0]
    out_grad = grad_out[0]
    listed = jnp.where(intersection[0] == 1, 1, 0)
    rows, width = ref_rows.shape
    core_step = bit_steps("core")[0]
    chip_steps = bit_steps("chip")
    key_rows = src_rows.shape[0]
    key_total = key_rows * lax.axis_size("chip") * lax.axis_size("core")

    source_all = src_rows
    projections = (w_query, w_out, w_key, w_value)
    for count, step in enumerate(chip_steps[::-1]):
        source_all = double(source_all, step, count)
        if count == 0:
            source_all, projections = lax.optimization_barrier((source_all, projections))
    near_pack = jnp.concatenate([ref_rows, out_grad, *projections[:2]], axis=0)
    far_pack = jnp.concatenate(projections[2:], axis=0)
    source_all = double(source_all, core_step, len(chip_steps)).reshape(key_total, width)

    f32, b16 = jnp.float32, jnp.bfloat16
    shape, vmem = jax.ShapeDtypeStruct, pltpu.VMEM
    unit = 2 * rows * width * width
    query_blocks, steps = rows // BLOCK, key_total // STEP
    stacked = HEADS * BLOCK
    blocks = (query_blocks * steps, stacked, STEP)
    row_like = (query_blocks, stacked, 128)
    col_like = vmem((steps, HEADS, 8, STEP), f32)
    room = (16 << 20) + max(0, rows * key_total * HEADS * 18 - (36 << 20))
    left, grad_left = vmem_call(
        functools.partial(project_kernel, HEADS),
        "project_reference",
        [
            shape((query_blocks, stacked, width), b16),
            shape((query_blocks, stacked, width), b16),
        ],
        [],
        8 << 20,
        4 * unit,
        1 << 20,
        (near_pack,),
    )
    row_peak, row_inverse, col_stats, scores, product = vmem_call(
        functools.partial(stats_kernel, HEADS),
        "match_stats",
        [
            shape(row_like, f32),
            shape(row_like, f32),
            shape((3, HEADS, key_total), f32),
            shape(blocks, f32),
            shape(blocks, b16),
        ],
        [
            vmem((width, key_total), b16),
            vmem((width, key_total), b16),
            vmem((stacked, STEP), f32),
            vmem(row_like, f32),
            col_like,
            col_like,
            col_like,
        ],
        room,
        60 * unit,
        8 << 20,
        (listed, left, grad_left, far_pack, source_all),
        scalars=1,
    )
    near_stats = col_stats
    keys, values, query_t, grad_t = vmem_call(
        functools.partial(side_kernel, HEADS),
        "project_for_grads",
        [
            shape((key_total, width), b16),
            shape((key_total, width), b16),
            shape((query_blocks, width, stacked), b16),
            shape((query_blocks, width, stacked), b16),
        ],
        [],
        8 << 20,
        8 * unit,
        2 << 20,
        (near_pack, far_pack, source_all),
    )
    for mesh_axis, bit, _ in chip_steps:
        near_stats = combine_stats([near_stats, swap(near_stats, mesh_axis, bit)])
    far_stats = swap(near_stats, "core", 1)
    attended, grad_query, grad_key, grad_value, weight_part = vmem_call(
        functools.partial(grads_kernel, HEADS),
        "match_grads",
        [
            shape((rows, width), b16),
            shape((rows, width), b16),
            shape((width, key_total), b16),
            shape((width, key_total), b16),
            shape((4, width, width), b16),
        ],
        [
            vmem((steps, stacked, STEP), f32),
            vmem((steps, stacked, STEP), b16),
            vmem((stacked, STEP), b16),
            vmem((stacked, 128), f32),
            vmem((4, steps, HEADS, 8, STEP), f32),
            vmem((query_blocks, BLOCK, width), f32),
            vmem((query_blocks, BLOCK, width), f32),
            vmem((steps, width, STEP), f32),
            vmem((steps, width, STEP), f32),
        ],
        room,
        100 * unit,
        8 << 20,
        (listed, scores, product, keys, values, query_t, grad_t, row_peak, row_inverse, col_stats,
         near_stats, far_stats, near_pack, source_all),
        scalars=1,
    )
    (source_part,) = vmem_call(
        source_kernel,
        "source_grads",
        [shape((key_total, width), b16)],
        [],
        8 << 20,
        8 * unit,
        2 << 20,
        (far_pack, grad_key, grad_value),
    )

    scans = lax.axis_size("scan")
    weights = weight_part.reshape((2, scans // 2, 2, -1, width))
    sources = source_part.reshape((2,) * (len(chip_steps) + 1) + (key_rows, width))
    source_steps = chip_steps[::-1]
    weights = halve(weights, core_step)
    sources = halve(sources, core_step, len(chip_steps))
    weights, sources = lax.optimization_barrier((weights, sources))
    weights = scatter_direct(weights.reshape((scans,) + weights.shape[2:]), "scan")
    sources = halve(sources, source_steps[0])
    weights, sources, attended, grad_query = lax.optimization_barrier(
        (weights, sources, attended, grad_query)
    )
    matched, grad_ref = vmem_call(
        rows_kernel,
        "row_outputs",
        [shape((rows, width), b16), shape((rows, width), b16)],
        [],
        8 << 20,
        4 * unit,
        2 << 20,
        (near_pack, attended, grad_query),
    )
    for step in source_steps[1:]:
        sources = halve(sources, step)
    for mesh_axis, bit, _ in chip_steps:
        weights = add(weights, swap(weights, mesh_axis, bit))
    weights, grad_src = lax.optimization_barrier((weights, sources))
    weights = gather_direct(weights, "scan")
    weights = double(weights, core_step)
    weights = weights.reshape(4, width, width).astype(f32)
    return (
        matched[None],
        grad_ref[None],
        grad_src[None],
        weights[0],
        weights[1],
        weights[2],
        weights[3],
    )


def solution(mesh):
    scans, blks = mesh.shape["scan"], mesh.shape["blk"]
    mesh = jax.sharding.Mesh(
        mesh.devices.reshape(scans, blks // 2, 2), ("scan", "chip", "core")
    )
    split = P("scan", ("chip", "core"), None)
    whole = P()
    return jax.shard_map(
        on_device,
        mesh=mesh,
        in_specs=(split, split, split, whole, whole, whole, whole, split),
        out_specs=(split, split, split, whole, whole, whole, whole),
        check_vma=False,
    )
```

```python
import functools
import math

import jax
import jax.numpy as jnp
from jax import lax
from jax.experimental import pallas as pl
from jax.experimental.pallas import tpu as pltpu
from jax.sharding import PartitionSpec as P

HEADS = 4
BLOCK = 128
NEG = -1e30
FLOOR = -1e29
LOG2E = math.log2(math.e)

NT = (((1,), (1,)), ((), ()))
TN = (((0,), (0,)), ((), ()))
TT = (((0,), (1,)), ((), ()))


def mm(left, right):
    return jnp.dot(left, right, preferred_element_type=jnp.float32)


def mm_general(left, right, dims):
    return lax.dot_general(left, right, dims, preferred_element_type=jnp.float32)


def bf(x):
    return x.astype(jnp.bfloat16)


def lane_row(width, head, head_dim):
    lanes = lax.broadcasted_iota(jnp.int32, (1, width), 1) // head_dim
    return bf(jnp.where(lanes == head, 1.0, 0.0))


def spread(reduced, like):
    return jnp.broadcast_to(reduced, like.shape)


STRIP = 32
STEP = 256


def by_eight(x):
    return x.reshape(x.shape[0] // 8, 8, x.shape[1])


def listed_steps(inter_ref, query_block, work):
    per_step = STEP // BLOCK

    def visit(step, carry):
        listed = [inter_ref[query_block, step * per_step + k] == 1 for k in range(per_step)]

        @pl.when(functools.reduce(jnp.logical_or, listed))
        def _():
            work(query_block, step, listed)

        return carry

    lax.fori_loop(0, inter_ref.shape[1] // per_step, visit, 0)


def each_listed(inter_ref, work):
    def visit(query_block, carry):
        listed_steps(inter_ref, query_block, work)
        return carry

    lax.fori_loop(0, inter_ref.shape[0], visit, 0)


def head_strips(heads):
    for head in range(heads):
        spans = [slice(first, first + STRIP) for first in range(0, BLOCK, STRIP)]
        yield head, [slice(head * BLOCK + a.start, head * BLOCK + a.stop) for a in spans]


def score_block(query_block, step, listed, left_ref, key_t_ref, score_ref):
    span = pl.ds(pl.multiple_of(step * STEP, STEP), STEP)
    bias = jnp.concatenate(
        [jnp.full((1, BLOCK), jnp.where(flag, 0.0, NEG), jnp.float32) for flag in listed], axis=1
    )
    score_ref[...] = mm(left_ref[query_block], key_t_ref[:, span]) * LOG2E + bias


def unpack(packed_ref, count):
    total, width = packed_ref.shape
    rows = (total - 2 * width) // 2
    sizes = [rows] * (count - 2) + [width, width]
    return [packed_ref.at[pl.ds(sum(sizes[:k]), sizes[k])] for k in range(count)]


def project_kernel(heads, near_ref, left_ref, gleft_ref):
    ref_ref, gout_ref, wq_ref, wo_ref = unpack(near_ref, 4)
    rows, width = ref_ref.shape
    head_dim = width // heads
    query = bf(bf(mm(ref_ref[...], wq_ref[...])).astype(jnp.float32) * head_dim ** -0.5)
    grad = bf(mm_general(gout_ref[...], wo_ref[...], NT))
    for query_block in range(rows // BLOCK):
        span = slice(query_block * BLOCK, (query_block + 1) * BLOCK)
        for head in range(heads):
            own = lane_row(width, head, head_dim)
            left_ref[query_block, head * BLOCK : (head + 1) * BLOCK, :] = query[span] * own
            gleft_ref[query_block, head * BLOCK : (head + 1) * BLOCK, :] = grad[span] * own


def stats_kernel(
    heads, inter_ref, left_ref, gleft_ref, far_ref, src_ref,
    peak_ref, inverse_ref, col_ref, score_ref, product_ref,
    key_t_ref, value_t_ref, prob_ref, total_ref, col_peak_ref, col_total_ref, col_dot_ref,
):
    wk_ref, wv_ref = unpack(far_ref, 2)
    rows, key_total = left_ref.shape[0] * BLOCK, src_ref.shape[0]
    key_t_ref[...] = bf(mm_general(wk_ref[...], src_ref[...], TT))
    value_t_ref[...] = bf(mm_general(wv_ref[...], src_ref[...], TT))
    steps = key_total // STEP
    peak_ref[...] = jnp.full(peak_ref.shape, 2.0 * NEG, jnp.float32)
    total_ref[...] = jnp.zeros(total_ref.shape, jnp.float32)
    col_peak_ref[...] = jnp.full(col_peak_ref.shape, FLOOR, jnp.float32)
    col_total_ref[...] = jnp.zeros(col_total_ref.shape, jnp.float32)
    col_dot_ref[...] = jnp.zeros(col_dot_ref.shape, jnp.float32)
    tiles = [slice(first, first + 128) for first in range(0, STEP, 128)]

    def peaks(query_block, step, listed):
        block_ref = score_ref.at[query_block * steps + step]
        score_block(query_block, step, listed, left_ref, key_t_ref, block_ref)
        for head, spans in head_strips(heads):
            col_peaks = [col_peak_ref[step, head, :, lanes] for lanes in tiles]
            for span in spans:
                row_peak = peak_ref[query_block, span, :]
                for at, lanes in enumerate(tiles):
                    scores = block_ref[span, lanes]
                    row_peak = jnp.maximum(row_peak, scores)
                    col_peaks[at] = jnp.maximum(col_peaks[at], by_eight(scores).max(axis=0))
                peak_ref[query_block, span, :] = row_peak
            for at, lanes in enumerate(tiles):
                col_peak_ref[step, head, :, lanes] = col_peaks[at]

    each_listed(inter_ref, peaks)
    for query_block in range(rows // BLOCK):
        peak = peak_ref[query_block]
        peak_ref[query_block] = spread(peak.max(axis=1, keepdims=True), peak)
    for step in range(steps):
        for head in range(heads):
            peak = col_peak_ref[step, head]
            col_peak_ref[step, head] = spread(peak.max(axis=0, keepdims=True), peak)

    def totals(query_block, step, listed):
        score_now, product_now = [
            ref.at[query_block * steps + step] for ref in (score_ref, product_ref)
        ]
        span = pl.ds(pl.multiple_of(step * STEP, STEP), STEP)
        prob_ref[...] = mm(gleft_ref[query_block], value_t_ref[:, span])
        for head, spans in head_strips(heads):
            col_totals = [col_total_ref[step, head, :, lanes] for lanes in tiles]
            for span in spans:
                row_peak = by_eight(peak_ref[query_block, span, :])
                row_total = by_eight(total_ref[query_block, span, :])
                for at, lanes in enumerate(tiles):
                    scores = by_eight(score_now[span, lanes])
                    row_exp = jnp.exp2(scores - row_peak)
                    col_exp = jnp.exp2(scores - col_peak_ref[step, head, :, lanes][None])
                    row_total = row_total + row_exp
                    product = row_exp * col_exp * by_eight(prob_ref[span, lanes])
                    product_now[span, lanes] = bf(product.reshape(STRIP, 128))
                    col_totals[at] = col_totals[at] + col_exp.sum(axis=0)
                total_ref[query_block, span, :] = row_total.reshape(STRIP, 128)
            for at, lanes in enumerate(tiles):
                col_total_ref[step, head, :, lanes] = col_totals[at]

    each_listed(inter_ref, totals)
    for query_block in range(rows // BLOCK):
        total = total_ref[query_block]
        inverse_ref[query_block] = spread(1.0 / total.sum(axis=1, keepdims=True), total)

    def dots(query_block, step, listed):
        product_now = product_ref.at[query_block * steps + step]
        for head, spans in head_strips(heads):
            col_dots = [col_dot_ref[step, head, :, lanes] for lanes in tiles]
            for span in spans:
                inverse = inverse_ref[query_block, span, :]
                for at, lanes in enumerate(tiles):
                    product = by_eight(product_now[span, lanes].astype(jnp.float32) * inverse)
                    col_dots[at] = col_dots[at] + product.sum(axis=0)
            for at, lanes in enumerate(tiles):
                col_dot_ref[step, head, :, lanes] = col_dots[at]

    each_listed(inter_ref, dots)
    for step in range(steps):
        lanes = slice(step * STEP, (step + 1) * STEP)
        for head in range(heads):
            mine = slice(head, head + 1)
            col_ref[0, mine, lanes] = col_peak_ref[step, head, 0:1, :]
            col_ref[1, mine, lanes] = col_total_ref[step, head].sum(axis=0, keepdims=True)
            col_ref[2, mine, lanes] = col_dot_ref[step, head].sum(axis=0, keepdims=True)


def side_kernel(
    heads, near_ref, far_ref, src_ref, key_ref, value_ref, query_t_ref, grad_t_ref
):
    ref_ref, gout_ref, wq_ref, wo_ref = unpack(near_ref, 4)
    wk_ref, wv_ref = unpack(far_ref, 2)
    rows, width = ref_ref.shape
    head_dim = width // heads
    key_ref[...] = bf(mm(src_ref[...], wk_ref[...]))
    value_ref[...] = bf(mm(src_ref[...], wv_ref[...]))
    query_t = bf(mm_general(wq_ref[...], ref_ref[...], TT)).astype(jnp.float32)
    query_t = query_t * (2.0 * head_dim ** -0.5)
    grad_t = mm_general(wo_ref[...], gout_ref[...], NT)
    for query_block in range(rows // BLOCK):
        span = slice(query_block * BLOCK, (query_block + 1) * BLOCK)
        query_t_ref[query_block] = bf(query_t[:, span])
        grad_t_ref[query_block] = bf(grad_t[:, span])


def grads_kernel(
    heads, inter_ref, score_ref, product_ref, key_ref, value_ref,
    query_t_ref, grad_t_ref, peak_ref, inverse_ref, own_ref, near_ref, far_ref, packed_ref, src_ref,
    attended_ref, gquery_ref, gkey_ref, gvalue_ref, weight_ref,
    rest_ref, match_ref, gscore_ref, dot_ref, col_ref,
    att_ref, gq_ref, gk_ref, gv_ref,
):
    ref_ref, gout_ref = unpack(packed_ref, 4)[:2]
    rows, width = ref_ref.shape
    key_total = src_ref.shape[0]
    steps = key_total // STEP
    head_dim = width // heads
    tiles = [slice(first, first + 128) for first in range(0, STEP, 128)]

    peak = jnp.maximum(near_ref[0], far_ref[0])
    near, far = jnp.exp2(near_ref[0] - peak), jnp.exp2(far_ref[0] - peak)
    inverse = 1.0 / (near * near_ref[1] + far * far_ref[1])
    half = (near * near_ref[2] + far * far_ref[2]) * inverse * 0.5
    factor = jnp.exp2(own_ref[0] - peak) * inverse
    for kind, values in enumerate((peak, inverse, factor, half)):
        for head in range(heads):
            for step in range(steps):
                piece = values[head : head + 1, step * STEP : (step + 1) * STEP]
                col_ref[kind, step, head] = jnp.broadcast_to(piece, (8, STEP))
    for ref in (att_ref, gq_ref, gk_ref, gv_ref):
        ref[...] = jnp.zeros(ref.shape, jnp.float32)

    def products(query_block, step, listed):
        score_now, product_now = [
            ref.at[query_block * steps + step] for ref in (score_ref, product_ref)
        ]
        rest_now, match_now = rest_ref.at[step], match_ref.at[step]
        for head, spans in head_strips(heads):
            for span in spans:
                row_peak = by_eight(peak_ref[query_block, span, :])
                row_inverse = by_eight(inverse_ref[query_block, span, :])
                row_dot = by_eight(dot_ref[span, :])
                for lanes in tiles:
                    col_peak, col_inverse, col_factor, col_half = [
                        col_ref[kind, step, head, :, lanes][None] for kind in range(4)
                    ]
                    scores = by_eight(score_now[span, lanes])
                    row_prob = jnp.exp2(scores - row_peak) * row_inverse
                    col_prob = jnp.exp2(scores - col_peak) * col_inverse
                    product = by_eight(product_now[span, lanes].astype(jnp.float32))
                    product = product * row_inverse * col_factor
                    row_dot = row_dot + product
                    match_now[span, lanes] = bf((row_prob * col_prob).reshape(STRIP, 128))
                    rest_now[span, lanes] = (product - col_prob * col_half).reshape(STRIP, 128)
                dot_ref[span, :] = row_dot.reshape(STRIP, 128)

    def own_lanes(stacked):
        lane = lax.broadcasted_iota(jnp.int32, (BLOCK, 128), 1)
        tiles_out = []
        for first in range(0, width, 128):
            out = None
            for head in range(first // head_dim, (first + 128) // head_dim):
                piece = stacked[head * BLOCK : (head + 1) * BLOCK, first : first + 128]
                out = piece if out is None else jnp.where(lane < head * head_dim - first, out, piece)
            tiles_out.append(out)
        return jnp.concatenate(tiles_out, axis=1)

    def outputs(query_block, step, listed):
        score_now, rest_now, match_now = [
            score_ref.at[query_block * steps + step], rest_ref.at[step], match_ref.at[step]
        ]
        for _, spans in head_strips(heads):
            for span in spans:
                row_peak = peak_ref[query_block, span, :]
                row_half = dot_ref[span, :] * inverse_ref[query_block, span, :]
                for lanes in tiles:
                    row_part = jnp.exp2(score_now[span, lanes] - row_peak) * row_half
                    gscore_ref[span, lanes] = bf(rest_now[span, lanes] - row_part)
        span = pl.ds(pl.multiple_of(step * STEP, STEP), STEP)
        att_ref[query_block] += own_lanes(mm(match_now[...], value_ref[span, :]))
        gq_ref[query_block] += own_lanes(mm(gscore_ref[...], key_ref[span, :]))
        for head in range(heads):
            mine = slice(head * head_dim, (head + 1) * head_dim)
            rows_of = slice(head * BLOCK, (head + 1) * BLOCK)
            gk_ref[step, mine, :] += mm(query_t_ref[query_block, mine, :], gscore_ref[rows_of, :])
            gv_ref[step, mine, :] += mm(grad_t_ref[query_block, mine, :], match_now[rows_of, :])

    def query_rows(query_block, carry):
        dot_ref[...] = jnp.zeros(dot_ref.shape, jnp.float32)
        listed_steps(inter_ref, query_block, products)
        dot = dot_ref[...]
        dot_ref[...] = spread(dot.sum(axis=1, keepdims=True) * 0.5, dot)
        listed_steps(inter_ref, query_block, outputs)
        return carry

    lax.fori_loop(0, rows // BLOCK, query_rows, 0)
    attended = bf(att_ref[...]).reshape(rows, width)
    gquery = bf(gq_ref[...] * (2.0 * head_dim ** -0.5)).reshape(rows, width)
    attended_ref[...] = attended
    gquery_ref[...] = gquery
    for step in range(steps):
        gkey_ref[:, step * STEP : (step + 1) * STEP] = bf(gk_ref[step])
        gvalue_ref[:, step * STEP : (step + 1) * STEP] = bf(gv_ref[step])
    weight_ref[0] = bf(mm_general(ref_ref[...], gquery, TN))
    weight_ref[1] = bf(mm(gkey_ref[...], src_ref[...]).T)
    weight_ref[2] = bf(mm(gvalue_ref[...], src_ref[...]).T)
    weight_ref[3] = bf(mm_general(attended, gout_ref[...], TN))


def source_kernel(far_ref, gkey_ref, gvalue_ref, gsrc_ref):
    wk_ref, wv_ref = unpack(far_ref, 2)
    gsrc_t = mm(wk_ref[...], gkey_ref[...]) + mm(wv_ref[...], gvalue_ref[...])
    gsrc_ref[...] = bf(gsrc_t.T)


def rows_kernel(near_ref, attended_ref, gquery_ref, matched_ref, gref_ref):
    ref_ref, gout_ref, wq_ref, wo_ref = unpack(near_ref, 4)
    matched = ref_ref[...].astype(jnp.float32) + mm(attended_ref[...], wo_ref[...])
    matched_ref[...] = bf(matched)
    gref = gout_ref[...].astype(jnp.float32) + mm_general(gquery_ref[...], wq_ref[...], NT)
    gref_ref[...] = bf(gref)


def swap(x, axis, apart):
    pairs = [(i, i ^ apart) for i in range(lax.axis_size(axis))]
    return lax.ppermute(x, axis, pairs)


def at(x, index, axis=0):
    return lax.dynamic_index_in_dim(x, index, axis, False)


def laid(near, far, side, axis=0):
    shape = near.shape[:axis] + (2,) + near.shape[axis:]
    out = lax.dynamic_update_index_in_dim(jnp.zeros(shape, near.dtype), near, side, axis)
    return lax.dynamic_update_index_in_dim(out, far, 1 - side, axis)


def add(near, far):
    return (near.astype(jnp.float32) + far.astype(jnp.float32)).astype(near.dtype)


def halve(x, step, axis=0):
    mesh_axis, bit, side = step
    return add(at(x, side, axis), swap(at(x, 1 - side, axis), mesh_axis, bit))


def double(x, step, axis=0):
    mesh_axis, bit, side = step
    return laid(x, swap(x, mesh_axis, bit), side, axis)


def bit_steps(mesh_axis):
    me = lax.axis_index(mesh_axis)
    bits = range(lax.axis_size(mesh_axis).bit_length() - 1)
    return [(mesh_axis, 1 << bit, (me >> bit) % 2) for bit in bits]


def scatter_direct(x, mesh_axis):
    me, count = lax.axis_index(mesh_axis), lax.axis_size(mesh_axis)
    total = at(x, me).astype(jnp.float32)
    for piece in [swap(at(x, me ^ apart), mesh_axis, apart) for apart in range(1, count)]:
        total = total + piece.astype(jnp.float32)
    return total.astype(x.dtype)


def gather_direct(x, mesh_axis):
    me, count = lax.axis_index(mesh_axis), lax.axis_size(mesh_axis)
    pieces = [x] + [swap(x, mesh_axis, apart) for apart in range(1, count)]
    out = jnp.zeros((count,) + x.shape, x.dtype)
    for apart, piece in enumerate(pieces):
        out = lax.dynamic_update_index_in_dim(out, piece, me ^ apart, 0)
    return out


def combine_stats(parts):
    peak = functools.reduce(jnp.maximum, [part[0] for part in parts])
    factors = [jnp.exp2(part[0] - peak) for part in parts]
    total = sum(factor * part[1] for factor, part in zip(factors, parts))
    dots = sum(factor * part[2] for factor, part in zip(factors, parts))
    return jnp.stack([peak, total, dots])


def vmem_call(kernel, name, out_shape, scratch, limit, flops, moved, args, scalars=0):
    specs = [pl.BlockSpec(memory_space=pltpu.SMEM)] * scalars
    specs += [pl.BlockSpec(memory_space=pltpu.VMEM)] * (len(args) - scalars)
    return pl.pallas_call(
        kernel,
        name=name,
        out_shape=out_shape,
        in_specs=specs,
        out_specs=[pl.BlockSpec(memory_space=pltpu.VMEM)] * len(out_shape),
        scratch_shapes=scratch,
        compiler_params=pltpu.CompilerParams(vmem_limit_bytes=limit),
        cost_estimate=pl.CostEstimate(flops=flops, bytes_accessed=moved, transcendentals=0),
    )(*args)


def on_device(ref_feats, src_feats, grad_out, w_query, w_key, w_value, w_out, intersection):
    ref_rows = ref_feats[0]
    src_rows = src_feats[0]
    out_grad = grad_out[0]
    listed = jnp.where(intersection[0] == 1, 1, 0)
    rows, width = ref_rows.shape
    core_step = bit_steps("core")[0]
    chip_steps = bit_steps("chip")
    key_rows = src_rows.shape[0]
    key_total = key_rows * lax.axis_size("chip") * lax.axis_size("core")

    source_all = src_rows
    projections = (w_query, w_out, w_key, w_value)
    for count, step in enumerate(chip_steps[::-1]):
        source_all = double(source_all, step, count)
        if count == 0:
            source_all, projections = lax.optimization_barrier((source_all, projections))
    near_pack = jnp.concatenate([ref_rows, out_grad, *projections[:2]], axis=0)
    far_pack = jnp.concatenate(projections[2:], axis=0)
    source_all = double(source_all, core_step, len(chip_steps)).reshape(key_total, width)

    f32, b16 = jnp.float32, jnp.bfloat16
    shape, vmem = jax.ShapeDtypeStruct, pltpu.VMEM
    unit = 2 * rows * width * width
    query_blocks, steps = rows // BLOCK, key_total // STEP
    stacked = HEADS * BLOCK
    blocks = (query_blocks * steps, stacked, STEP)
    row_like = (query_blocks, stacked, 128)
    col_like = vmem((steps, HEADS, 8, STEP), f32)
    room = (16 << 20) + max(0, rows * key_total * HEADS * 18 - (36 << 20))
    left, grad_left = vmem_call(
        functools.partial(project_kernel, HEADS),
        "project_reference",
        [
            shape((query_blocks, stacked, width), b16),
            shape((query_blocks, stacked, width), b16),
        ],
        [],
        8 << 20,
        4 * unit,
        1 << 20,
        (near_pack,),
    )
    row_peak, row_inverse, col_stats, scores, product = vmem_call(
        functools.partial(stats_kernel, HEADS),
        "match_stats",
        [
            shape(row_like, f32),
            shape(row_like, f32),
            shape((3, HEADS, key_total), f32),
            shape(blocks, f32),
            shape(blocks, b16),
        ],
        [
            vmem((width, key_total), b16),
            vmem((width, key_total), b16),
            vmem((stacked, STEP), f32),
            vmem(row_like, f32),
            col_like,
            col_like,
            col_like,
        ],
        room,
        60 * unit,
        8 << 20,
        (listed, left, grad_left, far_pack, source_all),
        scalars=1,
    )
    near_stats = col_stats
    keys, values, query_t, grad_t = vmem_call(
        functools.partial(side_kernel, HEADS),
        "project_for_grads",
        [
            shape((key_total, width), b16),
            shape((key_total, width), b16),
            shape((query_blocks, width, BLOCK), b16),
            shape((query_blocks, width, BLOCK), b16),
        ],
        [],
        8 << 20,
        8 * unit,
        2 << 20,
        (near_pack, far_pack, source_all),
    )
    for mesh_axis, bit, _ in chip_steps:
        near_stats = combine_stats([near_stats, swap(near_stats, mesh_axis, bit)])
    far_stats = swap(near_stats, "core", 1)
    attended, grad_query, grad_key, grad_value, weight_part = vmem_call(
        functools.partial(grads_kernel, HEADS),
        "match_grads",
        [
            shape((rows, width), b16),
            shape((rows, width), b16),
            shape((width, key_total), b16),
            shape((width, key_total), b16),
            shape((4, width, width), b16),
        ],
        [
            vmem((steps, stacked, STEP), f32),
            vmem((steps, stacked, STEP), b16),
            vmem((stacked, STEP), b16),
            vmem((stacked, 128), f32),
            vmem((4, steps, HEADS, 8, STEP), f32),
            vmem((query_blocks, BLOCK, width), f32),
            vmem((query_blocks, BLOCK, width), f32),
            vmem((steps, width, STEP), f32),
            vmem((steps, width, STEP), f32),
        ],
        room,
        100 * unit,
        8 << 20,
        (listed, scores, product, keys, values, query_t, grad_t, row_peak, row_inverse, col_stats,
         near_stats, far_stats, near_pack, source_all),
        scalars=1,
    )
    (source_part,) = vmem_call(
        source_kernel,
        "source_grads",
        [shape((key_total, width), b16)],
        [],
        8 << 20,
        8 * unit,
        2 << 20,
        (far_pack, grad_key, grad_value),
    )

    scans = lax.axis_size("scan")
    weights = weight_part.reshape((2, scans // 2, 2, -1, width))
    sources = source_part.reshape((2,) * (len(chip_steps) + 1) + (key_rows, width))
    source_steps = list(zip(chip_steps, range(len(chip_steps) - 1, -1, -1)))
    weights = halve(weights, core_step)
    sources = halve(sources, core_step, len(chip_steps))
    weights, sources = lax.optimization_barrier((weights, sources))
    weights = scatter_direct(weights.reshape((scans,) + weights.shape[2:]), "scan")
    sources = halve(sources, *source_steps[0])
    weights, sources, attended, grad_query = lax.optimization_barrier(
        (weights, sources, attended, grad_query)
    )
    matched, grad_ref = vmem_call(
        rows_kernel,
        "row_outputs",
        [shape((rows, width), b16), shape((rows, width), b16)],
        [],
        8 << 20,
        4 * unit,
        2 << 20,
        (near_pack, attended, grad_query),
    )
    for step in source_steps[1:]:
        sources = halve(sources, *step)
    for mesh_axis, bit, _ in chip_steps:
        weights = add(weights, swap(weights, mesh_axis, bit))
    weights, grad_src = lax.optimization_barrier((weights, sources))
    weights = gather_direct(weights, "scan")
    weights = double(weights, core_step)
    weights = weights.reshape(4, width, width).astype(f32)
    return (
        matched[None],
        grad_ref[None],
        grad_src[None],
        weights[0],
        weights[1],
        weights[2],
        weights[3],
    )


def solution(mesh):
    scans, blks = mesh.shape["scan"], mesh.shape["blk"]
    mesh = jax.sharding.Mesh(
        mesh.devices.reshape(scans, blks // 2, 2), ("scan", "chip", "core")
    )
    split = P("scan", ("chip", "core"), None)
    whole = P()
    return jax.shard_map(
        on_device,
        mesh=mesh,
        in_specs=(split, split, split, whole, whole, whole, whole, split),
        out_specs=(split, split, split, whole, whole, whole, whole),
        check_vma=False,
    )
```

```python
import functools
import math

import jax
import jax.numpy as jnp
from jax import lax
from jax.experimental import pallas as pl
from jax.experimental.pallas import tpu as pltpu
from jax.sharding import PartitionSpec as P

HEADS = 4
BLOCK = 128
NEG = -1e30
FLOOR = -1e29
LOG2E = math.log2(math.e)

NT = (((1,), (1,)), ((), ()))
TN = (((0,), (0,)), ((), ()))
TT = (((0,), (1,)), ((), ()))


def mm(left, right):
    return jnp.dot(left, right, preferred_element_type=jnp.float32)


def mm_general(left, right, dims):
    return lax.dot_general(left, right, dims, preferred_element_type=jnp.float32)


def bf(x):
    return x.astype(jnp.bfloat16)


def lane_row(width, head, head_dim):
    lanes = lax.broadcasted_iota(jnp.int32, (1, width), 1) // head_dim
    return bf(jnp.where(lanes == head, 1.0, 0.0))


def spread(reduced, like):
    return jnp.broadcast_to(reduced, like.shape)


STRIP = 64
STEP = 256


def by_eight(x):
    return x.reshape(x.shape[0] // 8, 8, x.shape[1])


def listed_steps(inter_ref, query_block, work):
    per_step = STEP // BLOCK

    def visit(step, carry):
        listed = [inter_ref[query_block, step * per_step + k] == 1 for k in range(per_step)]

        @pl.when(functools.reduce(jnp.logical_or, listed))
        def _():
            work(query_block, step, listed)

        return carry

    lax.fori_loop(0, inter_ref.shape[1] // per_step, visit, 0)


def each_listed(inter_ref, work):
    def visit(query_block, carry):
        listed_steps(inter_ref, query_block, work)
        return carry

    lax.fori_loop(0, inter_ref.shape[0], visit, 0)


def head_strips(heads):
    for head in range(heads):
        spans = [slice(first, first + STRIP) for first in range(0, BLOCK, STRIP)]
        yield head, [slice(head * BLOCK + a.start, head * BLOCK + a.stop) for a in spans]


def score_block(query_block, step, listed, left_ref, key_t_ref, score_ref):
    span = pl.ds(pl.multiple_of(step * STEP, STEP), STEP)
    bias = jnp.concatenate(
        [jnp.full((1, BLOCK), jnp.where(flag, 0.0, NEG), jnp.float32) for flag in listed], axis=1
    )
    score_ref[...] = mm(left_ref[query_block], key_t_ref[:, span]) * LOG2E + bias


def unpack(packed_ref, count):
    total, width = packed_ref.shape
    rows = (total - 2 * width) // 2
    sizes = [rows] * (count - 2) + [width, width]
    return [packed_ref.at[pl.ds(sum(sizes[:k]), sizes[k])] for k in range(count)]


def project_kernel(heads, near_ref, left_ref, gleft_ref):
    ref_ref, gout_ref, wq_ref, wo_ref = unpack(near_ref, 4)
    rows, width = ref_ref.shape
    head_dim = width // heads
    query = bf(bf(mm(ref_ref[...], wq_ref[...])).astype(jnp.float32) * head_dim ** -0.5)
    grad = bf(mm_general(gout_ref[...], wo_ref[...], NT))
    for query_block in range(rows // BLOCK):
        span = slice(query_block * BLOCK, (query_block + 1) * BLOCK)
        for head in range(heads):
            own = lane_row(width, head, head_dim)
            left_ref[query_block, head * BLOCK : (head + 1) * BLOCK, :] = query[span] * own
            gleft_ref[query_block, head * BLOCK : (head + 1) * BLOCK, :] = grad[span] * own


def stats_kernel(
    heads, inter_ref, left_ref, gleft_ref, far_ref, src_ref,
    peak_ref, inverse_ref, col_ref, score_ref, product_ref,
    key_t_ref, value_t_ref, prob_ref, total_ref, col_peak_ref, col_total_ref, col_dot_ref,
):
    wk_ref, wv_ref = unpack(far_ref, 2)
    rows, key_total = left_ref.shape[0] * BLOCK, src_ref.shape[0]
    key_t_ref[...] = bf(mm_general(wk_ref[...], src_ref[...], TT))
    value_t_ref[...] = bf(mm_general(wv_ref[...], src_ref[...], TT))
    steps = key_total // STEP
    peak_ref[...] = jnp.full(peak_ref.shape, 2.0 * NEG, jnp.float32)
    total_ref[...] = jnp.zeros(total_ref.shape, jnp.float32)
    col_peak_ref[...] = jnp.full(col_peak_ref.shape, FLOOR, jnp.float32)
    col_total_ref[...] = jnp.zeros(col_total_ref.shape, jnp.float32)
    col_dot_ref[...] = jnp.zeros(col_dot_ref.shape, jnp.float32)
    tiles = [slice(first, first + 128) for first in range(0, STEP, 128)]

    def peaks(query_block, step, listed):
        block_ref = score_ref.at[query_block * steps + step]
        score_block(query_block, step, listed, left_ref, key_t_ref, block_ref)
        for head, spans in head_strips(heads):
            col_peaks = [col_peak_ref[step, head, :, lanes] for lanes in tiles]
            for span in spans:
                row_peak = peak_ref[query_block, span, :]
                for at, lanes in enumerate(tiles):
                    scores = block_ref[span, lanes]
                    row_peak = jnp.maximum(row_peak, scores)
                    col_peaks[at] = jnp.maximum(col_peaks[at], by_eight(scores).max(axis=0))
                peak_ref[query_block, span, :] = row_peak
            for at, lanes in enumerate(tiles):
                col_peak_ref[step, head, :, lanes] = col_peaks[at]

    each_listed(inter_ref, peaks)
    for query_block in range(rows // BLOCK):
        peak = peak_ref[query_block]
        peak_ref[query_block] = spread(peak.max(axis=1, keepdims=True), peak)
    for step in range(steps):
        for head in range(heads):
            peak = col_peak_ref[step, head]
            col_peak_ref[step, head] = spread(peak.max(axis=0, keepdims=True), peak)

    def totals(query_block, step, listed):
        score_now, product_now = [
            ref.at[query_block * steps + step] for ref in (score_ref, product_ref)
        ]
        span = pl.ds(pl.multiple_of(step * STEP, STEP), STEP)
        prob_ref[...] = mm(gleft_ref[query_block], value_t_ref[:, span])
        for head, spans in head_strips(heads):
            col_totals = [col_total_ref[step, head, :, lanes] for lanes in tiles]
            for span in spans:
                row_peak = by_eight(peak_ref[query_block, span, :])
                row_total = by_eight(total_ref[query_block, span, :])
                for at, lanes in enumerate(tiles):
                    scores = by_eight(score_now[span, lanes])
                    row_exp = jnp.exp2(scores - row_peak)
                    col_exp = jnp.exp2(scores - col_peak_ref[step, head, :, lanes][None])
                    row_total = row_total + row_exp
                    product = row_exp * col_exp * by_eight(prob_ref[span, lanes])
                    product_now[span, lanes] = bf(product.reshape(STRIP, 128))
                    col_totals[at] = col_totals[at] + col_exp.sum(axis=0)
                total_ref[query_block, span, :] = row_total.reshape(STRIP, 128)
            for at, lanes in enumerate(tiles):
                col_total_ref[step, head, :, lanes] = col_totals[at]

    each_listed(inter_ref, totals)
    for query_block in range(rows // BLOCK):
        total = total_ref[query_block]
        inverse_ref[query_block] = spread(1.0 / total.sum(axis=1, keepdims=True), total)

    def dots(query_block, step, listed):
        product_now = product_ref.at[query_block * steps + step]
        for head, spans in head_strips(heads):
            col_dots = [col_dot_ref[step, head, :, lanes] for lanes in tiles]
            for span in spans:
                inverse = inverse_ref[query_block, span, :]
                for at, lanes in enumerate(tiles):
                    product = by_eight(product_now[span, lanes].astype(jnp.float32) * inverse)
                    col_dots[at] = col_dots[at] + product.sum(axis=0)
            for at, lanes in enumerate(tiles):
                col_dot_ref[step, head, :, lanes] = col_dots[at]

    each_listed(inter_ref, dots)
    for step in range(steps):
        lanes = slice(step * STEP, (step + 1) * STEP)
        for head in range(heads):
            mine = slice(head, head + 1)
            col_ref[0, mine, lanes] = col_peak_ref[step, head, 0:1, :]
            col_ref[1, mine, lanes] = col_total_ref[step, head].sum(axis=0, keepdims=True)
            col_ref[2, mine, lanes] = col_dot_ref[step, head].sum(axis=0, keepdims=True)


def side_kernel(
    heads, near_ref, far_ref, src_ref, key_ref, value_ref, query_t_ref, grad_t_ref
):
    ref_ref, gout_ref, wq_ref, wo_ref = unpack(near_ref, 4)
    wk_ref, wv_ref = unpack(far_ref, 2)
    rows, width = ref_ref.shape
    head_dim = width // heads
    key_ref[...] = bf(mm(src_ref[...], wk_ref[...]))
    value_ref[...] = bf(mm(src_ref[...], wv_ref[...]))
    query_t = bf(mm_general(wq_ref[...], ref_ref[...], TT)).astype(jnp.float32)
    query_t = query_t * (2.0 * head_dim ** -0.5)
    grad_t = mm_general(wo_ref[...], gout_ref[...], NT)
    for query_block in range(rows // BLOCK):
        span = slice(query_block * BLOCK, (query_block + 1) * BLOCK)
        query_t_ref[query_block] = bf(query_t[:, span])
        grad_t_ref[query_block] = bf(grad_t[:, span])


def grads_kernel(
    heads, inter_ref, score_ref, product_ref, key_ref, value_ref,
    query_t_ref, grad_t_ref, peak_ref, inverse_ref, own_ref, near_ref, far_ref, packed_ref, src_ref,
    attended_ref, gquery_ref, gkey_ref, gvalue_ref, weight_ref,
    rest_ref, match_ref, gscore_ref, dot_ref, col_ref,
    att_ref, gq_ref, gk_ref, gv_ref,
):
    ref_ref, gout_ref = unpack(packed_ref, 4)[:2]
    rows, width = ref_ref.shape
    key_total = src_ref.shape[0]
    steps = key_total // STEP
    head_dim = width // heads
    tiles = [slice(first, first + 128) for first in range(0, STEP, 128)]

    peak = jnp.maximum(near_ref[0], far_ref[0])
    near, far = jnp.exp2(near_ref[0] - peak), jnp.exp2(far_ref[0] - peak)
    inverse = 1.0 / (near * near_ref[1] + far * far_ref[1])
    half = (near * near_ref[2] + far * far_ref[2]) * inverse * 0.5
    factor = jnp.exp2(own_ref[0] - peak) * inverse
    for kind, values in enumerate((peak, inverse, factor, half)):
        for head in range(heads):
            for step in range(steps):
                piece = values[head : head + 1, step * STEP : (step + 1) * STEP]
                col_ref[kind, step, head] = jnp.broadcast_to(piece, (8, STEP))
    for ref in (att_ref, gq_ref, gk_ref, gv_ref):
        ref[...] = jnp.zeros(ref.shape, jnp.float32)

    def products(query_block, step, listed):
        score_now, product_now = [
            ref.at[query_block * steps + step] for ref in (score_ref, product_ref)
        ]
        rest_now, match_now = rest_ref.at[step], match_ref.at[step]
        for head, spans in head_strips(heads):
            for span in spans:
                row_peak = by_eight(peak_ref[query_block, span, :])
                row_inverse = by_eight(inverse_ref[query_block, span, :])
                row_dot = by_eight(dot_ref[span, :])
                for lanes in tiles:
                    col_peak, col_inverse, col_factor, col_half = [
                        col_ref[kind, step, head, :, lanes][None] for kind in range(4)
                    ]
                    scores = by_eight(score_now[span, lanes])
                    row_prob = jnp.exp2(scores - row_peak) * row_inverse
                    col_prob = jnp.exp2(scores - col_peak) * col_inverse
                    product = by_eight(product_now[span, lanes].astype(jnp.float32))
                    product = product * row_inverse * col_factor
                    row_dot = row_dot + product
                    match_now[span, lanes] = bf((row_prob * col_prob).reshape(STRIP, 128))
                    rest_now[span, lanes] = (product - col_prob * col_half).reshape(STRIP, 128)
                dot_ref[span, :] = row_dot.reshape(STRIP, 128)

    def own_lanes(stacked):
        lane = lax.broadcasted_iota(jnp.int32, (BLOCK, 128), 1)
        tiles_out = []
        for first in range(0, width, 128):
            out = None
            for head in range(first // head_dim, (first + 128) // head_dim):
                piece = stacked[head * BLOCK : (head + 1) * BLOCK, first : first + 128]
                out = piece if out is None else jnp.where(lane < head * head_dim - first, out, piece)
            tiles_out.append(out)
        return jnp.concatenate(tiles_out, axis=1)

    def outputs(query_block, step, listed):
        score_now, rest_now, match_now = [
            score_ref.at[query_block * steps + step], rest_ref.at[step], match_ref.at[step]
        ]
        for _, spans in head_strips(heads):
            for span in spans:
                row_peak = peak_ref[query_block, span, :]
                row_half = dot_ref[span, :] * inverse_ref[query_block, span, :]
                for lanes in tiles:
                    row_part = jnp.exp2(score_now[span, lanes] - row_peak) * row_half
                    gscore_ref[span, lanes] = bf(rest_now[span, lanes] - row_part)
        span = pl.ds(pl.multiple_of(step * STEP, STEP), STEP)
        att_ref[query_block] += own_lanes(mm(match_now[...], value_ref[span, :]))
        gq_ref[query_block] += own_lanes(mm(gscore_ref[...], key_ref[span, :]))
        for head in range(heads):
            mine = slice(head * head_dim, (head + 1) * head_dim)
            rows_of = slice(head * BLOCK, (head + 1) * BLOCK)
            gk_ref[step, mine, :] += mm(query_t_ref[query_block, mine, :], gscore_ref[rows_of, :])
            gv_ref[step, mine, :] += mm(grad_t_ref[query_block, mine, :], match_now[rows_of, :])

    def query_rows(query_block, carry):
        dot_ref[...] = jnp.zeros(dot_ref.shape, jnp.float32)
        listed_steps(inter_ref, query_block, products)
        dot = dot_ref[...]
        dot_ref[...] = spread(dot.sum(axis=1, keepdims=True) * 0.5, dot)
        listed_steps(inter_ref, query_block, outputs)
        return carry

    lax.fori_loop(0, rows // BLOCK, query_rows, 0)
    attended = bf(att_ref[...]).reshape(rows, width)
    gquery = bf(gq_ref[...] * (2.0 * head_dim ** -0.5)).reshape(rows, width)
    attended_ref[...] = attended
    gquery_ref[...] = gquery
    for step in range(steps):
        gkey_ref[:, step * STEP : (step + 1) * STEP] = bf(gk_ref[step])
        gvalue_ref[:, step * STEP : (step + 1) * STEP] = bf(gv_ref[step])
    weight_ref[0] = bf(mm_general(ref_ref[...], gquery, TN))
    weight_ref[1] = bf(mm(gkey_ref[...], src_ref[...]).T)
    weight_ref[2] = bf(mm(gvalue_ref[...], src_ref[...]).T)
    weight_ref[3] = bf(mm_general(attended, gout_ref[...], TN))


def source_kernel(far_ref, gkey_ref, gvalue_ref, gsrc_ref):
    wk_ref, wv_ref = unpack(far_ref, 2)
    gsrc_t = mm(wk_ref[...], gkey_ref[...]) + mm(wv_ref[...], gvalue_ref[...])
    gsrc_ref[...] = bf(gsrc_t.T)


def rows_kernel(near_ref, attended_ref, gquery_ref, matched_ref, gref_ref):
    ref_ref, gout_ref, wq_ref, wo_ref = unpack(near_ref, 4)
    matched = ref_ref[...].astype(jnp.float32) + mm(attended_ref[...], wo_ref[...])
    matched_ref[...] = bf(matched)
    gref = gout_ref[...].astype(jnp.float32) + mm_general(gquery_ref[...], wq_ref[...], NT)
    gref_ref[...] = bf(gref)


def swap(x, axis, apart):
    pairs = [(i, i ^ apart) for i in range(lax.axis_size(axis))]
    return lax.ppermute(x, axis, pairs)


def at(x, index, axis=0):
    return lax.dynamic_index_in_dim(x, index, axis, False)


def laid(near, far, side, axis=0):
    shape = near.shape[:axis] + (2,) + near.shape[axis:]
    out = lax.dynamic_update_index_in_dim(jnp.zeros(shape, near.dtype), near, side, axis)
    return lax.dynamic_update_index_in_dim(out, far, 1 - side, axis)


def add(near, far):
    return (near.astype(jnp.float32) + far.astype(jnp.float32)).astype(near.dtype)


def halve(x, step, axis=0):
    mesh_axis, bit, side = step
    return add(at(x, side, axis), swap(at(x, 1 - side, axis), mesh_axis, bit))


def double(x, step, axis=0):
    mesh_axis, bit, side = step
    return laid(x, swap(x, mesh_axis, bit), side, axis)


def bit_steps(mesh_axis):
    me = lax.axis_index(mesh_axis)
    bits = range(lax.axis_size(mesh_axis).bit_length() - 1)
    return [(mesh_axis, 1 << bit, (me >> bit) % 2) for bit in bits]


def scatter_direct(x, mesh_axis):
    me, count = lax.axis_index(mesh_axis), lax.axis_size(mesh_axis)
    total = at(x, me).astype(jnp.float32)
    for piece in [swap(at(x, me ^ apart), mesh_axis, apart) for apart in range(1, count)]:
        total = total + piece.astype(jnp.float32)
    return total.astype(x.dtype)


def gather_direct(x, mesh_axis):
    me, count = lax.axis_index(mesh_axis), lax.axis_size(mesh_axis)
    pieces = [x] + [swap(x, mesh_axis, apart) for apart in range(1, count)]
    out = jnp.zeros((count,) + x.shape, x.dtype)
    for apart, piece in enumerate(pieces):
        out = lax.dynamic_update_index_in_dim(out, piece, me ^ apart, 0)
    return out


def combine_stats(parts):
    peak = functools.reduce(jnp.maximum, [part[0] for part in parts])
    factors = [jnp.exp2(part[0] - peak) for part in parts]
    total = sum(factor * part[1] for factor, part in zip(factors, parts))
    dots = sum(factor * part[2] for factor, part in zip(factors, parts))
    return jnp.stack([peak, total, dots])


def vmem_call(kernel, name, out_shape, scratch, limit, flops, moved, args, scalars=0):
    specs = [pl.BlockSpec(memory_space=pltpu.SMEM)] * scalars
    specs += [pl.BlockSpec(memory_space=pltpu.VMEM)] * (len(args) - scalars)
    return pl.pallas_call(
        kernel,
        name=name,
        out_shape=out_shape,
        in_specs=specs,
        out_specs=[pl.BlockSpec(memory_space=pltpu.VMEM)] * len(out_shape),
        scratch_shapes=scratch,
        compiler_params=pltpu.CompilerParams(vmem_limit_bytes=limit),
        cost_estimate=pl.CostEstimate(flops=flops, bytes_accessed=moved, transcendentals=0),
    )(*args)


def on_device(ref_feats, src_feats, grad_out, w_query, w_key, w_value, w_out, intersection):
    ref_rows = ref_feats[0]
    src_rows = src_feats[0]
    out_grad = grad_out[0]
    listed = jnp.where(intersection[0] == 1, 1, 0)
    rows, width = ref_rows.shape
    core_step = bit_steps("core")[0]
    chip_steps = bit_steps("chip")
    key_rows = src_rows.shape[0]
    key_total = key_rows * lax.axis_size("chip") * lax.axis_size("core")

    source_all = src_rows
    projections = (w_query, w_out, w_key, w_value)
    for count, step in enumerate(chip_steps[::-1]):
        source_all = double(source_all, step, count)
        if count == 0:
            source_all, projections = lax.optimization_barrier((source_all, projections))
    near_pack = jnp.concatenate([ref_rows, out_grad, *projections[:2]], axis=0)
    far_pack = jnp.concatenate(projections[2:], axis=0)
    source_all = double(source_all, core_step, len(chip_steps)).reshape(key_total, width)

    f32, b16 = jnp.float32, jnp.bfloat16
    shape, vmem = jax.ShapeDtypeStruct, pltpu.VMEM
    unit = 2 * rows * width * width
    query_blocks, steps = rows // BLOCK, key_total // STEP
    stacked = HEADS * BLOCK
    blocks = (query_blocks * steps, stacked, STEP)
    row_like = (query_blocks, stacked, 128)
    col_like = vmem((steps, HEADS, 8, STEP), f32)
    room = (16 << 20) + max(0, rows * key_total * HEADS * 18 - (36 << 20))
    left, grad_left = vmem_call(
        functools.partial(project_kernel, HEADS),
        "project_reference",
        [
            shape((query_blocks, stacked, width), b16),
            shape((query_blocks, stacked, width), b16),
        ],
        [],
        8 << 20,
        4 * unit,
        1 << 20,
        (near_pack,),
    )
    row_peak, row_inverse, col_stats, scores, product = vmem_call(
        functools.partial(stats_kernel, HEADS),
        "match_stats",
        [
            shape(row_like, f32),
            shape(row_like, f32),
            shape((3, HEADS, key_total), f32),
            shape(blocks, f32),
            shape(blocks, b16),
        ],
        [
            vmem((width, key_total), b16),
            vmem((width, key_total), b16),
            vmem((stacked, STEP), f32),
            vmem(row_like, f32),
            col_like,
            col_like,
            col_like,
        ],
        room,
        60 * unit,
        8 << 20,
        (listed, left, grad_left, far_pack, source_all),
        scalars=1,
    )
    near_stats = col_stats
    keys, values, query_t, grad_t = vmem_call(
        functools.partial(side_kernel, HEADS),
        "project_for_grads",
        [
            shape((key_total, width), b16),
            shape((key_total, width), b16),
            shape((query_blocks, width, BLOCK), b16),
            shape((query_blocks, width, BLOCK), b16),
        ],
        [],
        8 << 20,
        8 * unit,
        2 << 20,
        (near_pack, far_pack, source_all),
    )
    for mesh_axis, bit, _ in chip_steps:
        near_stats = combine_stats([near_stats, swap(near_stats, mesh_axis, bit)])
    far_stats = swap(near_stats, "core", 1)
    attended, grad_query, grad_key, grad_value, weight_part = vmem_call(
        functools.partial(grads_kernel, HEADS),
        "match_grads",
        [
            shape((rows, width), b16),
            shape((rows, width), b16),
            shape((width, key_total), b16),
            shape((width, key_total), b16),
            shape((4, width, width), b16),
        ],
        [
            vmem((steps, stacked, STEP), f32),
            vmem((steps, stacked, STEP), b16),
            vmem((stacked, STEP), b16),
            vmem((stacked, 128), f32),
            vmem((4, steps, HEADS, 8, STEP), f32),
            vmem((query_blocks, BLOCK, width), f32),
            vmem((query_blocks, BLOCK, width), f32),
            vmem((steps, width, STEP), f32),
            vmem((steps, width, STEP), f32),
        ],
        room,
        100 * unit,
        8 << 20,
        (listed, scores, product, keys, values, query_t, grad_t, row_peak, row_inverse, col_stats,
         near_stats, far_stats, near_pack, source_all),
        scalars=1,
    )
    (source_part,) = vmem_call(
        source_kernel,
        "source_grads",
        [shape((key_total, width), b16)],
        [],
        8 << 20,
        8 * unit,
        2 << 20,
        (far_pack, grad_key, grad_value),
    )

    scans = lax.axis_size("scan")
    weights = weight_part.reshape((2, scans // 2, 2, -1, width))
    sources = source_part.reshape((2,) * (len(chip_steps) + 1) + (key_rows, width))
    source_steps = list(zip(chip_steps, range(len(chip_steps) - 1, -1, -1)))
    weights = halve(weights, core_step)
    sources = halve(sources, core_step, len(chip_steps))
    weights, sources = lax.optimization_barrier((weights, sources))
    weights = scatter_direct(weights.reshape((scans,) + weights.shape[2:]), "scan")
    sources = halve(sources, *source_steps[0])
    weights, attended, grad_query = lax.optimization_barrier((weights, attended, grad_query))
    matched, grad_ref = vmem_call(
        rows_kernel,
        "row_outputs",
        [shape((rows, width), b16), shape((rows, width), b16)],
        [],
        8 << 20,
        4 * unit,
        2 << 20,
        (near_pack, attended, grad_query),
    )
    for step in source_steps[1:]:
        sources = halve(sources, *step)
    for mesh_axis, bit, _ in chip_steps:
        weights = add(weights, swap(weights, mesh_axis, bit))
    weights, grad_src = lax.optimization_barrier((weights, sources))
    weights = gather_direct(weights, "scan")
    weights = double(weights, core_step)
    weights = weights.reshape(4, width, width).astype(f32)
    return (
        matched[None],
        grad_ref[None],
        grad_src[None],
        weights[0],
        weights[1],
        weights[2],
        weights[3],
    )


def solution(mesh):
    scans, blks = mesh.shape["scan"], mesh.shape["blk"]
    mesh = jax.sharding.Mesh(
        mesh.devices.reshape(scans, blks // 2, 2), ("scan", "chip", "core")
    )
    split = P("scan", ("chip", "core"), None)
    whole = P()
    return jax.shard_map(
        on_device,
        mesh=mesh,
        in_specs=(split, split, split, whole, whole, whole, whole, split),
        out_specs=(split, split, split, whole, whole, whole, whole),
        check_vma=False,
    )
```

```python
import functools
import math

import jax
import jax.numpy as jnp
from jax import lax
from jax.experimental import pallas as pl
from jax.experimental.pallas import tpu as pltpu
from jax.sharding import PartitionSpec as P

HEADS = 4
BLOCK = 128
NEG = -1e30
FLOOR = -1e29
LOG2E = math.log2(math.e)

NT = (((1,), (1,)), ((), ()))
TN = (((0,), (0,)), ((), ()))
TT = (((0,), (1,)), ((), ()))


def mm(left, right):
    return jnp.dot(left, right, preferred_element_type=jnp.float32)


def mm_general(left, right, dims):
    return lax.dot_general(left, right, dims, preferred_element_type=jnp.float32)


def bf(x):
    return x.astype(jnp.bfloat16)


def lane_row(width, head, head_dim):
    lanes = lax.broadcasted_iota(jnp.int32, (1, width), 1) // head_dim
    return bf(jnp.where(lanes == head, 1.0, 0.0))


def spread(reduced, like):
    return jnp.broadcast_to(reduced, like.shape)


STRIP = 64
STEP = 256


def by_eight(x):
    return x.reshape(x.shape[0] // 8, 8, x.shape[1])


def listed_steps(inter_ref, query_block, work):
    per_step = STEP // BLOCK

    def visit(step, carry):
        listed = [inter_ref[query_block, step * per_step + k] == 1 for k in range(per_step)]

        @pl.when(functools.reduce(jnp.logical_or, listed))
        def _():
            work(query_block, step, listed)

        return carry

    lax.fori_loop(0, inter_ref.shape[1] // per_step, visit, 0)


def each_listed(inter_ref, work):
    def visit(query_block, carry):
        listed_steps(inter_ref, query_block, work)
        return carry

    lax.fori_loop(0, inter_ref.shape[0], visit, 0)


def head_strips(heads):
    for head in range(heads):
        spans = [slice(first, first + STRIP) for first in range(0, BLOCK, STRIP)]
        yield head, [slice(head * BLOCK + a.start, head * BLOCK + a.stop) for a in spans]


def score_block(query_block, step, listed, left_ref, key_t_ref, score_ref):
    span = pl.ds(pl.multiple_of(step * STEP, STEP), STEP)
    bias = jnp.concatenate(
        [jnp.full((1, BLOCK), jnp.where(flag, 0.0, NEG), jnp.float32) for flag in listed], axis=1
    )
    score_ref[...] = mm(left_ref[query_block], key_t_ref[:, span]) * LOG2E + bias


def unpack(packed_ref, count):
    total, width = packed_ref.shape
    rows = (total - 2 * width) // 2
    sizes = [rows] * (count - 2) + [width, width]
    return [packed_ref.at[pl.ds(sum(sizes[:k]), sizes[k])] for k in range(count)]


def project_kernel(heads, near_ref, left_ref, gleft_ref):
    ref_ref, gout_ref, wq_ref, wo_ref = unpack(near_ref, 4)
    rows, width = ref_ref.shape
    head_dim = width // heads
    query = bf(bf(mm(ref_ref[...], wq_ref[...])).astype(jnp.float32) * head_dim ** -0.5)
    grad = bf(mm_general(gout_ref[...], wo_ref[...], NT))
    for query_block in range(rows // BLOCK):
        span = slice(query_block * BLOCK, (query_block + 1) * BLOCK)
        for head in range(heads):
            own = lane_row(width, head, head_dim)
            left_ref[query_block, head * BLOCK : (head + 1) * BLOCK, :] = query[span] * own
            gleft_ref[query_block, head * BLOCK : (head + 1) * BLOCK, :] = grad[span] * own


def stats_kernel(
    heads, inter_ref, left_ref, gleft_ref, far_ref, src_ref,
    peak_ref, inverse_ref, col_ref, score_ref, product_ref,
    key_t_ref, value_t_ref, prob_ref, total_ref, col_peak_ref, col_total_ref, col_dot_ref,
):
    wk_ref, wv_ref = unpack(far_ref, 2)
    rows, key_total = left_ref.shape[0] * BLOCK, src_ref.shape[0]
    key_t_ref[...] = bf(mm_general(wk_ref[...], src_ref[...], TT))
    value_t_ref[...] = bf(mm_general(wv_ref[...], src_ref[...], TT))
    steps = key_total // STEP
    peak_ref[...] = jnp.full(peak_ref.shape, 2.0 * NEG, jnp.float32)
    total_ref[...] = jnp.zeros(total_ref.shape, jnp.float32)
    col_peak_ref[...] = jnp.full(col_peak_ref.shape, FLOOR, jnp.float32)
    col_total_ref[...] = jnp.zeros(col_total_ref.shape, jnp.float32)
    col_dot_ref[...] = jnp.zeros(col_dot_ref.shape, jnp.float32)
    tiles = [slice(first, first + 128) for first in range(0, STEP, 128)]

    def peaks(query_block, step, listed):
        block_ref = score_ref.at[query_block * steps + step]
        score_block(query_block, step, listed, left_ref, key_t_ref, block_ref)
        for head, spans in head_strips(heads):
            col_peaks = [col_peak_ref[step, head, :, lanes] for lanes in tiles]
            for span in spans:
                row_peak = peak_ref[query_block, span, :]
                for at, lanes in enumerate(tiles):
                    scores = block_ref[span, lanes]
                    row_peak = jnp.maximum(row_peak, scores)
                    col_peaks[at] = jnp.maximum(col_peaks[at], by_eight(scores).max(axis=0))
                peak_ref[query_block, span, :] = row_peak
            for at, lanes in enumerate(tiles):
                col_peak_ref[step, head, :, lanes] = col_peaks[at]

    each_listed(inter_ref, peaks)
    for query_block in range(rows // BLOCK):
        peak = peak_ref[query_block]
        peak_ref[query_block] = spread(peak.max(axis=1, keepdims=True), peak)
    for step in range(steps):
        for head in range(heads):
            peak = col_peak_ref[step, head]
            col_peak_ref[step, head] = spread(peak.max(axis=0, keepdims=True), peak)

    def totals(query_block, step, listed):
        score_now, product_now = [
            ref.at[query_block * steps + step] for ref in (score_ref, product_ref)
        ]
        span = pl.ds(pl.multiple_of(step * STEP, STEP), STEP)
        prob_ref[...] = mm(gleft_ref[query_block], value_t_ref[:, span])
        for head, spans in head_strips(heads):
            col_totals = [col_total_ref[step, head, :, lanes] for lanes in tiles]
            for span in spans:
                row_peak = by_eight(peak_ref[query_block, span, :])
                row_total = by_eight(total_ref[query_block, span, :])
                for at, lanes in enumerate(tiles):
                    scores = by_eight(score_now[span, lanes])
                    row_exp = jnp.exp2(scores - row_peak)
                    col_exp = jnp.exp2(scores - col_peak_ref[step, head, :, lanes][None])
                    row_total = row_total + row_exp
                    product = row_exp * col_exp * by_eight(prob_ref[span, lanes])
                    product_now[span, lanes] = bf(product.reshape(STRIP, 128))
                    col_totals[at] = col_totals[at] + col_exp.sum(axis=0)
                total_ref[query_block, span, :] = row_total.reshape(STRIP, 128)
            for at, lanes in enumerate(tiles):
                col_total_ref[step, head, :, lanes] = col_totals[at]

    each_listed(inter_ref, totals)
    for query_block in range(rows // BLOCK):
        total = total_ref[query_block]
        inverse_ref[query_block] = spread(1.0 / total.sum(axis=1, keepdims=True), total)

    def dots(query_block, step, listed):
        product_now = product_ref.at[query_block * steps + step]
        for head, spans in head_strips(heads):
            col_dots = [col_dot_ref[step, head, :, lanes] for lanes in tiles]
            for span in spans:
                inverse = inverse_ref[query_block, span, :]
                for at, lanes in enumerate(tiles):
                    product = by_eight(product_now[span, lanes].astype(jnp.float32) * inverse)
                    col_dots[at] = col_dots[at] + product.sum(axis=0)
            for at, lanes in enumerate(tiles):
                col_dot_ref[step, head, :, lanes] = col_dots[at]

    each_listed(inter_ref, dots)
    for step in range(steps):
        lanes = slice(step * STEP, (step + 1) * STEP)
        for head in range(heads):
            mine = slice(head, head + 1)
            col_ref[0, mine, lanes] = col_peak_ref[step, head, 0:1, :]
            col_ref[1, mine, lanes] = col_total_ref[step, head].sum(axis=0, keepdims=True)
            col_ref[2, mine, lanes] = col_dot_ref[step, head].sum(axis=0, keepdims=True)


def side_kernel(
    heads, near_ref, far_ref, src_ref, key_ref, value_ref, query_t_ref, grad_t_ref
):
    ref_ref, gout_ref, wq_ref, wo_ref = unpack(near_ref, 4)
    wk_ref, wv_ref = unpack(far_ref, 2)
    rows, width = ref_ref.shape
    head_dim = width // heads
    key_ref[...] = bf(mm(src_ref[...], wk_ref[...]))
    value_ref[...] = bf(mm(src_ref[...], wv_ref[...]))
    query_t = bf(mm_general(wq_ref[...], ref_ref[...], TT)).astype(jnp.float32)
    query_t = query_t * (2.0 * head_dim ** -0.5)
    grad_t = mm_general(wo_ref[...], gout_ref[...], NT)
    for query_block in range(rows // BLOCK):
        span = slice(query_block * BLOCK, (query_block + 1) * BLOCK)
        query_t_ref[query_block] = bf(query_t[:, span])
        grad_t_ref[query_block] = bf(grad_t[:, span])


def grads_kernel(
    heads, inter_ref, score_ref, product_ref, key_ref, value_ref,
    query_t_ref, grad_t_ref, peak_ref, inverse_ref, own_ref, near_ref, far_ref, packed_ref, src_ref,
    attended_ref, gquery_ref, gkey_ref, gvalue_ref, weight_ref,
    rest_ref, match_ref, gscore_ref, dot_ref, col_ref,
    att_ref, gq_ref, gk_ref, gv_ref,
):
    ref_ref, gout_ref = unpack(packed_ref, 4)[:2]
    rows, width = ref_ref.shape
    key_total = src_ref.shape[0]
    steps = key_total // STEP
    head_dim = width // heads
    tiles = [slice(first, first + 128) for first in range(0, STEP, 128)]

    peak = jnp.maximum(near_ref[0], far_ref[0])
    near, far = jnp.exp2(near_ref[0] - peak), jnp.exp2(far_ref[0] - peak)
    inverse = 1.0 / (near * near_ref[1] + far * far_ref[1])
    half = (near * near_ref[2] + far * far_ref[2]) * inverse * 0.5
    factor = jnp.exp2(own_ref[0] - peak) * inverse
    for kind, values in enumerate((peak, inverse, factor, half)):
        for head in range(heads):
            for step in range(steps):
                piece = values[head : head + 1, step * STEP : (step + 1) * STEP]
                col_ref[kind, step, head] = jnp.broadcast_to(piece, (8, STEP))
    for ref in (att_ref, gq_ref, gk_ref, gv_ref):
        ref[...] = jnp.zeros(ref.shape, jnp.float32)

    def products(query_block, step, listed):
        score_now, product_now = [
            ref.at[query_block * steps + step] for ref in (score_ref, product_ref)
        ]
        rest_now, match_now = rest_ref.at[step], match_ref.at[step]
        for head, spans in head_strips(heads):
            for span in spans:
                row_peak = by_eight(peak_ref[query_block, span, :])
                row_inverse = by_eight(inverse_ref[query_block, span, :])
                row_dot = by_eight(dot_ref[span, :])
                for lanes in tiles:
                    col_peak, col_inverse, col_factor, col_half = [
                        col_ref[kind, step, head, :, lanes][None] for kind in range(4)
                    ]
                    scores = by_eight(score_now[span, lanes])
                    row_prob = jnp.exp2(scores - row_peak) * row_inverse
                    col_prob = jnp.exp2(scores - col_peak) * col_inverse
                    product = by_eight(product_now[span, lanes].astype(jnp.float32))
                    product = product * row_inverse * col_factor
                    row_dot = row_dot + product
                    match_now[span, lanes] = bf((row_prob * col_prob).reshape(STRIP, 128))
                    rest_now[span, lanes] = (product - col_prob * col_half).reshape(STRIP, 128)
                dot_ref[span, :] = row_dot.reshape(STRIP, 128)

    def own_lanes(stacked):
        lane = lax.broadcasted_iota(jnp.int32, (BLOCK, 128), 1)
        tiles_out = []
        for first in range(0, width, 128):
            out = None
            for head in range(first // head_dim, (first + 128) // head_dim):
                piece = stacked[head * BLOCK : (head + 1) * BLOCK, first : first + 128]
                out = piece if out is None else jnp.where(lane < head * head_dim - first, out, piece)
            tiles_out.append(out)
        return jnp.concatenate(tiles_out, axis=1)

    def outputs(query_block, step, listed):
        score_now, rest_now, match_now = [
            score_ref.at[query_block * steps + step], rest_ref.at[step], match_ref.at[step]
        ]
        for _, spans in head_strips(heads):
            for span in spans:
                row_peak = peak_ref[query_block, span, :]
                row_half = dot_ref[span, :] * inverse_ref[query_block, span, :]
                for lanes in tiles:
                    row_part = jnp.exp2(score_now[span, lanes] - row_peak) * row_half
                    gscore_ref[span, lanes] = bf(rest_now[span, lanes] - row_part)
        span = pl.ds(pl.multiple_of(step * STEP, STEP), STEP)
        att_ref[query_block] += own_lanes(mm(match_now[...], value_ref[span, :]))
        gq_ref[query_block] += own_lanes(mm(gscore_ref[...], key_ref[span, :]))
        for head in range(heads):
            mine = slice(head * head_dim, (head + 1) * head_dim)
            rows_of = slice(head * BLOCK, (head + 1) * BLOCK)
            gk_ref[step, mine, :] += mm(query_t_ref[query_block, mine, :], gscore_ref[rows_of, :])
            gv_ref[step, mine, :] += mm(grad_t_ref[query_block, mine, :], match_now[rows_of, :])

    def query_rows(query_block, carry):
        dot_ref[...] = jnp.zeros(dot_ref.shape, jnp.float32)
        listed_steps(inter_ref, query_block, products)
        dot = dot_ref[...]
        dot_ref[...] = spread(dot.sum(axis=1, keepdims=True) * 0.5, dot)
        listed_steps(inter_ref, query_block, outputs)
        return carry

    lax.fori_loop(0, rows // BLOCK, query_rows, 0)
    attended = bf(att_ref[...]).reshape(rows, width)
    gquery = bf(gq_ref[...] * (2.0 * head_dim ** -0.5)).reshape(rows, width)
    attended_ref[...] = attended
    gquery_ref[...] = gquery
    for step in range(steps):
        gkey_ref[:, step * STEP : (step + 1) * STEP] = bf(gk_ref[step])
        gvalue_ref[:, step * STEP : (step + 1) * STEP] = bf(gv_ref[step])
    weight_ref[0] = bf(mm_general(ref_ref[...], gquery, TN))
    weight_ref[1] = bf(mm(gkey_ref[...], src_ref[...]).T)
    weight_ref[2] = bf(mm(gvalue_ref[...], src_ref[...]).T)
    weight_ref[3] = bf(mm_general(attended, gout_ref[...], TN))


def source_kernel(far_ref, gkey_ref, gvalue_ref, gsrc_ref):
    wk_ref, wv_ref = unpack(far_ref, 2)
    gsrc_t = mm(wk_ref[...], gkey_ref[...]) + mm(wv_ref[...], gvalue_ref[...])
    gsrc_ref[...] = bf(gsrc_t.T)


def rows_kernel(near_ref, attended_ref, gquery_ref, matched_ref, gref_ref):
    ref_ref, gout_ref, wq_ref, wo_ref = unpack(near_ref, 4)
    matched = ref_ref[...].astype(jnp.float32) + mm(attended_ref[...], wo_ref[...])
    matched_ref[...] = bf(matched)
    gref = gout_ref[...].astype(jnp.float32) + mm_general(gquery_ref[...], wq_ref[...], NT)
    gref_ref[...] = bf(gref)


def swap(x, axis, apart):
    pairs = [(i, i ^ apart) for i in range(lax.axis_size(axis))]
    return lax.ppermute(x, axis, pairs)


def at(x, index, axis=0):
    return lax.dynamic_index_in_dim(x, index, axis, False)


def laid(near, far, side, axis=0):
    shape = near.shape[:axis] + (2,) + near.shape[axis:]
    out = lax.dynamic_update_index_in_dim(jnp.zeros(shape, near.dtype), near, side, axis)
    return lax.dynamic_update_index_in_dim(out, far, 1 - side, axis)


def add(near, far):
    return (near.astype(jnp.float32) + far.astype(jnp.float32)).astype(near.dtype)


def halve(x, step, axis=0):
    mesh_axis, bit, side = step
    return add(at(x, side, axis), swap(at(x, 1 - side, axis), mesh_axis, bit))


def double(x, step, axis=0):
    mesh_axis, bit, side = step
    return laid(x, swap(x, mesh_axis, bit), side, axis)


def bit_steps(mesh_axis):
    me = lax.axis_index(mesh_axis)
    bits = range(lax.axis_size(mesh_axis).bit_length() - 1)
    return [(mesh_axis, 1 << bit, (me >> bit) % 2) for bit in bits]


def scatter_direct(x, mesh_axis):
    me, count = lax.axis_index(mesh_axis), lax.axis_size(mesh_axis)
    total = at(x, me).astype(jnp.float32)
    for piece in [swap(at(x, me ^ apart), mesh_axis, apart) for apart in range(1, count)]:
        total = total + piece.astype(jnp.float32)
    return total.astype(x.dtype)


def gather_direct(x, mesh_axis):
    me, count = lax.axis_index(mesh_axis), lax.axis_size(mesh_axis)
    pieces = [x] + [swap(x, mesh_axis, apart) for apart in range(1, count)]
    out = jnp.zeros((count,) + x.shape, x.dtype)
    for apart, piece in enumerate(pieces):
        out = lax.dynamic_update_index_in_dim(out, piece, me ^ apart, 0)
    return out


def combine_stats(parts):
    peak = functools.reduce(jnp.maximum, [part[0] for part in parts])
    factors = [jnp.exp2(part[0] - peak) for part in parts]
    total = sum(factor * part[1] for factor, part in zip(factors, parts))
    dots = sum(factor * part[2] for factor, part in zip(factors, parts))
    return jnp.stack([peak, total, dots])


def vmem_call(kernel, name, out_shape, scratch, limit, flops, moved, args, scalars=0):
    specs = [pl.BlockSpec(memory_space=pltpu.SMEM)] * scalars
    specs += [pl.BlockSpec(memory_space=pltpu.VMEM)] * (len(args) - scalars)
    return pl.pallas_call(
        kernel,
        name=name,
        out_shape=out_shape,
        in_specs=specs,
        out_specs=[pl.BlockSpec(memory_space=pltpu.VMEM)] * len(out_shape),
        scratch_shapes=scratch,
        compiler_params=pltpu.CompilerParams(vmem_limit_bytes=limit),
        cost_estimate=pl.CostEstimate(flops=flops, bytes_accessed=moved, transcendentals=0),
    )(*args)


def on_device(ref_feats, src_feats, grad_out, w_query, w_key, w_value, w_out, intersection):
    ref_rows = ref_feats[0]
    src_rows = src_feats[0]
    out_grad = grad_out[0]
    listed = jnp.where(intersection[0] == 1, 1, 0)
    rows, width = ref_rows.shape
    core_step = bit_steps("core")[0]
    chip_steps = bit_steps("chip")
    key_rows = src_rows.shape[0]
    key_total = key_rows * lax.axis_size("chip") * lax.axis_size("core")

    source_all = src_rows
    projections = (w_query, w_out, w_key, w_value)
    for count, step in enumerate(chip_steps[::-1]):
        source_all = double(source_all, step, count)
        if count == 0:
            source_all, projections = lax.optimization_barrier((source_all, projections))
    near_pack = jnp.concatenate([ref_rows, out_grad, *projections[:2]], axis=0)
    far_pack = jnp.concatenate(projections[2:], axis=0)
    source_all = double(source_all, core_step, len(chip_steps)).reshape(key_total, width)

    f32, b16 = jnp.float32, jnp.bfloat16
    shape, vmem = jax.ShapeDtypeStruct, pltpu.VMEM
    unit = 2 * rows * width * width
    query_blocks, steps = rows // BLOCK, key_total // STEP
    stacked = HEADS * BLOCK
    blocks = (query_blocks * steps, stacked, STEP)
    row_like = (query_blocks, stacked, 128)
    col_like = vmem((steps, HEADS, 8, STEP), f32)
    room = (16 << 20) + max(0, rows * key_total * HEADS * 18 - (36 << 20))
    left, grad_left = vmem_call(
        functools.partial(project_kernel, HEADS),
        "project_reference",
        [
            shape((query_blocks, stacked, width), b16),
            shape((query_blocks, stacked, width), b16),
        ],
        [],
        8 << 20,
        4 * unit,
        1 << 20,
        (near_pack,),
    )
    row_peak, row_inverse, col_stats, scores, product = vmem_call(
        functools.partial(stats_kernel, HEADS),
        "match_stats",
        [
            shape(row_like, f32),
            shape(row_like, f32),
            shape((3, HEADS, key_total), f32),
            shape(blocks, f32),
            shape(blocks, b16),
        ],
        [
            vmem((width, key_total), b16),
            vmem((width, key_total), b16),
            vmem((stacked, STEP), f32),
            vmem(row_like, f32),
            col_like,
            col_like,
            col_like,
        ],
        room,
        60 * unit,
        8 << 20,
        (listed, left, grad_left, far_pack, source_all),
        scalars=1,
    )
    near_stats = col_stats
    keys, values, query_t, grad_t = vmem_call(
        functools.partial(side_kernel, HEADS),
        "project_for_grads",
        [
            shape((key_total, width), b16),
            shape((key_total, width), b16),
            shape((query_blocks, width, BLOCK), b16),
            shape((query_blocks, width, BLOCK), b16),
        ],
        [],
        8 << 20,
        8 * unit,
        2 << 20,
        (near_pack, far_pack, source_all),
    )
    for mesh_axis, bit, _ in chip_steps:
        near_stats = combine_stats([near_stats, swap(near_stats, mesh_axis, bit)])
    far_stats = swap(near_stats, "core", 1)
    attended, grad_query, grad_key, grad_value, weight_part = vmem_call(
        functools.partial(grads_kernel, HEADS),
        "match_grads",
        [
            shape((rows, width), b16),
            shape((rows, width), b16),
            shape((width, key_total), b16),
            shape((width, key_total), b16),
            shape((4, width, width), b16),
        ],
        [
            vmem((steps, stacked, STEP), f32),
            vmem((steps, stacked, STEP), b16),
            vmem((stacked, STEP), b16),
            vmem((stacked, 128), f32),
            vmem((4, steps, HEADS, 8, STEP), f32),
            vmem((query_blocks, BLOCK, width), f32),
            vmem((query_blocks, BLOCK, width), f32),
            vmem((steps, width, STEP), f32),
            vmem((steps, width, STEP), f32),
        ],
        room,
        100 * unit,
        8 << 20,
        (listed, scores, product, keys, values, query_t, grad_t, row_peak, row_inverse, col_stats,
         near_stats, far_stats, near_pack, source_all),
        scalars=1,
    )
    (source_part,) = vmem_call(
        source_kernel,
        "source_grads",
        [shape((key_total, width), b16)],
        [],
        8 << 20,
        8 * unit,
        2 << 20,
        (far_pack, grad_key, grad_value),
    )

    scans = lax.axis_size("scan")
    weights = weight_part.reshape((2, scans // 2, 2, -1, width))
    sources = source_part.reshape((2,) * (len(chip_steps) + 1) + (key_rows, width))
    source_steps = list(zip(chip_steps, range(len(chip_steps) - 1, -1, -1)))
    weights = halve(weights, core_step)
    sources = halve(sources, core_step, len(chip_steps))
    weights = scatter_direct(weights.reshape((scans,) + weights.shape[2:]), "scan")
    sources = halve(sources, *source_steps[0])
    weights, attended, grad_query = lax.optimization_barrier((weights, attended, grad_query))
    matched, grad_ref = vmem_call(
        rows_kernel,
        "row_outputs",
        [shape((rows, width), b16), shape((rows, width), b16)],
        [],
        8 << 20,
        4 * unit,
        2 << 20,
        (near_pack, attended, grad_query),
    )
    for step in source_steps[1:]:
        sources = halve(sources, *step)
    for mesh_axis, bit, _ in chip_steps:
        weights = add(weights, swap(weights, mesh_axis, bit))
    weights, grad_src = lax.optimization_barrier((weights, sources))
    weights = gather_direct(weights, "scan")
    weights = double(weights, core_step)
    weights = weights.reshape(4, width, width).astype(f32)
    return (
        matched[None],
        grad_ref[None],
        grad_src[None],
        weights[0],
        weights[1],
        weights[2],
        weights[3],
    )


def solution(mesh):
    scans, blks = mesh.shape["scan"], mesh.shape["blk"]
    mesh = jax.sharding.Mesh(
        mesh.devices.reshape(scans, blks // 2, 2), ("scan", "chip", "core")
    )
    split = P("scan", ("chip", "core"), None)
    whole = P()
    return jax.shard_map(
        on_device,
        mesh=mesh,
        in_specs=(split, split, split, whole, whole, whole, whole, split),
        out_specs=(split, split, split, whole, whole, whole, whole),
        check_vma=False,
    )
```

```python
import functools
import math

import jax
import jax.numpy as jnp
from jax import lax
from jax.experimental import pallas as pl
from jax.experimental.pallas import tpu as pltpu
from jax.sharding import PartitionSpec as P

HEADS = 4
BLOCK = 128
NEG = -1e30
FLOOR = -1e29
LOG2E = math.log2(math.e)

NT = (((1,), (1,)), ((), ()))
TN = (((0,), (0,)), ((), ()))
TT = (((0,), (1,)), ((), ()))


def mm(left, right):
    return jnp.dot(left, right, preferred_element_type=jnp.float32)


def mm_general(left, right, dims):
    return lax.dot_general(left, right, dims, preferred_element_type=jnp.float32)


def bf(x):
    return x.astype(jnp.bfloat16)


def lane_row(width, head, head_dim):
    lanes = lax.broadcasted_iota(jnp.int32, (1, width), 1) // head_dim
    return bf(jnp.where(lanes == head, 1.0, 0.0))


def spread(reduced, like):
    return jnp.broadcast_to(reduced, like.shape)


STRIP = 64
STEP = 256


def by_eight(x):
    return x.reshape(x.shape[0] // 8, 8, x.shape[1])


def listed_steps(inter_ref, query_block, work):
    per_step = STEP // BLOCK

    def visit(step, carry):
        listed = [inter_ref[query_block, step * per_step + k] == 1 for k in range(per_step)]

        @pl.when(functools.reduce(jnp.logical_or, listed))
        def _():
            work(query_block, step, listed)

        return carry

    lax.fori_loop(0, inter_ref.shape[1] // per_step, visit, 0)


def each_listed(inter_ref, work):
    def visit(query_block, carry):
        listed_steps(inter_ref, query_block, work)
        return carry

    lax.fori_loop(0, inter_ref.shape[0], visit, 0)


def head_strips(heads):
    for head in range(heads):
        spans = [slice(first, first + STRIP) for first in range(0, BLOCK, STRIP)]
        yield head, [slice(head * BLOCK + a.start, head * BLOCK + a.stop) for a in spans]


def score_block(query_block, step, listed, left_ref, key_t_ref, score_ref):
    span = pl.ds(pl.multiple_of(step * STEP, STEP), STEP)
    bias = jnp.concatenate(
        [jnp.full((1, BLOCK), jnp.where(flag, 0.0, NEG), jnp.float32) for flag in listed], axis=1
    )
    score_ref[...] = mm(left_ref[query_block], key_t_ref[:, span]) * LOG2E + bias


def unpack(packed_ref, count):
    total, width = packed_ref.shape
    rows = (total - 2 * width) // 2
    sizes = [rows] * (count - 2) + [width, width]
    return [packed_ref.at[pl.ds(sum(sizes[:k]), sizes[k])] for k in range(count)]


def project_kernel(heads, near_ref, left_ref, gleft_ref):
    ref_ref, gout_ref, wq_ref, wo_ref = unpack(near_ref, 4)
    rows, width = ref_ref.shape
    head_dim = width // heads
    query = bf(bf(mm(ref_ref[...], wq_ref[...])).astype(jnp.float32) * head_dim ** -0.5)
    grad = bf(mm_general(gout_ref[...], wo_ref[...], NT))
    for query_block in range(rows // BLOCK):
        span = slice(query_block * BLOCK, (query_block + 1) * BLOCK)
        for head in range(heads):
            own = lane_row(width, head, head_dim)
            left_ref[query_block, head * BLOCK : (head + 1) * BLOCK, :] = query[span] * own
            gleft_ref[query_block, head * BLOCK : (head + 1) * BLOCK, :] = grad[span] * own


def stats_kernel(
    heads, inter_ref, left_ref, gleft_ref, far_ref, src_ref,
    peak_ref, inverse_ref, col_ref, score_ref, product_ref,
    key_t_ref, value_t_ref, prob_ref, total_ref, col_peak_ref, col_total_ref, col_dot_ref,
):
    wk_ref, wv_ref = unpack(far_ref, 2)
    rows, key_total = left_ref.shape[0] * BLOCK, src_ref.shape[0]
    key_t_ref[...] = bf(mm_general(wk_ref[...], src_ref[...], TT))
    value_t_ref[...] = bf(mm_general(wv_ref[...], src_ref[...], TT))
    steps = key_total // STEP
    peak_ref[...] = jnp.full(peak_ref.shape, 2.0 * NEG, jnp.float32)
    total_ref[...] = jnp.zeros(total_ref.shape, jnp.float32)
    col_peak_ref[...] = jnp.full(col_peak_ref.shape, FLOOR, jnp.float32)
    col_total_ref[...] = jnp.zeros(col_total_ref.shape, jnp.float32)
    col_dot_ref[...] = jnp.zeros(col_dot_ref.shape, jnp.float32)
    tiles = [slice(first, first + 128) for first in range(0, STEP, 128)]

    def peaks(query_block, step, listed):
        block_ref = score_ref.at[query_block * steps + step]
        score_block(query_block, step, listed, left_ref, key_t_ref, block_ref)
        for head, spans in head_strips(heads):
            col_peaks = [col_peak_ref[step, head, :, lanes] for lanes in tiles]
            for span in spans:
                row_peak = peak_ref[query_block, span, :]
                for at, lanes in enumerate(tiles):
                    scores = block_ref[span, lanes]
                    row_peak = jnp.maximum(row_peak, scores)
                    col_peaks[at] = jnp.maximum(col_peaks[at], by_eight(scores).max(axis=0))
                peak_ref[query_block, span, :] = row_peak
            for at, lanes in enumerate(tiles):
                col_peak_ref[step, head, :, lanes] = col_peaks[at]

    each_listed(inter_ref, peaks)
    for query_block in range(rows // BLOCK):
        peak = peak_ref[query_block]
        peak_ref[query_block] = spread(peak.max(axis=1, keepdims=True), peak)
    for step in range(steps):
        for head in range(heads):
            peak = col_peak_ref[step, head]
            col_peak_ref[step, head] = spread(peak.max(axis=0, keepdims=True), peak)

    def totals(query_block, step, listed):
        score_now, product_now = [
            ref.at[query_block * steps + step] for ref in (score_ref, product_ref)
        ]
        span = pl.ds(pl.multiple_of(step * STEP, STEP), STEP)
        prob_ref[...] = mm(gleft_ref[query_block], value_t_ref[:, span])
        for head, spans in head_strips(heads):
            col_totals = [col_total_ref[step, head, :, lanes] for lanes in tiles]
            for span in spans:
                row_peak = by_eight(peak_ref[query_block, span, :])
                row_total = by_eight(total_ref[query_block, span, :])
                for at, lanes in enumerate(tiles):
                    scores = by_eight(score_now[span, lanes])
                    row_exp = jnp.exp2(scores - row_peak)
                    col_exp = jnp.exp2(scores - col_peak_ref[step, head, :, lanes][None])
                    row_total = row_total + row_exp
                    product = row_exp * col_exp * by_eight(prob_ref[span, lanes])
                    product_now[span, lanes] = bf(product.reshape(STRIP, 128))
                    col_totals[at] = col_totals[at] + col_exp.sum(axis=0)
                total_ref[query_block, span, :] = row_total.reshape(STRIP, 128)
            for at, lanes in enumerate(tiles):
                col_total_ref[step, head, :, lanes] = col_totals[at]

    each_listed(inter_ref, totals)
    for query_block in range(rows // BLOCK):
        total = total_ref[query_block]
        inverse_ref[query_block] = spread(1.0 / total.sum(axis=1, keepdims=True), total)

    def dots(query_block, step, listed):
        product_now = product_ref.at[query_block * steps + step]
        for head, spans in head_strips(heads):
            col_dots = [col_dot_ref[step, head, :, lanes] for lanes in tiles]
            for span in spans:
                inverse = inverse_ref[query_block, span, :]
                for at, lanes in enumerate(tiles):
                    product = by_eight(product_now[span, lanes].astype(jnp.float32) * inverse)
                    col_dots[at] = col_dots[at] + product.sum(axis=0)
            for at, lanes in enumerate(tiles):
                col_dot_ref[step, head, :, lanes] = col_dots[at]

    each_listed(inter_ref, dots)
    for step in range(steps):
        lanes = slice(step * STEP, (step + 1) * STEP)
        for head in range(heads):
            mine = slice(head, head + 1)
            col_ref[0, mine, lanes] = col_peak_ref[step, head, 0:1, :]
            col_ref[1, mine, lanes] = col_total_ref[step, head].sum(axis=0, keepdims=True)
            col_ref[2, mine, lanes] = col_dot_ref[step, head].sum(axis=0, keepdims=True)


def side_kernel(
    heads, near_ref, far_ref, src_ref, key_ref, value_ref, query_t_ref, grad_t_ref
):
    ref_ref, gout_ref, wq_ref, wo_ref = unpack(near_ref, 4)
    wk_ref, wv_ref = unpack(far_ref, 2)
    rows, width = ref_ref.shape
    head_dim = width // heads
    key_ref[...] = bf(mm(src_ref[...], wk_ref[...]))
    value_ref[...] = bf(mm(src_ref[...], wv_ref[...]))
    query_t = bf(mm_general(wq_ref[...], ref_ref[...], TT)).astype(jnp.float32)
    query_t = query_t * (2.0 * head_dim ** -0.5)
    grad_t = mm_general(wo_ref[...], gout_ref[...], NT)
    for query_block in range(rows // BLOCK):
        span = slice(query_block * BLOCK, (query_block + 1) * BLOCK)
        query_t_ref[query_block] = bf(query_t[:, span])
        grad_t_ref[query_block] = bf(grad_t[:, span])


def grads_kernel(
    heads, inter_ref, score_ref, product_ref, key_ref, value_ref,
    query_t_ref, grad_t_ref, peak_ref, inverse_ref, own_ref, near_ref, far_ref, packed_ref, src_ref,
    attended_ref, gquery_ref, gkey_ref, gvalue_ref, weight_ref,
    rest_ref, match_ref, gscore_ref, dot_ref, col_ref,
    att_ref, gq_ref, gk_ref, gv_ref,
):
    ref_ref, gout_ref = unpack(packed_ref, 4)[:2]
    rows, width = ref_ref.shape
    key_total = src_ref.shape[0]
    steps = key_total // STEP
    head_dim = width // heads
    tiles = [slice(first, first + 128) for first in range(0, STEP, 128)]

    peak = jnp.maximum(near_ref[0], far_ref[0])
    near, far = jnp.exp2(near_ref[0] - peak), jnp.exp2(far_ref[0] - peak)
    inverse = 1.0 / (near * near_ref[1] + far * far_ref[1])
    half = (near * near_ref[2] + far * far_ref[2]) * inverse * 0.5
    factor = jnp.exp2(own_ref[0] - peak) * inverse
    for kind, values in enumerate((peak, inverse, factor, half)):
        for head in range(heads):
            for step in range(steps):
                piece = values[head : head + 1, step * STEP : (step + 1) * STEP]
                col_ref[kind, step, head] = jnp.broadcast_to(piece, (8, STEP))
    for ref in (att_ref, gq_ref, gk_ref, gv_ref):
        ref[...] = jnp.zeros(ref.shape, jnp.float32)

    def products(query_block, step, listed):
        score_now, product_now = [
            ref.at[query_block * steps + step] for ref in (score_ref, product_ref)
        ]
        rest_now, match_now = rest_ref.at[step], match_ref.at[step]
        for head, spans in head_strips(heads):
            for span in spans:
                row_peak = by_eight(peak_ref[query_block, span, :])
                row_inverse = by_eight(inverse_ref[query_block, span, :])
                row_dot = by_eight(dot_ref[span, :])
                for lanes in tiles:
                    col_peak, col_inverse, col_factor, col_half = [
                        col_ref[kind, step, head, :, lanes][None] for kind in range(4)
                    ]
                    scores = by_eight(score_now[span, lanes])
                    row_prob = jnp.exp2(scores - row_peak) * row_inverse
                    col_prob = jnp.exp2(scores - col_peak) * col_inverse
                    product = by_eight(product_now[span, lanes].astype(jnp.float32))
                    product = product * row_inverse * col_factor
                    row_dot = row_dot + product
                    match_now[span, lanes] = bf((row_prob * col_prob).reshape(STRIP, 128))
                    rest_now[span, lanes] = (product - col_prob * col_half).reshape(STRIP, 128)
                dot_ref[span, :] = row_dot.reshape(STRIP, 128)

    def own_lanes(stacked):
        lane = lax.broadcasted_iota(jnp.int32, (BLOCK, 128), 1)
        tiles_out = []
        for first in range(0, width, 128):
            out = None
            for head in range(first // head_dim, (first + 128) // head_dim):
                piece = stacked[head * BLOCK : (head + 1) * BLOCK, first : first + 128]
                out = piece if out is None else jnp.where(lane < head * head_dim - first, out, piece)
            tiles_out.append(out)
        return jnp.concatenate(tiles_out, axis=1)

    def outputs(query_block, step, listed):
        score_now, rest_now, match_now = [
            score_ref.at[query_block * steps + step], rest_ref.at[step], match_ref.at[step]
        ]
        for _, spans in head_strips(heads):
            for span in spans:
                row_peak = peak_ref[query_block, span, :]
                row_half = dot_ref[span, :] * inverse_ref[query_block, span, :]
                for lanes in tiles:
                    row_part = jnp.exp2(score_now[span, lanes] - row_peak) * row_half
                    gscore_ref[span, lanes] = bf(rest_now[span, lanes] - row_part)
        span = pl.ds(pl.multiple_of(step * STEP, STEP), STEP)
        att_ref[query_block] += own_lanes(mm(match_now[...], value_ref[span, :]))
        gq_ref[query_block] += own_lanes(mm(gscore_ref[...], key_ref[span, :]))
        for head in range(heads):
            mine = slice(head * head_dim, (head + 1) * head_dim)
            rows_of = slice(head * BLOCK, (head + 1) * BLOCK)
            gk_ref[step, mine, :] += mm(query_t_ref[query_block, mine, :], gscore_ref[rows_of, :])
            gv_ref[step, mine, :] += mm(grad_t_ref[query_block, mine, :], match_now[rows_of, :])

    def query_rows(query_block, carry):
        dot_ref[...] = jnp.zeros(dot_ref.shape, jnp.float32)
        listed_steps(inter_ref, query_block, products)
        dot = dot_ref[...]
        dot_ref[...] = spread(dot.sum(axis=1, keepdims=True) * 0.5, dot)
        listed_steps(inter_ref, query_block, outputs)
        return carry

    lax.fori_loop(0, rows // BLOCK, query_rows, 0)
    attended = bf(att_ref[...]).reshape(rows, width)
    gquery = bf(gq_ref[...] * (2.0 * head_dim ** -0.5)).reshape(rows, width)
    attended_ref[...] = attended
    gquery_ref[...] = gquery
    for step in range(steps):
        gkey_ref[:, step * STEP : (step + 1) * STEP] = bf(gk_ref[step])
        gvalue_ref[:, step * STEP : (step + 1) * STEP] = bf(gv_ref[step])
    weight_ref[0] = bf(mm_general(ref_ref[...], gquery, TN))
    weight_ref[1] = bf(mm(gkey_ref[...], src_ref[...]).T)
    weight_ref[2] = bf(mm(gvalue_ref[...], src_ref[...]).T)
    weight_ref[3] = bf(mm_general(attended, gout_ref[...], TN))


def source_kernel(far_ref, gkey_ref, gvalue_ref, gsrc_ref):
    wk_ref, wv_ref = unpack(far_ref, 2)
    gsrc_t = mm(wk_ref[...], gkey_ref[...]) + mm(wv_ref[...], gvalue_ref[...])
    gsrc_ref[...] = bf(gsrc_t.T)


def rows_kernel(near_ref, attended_ref, gquery_ref, matched_ref, gref_ref):
    ref_ref, gout_ref, wq_ref, wo_ref = unpack(near_ref, 4)
    matched = ref_ref[...].astype(jnp.float32) + mm(attended_ref[...], wo_ref[...])
    matched_ref[...] = bf(matched)
    gref = gout_ref[...].astype(jnp.float32) + mm_general(gquery_ref[...], wq_ref[...], NT)
    gref_ref[...] = bf(gref)


def swap(x, axis, apart):
    pairs = [(i, i ^ apart) for i in range(lax.axis_size(axis))]
    return lax.ppermute(x, axis, pairs)


def at(x, index, axis=0):
    return lax.dynamic_index_in_dim(x, index, axis, False)


def laid(near, far, side, axis=0):
    shape = near.shape[:axis] + (2,) + near.shape[axis:]
    out = lax.dynamic_update_index_in_dim(jnp.zeros(shape, near.dtype), near, side, axis)
    return lax.dynamic_update_index_in_dim(out, far, 1 - side, axis)


def add(near, far):
    return (near.astype(jnp.float32) + far.astype(jnp.float32)).astype(near.dtype)


def halve(x, step, axis=0):
    mesh_axis, bit, side = step
    return add(at(x, side, axis), swap(at(x, 1 - side, axis), mesh_axis, bit))


def double(x, step, axis=0):
    mesh_axis, bit, side = step
    return laid(x, swap(x, mesh_axis, bit), side, axis)


def bit_steps(mesh_axis):
    me = lax.axis_index(mesh_axis)
    bits = range(lax.axis_size(mesh_axis).bit_length() - 1)
    return [(mesh_axis, 1 << bit, (me >> bit) % 2) for bit in bits]


def scatter_direct(x, mesh_axis):
    me, count = lax.axis_index(mesh_axis), lax.axis_size(mesh_axis)
    total = at(x, me).astype(jnp.float32)
    for piece in [swap(at(x, me ^ apart), mesh_axis, apart) for apart in range(1, count)]:
        total = total + piece.astype(jnp.float32)
    return total.astype(x.dtype)


def gather_direct(x, mesh_axis):
    me, count = lax.axis_index(mesh_axis), lax.axis_size(mesh_axis)
    pieces = [x] + [swap(x, mesh_axis, apart) for apart in range(1, count)]
    out = jnp.zeros((count,) + x.shape, x.dtype)
    for apart, piece in enumerate(pieces):
        out = lax.dynamic_update_index_in_dim(out, piece, me ^ apart, 0)
    return out


def combine_stats(parts):
    peak = functools.reduce(jnp.maximum, [part[0] for part in parts])
    factors = [jnp.exp2(part[0] - peak) for part in parts]
    total = sum(factor * part[1] for factor, part in zip(factors, parts))
    dots = sum(factor * part[2] for factor, part in zip(factors, parts))
    return jnp.stack([peak, total, dots])


def vmem_call(kernel, name, out_shape, scratch, limit, flops, moved, args, scalars=0):
    specs = [pl.BlockSpec(memory_space=pltpu.SMEM)] * scalars
    specs += [pl.BlockSpec(memory_space=pltpu.VMEM)] * (len(args) - scalars)
    return pl.pallas_call(
        kernel,
        name=name,
        out_shape=out_shape,
        in_specs=specs,
        out_specs=[pl.BlockSpec(memory_space=pltpu.VMEM)] * len(out_shape),
        scratch_shapes=scratch,
        compiler_params=pltpu.CompilerParams(vmem_limit_bytes=limit),
        cost_estimate=pl.CostEstimate(flops=flops, bytes_accessed=moved, transcendentals=0),
    )(*args)


def on_device(ref_feats, src_feats, grad_out, w_query, w_key, w_value, w_out, intersection):
    ref_rows = ref_feats[0]
    src_rows = src_feats[0]
    out_grad = grad_out[0]
    listed = jnp.where(intersection[0] == 1, 1, 0)
    rows, width = ref_rows.shape
    core_step = bit_steps("core")[0]
    chip_steps = bit_steps("chip")
    key_rows = src_rows.shape[0]
    key_total = key_rows * lax.axis_size("chip") * lax.axis_size("core")

    source_all = src_rows
    projections = (w_query, w_out, w_key, w_value)
    for count, step in enumerate(chip_steps[::-1]):
        source_all = double(source_all, step, count)
        if count == 0:
            source_all, projections = lax.optimization_barrier((source_all, projections))
    near_pack = jnp.concatenate([ref_rows, out_grad, *projections[:2]], axis=0)
    far_pack = jnp.concatenate(projections[2:], axis=0)
    source_all = double(source_all, core_step, len(chip_steps)).reshape(key_total, width)

    f32, b16 = jnp.float32, jnp.bfloat16
    shape, vmem = jax.ShapeDtypeStruct, pltpu.VMEM
    unit = 2 * rows * width * width
    query_blocks, steps = rows // BLOCK, key_total // STEP
    stacked = HEADS * BLOCK
    blocks = (query_blocks * steps, stacked, STEP)
    row_like = (query_blocks, stacked, 128)
    col_like = vmem((steps, HEADS, 8, STEP), f32)
    room = (16 << 20) + max(0, rows * key_total * HEADS * 18 - (36 << 20))
    left, grad_left = vmem_call(
        functools.partial(project_kernel, HEADS),
        "project_reference",
        [
            shape((query_blocks, stacked, width), b16),
            shape((query_blocks, stacked, width), b16),
        ],
        [],
        8 << 20,
        4 * unit,
        1 << 20,
        (near_pack,),
    )
    row_peak, row_inverse, col_stats, scores, product = vmem_call(
        functools.partial(stats_kernel, HEADS),
        "match_stats",
        [
            shape(row_like, f32),
            shape(row_like, f32),
            shape((3, HEADS, key_total), f32),
            shape(blocks, f32),
            shape(blocks, b16),
        ],
        [
            vmem((width, key_total), b16),
            vmem((width, key_total), b16),
            vmem((stacked, STEP), f32),
            vmem(row_like, f32),
            col_like,
            col_like,
            col_like,
        ],
        room,
        60 * unit,
        8 << 20,
        (listed, left, grad_left, far_pack, source_all),
        scalars=1,
    )
    near_stats = col_stats
    keys, values, query_t, grad_t = vmem_call(
        functools.partial(side_kernel, HEADS),
        "project_for_grads",
        [
            shape((key_total, width), b16),
            shape((key_total, width), b16),
            shape((query_blocks, width, BLOCK), b16),
            shape((query_blocks, width, BLOCK), b16),
        ],
        [],
        8 << 20,
        8 * unit,
        2 << 20,
        (near_pack, far_pack, source_all),
    )
    for mesh_axis, bit, _ in chip_steps:
        near_stats = combine_stats([near_stats, swap(near_stats, mesh_axis, bit)])
    far_stats = swap(near_stats, "core", 1)
    attended, grad_query, grad_key, grad_value, weight_part = vmem_call(
        functools.partial(grads_kernel, HEADS),
        "match_grads",
        [
            shape((rows, width), b16),
            shape((rows, width), b16),
            shape((width, key_total), b16),
            shape((width, key_total), b16),
            shape((4, width, width), b16),
        ],
        [
            vmem((steps, stacked, STEP), f32),
            vmem((steps, stacked, STEP), b16),
            vmem((stacked, STEP), b16),
            vmem((stacked, 128), f32),
            vmem((4, steps, HEADS, 8, STEP), f32),
            vmem((query_blocks, BLOCK, width), f32),
            vmem((query_blocks, BLOCK, width), f32),
            vmem((steps, width, STEP), f32),
            vmem((steps, width, STEP), f32),
        ],
        room,
        100 * unit,
        8 << 20,
        (listed, scores, product, keys, values, query_t, grad_t, row_peak, row_inverse, col_stats,
         near_stats, far_stats, near_pack, source_all),
        scalars=1,
    )
    (source_part,) = vmem_call(
        source_kernel,
        "source_grads",
        [shape((key_total, width), b16)],
        [],
        8 << 20,
        8 * unit,
        2 << 20,
        (far_pack, grad_key, grad_value),
    )

    scans = lax.axis_size("scan")
    weights = weight_part.reshape((2, scans // 2, 2, -1, width))
    sources = source_part.reshape((2,) * (len(chip_steps) + 1) + (key_rows, width))
    source_steps = list(zip(chip_steps, range(len(chip_steps) - 1, -1, -1)))
    weights = halve(weights, core_step)
    sources = halve(sources, core_step, len(chip_steps))
    weights = lax.optimization_barrier(weights)
    weights = scatter_direct(weights.reshape((scans,) + weights.shape[2:]), "scan")
    sources = halve(sources, *source_steps[0])
    weights, attended, grad_query = lax.optimization_barrier((weights, attended, grad_query))
    matched, grad_ref = vmem_call(
        rows_kernel,
        "row_outputs",
        [shape((rows, width), b16), shape((rows, width), b16)],
        [],
        8 << 20,
        4 * unit,
        2 << 20,
        (near_pack, attended, grad_query),
    )
    for step in source_steps[1:]:
        sources = halve(sources, *step)
    for mesh_axis, bit, _ in chip_steps:
        weights = add(weights, swap(weights, mesh_axis, bit))
    weights, grad_src = lax.optimization_barrier((weights, sources))
    weights = gather_direct(weights, "scan")
    weights = double(weights, core_step)
    weights = weights.reshape(4, width, width).astype(f32)
    return (
        matched[None],
        grad_ref[None],
        grad_src[None],
        weights[0],
        weights[1],
        weights[2],
        weights[3],
    )


def solution(mesh):
    scans, blks = mesh.shape["scan"], mesh.shape["blk"]
    mesh = jax.sharding.Mesh(
        mesh.devices.reshape(scans, blks // 2, 2), ("scan", "chip", "core")
    )
    split = P("scan", ("chip", "core"), None)
    whole = P()
    return jax.shard_map(
        on_device,
        mesh=mesh,
        in_specs=(split, split, split, whole, whole, whole, whole, split),
        out_specs=(split, split, split, whole, whole, whole, whole),
        check_vma=False,
    )
```
